32 devices in a mesh: dom: 8 (over z, core), sub: 4 (over y, x).
Axes of the slice: x: 2, y: 2, z: 4, core: 2. Of those that a mesh axis runs over, the one named last changes fastest.
Arguments:
- state: bfloat16 [32768, 256], P(('dom', 'sub')), may hold values from -6 to 6
- tile_values: float32 [32, 24, 128, 128], P(('dom', 'sub')), may hold values from 0.0003125 to 0.009375
- tile_rows: int32 [32, 24], P(('dom', 'sub')), may hold values from 0 to 7, as said below
- tile_columns: int32 [32, 24], P(('dom', 'sub')), may hold values from 0 to 7, as said below
- tile_counts: int32 [32], P(('dom', 'sub')), may hold values from 8 to 24, as said below
- send_nodes: int32 [32, 4, 256], P(('dom', 'sub')), may hold values from 0 to 1023
- face_counts: int32 [32, 4], P(('dom', 'sub')), may hold values from 0 to 256, as said below
- capacity: float32 [32768], P(('dom', 'sub')), may hold values from 0.05 to 2
- source: float32 [32768], P(('dom', 'sub')), may hold values from -12 to 12
- w_self: bfloat16 [2, 256, 256], replicated, may hold values from -0.375 to 0.375
- w_neighbour: bfloat16 [2, 256, 256], replicated, may hold values from -0.375 to 0.375
- w_out: bfloat16 [2, 256, 256], replicated, may hold values from -0.375 to 0.375
- gains: float32 [2, 2, 256], replicated, may hold values from 0.25 to 1.75
- bias: float32 [2, 256], replicated, may hold values from -3 to 3
- w_decode: float32 [256], replicated, may hold values from -0.375 to 0.375
Outputs:
- heat_level_field: float32 [32768], P(('dom', 'sub'))
- equation_defect: float32 [32768], P(('dom', 'sub'))
The draws below stay inside these ranges and needn't reach their ends.
Inputs may be any that keep to these rules, and one draw needn't show every extreme that they name: `tile_counts`: slots at or beyond a device's count are ignored; some device has all 24 slots live. `tile_rows`: slot t < 8 names tile t, in tile_columns as well. `tile_columns`: slot t < 8 names tile t, in tile_rows as well. `face_counts`: two neighbouring devices give each other the same count; the count is 0 toward a side where the slice has no neighbour; some pair of neighbours fills all 256 slots.
All inputs are finite; a program needn't handle non-finite values.
Results may differ from the reference program's by a relative error of at most 0.005.
Values may be sent and summed in bfloat16 or wider, within the bound.
No kernel may reach another device: no remote copies, remote signals or barrier semaphores. Data moves between devices by JAX's collectives and lax.ppermute only.
A program may use at most 64 MiB of HBM per device.

```python
import math
import jax
import jax.numpy as jnp
from jax import lax

F = 256
TILE = 128
TL = 8
LAYERS = 2
ITERS = 3
NB = 24
IFACE = 256
NODE_DEV = 1024
VERTEX_NUMBER = 32768
N_DOM = 8
N_SUB = 4
DEVICES = 32


def slot_tiles(key, salt):
    drawn = jax.random.randint(jax.random.fold_in(key, salt), (DEVICES, NB), 0, TL)
    own = jnp.arange(TL, dtype=jnp.int32)[None, :] + jnp.zeros((DEVICES, 1), jnp.int32)
    return drawn.at[:, :TL].set(own).astype(jnp.int32)


def draw_tile_rows(key, part):
    return slot_tiles(key, 11)


def draw_tile_columns(key, part):
    return slot_tiles(key, 13)


def draw_tile_counts(key, part):
    counts = jax.random.randint(key, (DEVICES,), TL, NB + 1)
    fullest = jax.random.randint(jax.random.fold_in(key, 7), (), 0, DEVICES)
    return counts.at[fullest].set(NB).astype(jnp.int32)


def draw_face_counts(key, part):
    dom_edges = jax.random.randint(jax.random.fold_in(key, 1), ((N_DOM - 1) * N_SUB,), IFACE // 4, IFACE + 1)
    fullest = jax.random.randint(jax.random.fold_in(key, 3), (), 0, (N_DOM - 1) * N_SUB)
    dom_edges = dom_edges.at[fullest].set(IFACE).reshape(N_DOM - 1, N_SUB)
    sub_edges = jax.random.randint(jax.random.fold_in(key, 2), (N_DOM, N_SUB - 1), IFACE // 4, IFACE + 1)
    zero_row = jnp.zeros((1, N_SUB), jnp.int32)
    zero_column = jnp.zeros((N_DOM, 1), jnp.int32)
    toward_low = jnp.concatenate([zero_row, dom_edges], axis=0)
    toward_upper_side = jnp.concatenate([dom_edges, zero_row], axis=0)
    toward_left = jnp.concatenate([zero_column, sub_edges], axis=1)
    toward_right = jnp.concatenate([sub_edges, zero_column], axis=1)
    stacked = jnp.stack([toward_low, toward_upper_side, toward_left, toward_right], axis=-1)
    return stacked.reshape(DEVICES, 4).astype(jnp.int32)


def draw_source(key, part):
    position = jnp.arange(VERTEX_NUMBER, dtype=jnp.float32) / (VERTEX_NUMBER - 1)
    rising = 1.0 + 2.0 * position
    values = jnp.clip(jax.random.normal(key, (VERTEX_NUMBER,), jnp.float32), -4.0, 4.0)
    return values * rising


def place_ends(values, rng, low, high):
    index_at = [jax.random.randint(jax.random.fold_in(rng, axis), (), 0, length) for axis, length in enumerate(values.shape)]
    main_axis = values.shape.index(max(values.shape))
    next_to = index_at[:main_axis] + [(index_at[main_axis] + 1) % values.shape[main_axis]] + index_at[main_axis + 1:]
    return values.at[tuple(index_at)].set(low).at[tuple(next_to)].set(high)


def shard_levels(rng, shape, cuts, smallest, high):
    level = 1.0
    for dim, parts in cuts:
        heights = jax.random.uniform(jax.random.fold_in(jax.random.fold_in(rng, 6), dim), (parts,), jnp.float32, smallest / len(cuts), high / len(cuts))
        level = level * jnp.repeat(jnp.exp(heights), shape[dim] // parts).reshape((-1,) + (1,) * (len(shape) - 1 - dim))
    return level


def scatter_about(stream_key, extent, spread, limit, cuts=(), kind=jnp.bfloat16):
    values = jax.random.normal(stream_key, extent, jnp.float32) * spread
    if len(cuts) > 0:
        values = shard_levels(stream_key, extent, cuts, -0.22, 0.18) * values
    return jnp.clip(values, min=-limit, max=limit).astype(kind)


def setup_inputs(seed: int = 0) -> dict:
    key_of = jax.random.split(jax.random.key(seed), 16)
    state = scatter_about(key_of[0], (VERTEX_NUMBER, F), 1.0, 6.0, ((0, 32),))
    tile_values = jnp.clip(jnp.exp(math.log(0.009375) - 3.4011974 * jax.random.uniform(key_of[1], (DEVICES, NB, TILE, TILE), jnp.float32) ** shard_levels(key_of[1], (DEVICES, NB, TILE, TILE), ((0, 32),), -0.2, 0.2)), 0.0003125, 0.009375)
    tile_rows = draw_tile_rows(jax.random.fold_in(key_of[15], 71), 0)
    tile_columns = draw_tile_columns(jax.random.fold_in(key_of[15], 71), 0)
    tile_counts = draw_tile_counts(jax.random.fold_in(key_of[15], 71), 0)
    send_nodes = place_ends(jax.random.randint(key_of[5], (DEVICES, 4, IFACE), 0, NODE_DEV), jax.random.fold_in(key_of[5], 1), 0, NODE_DEV - 1).astype(jnp.int32)
    face_counts = draw_face_counts(jax.random.fold_in(key_of[15], 71), 0)
    capacity = jnp.clip(jnp.exp(math.log(2.0) - 3.6888794 * jax.random.uniform(key_of[7], (VERTEX_NUMBER,), jnp.float32) ** shard_levels(key_of[7], (VERTEX_NUMBER,), ((0, 32),), -0.2, 0.2)), 0.05, 2.0)
    source = draw_source(jax.random.fold_in(key_of[15], 71), 0)
    w_self = scatter_about(key_of[9], (LAYERS, F, F), F ** -0.5, 0.375)
    w_neighbour = scatter_about(key_of[10], (LAYERS, F, F), F ** -0.5, 0.375)
    w_out = scatter_about(key_of[11], (LAYERS, F, F), F ** -0.5, 0.375)
    gains = jnp.clip(1.0 + 0.15 * jax.random.normal(key_of[12], (LAYERS, 2, F), jnp.float32), 0.25, 1.75)
    bias = scatter_about(key_of[13], (LAYERS, F), 0.5, 3.0, (), jnp.float32)
    w_decode = scatter_about(key_of[14], (F,), F ** -0.5, 0.375, (), jnp.float32)
    return dict(state=state, tile_values=tile_values, tile_rows=tile_rows, tile_columns=tile_columns, tile_counts=tile_counts, send_nodes=send_nodes, face_counts=face_counts, capacity=capacity, source=source, w_self=w_self, w_neighbour=w_neighbour, w_out=w_out, gains=gains, bias=bias, w_decode=w_decode)


EXACT = lax.Precision.HIGHEST

def placement(index, live_slots, groups):
    hits = index[:, None] == jnp.arange(groups, dtype=jnp.int32)[None, :]
    return (hits & live_slots[:, None]).astype(jnp.float32)

def block_product(tiles, rows, columns, live_slots, values):
    tile_count = values.shape[0] // TILE
    blocks = values.reshape((tile_count, TILE) + values.shape[1:])
    forward = jnp.einsum('tij,tj...->ti...', tiles, blocks[columns], precision=EXACT)
    backward = jnp.einsum('tji,tj...->ti...', tiles, blocks[rows], precision=EXACT)
    place_rows = placement(rows, live_slots, tile_count)
    place_columns = placement(columns, live_slots, tile_count)
    summed = jnp.einsum('tk,t...->k...', place_rows, forward, precision=EXACT)
    summed = summed + jnp.einsum('tk,t...->k...', place_columns, backward, precision=EXACT)
    return summed.reshape(values.shape)

def partner_rows(sent):
    grid = sent.reshape((N_DOM, N_SUB) + sent.shape[1:])
    from_low = jnp.concatenate([jnp.zeros_like(grid[:1, :, 1]), grid[:-1, :, 1]], axis=0)
    from_high = jnp.concatenate([grid[1:, :, 0], jnp.zeros_like(grid[:1, :, 0])], axis=0)
    from_left = jnp.concatenate([jnp.zeros_like(grid[:, :1, 3]), grid[:, :-1, 3]], axis=1)
    from_right = jnp.concatenate([grid[:, 1:, 2], jnp.zeros_like(grid[:, :1, 2])], axis=1)
    return jnp.stack([from_low, from_high, from_left, from_right], axis=2).reshape(sent.shape)

def interface_term(values, send_nodes, live_faces):
    picked = jax.vmap(lambda field, index: field[index])(values, send_nodes)
    mask = live_faces.reshape(live_faces.shape + (1,) * (values.ndim - 2))
    sent = jnp.where(mask, picked, jnp.zeros_like(picked))
    arrived = partner_rows(sent)

    def add_one(field, index, incoming):
        flat = incoming.reshape((-1,) + field.shape[1:]).astype(jnp.float32)
        return jnp.zeros(field.shape, jnp.float32).at[index.reshape(-1)].add(flat)
    return jax.vmap(add_one)(values, send_nodes, arrived)

def inverse_sqrt_diagonal_scaling(values, gain):
    return values * lax.rsqrt(lax.optimization_barrier(jnp.mean(values * values, axis=-1, keepdims=True)) + 1e-06) * gain

def reference(state, tile_values, tile_rows, tile_columns, tile_counts, send_nodes, face_counts, capacity, source, w_self, w_neighbour, w_out, gains, bias, w_decode):
    tile_count = NODE_DEV // TILE
    live_tiles = jnp.arange(NB, dtype=jnp.int32)[None, :] < tile_counts[:, None]
    live_faces = jnp.arange(IFACE, dtype=jnp.int32)[None, None, :] < face_counts[:, :, None]

    def tile_partial_sums(pieces):
        tiles, rows, columns, live_slots = pieces
        row_part = jnp.einsum('tk,ti->ki', placement(rows, live_slots, tile_count), lax.optimization_barrier(jnp.sum(tiles, axis=2)), precision=EXACT)
        column_part = jnp.einsum('tk,ti->ki', placement(columns, live_slots, tile_count), lax.optimization_barrier(jnp.sum(tiles, axis=1)), precision=EXACT)
        return (row_part + column_part).reshape(-1)
    rowsum = lax.map(tile_partial_sums, (tile_values, tile_rows, tile_columns, live_tiles))
    rowsum = rowsum + interface_term(jnp.ones((DEVICES, NODE_DEV), jnp.float32), send_nodes, live_faces)
    tile_half = tile_values.astype(jnp.bfloat16)

    def feature_blocks(pieces):
        tiles, rows, columns, live_slots, values = pieces
        return block_product(tiles.astype(jnp.float32), rows, columns, live_slots, values.astype(jnp.float32))
    latents = state
    for layer in range(LAYERS):
        grouped = latents.reshape(DEVICES, NODE_DEV, F)
        local = lax.map(feature_blocks, (tile_half, tile_rows, tile_columns, live_tiles, grouped))
        neighbour_mean = (local + interface_term(grouped, send_nodes, live_faces)) / rowsum[:, :, None]
        neighbour_mean = neighbour_mean.reshape(VERTEX_NUMBER, F)
        scaled_own_feature = inverse_sqrt_diagonal_scaling(latents.astype(jnp.float32), gains[layer, 0]).astype(jnp.bfloat16)
        normed_neighbour = inverse_sqrt_diagonal_scaling(neighbour_mean, gains[layer, 1]).astype(jnp.bfloat16)
        linear = jnp.dot(scaled_own_feature, w_self[layer], preferred_element_type=jnp.float32)
        linear = linear + jnp.dot(normed_neighbour, w_neighbour[layer], preferred_element_type=jnp.float32) + bias[layer]
        activated = jax.nn.silu(linear).astype(jnp.bfloat16)
        update = jnp.dot(activated, w_out[layer], preferred_element_type=jnp.float32)
        latents = (latents.astype(jnp.float32) + update).astype(jnp.bfloat16)
    network_prediction = jnp.dot(latents.astype(jnp.float32), w_decode, precision=EXACT).reshape(DEVICES, NODE_DEV)
    diagonal = capacity.reshape(DEVICES, NODE_DEV) + rowsum
    scaling = 1.0 / diagonal

    def vector_block_list(pieces):
        tiles, rows, columns, live_slots, values = pieces
        return block_product(tiles, rows, columns, live_slots, values)

    def operator(vector):
        local = lax.map(vector_block_list, (tile_values, tile_rows, tile_columns, live_tiles, vector))
        return diagonal * vector - local - interface_term(vector, send_nodes, live_faces)
    heat_level_field = network_prediction
    equation_defect = source.reshape(DEVICES, NODE_DEV) - operator(network_prediction)
    scaled = scaling * equation_defect
    conjugate_heading = scaled
    residual_dot = jnp.sum(equation_defect * scaled)
    for step in range(ITERS):
        image = operator(conjugate_heading)
        descent_factor = residual_dot / jnp.sum(conjugate_heading * image)
        heat_level_field = heat_level_field + descent_factor * conjugate_heading
        equation_defect = equation_defect - descent_factor * image
        scaled = scaling * equation_defect
        following = jnp.sum(equation_defect * scaled)
        conjugate_heading = scaled + following / residual_dot * conjugate_heading
        residual_dot = following
    return (heat_level_field.reshape(VERTEX_NUMBER), equation_defect.reshape(VERTEX_NUMBER))
```

```python
import jax
import jax.numpy as jnp
from jax import lax
from jax.experimental import pallas as pl
from jax.experimental.pallas import tpu as pltpu
from jax.sharding import PartitionSpec as P

LAYERS = 2
ITERS = 3
LANES = 128
VMEM_LIMIT = 24 * 1024 * 1024

F32 = jnp.float32
BF16 = jnp.bfloat16


def shape(dims, dtype=F32):
    return jax.ShapeDtypeStruct(dims, dtype)


def run(body, outs, operands, scalars=(), flops=1_000_000, moved=1_000_000):
    smem = pl.BlockSpec(memory_space=pltpu.SMEM)
    vmem = pl.BlockSpec(memory_space=pltpu.VMEM)
    return pl.pallas_call(
        body,
        out_shape=outs,
        in_specs=[smem] * len(scalars) + [vmem] * len(operands),
        out_specs=[vmem] * len(outs),
        compiler_params=pltpu.CompilerParams(vmem_limit_bytes=VMEM_LIMIT),
        cost_estimate=pl.CostEstimate(flops=flops, bytes_accessed=moved, transcendentals=0),
    )(*scalars, *operands)


def slot_rows(counts_ref, index_ref):
    rows = []
    for k in range(index_ref.shape[1]):
        for h in range(index_ref.shape[2] // LANES):
            row = index_ref[0, k : k + 1, h * LANES : (h + 1) * LANES]
            slot = lax.broadcasted_iota(jnp.int32, (1, LANES), 1) + h * LANES
            rows.append(jnp.where(slot < counts_ref[0, k], row, -1))
    return rows


def pick(vector, rows):
    index = jnp.concatenate(rows, axis=0)
    low = jnp.bitwise_and(index, LANES - 1)
    high = jnp.right_shift(index, 7)
    out = jnp.zeros(index.shape, F32)
    for t in range(vector.shape[0]):
        spread = jnp.broadcast_to(vector[t : t + 1, :], index.shape)
        got = jnp.take_along_axis(spread, low, axis=1, mode="promise_in_bounds")
        out = jnp.where(high == t, got, out)
    return out


def pieces(value):
    first = value.astype(BF16)
    rest = value - first.astype(F32)
    second = rest.astype(BF16)
    third = (rest - second.astype(F32)).astype(BF16)
    return first, second, third


def low_hits(rows):
    lane = lax.broadcasted_iota(jnp.int32, (LANES, LANES), 0)
    return jnp.concatenate(
        [(lane == jnp.bitwise_and(row, LANES - 1)).astype(F32).astype(BF16) for row in rows], axis=1
    )


def spread_sum(values, rows, tiles):
    tile = lax.broadcasted_iota(jnp.int32, (tiles, LANES), 0)
    parts = [
        jnp.where(tile == jnp.right_shift(row, 7), value, 0.0) for value, row in zip(values, rows)
    ]
    held = jnp.concatenate(parts, axis=1)
    stacked = jnp.concatenate([p.astype(F32) for p in pieces(held)], axis=0).astype(BF16)
    out = lax.dot_general(
        stacked, low_hits(rows), (((1,), (1,)), ((), ())), preferred_element_type=F32
    )
    return out[:tiles] + out[tiles : 2 * tiles] + out[2 * tiles :]


def arrived_rows(refs):
    return [ref[h : h + 1, :] for ref in refs for h in range(ref.shape[0])]


def store_sent(refs, sent):
    per = refs[0].shape[0]
    for k, ref in enumerate(refs):
        ref[...] = sent[k * per : (k + 1) * per, :]


def lane_rows(vector):
    return jnp.concatenate([vector[t : t + 1, :] for t in range(vector.shape[0])], axis=1)


def tile_rows_of(row):
    return jnp.concatenate(
        [row[:, t * LANES : (t + 1) * LANES] for t in range(row.shape[1] // LANES)], axis=0
    )


def gather_first(counts, index, state, lat, hits, s0, s1, s2, s3):
    rows = slot_rows(counts, index)
    nodes = state.shape[0]
    node = lax.broadcasted_iota(jnp.int32, (nodes, LANES), 0)
    for c, row in enumerate(rows):
        hits[:, c * LANES : (c + 1) * LANES] = (node == row).astype(F32).astype(BF16)
    lat[...] = state[...].T
    send_features(lat[...], hits, (s0, s1, s2, s3))


def send_features(lat, hits, outs):
    width = outs[0].shape[1]
    for k, out in enumerate(outs):
        out[...] = jnp.dot(
            lat, hits[:, k * width : (k + 1) * width], preferred_element_type=F32
        ).astype(BF16)


def build(
    tile_rows, tile_columns, tile_counts, counts, index, tiles, lat, capacity,
    matrix, half, inverse_rowsum, diagonal, local,
):
    count = tiles.shape[2]
    node_tiles = matrix.shape[0] // count
    matrix[...] = jnp.zeros(matrix.shape, F32)
    for t in range(node_tiles):
        span = slice(t * count, (t + 1) * count)
        block = tiles[0, t]
        matrix[span, span] = block + block.T

    def add(t, carry):
        r = pl.multiple_of(tile_rows[0, t] * count, count)
        c = pl.multiple_of(tile_columns[0, t] * count, count)
        block = tiles[0, t]
        matrix[pl.ds(r, count), pl.ds(c, count)] += block
        matrix[pl.ds(c, count), pl.ds(r, count)] += block.T
        return carry

    lax.fori_loop(node_tiles, tile_counts[0], add, 0)
    rows = slot_rows(counts, index)
    faces = spread_sum([jnp.ones((1, LANES), F32)] * len(rows), rows, node_tiles)
    total = jnp.sum(matrix[...], axis=0, keepdims=True)
    rowsum = tile_rows_of(total) + faces
    inverse_rowsum[...] = lane_rows(1.0 / rowsum)
    diagonal[...] = capacity[...] + rowsum
    half[...] = matrix[...].astype(BF16)
    local[...] = jnp.dot(lat[...], half[...], preferred_element_type=F32)


def local_features(lat, half, local):
    local[...] = jnp.dot(lat[...], half[...], preferred_element_type=F32)


def layer_step(layer, arrived, local, inverse_rowsum, lat, hits, w_self, w_neighbour, w_out, gains, bias):
    came = jnp.concatenate([a[...] for a in arrived], axis=1)
    coupled = lax.dot_general(
        came, hits[...], (((1,), (1,)), ((), ())), preferred_element_type=F32
    )
    mean = (local[...] + coupled) * inverse_rowsum[...]
    columns = jnp.concatenate(
        [gains[layer], bias[...], jnp.zeros((8 - 4, bias.shape[1]), F32)], axis=0
    ).T
    own = lat[...].astype(F32)

    def normed(value, gain):
        scale = lax.rsqrt(jnp.mean(value * value, axis=0, keepdims=True) + 1e-06)
        return (value * scale * gain).astype(BF16)

    normed_self = normed(own, columns[:, 0:1])
    normed_neighbour = normed(mean, columns[:, 1:2])

    def project(weight, value):
        return lax.dot_general(
            weight, value, (((0,), (0,)), ((), ())), preferred_element_type=F32
        )

    linear = project(w_self[layer], normed_self) + project(w_neighbour[layer], normed_neighbour)
    linear = linear + columns[:, 2 + layer : 3 + layer]
    activated = (linear / (1.0 + jnp.exp(-linear))).astype(BF16)
    return (own + project(w_out[layer], activated)).astype(BF16)


def first_layer(
    a0, a1, a2, a3, local, inverse_rowsum, lat, hits, w_self, w_neighbour, w_out, gains, bias,
    new, s0, s1, s2, s3,
):
    value = layer_step(
        0, (a0, a1, a2, a3), local, inverse_rowsum, lat, hits, w_self, w_neighbour, w_out, gains, bias
    )
    new[...] = value
    send_features(value, hits, (s0, s1, s2, s3))


def last_layer(
    counts, index, a0, a1, a2, a3, local, inverse_rowsum, lat, hits, w_self, w_neighbour, w_out,
    gains, bias, w_decode, guess, s0, s1, s2, s3,
):
    value = layer_step(
        LAYERS - 1, (a0, a1, a2, a3), local, inverse_rowsum, lat, hits, w_self, w_neighbour, w_out,
        gains, bias,
    )
    decode = jnp.broadcast_to(w_decode[...], (8, w_decode.shape[1])).T[:, 0:1]
    row = jnp.sum(value.astype(F32) * decode, axis=0, keepdims=True)
    field = tile_rows_of(row)
    guess[...] = field
    store_sent((s0, s1, s2, s3), pick(field, slot_rows(counts, index)))


def matvec(matrix, vector, out):
    count = LANES
    width = matrix.shape[1]
    field = vector[...]
    total = jnp.zeros((8, width), F32)
    for t in range(field.shape[0]):
        column = jnp.broadcast_to(field[t : t + 1, :], (count, count)).T
        wide = jnp.concatenate([column] * (width // count), axis=1)
        product = matrix[t * count : (t + 1) * count, :] * wide
        total = total + jnp.sum(product.reshape(count // 8, 8, width), axis=0)
    out[...] = tile_rows_of(jnp.sum(total, axis=0, keepdims=True))


def start_basis(counts, index, a0, a1, a2, a3, local, guess, source, diagonal, basis, s0, s1, s2, s3):
    rows = slot_rows(counts, index)
    came = spread_sum(arrived_rows((a0, a1, a2, a3)), rows, guess.shape[0])
    value = (source[...] + local[...] + came) / diagonal[...] - guess[...]
    basis[...] = value
    store_sent((s0, s1, s2, s3), pick(value, rows))


def next_basis(counts, index, a0, a1, a2, a3, local, diagonal, basis, s0, s1, s2, s3):
    rows = slot_rows(counts, index)
    came = spread_sum(arrived_rows((a0, a1, a2, a3)), rows, local.shape[0])
    value = (local[...] + came) / diagonal[...]
    basis[...] = value
    store_sent((s0, s1, s2, s3), pick(value, rows))


def last_basis(counts, index, a0, a1, a2, a3, local, diagonal, b0, b1, b2, basis, moments):
    rows = slot_rows(counts, index)
    came = spread_sum(arrived_rows((a0, a1, a2, a3)), rows, local.shape[0])
    value = (local[...] + came) / diagonal[...]
    basis[...] = value
    held = [b0[...], b1[...], b2[...], value]
    parts = []
    for k in range(2 * ITERS):
        left, right = held[k // 2], held[(k + 1) // 2]
        parts.append(jnp.sum(left * right * diagonal[...], axis=0, keepdims=True))
    parts.append(jnp.zeros((8 - 2 * ITERS, LANES), F32))
    moments[...] = jnp.concatenate(parts, axis=0)


def finish(moments, guess, diagonal, b0, b1, b2, b3, field, defect):
    sums = jnp.sum(moments[...], axis=1, keepdims=True)
    n = [jnp.broadcast_to(sums[k : k + 1, :], (8, LANES)) for k in range(2 * ITERS)]
    one, zero = jnp.ones((8, LANES), F32), jnp.zeros((8, LANES), F32)

    def paired(left, values):
        total = zero
        for i, a in enumerate(left):
            for j, b in enumerate(left):
                total = total + a * b * values[i + j]
        return total

    gaps = [n[k] - n[k + 1] for k in range(2 * ITERS - 1)]
    residual = [one]
    heading = [one]
    moved = [zero] * ITERS
    size = n[0]
    for step in range(ITERS):
        alpha = size / paired(heading, gaps)
        for i, h in enumerate(heading):
            moved[i] = moved[i] + alpha * h
        image = [
            (heading[i] if i < len(heading) else zero) - (heading[i - 1] if i > 0 else zero)
            for i in range(len(heading) + 1)
        ]
        residual = [
            (residual[i] if i < len(residual) else zero) - alpha * image[i]
            for i in range(len(image))
        ]
        if step + 1 < ITERS:
            following = paired(residual, n)
            beta = following / size
            heading = [
                residual[i] + (beta * heading[i] if i < len(heading) else zero)
                for i in range(len(residual))
            ]
            size = following
    held = [b0[...], b1[...], b2[...], b3[...]]
    total = guess[...]
    for c, b in zip(moved, held):
        total = total + c * b
    field[...] = total
    left = zero
    for c, b in zip(residual, held):
        left = left + c * b
    defect[...] = left * diagonal[...]


def exchange(sent):
    arrived = []
    for axis, toward_low, toward_high in (("dom", sent[0], sent[1]), ("sub", sent[2], sent[3])):
        size = lax.axis_size(axis)
        up = [(i, i + 1) for i in range(size - 1)]
        down = [(i + 1, i) for i in range(size - 1)]
        arrived.append(lax.ppermute(toward_high, axis, up))
        arrived.append(lax.ppermute(toward_low, axis, down))
    return arrived


def total_over(value, axes):
    for axis in axes:
        size = lax.axis_size(axis)
        if size & (size - 1):
            value = lax.psum(value, axis)
            continue
        step = 1
        while step < size:
            value = value + lax.ppermute(value, axis, [(i, i ^ step) for i in range(size)])
            step *= 2
    return value


def per_device(
    state, tile_values, tile_rows, tile_columns, tile_counts, send_nodes, face_counts, capacity,
    source, w_self, w_neighbour, w_out, gains, bias, w_decode,
):
    nodes, width = state.shape
    slots = send_nodes.shape[2]
    tiles = nodes // LANES
    field = shape((tiles, LANES))
    feature_sent = [shape((width, slots), BF16)] * 4
    vector_sent = [shape((slots // LANES, LANES))] * 4
    faces = (face_counts,)
    weights = (w_self, w_neighbour, w_out, gains, bias)
    capacity = capacity.reshape(tiles, LANES)
    source = source.reshape(tiles, LANES)

    lat, hits, *sent = run(
        gather_first,
        [shape((width, nodes), BF16), shape((nodes, 4 * slots), BF16)] + feature_sent,
        (send_nodes, state), faces, flops=2 * nodes * 4 * slots * width,
    )
    arrived = exchange(sent)
    matrix, half, inverse_rowsum, diagonal, local = run(
        build,
        [shape((nodes, nodes)), shape((nodes, nodes), BF16), shape((1, nodes)), field, shape((width, nodes))],
        (send_nodes, tile_values, lat, capacity),
        (tile_rows, tile_columns, tile_counts, face_counts), flops=2 * nodes * nodes * width, moved=6_000_000,
    )
    lat, *sent = run(
        first_layer, [shape((width, nodes), BF16)] + feature_sent,
        (*arrived, local, inverse_rowsum, lat, hits, *weights), flops=6 * nodes * nodes * width,
    )
    arrived = exchange(sent)
    (local,) = run(
        local_features, [shape((width, nodes))], (lat, half), flops=2 * nodes * nodes * width, moved=4_000_000
    )
    guess, *sent = run(
        last_layer, [field] + vector_sent,
        (send_nodes, *arrived, local, inverse_rowsum, lat, hits, *weights, w_decode.reshape(1, width)),
        faces, flops=6 * nodes * nodes * width,
    )

    def product(vector):
        return run(matvec, [field], (matrix, vector), flops=2 * nodes * nodes, moved=4 * nodes * nodes)[0]

    arrived = exchange(sent)
    local = product(guess)
    b0, *sent = run(
        start_basis, [field] + vector_sent,
        (send_nodes, *arrived, local, guess, source, diagonal), faces,
    )
    held = [b0]
    for _ in range(ITERS - 1):
        arrived = exchange(sent)
        local = product(held[-1])
        b, *sent = run(
            next_basis, [field] + vector_sent, (send_nodes, *arrived, local, diagonal), faces
        )
        held.append(b)
    arrived = exchange(sent)
    local = product(held[-1])
    b, moments = run(
        last_basis, [field, shape((8, LANES))],
        (send_nodes, *arrived, local, diagonal, *held), faces,
    )
    held.append(b)
    moments = total_over(moments, ("sub", "dom"))
    heat, defect = run(finish, [field, field], (moments, guess, diagonal, *held))
    return heat.reshape(nodes), defect.reshape(nodes)


def solution(mesh):
    both = ("dom", "sub")
    return jax.shard_map(
        per_device,
        mesh=mesh,
        in_specs=(
            P(both, None),
            P(both, None, None, None),
            P(both, None),
            P(both, None),
            P(both),
            P(both, None, None),
            P(both, None),
            P(both),
            P(both),
            P(),
            P(),
            P(),
            P(),
            P(),
            P(),
        ),
        out_specs=(P(both), P(both)),
        check_vma=False,
    )
```

```python
import jax
import jax.numpy as jnp
from jax import lax
from jax.experimental import pallas as pl
from jax.experimental.pallas import tpu as pltpu
from jax.sharding import PartitionSpec as P

LAYERS = 2
ITERS = 3
LANES = 128
VMEM_LIMIT = 24 * 1024 * 1024

F32 = jnp.float32
BF16 = jnp.bfloat16


def shape(dims, dtype=F32):
    return jax.ShapeDtypeStruct(dims, dtype)


def run(body, outs, operands, scalars=(), flops=1_000_000, moved=1_000_000):
    smem = pl.BlockSpec(memory_space=pltpu.SMEM)
    vmem = pl.BlockSpec(memory_space=pltpu.VMEM)
    return pl.pallas_call(
        body,
        out_shape=outs,
        in_specs=[smem] * len(scalars) + [vmem] * len(operands),
        out_specs=[vmem] * len(outs),
        compiler_params=pltpu.CompilerParams(vmem_limit_bytes=VMEM_LIMIT),
        cost_estimate=pl.CostEstimate(flops=flops, bytes_accessed=moved, transcendentals=0),
    )(*scalars, *operands)


def slot_rows(places):
    return [places[r : r + 1, :] for r in range(places.shape[0])]


def pick(vector, rows):
    index = jnp.concatenate(rows, axis=0)
    low = jnp.bitwise_and(index, LANES - 1)
    high = jnp.right_shift(index, 7)
    out = jnp.zeros(index.shape, F32)
    for t in range(vector.shape[0]):
        spread = jnp.broadcast_to(vector[t : t + 1, :], index.shape)
        got = jnp.take_along_axis(spread, low, axis=1, mode="promise_in_bounds")
        out = jnp.where(high == t, got, out)
    return out


def pieces(value):
    first = value.astype(BF16)
    rest = value - first.astype(F32)
    second = rest.astype(BF16)
    third = (rest - second.astype(F32)).astype(BF16)
    return first, second, third


def low_hits(rows):
    lane = lax.broadcasted_iota(jnp.int32, (LANES, LANES), 0)
    return jnp.concatenate(
        [(lane == jnp.bitwise_and(row, LANES - 1)).astype(F32).astype(BF16) for row in rows], axis=1
    )


def spread_sum(values, rows, tiles):
    tile = lax.broadcasted_iota(jnp.int32, (tiles, LANES), 0)
    parts = [
        jnp.where(tile == jnp.right_shift(row, 7), value, 0.0) for value, row in zip(values, rows)
    ]
    held = jnp.concatenate(parts, axis=1)
    stacked = jnp.concatenate([p.astype(F32) for p in pieces(held)], axis=0).astype(BF16)
    out = lax.dot_general(
        stacked, low_hits(rows), (((1,), (1,)), ((), ())), preferred_element_type=F32
    )
    return out[:tiles] + out[tiles : 2 * tiles] + out[2 * tiles :]


def arrived_rows(refs):
    return [ref[h : h + 1, :] for ref in refs for h in range(ref.shape[0])]


def store_sent(refs, sent):
    per = refs[0].shape[0]
    for k, ref in enumerate(refs):
        ref[...] = sent[k * per : (k + 1) * per, :]


def lane_rows(vector):
    return jnp.concatenate([vector[t : t + 1, :] for t in range(vector.shape[0])], axis=1)


def tile_rows_of(row):
    return jnp.concatenate(
        [row[:, t * LANES : (t + 1) * LANES] for t in range(row.shape[1] // LANES)], axis=0
    )


def gather_first(sides, counts, index, state, lat, hits, places, s0, s1, s2, s3):
    per = index.shape[2] // LANES
    for g in range(index.shape[1]):
        side = sides[g]
        for h in range(per):
            low, high = g // 2 * 2, g // 2 * 2 + 1
            span = slice(h * LANES, (h + 1) * LANES)
            row = jnp.where(side == low, index[0, low : low + 1, span], index[0, high : high + 1, span])
            slot = lax.broadcasted_iota(jnp.int32, (1, LANES), 1) + h * LANES
            r = g * per + h
            places[r : r + 1, :] = jnp.where(slot < counts[0, side], row, -1)
    node = lax.broadcasted_iota(jnp.int32, (state.shape[0], LANES), 0)
    for c, row in enumerate(slot_rows(places)):
        hits[:, c * LANES : (c + 1) * LANES] = (node == row).astype(F32).astype(BF16)
    lat[...] = state[...].T
    send_features(lat[...], hits, (s0, s1, s2, s3))


def send_features(lat, hits, outs):
    width = outs[0].shape[1]
    for k, out in enumerate(outs):
        out[...] = jnp.dot(
            lat, hits[:, k * width : (k + 1) * width], preferred_element_type=F32
        ).astype(BF16)


def build(
    tile_rows, tile_columns, tile_counts, places, tiles, lat, capacity,
    matrix, half, inverse_rowsum, diagonal, local,
):
    count = tiles.shape[2]
    node_tiles = matrix.shape[0] // count
    matrix[...] = jnp.zeros(matrix.shape, F32)
    for t in range(node_tiles):
        span = slice(t * count, (t + 1) * count)
        block = tiles[0, t]
        matrix[span, span] = block + block.T

    def add(t, carry):
        r = pl.multiple_of(tile_rows[0, t] * count, count)
        c = pl.multiple_of(tile_columns[0, t] * count, count)
        block = tiles[0, t]
        matrix[pl.ds(r, count), pl.ds(c, count)] += block
        matrix[pl.ds(c, count), pl.ds(r, count)] += block.T
        return carry

    lax.fori_loop(node_tiles, tile_counts[0], add, 0)
    rows = slot_rows(places)
    faces = spread_sum([jnp.ones((1, LANES), F32)] * len(rows), rows, node_tiles)
    total = jnp.sum(matrix[...], axis=0, keepdims=True)
    rowsum = tile_rows_of(total) + faces
    inverse_rowsum[...] = lane_rows(1.0 / rowsum)
    diagonal[...] = capacity[...] + rowsum
    half[...] = matrix[...].astype(BF16)
    local[...] = jnp.dot(lat[...], half[...], preferred_element_type=F32)


def local_features(lat, half, local):
    local[...] = jnp.dot(lat[...], half[...], preferred_element_type=F32)


def layer_step(layer, arrived, local, inverse_rowsum, lat, hits, w_self, w_neighbour, w_out, gains, bias):
    came = jnp.concatenate([a[...] for a in arrived], axis=1)
    coupled = lax.dot_general(
        came, hits[...], (((1,), (1,)), ((), ())), preferred_element_type=F32
    )
    mean = (local[...] + coupled) * inverse_rowsum[...]
    columns = jnp.concatenate(
        [gains[layer], bias[...], jnp.zeros((8 - 4, bias.shape[1]), F32)], axis=0
    ).T
    own = lat[...].astype(F32)

    def normed(value, gain):
        scale = lax.rsqrt(jnp.mean(value * value, axis=0, keepdims=True) + 1e-06)
        return (value * scale * gain).astype(BF16)

    normed_self = normed(own, columns[:, 0:1])
    normed_neighbour = normed(mean, columns[:, 1:2])

    def project(weight, value):
        return lax.dot_general(
            weight, value, (((0,), (0,)), ((), ())), preferred_element_type=F32
        )

    linear = project(w_self[layer], normed_self) + project(w_neighbour[layer], normed_neighbour)
    linear = linear + columns[:, 2 + layer : 3 + layer]
    activated = (linear / (1.0 + jnp.exp(-linear))).astype(BF16)
    return (own + project(w_out[layer], activated)).astype(BF16)


def first_layer(
    a0, a1, a2, a3, local, inverse_rowsum, lat, hits, w_self, w_neighbour, w_out, gains, bias,
    new, s0, s1, s2, s3,
):
    value = layer_step(
        0, (a0, a1, a2, a3), local, inverse_rowsum, lat, hits, w_self, w_neighbour, w_out, gains, bias
    )
    new[...] = value
    send_features(value, hits, (s0, s1, s2, s3))


def last_layer(
    places, a0, a1, a2, a3, local, inverse_rowsum, lat, hits, w_self, w_neighbour, w_out,
    gains, bias, w_decode, guess, s0, s1, s2, s3,
):
    value = layer_step(
        LAYERS - 1, (a0, a1, a2, a3), local, inverse_rowsum, lat, hits, w_self, w_neighbour, w_out,
        gains, bias,
    )
    decode = jnp.broadcast_to(w_decode[...], (8, w_decode.shape[1])).T[:, 0:1]
    row = jnp.sum(value.astype(F32) * decode, axis=0, keepdims=True)
    field = tile_rows_of(row)
    guess[...] = field
    store_sent((s0, s1, s2, s3), pick(field, slot_rows(places)))


def matvec(matrix, vector, out):
    count = LANES
    width = matrix.shape[1]
    field = vector[...]
    total = jnp.zeros((8, width), F32)
    for t in range(field.shape[0]):
        column = jnp.broadcast_to(field[t : t + 1, :], (count, count)).T
        wide = jnp.concatenate([column] * (width // count), axis=1)
        product = matrix[t * count : (t + 1) * count, :] * wide
        total = total + jnp.sum(product.reshape(count // 8, 8, width), axis=0)
    out[...] = tile_rows_of(jnp.sum(total, axis=0, keepdims=True))


def start_basis(places, a0, a1, a2, a3, local, guess, source, diagonal, basis, s0, s1, s2, s3):
    rows = slot_rows(places)
    came = spread_sum(arrived_rows((a0, a1, a2, a3)), rows, guess.shape[0])
    value = (source[...] + local[...] + came) / diagonal[...] - guess[...]
    basis[...] = value
    store_sent((s0, s1, s2, s3), pick(value, rows))


def next_basis(places, a0, a1, a2, a3, local, diagonal, basis, s0, s1, s2, s3):
    rows = slot_rows(places)
    came = spread_sum(arrived_rows((a0, a1, a2, a3)), rows, local.shape[0])
    value = (local[...] + came) / diagonal[...]
    basis[...] = value
    store_sent((s0, s1, s2, s3), pick(value, rows))


def last_basis(places, a0, a1, a2, a3, local, diagonal, b0, b1, b2, basis, moments):
    rows = slot_rows(places)
    came = spread_sum(arrived_rows((a0, a1, a2, a3)), rows, local.shape[0])
    value = (local[...] + came) / diagonal[...]
    basis[...] = value
    held = [b0[...], b1[...], b2[...], value]
    parts = []
    for k in range(2 * ITERS):
        left, right = held[k // 2], held[(k + 1) // 2]
        parts.append(jnp.sum(left * right * diagonal[...], axis=0, keepdims=True))
    parts.append(jnp.zeros((8 - 2 * ITERS, LANES), F32))
    moments[...] = jnp.concatenate(parts, axis=0)


def finish(moments, guess, diagonal, b0, b1, b2, b3, field, defect):
    sums = jnp.sum(moments[...], axis=1, keepdims=True)
    n = [jnp.broadcast_to(sums[k : k + 1, :], (8, LANES)) for k in range(2 * ITERS)]
    one, zero = jnp.ones((8, LANES), F32), jnp.zeros((8, LANES), F32)

    def paired(left, values):
        total = zero
        for i, a in enumerate(left):
            for j, b in enumerate(left):
                total = total + a * b * values[i + j]
        return total

    gaps = [n[k] - n[k + 1] for k in range(2 * ITERS - 1)]
    residual = [one]
    heading = [one]
    moved = [zero] * ITERS
    size = n[0]
    for step in range(ITERS):
        alpha = size / paired(heading, gaps)
        for i, h in enumerate(heading):
            moved[i] = moved[i] + alpha * h
        image = [
            (heading[i] if i < len(heading) else zero) - (heading[i - 1] if i > 0 else zero)
            for i in range(len(heading) + 1)
        ]
        residual = [
            (residual[i] if i < len(residual) else zero) - alpha * image[i]
            for i in range(len(image))
        ]
        if step + 1 < ITERS:
            following = paired(residual, n)
            beta = following / size
            heading = [
                residual[i] + (beta * heading[i] if i < len(heading) else zero)
                for i in range(len(residual))
            ]
            size = following
    held = [b0[...], b1[...], b2[...], b3[...]]
    total = guess[...]
    for c, b in zip(moved, held):
        total = total + c * b
    field[...] = total
    left = zero
    for c, b in zip(residual, held):
        left = left + c * b
    defect[...] = left * diagonal[...]


def matching(size, first):
    pairs = []
    for i in range(first, size - 1, 2):
        pairs += [(i, i + 1), (i + 1, i)]
    return pairs


def sides_of_matchings():
    dom = lax.axis_index("dom") % 2
    sub = lax.axis_index("sub") % 2
    return jnp.stack([1 - dom, dom, 3 - sub, 2 + sub]).astype(jnp.int32)


def exchange(sent):
    arrived = []
    for g, axis in enumerate(("dom", "dom", "sub", "sub")):
        pairs = matching(lax.axis_size(axis), g % 2)
        arrived.append(lax.ppermute(sent[g], axis, pairs))
    return arrived


def total_over(value, axes):
    for axis in axes:
        size = lax.axis_size(axis)
        if size & (size - 1):
            value = lax.psum(value, axis)
            continue
        step = 1
        while step < size:
            value = value + lax.ppermute(value, axis, [(i, i ^ step) for i in range(size)])
            step *= 2
    return value


def per_device(
    state, tile_values, tile_rows, tile_columns, tile_counts, send_nodes, face_counts, capacity,
    source, w_self, w_neighbour, w_out, gains, bias, w_decode,
):
    nodes, width = state.shape
    slots = send_nodes.shape[2]
    tiles = nodes // LANES
    field = shape((tiles, LANES))
    feature_sent = [shape((width, slots), BF16)] * 4
    vector_sent = [shape((slots // LANES, LANES))] * 4
    weights = (w_self, w_neighbour, w_out, gains, bias)
    capacity = capacity.reshape(tiles, LANES)
    source = source.reshape(tiles, LANES)

    lat, hits, places, *sent = run(
        gather_first,
        [shape((width, nodes), BF16), shape((nodes, 4 * slots), BF16), shape((4 * slots // LANES, LANES), jnp.int32)]
        + feature_sent,
        (send_nodes, state), (sides_of_matchings(), face_counts), flops=2 * nodes * 4 * slots * width,
    )
    arrived = exchange(sent)
    matrix, half, inverse_rowsum, diagonal, local = run(
        build,
        [shape((nodes, nodes)), shape((nodes, nodes), BF16), shape((1, nodes)), field, shape((width, nodes))],
        (places, tile_values, lat, capacity),
        (tile_rows, tile_columns, tile_counts), flops=2 * nodes * nodes * width, moved=6_000_000,
    )
    lat, *sent = run(
        first_layer, [shape((width, nodes), BF16)] + feature_sent,
        (*arrived, local, inverse_rowsum, lat, hits, *weights), flops=6 * nodes * nodes * width,
    )
    arrived = exchange(sent)
    (local,) = run(
        local_features, [shape((width, nodes))], (lat, half), flops=2 * nodes * nodes * width, moved=4_000_000
    )
    guess, *sent = run(
        last_layer, [field] + vector_sent,
        (places, *arrived, local, inverse_rowsum, lat, hits, *weights, w_decode.reshape(1, width)),
        flops=6 * nodes * nodes * width,
    )

    def product(vector):
        return run(matvec, [field], (matrix, vector), flops=2 * nodes * nodes, moved=4 * nodes * nodes)[0]

    arrived = exchange(sent)
    local = product(guess)
    b0, *sent = run(
        start_basis, [field] + vector_sent,
        (places, *arrived, local, guess, source, diagonal),
    )
    held = [b0]
    for _ in range(ITERS - 1):
        arrived = exchange(sent)
        local = product(held[-1])
        b, *sent = run(
            next_basis, [field] + vector_sent, (places, *arrived, local, diagonal)
        )
        held.append(b)
    arrived = exchange(sent)
    local = product(held[-1])
    b, moments = run(
        last_basis, [field, shape((8, LANES))],
        (places, *arrived, local, diagonal, *held),
    )
    held.append(b)
    moments = total_over(moments, ("sub", "dom"))
    heat, defect = run(finish, [field, field], (moments, guess, diagonal, *held))
    return heat.reshape(nodes), defect.reshape(nodes)


def solution(mesh):
    both = ("dom", "sub")
    return jax.shard_map(
        per_device,
        mesh=mesh,
        in_specs=(
            P(both, None),
            P(both, None, None, None),
            P(both, None),
            P(both, None),
            P(both),
            P(both, None, None),
            P(both, None),
            P(both),
            P(both),
            P(),
            P(),
            P(),
            P(),
            P(),
            P(),
        ),
        out_specs=(P(both), P(both)),
        check_vma=False,
    )
```

```python
import jax
import jax.numpy as jnp
from jax import lax
from jax.experimental import pallas as pl
from jax.experimental.pallas import tpu as pltpu
from jax.sharding import PartitionSpec as P

LAYERS = 2
ITERS = 3
LANES = 128
VMEM_LIMIT = 24 * 1024 * 1024

F32 = jnp.float32
BF16 = jnp.bfloat16


def shape(dims, dtype=F32):
    return jax.ShapeDtypeStruct(dims, dtype)


def run(body, outs, operands, scalars=(), flops=1_000_000, moved=1_000_000):
    smem = pl.BlockSpec(memory_space=pltpu.SMEM)
    vmem = pl.BlockSpec(memory_space=pltpu.VMEM)
    return pl.pallas_call(
        body,
        out_shape=outs,
        in_specs=[smem] * len(scalars) + [vmem] * len(operands),
        out_specs=[vmem] * len(outs),
        compiler_params=pltpu.CompilerParams(vmem_limit_bytes=VMEM_LIMIT),
        cost_estimate=pl.CostEstimate(flops=flops, bytes_accessed=moved, transcendentals=0),
    )(*scalars, *operands)


def slot_rows(places):
    return [places[r : r + 1, :] for r in range(places.shape[0])]


def pick(vector, rows):
    index = jnp.concatenate(rows, axis=0)
    low = jnp.bitwise_and(index, LANES - 1)
    high = jnp.right_shift(index, 7)
    out = jnp.zeros(index.shape, F32)
    for t in range(vector.shape[0]):
        spread = jnp.broadcast_to(vector[t : t + 1, :], index.shape)
        got = jnp.take_along_axis(spread, low, axis=1, mode="promise_in_bounds")
        out = jnp.where(high == t, got, out)
    return out


def pieces(value):
    first = value.astype(BF16)
    rest = value - first.astype(F32)
    second = rest.astype(BF16)
    third = (rest - second.astype(F32)).astype(BF16)
    return first, second, third


def low_hits(rows):
    lane = lax.broadcasted_iota(jnp.int32, (LANES, LANES), 0)
    return jnp.concatenate(
        [(lane == jnp.bitwise_and(row, LANES - 1)).astype(F32).astype(BF16) for row in rows], axis=1
    )


def spread_sum(values, rows, tiles):
    tile = lax.broadcasted_iota(jnp.int32, (tiles, LANES), 0)
    parts = [
        jnp.where(tile == jnp.right_shift(row, 7), value, 0.0) for value, row in zip(values, rows)
    ]
    held = jnp.concatenate(parts, axis=1)
    stacked = jnp.concatenate([p.astype(F32) for p in pieces(held)], axis=0).astype(BF16)
    out = lax.dot_general(
        stacked, low_hits(rows), (((1,), (1,)), ((), ())), preferred_element_type=F32
    )
    return out[:tiles] + out[tiles : 2 * tiles] + out[2 * tiles :]


def arrived_rows(refs):
    return [ref[h : h + 1, :] for ref in refs for h in range(ref.shape[0])]


def store_sent(refs, sent):
    per = refs[0].shape[0]
    for k, ref in enumerate(refs):
        ref[...] = sent[k * per : (k + 1) * per, :]


def lane_rows(vector):
    return jnp.concatenate([vector[t : t + 1, :] for t in range(vector.shape[0])], axis=1)


def tile_rows_of(row):
    return jnp.concatenate(
        [row[:, t * LANES : (t + 1) * LANES] for t in range(row.shape[1] // LANES)], axis=0
    )


def gather_first(sides, counts, index, state, lat, hits, places, s0, s1, s2, s3):
    per = index.shape[2] // LANES
    for g in range(index.shape[1]):
        side = sides[g]
        for h in range(per):
            low, high = g // 2 * 2, g // 2 * 2 + 1
            span = slice(h * LANES, (h + 1) * LANES)
            row = jnp.where(side == low, index[0, low : low + 1, span], index[0, high : high + 1, span])
            slot = lax.broadcasted_iota(jnp.int32, (1, LANES), 1) + h * LANES
            r = g * per + h
            places[r : r + 1, :] = jnp.where(slot < counts[0, side], row, -1)
    node = lax.broadcasted_iota(jnp.int32, (state.shape[0], LANES), 0)
    for c, row in enumerate(slot_rows(places)):
        hits[:, c * LANES : (c + 1) * LANES] = (node == row).astype(F32).astype(BF16)
    lat[...] = state[...].T
    send_features(lat[...], hits, (s0, s1, s2, s3))


def send_features(lat, hits, outs):
    width = outs[0].shape[1]
    for k, out in enumerate(outs):
        out[...] = jnp.dot(
            lat, hits[:, k * width : (k + 1) * width], preferred_element_type=F32
        ).astype(BF16)


def build(
    tile_rows, tile_columns, tile_counts, places, tiles, lat, capacity,
    matrix, half, inverse_rowsum, diagonal, local,
):
    count = tiles.shape[2]
    node_tiles = matrix.shape[0] // count
    matrix[...] = jnp.zeros(matrix.shape, F32)
    for t in range(node_tiles):
        span = slice(t * count, (t + 1) * count)
        block = tiles[0, t]
        matrix[span, span] = block + block.T

    def add(t, carry):
        r = pl.multiple_of(tile_rows[0, t] * count, count)
        c = pl.multiple_of(tile_columns[0, t] * count, count)
        block = tiles[0, t]
        matrix[pl.ds(r, count), pl.ds(c, count)] += block
        matrix[pl.ds(c, count), pl.ds(r, count)] += block.T
        return carry

    lax.fori_loop(node_tiles, tile_counts[0], add, 0)
    rows = slot_rows(places)
    faces = spread_sum([jnp.ones((1, LANES), F32)] * len(rows), rows, node_tiles)
    total = jnp.sum(matrix[...], axis=0, keepdims=True)
    rowsum = tile_rows_of(total) + faces
    inverse_rowsum[...] = lane_rows(1.0 / rowsum)
    diagonal[...] = capacity[...] + rowsum
    half[...] = matrix[...].astype(BF16)
    local[...] = jnp.dot(lat[...], half[...], preferred_element_type=F32)


def local_features(lat, half, local):
    local[...] = jnp.dot(lat[...], half[...], preferred_element_type=F32)


def layer_step(layer, arrived, local, inverse_rowsum, lat, hits, w_self, w_neighbour, w_out, gains, bias):
    came = jnp.concatenate([a[...] for a in arrived], axis=1)
    coupled = lax.dot_general(
        came, hits[...], (((1,), (1,)), ((), ())), preferred_element_type=F32
    )
    mean = (local[...] + coupled) * inverse_rowsum[...]
    columns = jnp.concatenate(
        [gains[layer], bias[...], jnp.zeros((8 - 4, bias.shape[1]), F32)], axis=0
    ).T
    own = lat[...].astype(F32)

    def normed(value, gain):
        scale = lax.rsqrt(jnp.mean(value * value, axis=0, keepdims=True) + 1e-06)
        return (value * scale * gain).astype(BF16)

    normed_self = normed(own, columns[:, 0:1])
    normed_neighbour = normed(mean, columns[:, 1:2])

    def project(weight, value):
        return lax.dot_general(
            weight, value, (((0,), (0,)), ((), ())), preferred_element_type=F32
        )

    linear = project(w_self[layer], normed_self) + project(w_neighbour[layer], normed_neighbour)
    linear = linear + columns[:, 2 + layer : 3 + layer]
    activated = (linear / (1.0 + jnp.exp(-linear))).astype(BF16)
    return (own + project(w_out[layer], activated)).astype(BF16)


def first_layer(
    a0, a1, a2, a3, local, inverse_rowsum, lat, hits, w_self, w_neighbour, w_out, gains, bias,
    new, s0, s1, s2, s3,
):
    value = layer_step(
        0, (a0, a1, a2, a3), local, inverse_rowsum, lat, hits, w_self, w_neighbour, w_out, gains, bias
    )
    new[...] = value
    send_features(value, hits, (s0, s1, s2, s3))


def last_layer(
    places, a0, a1, a2, a3, local, inverse_rowsum, lat, hits, w_self, w_neighbour, w_out,
    gains, bias, w_decode, guess, s0, s1, s2, s3,
):
    value = layer_step(
        LAYERS - 1, (a0, a1, a2, a3), local, inverse_rowsum, lat, hits, w_self, w_neighbour, w_out,
        gains, bias,
    )
    decode = jnp.broadcast_to(w_decode[...], (8, w_decode.shape[1])).T[:, 0:1]
    row = jnp.sum(value.astype(F32) * decode, axis=0, keepdims=True)
    field = tile_rows_of(row)
    guess[...] = field
    store_sent((s0, s1, s2, s3), pick(field, slot_rows(places)))


def matvec(matrix, vector, out):
    count = LANES
    width = matrix.shape[1]
    field = vector[...]
    total = jnp.zeros((8, width), F32)
    for t in range(field.shape[0]):
        column = jnp.broadcast_to(field[t : t + 1, :], (count, count)).T
        wide = jnp.concatenate([column] * (width // count), axis=1)
        product = matrix[t * count : (t + 1) * count, :] * wide
        total = total + jnp.sum(product.reshape(count // 8, 8, width), axis=0)
    out[...] = tile_rows_of(jnp.sum(total, axis=0, keepdims=True))


def start_basis(places, a0, a1, a2, a3, local, guess, source, diagonal, basis, s0, s1, s2, s3):
    rows = slot_rows(places)
    came = spread_sum(arrived_rows((a0, a1, a2, a3)), rows, guess.shape[0])
    value = (source[...] + local[...] + came) / diagonal[...] - guess[...]
    basis[...] = value
    store_sent((s0, s1, s2, s3), pick(value, rows))


def next_basis(places, a0, a1, a2, a3, local, diagonal, basis, s0, s1, s2, s3):
    rows = slot_rows(places)
    came = spread_sum(arrived_rows((a0, a1, a2, a3)), rows, local.shape[0])
    value = (local[...] + came) / diagonal[...]
    basis[...] = value
    store_sent((s0, s1, s2, s3), pick(value, rows))


def last_basis(places, a0, a1, a2, a3, local, diagonal, b0, b1, b2, basis, moments):
    rows = slot_rows(places)
    came = spread_sum(arrived_rows((a0, a1, a2, a3)), rows, local.shape[0])
    value = (local[...] + came) / diagonal[...]
    basis[...] = value
    held = [b0[...], b1[...], b2[...], value]
    parts = []
    for k in range(2 * ITERS):
        left, right = held[k // 2], held[(k + 1) // 2]
        parts.append(jnp.sum(left * right * diagonal[...], axis=0, keepdims=True))
    parts.append(jnp.zeros((8 - 2 * ITERS, LANES), F32))
    moments[...] = jnp.concatenate(parts, axis=0)


def finish(moments, guess, diagonal, b0, b1, b2, b3, field, defect):
    sums = jnp.sum(moments[...], axis=1, keepdims=True)
    n = [jnp.broadcast_to(sums[k : k + 1, :], (8, LANES)) for k in range(2 * ITERS)]
    one, zero = jnp.ones((8, LANES), F32), jnp.zeros((8, LANES), F32)

    def paired(left, values):
        total = zero
        for i, a in enumerate(left):
            for j, b in enumerate(left):
                total = total + a * b * values[i + j]
        return total

    gaps = [n[k] - n[k + 1] for k in range(2 * ITERS - 1)]
    residual = [one]
    heading = [one]
    moved = [zero] * ITERS
    size = n[0]
    for step in range(ITERS):
        alpha = size / paired(heading, gaps)
        for i, h in enumerate(heading):
            moved[i] = moved[i] + alpha * h
        image = [
            (heading[i] if i < len(heading) else zero) - (heading[i - 1] if i > 0 else zero)
            for i in range(len(heading) + 1)
        ]
        residual = [
            (residual[i] if i < len(residual) else zero) - alpha * image[i]
            for i in range(len(image))
        ]
        if step + 1 < ITERS:
            following = paired(residual, n)
            beta = following / size
            heading = [
                residual[i] + (beta * heading[i] if i < len(heading) else zero)
                for i in range(len(residual))
            ]
            size = following
    held = [b0[...], b1[...], b2[...], b3[...]]
    total = guess[...]
    for c, b in zip(moved, held):
        total = total + c * b
    field[...] = total
    left = zero
    for c, b in zip(residual, held):
        left = left + c * b
    defect[...] = left * diagonal[...]


def matching(size, first):
    partner = list(range(size))
    for i in range(first, size - 1, 2):
        partner[i], partner[i + 1] = i + 1, i
    return list(enumerate(partner))


def sides_of_matchings():
    dom = lax.axis_index("dom") % 2
    sub = lax.axis_index("sub") % 2
    return jnp.stack([1 - dom, dom, 3 - sub, 2 + sub]).astype(jnp.int32)


def exchange(sent):
    arrived = []
    for g, axis in enumerate(("dom", "dom", "sub", "sub")):
        pairs = matching(lax.axis_size(axis), g % 2)
        arrived.append(lax.ppermute(sent[g], axis, pairs))
    return arrived


def total_over(value, axes):
    for axis in axes:
        size = lax.axis_size(axis)
        if size & (size - 1):
            value = lax.psum(value, axis)
            continue
        step = 1
        while step < size:
            value = value + lax.ppermute(value, axis, [(i, i ^ step) for i in range(size)])
            step *= 2
    return value


def per_device(
    state, tile_values, tile_rows, tile_columns, tile_counts, send_nodes, face_counts, capacity,
    source, w_self, w_neighbour, w_out, gains, bias, w_decode,
):
    nodes, width = state.shape
    slots = send_nodes.shape[2]
    tiles = nodes // LANES
    field = shape((tiles, LANES))
    feature_sent = [shape((width, slots), BF16)] * 4
    vector_sent = [shape((slots // LANES, LANES))] * 4
    weights = (w_self, w_neighbour, w_out, gains, bias)
    capacity = capacity.reshape(tiles, LANES)
    source = source.reshape(tiles, LANES)

    lat, hits, places, *sent = run(
        gather_first,
        [shape((width, nodes), BF16), shape((nodes, 4 * slots), BF16), shape((4 * slots // LANES, LANES), jnp.int32)]
        + feature_sent,
        (send_nodes, state), (sides_of_matchings(), face_counts), flops=2 * nodes * 4 * slots * width,
    )
    arrived = exchange(sent)
    matrix, half, inverse_rowsum, diagonal, local = run(
        build,
        [shape((nodes, nodes)), shape((nodes, nodes), BF16), shape((1, nodes)), field, shape((width, nodes))],
        (places, tile_values, lat, capacity),
        (tile_rows, tile_columns, tile_counts), flops=2 * nodes * nodes * width, moved=6_000_000,
    )
    lat, *sent = run(
        first_layer, [shape((width, nodes), BF16)] + feature_sent,
        (*arrived, local, inverse_rowsum, lat, hits, *weights), flops=6 * nodes * nodes * width,
    )
    arrived = exchange(sent)
    (local,) = run(
        local_features, [shape((width, nodes))], (lat, half), flops=2 * nodes * nodes * width, moved=4_000_000
    )
    guess, *sent = run(
        last_layer, [field] + vector_sent,
        (places, *arrived, local, inverse_rowsum, lat, hits, *weights, w_decode.reshape(1, width)),
        flops=6 * nodes * nodes * width,
    )

    def product(vector):
        return run(matvec, [field], (matrix, vector), flops=2 * nodes * nodes, moved=4 * nodes * nodes)[0]

    arrived = exchange(sent)
    local = product(guess)
    b0, *sent = run(
        start_basis, [field] + vector_sent,
        (places, *arrived, local, guess, source, diagonal),
    )
    held = [b0]
    for _ in range(ITERS - 1):
        arrived = exchange(sent)
        local = product(held[-1])
        b, *sent = run(
            next_basis, [field] + vector_sent, (places, *arrived, local, diagonal)
        )
        held.append(b)
    arrived = exchange(sent)
    local = product(held[-1])
    b, moments = run(
        last_basis, [field, shape((8, LANES))],
        (places, *arrived, local, diagonal, *held),
    )
    held.append(b)
    moments = total_over(moments, ("sub", "dom"))
    heat, defect = run(finish, [field, field], (moments, guess, diagonal, *held))
    return heat.reshape(nodes), defect.reshape(nodes)


def solution(mesh):
    both = ("dom", "sub")
    return jax.shard_map(
        per_device,
        mesh=mesh,
        in_specs=(
            P(both, None),
            P(both, None, None, None),
            P(both, None),
            P(both, None),
            P(both),
            P(both, None, None),
            P(both, None),
            P(both),
            P(both),
            P(),
            P(),
            P(),
            P(),
            P(),
            P(),
        ),
        out_specs=(P(both), P(both)),
        check_vma=False,
    )
```

```python
import jax
import jax.numpy as jnp
from jax import lax
from jax.experimental import pallas as pl
from jax.experimental.pallas import tpu as pltpu
from jax.sharding import PartitionSpec as P

LAYERS = 2
ITERS = 3
LANES = 128
VMEM_LIMIT = 24 * 1024 * 1024

F32 = jnp.float32
BF16 = jnp.bfloat16


def shape(dims, dtype=F32):
    return jax.ShapeDtypeStruct(dims, dtype)


def run(body, outs, operands, scalars=(), flops=1_000_000, moved=1_000_000):
    smem = pl.BlockSpec(memory_space=pltpu.SMEM)
    vmem = pl.BlockSpec(memory_space=pltpu.VMEM)
    return pl.pallas_call(
        body,
        out_shape=outs,
        in_specs=[smem] * len(scalars) + [vmem] * len(operands),
        out_specs=[vmem] * len(outs),
        compiler_params=pltpu.CompilerParams(vmem_limit_bytes=VMEM_LIMIT),
        cost_estimate=pl.CostEstimate(flops=flops, bytes_accessed=moved, transcendentals=0),
    )(*scalars, *operands)


def slot_rows(places):
    return [places[r : r + 1, :] for r in range(places.shape[0])]


def pick(vector, rows):
    index = jnp.concatenate(rows, axis=0)
    low = jnp.bitwise_and(index, LANES - 1)
    high = jnp.right_shift(index, 7)
    out = jnp.zeros(index.shape, F32)
    for t in range(vector.shape[0]):
        spread = jnp.broadcast_to(vector[t : t + 1, :], index.shape)
        got = jnp.take_along_axis(spread, low, axis=1, mode="promise_in_bounds")
        out = jnp.where(high == t, got, out)
    return out


def pieces(value):
    first = value.astype(BF16)
    rest = value - first.astype(F32)
    second = rest.astype(BF16)
    third = (rest - second.astype(F32)).astype(BF16)
    return first, second, third


def low_hits(rows):
    lane = lax.broadcasted_iota(jnp.int32, (LANES, LANES), 0)
    return jnp.concatenate(
        [(lane == jnp.bitwise_and(row, LANES - 1)).astype(F32).astype(BF16) for row in rows], axis=1
    )


def spread_sum(values, rows, tiles):
    tile = lax.broadcasted_iota(jnp.int32, (tiles, LANES), 0)
    parts = [
        jnp.where(tile == jnp.right_shift(row, 7), value, 0.0) for value, row in zip(values, rows)
    ]
    held = jnp.concatenate(parts, axis=1)
    stacked = jnp.concatenate([p.astype(F32) for p in pieces(held)], axis=0).astype(BF16)
    out = lax.dot_general(
        stacked, low_hits(rows), (((1,), (1,)), ((), ())), preferred_element_type=F32
    )
    return out[:tiles] + out[tiles : 2 * tiles] + out[2 * tiles :]


def arrived_rows(refs):
    return [ref[h : h + 1, :] for ref in refs for h in range(ref.shape[0])]


def store_sent(refs, sent):
    per = refs[0].shape[0]
    for k, ref in enumerate(refs):
        ref[...] = sent[k * per : (k + 1) * per, :]


def lane_rows(vector):
    return jnp.concatenate([vector[t : t + 1, :] for t in range(vector.shape[0])], axis=1)


def tile_rows_of(row):
    return jnp.concatenate(
        [row[:, t * LANES : (t + 1) * LANES] for t in range(row.shape[1] // LANES)], axis=0
    )


def gather_first(sides, counts, index, state, lat, hits, places, s0, s1, s2, s3):
    per = index.shape[2] // LANES
    for g in range(index.shape[1]):
        side = sides[g]
        for h in range(per):
            low, high = g // 2 * 2, g // 2 * 2 + 1
            span = slice(h * LANES, (h + 1) * LANES)
            row = jnp.where(side == low, index[0, low : low + 1, span], index[0, high : high + 1, span])
            slot = lax.broadcasted_iota(jnp.int32, (1, LANES), 1) + h * LANES
            r = g * per + h
            places[r : r + 1, :] = jnp.where(slot < counts[0, side], row, -1)
    node = lax.broadcasted_iota(jnp.int32, (state.shape[0], LANES), 0)
    for c, row in enumerate(slot_rows(places)):
        hits[:, c * LANES : (c + 1) * LANES] = (node == row).astype(F32).astype(BF16)
    lat[...] = state[...].T
    send_features(lat[...], hits, (s0, s1, s2, s3))


def send_features(lat, hits, outs):
    width = outs[0].shape[1]
    for k, out in enumerate(outs):
        out[...] = jnp.dot(
            lat, hits[:, k * width : (k + 1) * width], preferred_element_type=F32
        ).astype(BF16)


def build(
    tile_rows, tile_columns, tile_counts, places, tiles, lat, capacity,
    matrix, half, inverse_rowsum, diagonal, local,
):
    count = tiles.shape[2]
    node_tiles = matrix.shape[0] // count
    matrix[...] = jnp.zeros(matrix.shape, F32)
    for t in range(node_tiles):
        span = slice(t * count, (t + 1) * count)
        block = tiles[0, t]
        matrix[span, span] = block + block.T

    def add(t, carry):
        r = pl.multiple_of(tile_rows[0, t] * count, count)
        c = pl.multiple_of(tile_columns[0, t] * count, count)
        block = tiles[0, t]
        matrix[pl.ds(r, count), pl.ds(c, count)] += block
        matrix[pl.ds(c, count), pl.ds(r, count)] += block.T
        return carry

    lax.fori_loop(node_tiles, tile_counts[0], add, 0)
    rows = slot_rows(places)
    faces = spread_sum([jnp.ones((1, LANES), F32)] * len(rows), rows, node_tiles)
    total = jnp.sum(matrix[...], axis=0, keepdims=True)
    rowsum = tile_rows_of(total) + faces
    inverse_rowsum[...] = lane_rows(1.0 / rowsum)
    diagonal[...] = capacity[...] + rowsum
    half[...] = matrix[...].astype(BF16)
    local[...] = jnp.dot(lat[...], half[...], preferred_element_type=F32)


def local_features(lat, half, local):
    local[...] = jnp.dot(lat[...], half[...], preferred_element_type=F32)


def layer_step(layer, arrived, local, inverse_rowsum, lat, hits, w_self, w_neighbour, w_out, gains, bias):
    came = jnp.concatenate([a[...] for a in arrived], axis=1)
    coupled = lax.dot_general(
        came, hits[...], (((1,), (1,)), ((), ())), preferred_element_type=F32
    )
    mean = (local[...] + coupled) * inverse_rowsum[...]
    columns = jnp.concatenate(
        [gains[layer], bias[...], jnp.zeros((8 - 4, bias.shape[1]), F32)], axis=0
    ).T
    own = lat[...].astype(F32)

    def normed(value, gain):
        scale = lax.rsqrt(jnp.mean(value * value, axis=0, keepdims=True) + 1e-06)
        return (value * scale * gain).astype(BF16)

    normed_self = normed(own, columns[:, 0:1])
    normed_neighbour = normed(mean, columns[:, 1:2])

    def project(weight, value):
        return lax.dot_general(
            weight, value, (((0,), (0,)), ((), ())), preferred_element_type=F32
        )

    linear = project(w_self[layer], normed_self) + project(w_neighbour[layer], normed_neighbour)
    linear = linear + columns[:, 2 + layer : 3 + layer]
    activated = (linear / (1.0 + jnp.exp(-linear))).astype(BF16)
    return (own + project(w_out[layer], activated)).astype(BF16)


def first_layer(
    a0, a1, a2, a3, local, inverse_rowsum, lat, hits, w_self, w_neighbour, w_out, gains, bias,
    new, s0, s1, s2, s3,
):
    value = layer_step(
        0, (a0, a1, a2, a3), local, inverse_rowsum, lat, hits, w_self, w_neighbour, w_out, gains, bias
    )
    new[...] = value
    send_features(value, hits, (s0, s1, s2, s3))


def last_layer(
    places, a0, a1, a2, a3, local, inverse_rowsum, lat, hits, w_self, w_neighbour, w_out,
    gains, bias, w_decode, guess, s0, s1, s2, s3,
):
    value = layer_step(
        LAYERS - 1, (a0, a1, a2, a3), local, inverse_rowsum, lat, hits, w_self, w_neighbour, w_out,
        gains, bias,
    )
    decode = jnp.broadcast_to(w_decode[...], (8, w_decode.shape[1])).T[:, 0:1]
    row = jnp.sum(value.astype(F32) * decode, axis=0, keepdims=True)
    field = tile_rows_of(row)
    guess[...] = field
    store_sent((s0, s1, s2, s3), pick(field, slot_rows(places)))


def matvec(matrix, vector, out):
    count = LANES
    width = matrix.shape[1]
    field = vector[...]
    total = jnp.zeros((8, width), F32)
    for t in range(field.shape[0]):
        column = jnp.broadcast_to(field[t : t + 1, :], (count, count)).T
        wide = jnp.concatenate([column] * (width // count), axis=1)
        product = matrix[t * count : (t + 1) * count, :] * wide
        total = total + jnp.sum(product.reshape(count // 8, 8, width), axis=0)
    out[...] = tile_rows_of(jnp.sum(total, axis=0, keepdims=True))


def start_basis(places, a0, a1, a2, a3, local, guess, source, diagonal, basis, s0, s1, s2, s3):
    rows = slot_rows(places)
    came = spread_sum(arrived_rows((a0, a1, a2, a3)), rows, guess.shape[0])
    value = (source[...] + local[...] + came) / diagonal[...] - guess[...]
    basis[...] = value
    store_sent((s0, s1, s2, s3), pick(value, rows))


def next_basis(places, a0, a1, a2, a3, local, diagonal, basis, s0, s1, s2, s3):
    rows = slot_rows(places)
    came = spread_sum(arrived_rows((a0, a1, a2, a3)), rows, local.shape[0])
    value = (local[...] + came) / diagonal[...]
    basis[...] = value
    store_sent((s0, s1, s2, s3), pick(value, rows))


def last_basis(places, a0, a1, a2, a3, local, diagonal, b0, b1, b2, basis, moments):
    rows = slot_rows(places)
    came = spread_sum(arrived_rows((a0, a1, a2, a3)), rows, local.shape[0])
    value = (local[...] + came) / diagonal[...]
    basis[...] = value
    held = [b0[...], b1[...], b2[...], value]
    parts = []
    for k in range(2 * ITERS):
        left, right = held[k // 2], held[(k + 1) // 2]
        parts.append(jnp.sum(left * right * diagonal[...], axis=0, keepdims=True))
    parts.append(jnp.zeros((8 - 2 * ITERS, LANES), F32))
    moments[...] = jnp.concatenate(parts, axis=0)


def finish(moments, guess, diagonal, b0, b1, b2, b3, field, defect):
    sums = jnp.sum(moments[...], axis=1, keepdims=True)
    n = [jnp.broadcast_to(sums[k : k + 1, :], (8, LANES)) for k in range(2 * ITERS)]
    one, zero = jnp.ones((8, LANES), F32), jnp.zeros((8, LANES), F32)

    def paired(left, values):
        total = zero
        for i, a in enumerate(left):
            for j, b in enumerate(left):
                total = total + a * b * values[i + j]
        return total

    gaps = [n[k] - n[k + 1] for k in range(2 * ITERS - 1)]
    residual = [one]
    heading = [one]
    moved = [zero] * ITERS
    size = n[0]
    for step in range(ITERS):
        alpha = size / paired(heading, gaps)
        for i, h in enumerate(heading):
            moved[i] = moved[i] + alpha * h
        image = [
            (heading[i] if i < len(heading) else zero) - (heading[i - 1] if i > 0 else zero)
            for i in range(len(heading) + 1)
        ]
        residual = [
            (residual[i] if i < len(residual) else zero) - alpha * image[i]
            for i in range(len(image))
        ]
        if step + 1 < ITERS:
            following = paired(residual, n)
            beta = following / size
            heading = [
                residual[i] + (beta * heading[i] if i < len(heading) else zero)
                for i in range(len(residual))
            ]
            size = following
    held = [b0[...], b1[...], b2[...], b3[...]]
    total = guess[...]
    for c, b in zip(moved, held):
        total = total + c * b
    field[...] = total
    left = zero
    for c, b in zip(residual, held):
        left = left + c * b
    defect[...] = left * diagonal[...]


def matching(sizes, along, first):
    pairs = []
    for dom in range(sizes[0]):
        for sub in range(sizes[1]):
            at = [dom, sub]
            to = [dom, sub]
            other = 1 - along
            mate = (at[along] - first ^ 1) + first
            if at[along] >= first and mate < sizes[along]:
                to[along] = mate
            elif at[other] ^ 1 < sizes[other]:
                to[other] = at[other] ^ 1
            pairs.append((at[0] * sizes[1] + at[1], to[0] * sizes[1] + to[1]))
    return pairs


def sides_of_matchings():
    dom = lax.axis_index("dom") % 2
    sub = lax.axis_index("sub") % 2
    return jnp.stack([1 - dom, dom, 3 - sub, 2 + sub]).astype(jnp.int32)


def exchange(sent):
    axes = ("dom", "sub")
    sizes = [lax.axis_size(axis) for axis in axes]
    return [lax.ppermute(sent[g], axes, matching(sizes, g // 2, g % 2)) for g in range(4)]


def total_over(value, axes):
    for axis in axes:
        size = lax.axis_size(axis)
        if size & (size - 1):
            value = lax.psum(value, axis)
            continue
        step = 1
        while step < size:
            value = value + lax.ppermute(value, axis, [(i, i ^ step) for i in range(size)])
            step *= 2
    return value


def per_device(
    state, tile_values, tile_rows, tile_columns, tile_counts, send_nodes, face_counts, capacity,
    source, w_self, w_neighbour, w_out, gains, bias, w_decode,
):
    nodes, width = state.shape
    slots = send_nodes.shape[2]
    tiles = nodes // LANES
    field = shape((tiles, LANES))
    feature_sent = [shape((width, slots), BF16)] * 4
    vector_sent = [shape((slots // LANES, LANES))] * 4
    weights = (w_self, w_neighbour, w_out, gains, bias)
    capacity = capacity.reshape(tiles, LANES)
    source = source.reshape(tiles, LANES)

    lat, hits, places, *sent = run(
        gather_first,
        [shape((width, nodes), BF16), shape((nodes, 4 * slots), BF16), shape((4 * slots // LANES, LANES), jnp.int32)]
        + feature_sent,
        (send_nodes, state), (sides_of_matchings(), face_counts), flops=2 * nodes * 4 * slots * width,
    )
    arrived = exchange(sent)
    matrix, half, inverse_rowsum, diagonal, local = run(
        build,
        [shape((nodes, nodes)), shape((nodes, nodes), BF16), shape((1, nodes)), field, shape((width, nodes))],
        (places, tile_values, lat, capacity),
        (tile_rows, tile_columns, tile_counts), flops=2 * nodes * nodes * width, moved=6_000_000,
    )
    lat, *sent = run(
        first_layer, [shape((width, nodes), BF16)] + feature_sent,
        (*arrived, local, inverse_rowsum, lat, hits, *weights), flops=6 * nodes * nodes * width,
    )
    arrived = exchange(sent)
    (local,) = run(
        local_features, [shape((width, nodes))], (lat, half), flops=2 * nodes * nodes * width, moved=4_000_000
    )
    guess, *sent = run(
        last_layer, [field] + vector_sent,
        (places, *arrived, local, inverse_rowsum, lat, hits, *weights, w_decode.reshape(1, width)),
        flops=6 * nodes * nodes * width,
    )

    def product(vector):
        return run(matvec, [field], (matrix, vector), flops=2 * nodes * nodes, moved=4 * nodes * nodes)[0]

    arrived = exchange(sent)
    local = product(guess)
    b0, *sent = run(
        start_basis, [field] + vector_sent,
        (places, *arrived, local, guess, source, diagonal),
    )
    held = [b0]
    for _ in range(ITERS - 1):
        arrived = exchange(sent)
        local = product(held[-1])
        b, *sent = run(
            next_basis, [field] + vector_sent, (places, *arrived, local, diagonal)
        )
        held.append(b)
    arrived = exchange(sent)
    local = product(held[-1])
    b, moments = run(
        last_basis, [field, shape((8, LANES))],
        (places, *arrived, local, diagonal, *held),
    )
    held.append(b)
    moments = total_over(moments, ("sub", "dom"))
    heat, defect = run(finish, [field, field], (moments, guess, diagonal, *held))
    return heat.reshape(nodes), defect.reshape(nodes)


def solution(mesh):
    both = ("dom", "sub")
    return jax.shard_map(
        per_device,
        mesh=mesh,
        in_specs=(
            P(both, None),
            P(both, None, None, None),
            P(both, None),
            P(both, None),
            P(both),
            P(both, None, None),
            P(both, None),
            P(both),
            P(both),
            P(),
            P(),
            P(),
            P(),
            P(),
            P(),
        ),
        out_specs=(P(both), P(both)),
        check_vma=False,
    )
```

```python
import functools

import jax
import jax.numpy as jnp
from jax import lax
from jax.experimental import pallas as pl
from jax.experimental.pallas import tpu as pltpu
from jax.sharding import PartitionSpec as P

LAYERS = 2
ITERS = 3
LANES = 128
VMEM_LIMIT = 24 * 1024 * 1024

F32 = jnp.float32
BF16 = jnp.bfloat16


def shape(dims, dtype=F32):
    return jax.ShapeDtypeStruct(dims, dtype)


def run(body, outs, operands, scalars=(), flops=1_000_000, moved=1_000_000):
    smem = pl.BlockSpec(memory_space=pltpu.SMEM)
    vmem = pl.BlockSpec(memory_space=pltpu.VMEM)
    return pl.pallas_call(
        body,
        out_shape=outs,
        in_specs=[smem] * len(scalars) + [vmem] * len(operands),
        out_specs=[vmem] * len(outs),
        compiler_params=pltpu.CompilerParams(vmem_limit_bytes=VMEM_LIMIT),
        cost_estimate=pl.CostEstimate(flops=flops, bytes_accessed=moved, transcendentals=0),
    )(*scalars, *operands)


def slot_rows(places):
    return [places[r : r + 1, :] for r in range(places.shape[0])]


def pick(vector, rows):
    index = jnp.concatenate(rows, axis=0)
    low = jnp.bitwise_and(index, LANES - 1)
    high = jnp.right_shift(index, 7)
    out = jnp.zeros(index.shape, F32)
    for t in range(vector.shape[0]):
        spread = jnp.broadcast_to(vector[t : t + 1, :], index.shape)
        got = jnp.take_along_axis(spread, low, axis=1, mode="promise_in_bounds")
        out = jnp.where(high == t, got, out)
    return out


def pieces(value):
    first = value.astype(BF16)
    rest = value - first.astype(F32)
    second = rest.astype(BF16)
    third = (rest - second.astype(F32)).astype(BF16)
    return first, second, third


def low_hits(rows):
    lane = lax.broadcasted_iota(jnp.int32, (LANES, LANES), 0)
    return jnp.concatenate(
        [(lane == jnp.bitwise_and(row, LANES - 1)).astype(F32).astype(BF16) for row in rows], axis=1
    )


def spread_sum(values, rows, tiles):
    tile = lax.broadcasted_iota(jnp.int32, (tiles, LANES), 0)
    parts = [
        jnp.where(tile == jnp.right_shift(row, 7), value, 0.0) for value, row in zip(values, rows)
    ]
    held = jnp.concatenate(parts, axis=1)
    stacked = jnp.concatenate([p.astype(F32) for p in pieces(held)], axis=0).astype(BF16)
    out = lax.dot_general(
        stacked, low_hits(rows), (((1,), (1,)), ((), ())), preferred_element_type=F32
    )
    return out[:tiles] + out[tiles : 2 * tiles] + out[2 * tiles :]


def arrived_rows(refs):
    return [ref[h : h + 1, :] for ref in refs for h in range(ref.shape[0])]


def store_sent(refs, sent):
    per = refs[0].shape[0]
    for k, ref in enumerate(refs):
        ref[...] = sent[k * per : (k + 1) * per, :]


def lane_rows(vector):
    return jnp.concatenate([vector[t : t + 1, :] for t in range(vector.shape[0])], axis=1)


def tile_rows_of(row):
    return jnp.concatenate(
        [row[:, t * LANES : (t + 1) * LANES] for t in range(row.shape[1] // LANES)], axis=0
    )


def gather_first(sides, counts, index, state, lat, hits, places, s0, s1, s2, s3):
    per = index.shape[2] // LANES
    for g in range(index.shape[1]):
        side = sides[g]
        for h in range(per):
            low, high = g // 2 * 2, g // 2 * 2 + 1
            span = slice(h * LANES, (h + 1) * LANES)
            row = jnp.where(side == low, index[0, low : low + 1, span], index[0, high : high + 1, span])
            slot = lax.broadcasted_iota(jnp.int32, (1, LANES), 1) + h * LANES
            r = g * per + h
            places[r : r + 1, :] = jnp.where(slot < counts[0, side], row, -1)
    node = lax.broadcasted_iota(jnp.int32, (state.shape[0], LANES), 0)
    for c, row in enumerate(slot_rows(places)):
        hits[:, c * LANES : (c + 1) * LANES] = (node == row).astype(F32).astype(BF16)
    lat[...] = state[...].T
    send_features(lat[...], hits, (s0, s1, s2, s3))


def send_features(lat, hits, outs):
    width = outs[0].shape[1]
    for k, out in enumerate(outs):
        out[...] = jnp.dot(
            lat, hits[:, k * width : (k + 1) * width], preferred_element_type=F32
        ).astype(BF16)


def build(
    tile_rows, tile_columns, tile_counts, places, tiles, lat, capacity,
    matrix, half, inverse_rowsum, diagonal, local,
):
    count = tiles.shape[2]
    node_tiles = matrix.shape[0] // count
    matrix[...] = jnp.zeros(matrix.shape, F32)
    for t in range(node_tiles):
        span = slice(t * count, (t + 1) * count)
        block = tiles[0, t]
        matrix[span, span] = block + block.T

    def add(t, carry):
        r = pl.multiple_of(tile_rows[0, t] * count, count)
        c = pl.multiple_of(tile_columns[0, t] * count, count)
        block = tiles[0, t]
        matrix[pl.ds(r, count), pl.ds(c, count)] += block
        matrix[pl.ds(c, count), pl.ds(r, count)] += block.T
        return carry

    lax.fori_loop(node_tiles, tile_counts[0], add, 0)
    rows = slot_rows(places)
    faces = spread_sum([jnp.ones((1, LANES), F32)] * len(rows), rows, node_tiles)
    total = jnp.sum(matrix[...], axis=0, keepdims=True)
    rowsum = tile_rows_of(total) + faces
    inverse_rowsum[...] = lane_rows(1.0 / rowsum)
    diagonal[...] = capacity[...] + rowsum
    half[...] = matrix[...].astype(BF16)
    local[...] = jnp.dot(lat[...], half[...], preferred_element_type=F32)


def local_features(lat, half, local):
    local[...] = jnp.dot(lat[...], half[...], preferred_element_type=F32)


def layer_step(layer, arrived, local, inverse_rowsum, lat, hits, w_self, w_neighbour, w_out, gains, bias):
    came = jnp.concatenate([a[...] for a in arrived], axis=1)
    coupled = lax.dot_general(
        came, hits[...], (((1,), (1,)), ((), ())), preferred_element_type=F32
    )
    mean = (local[...] + coupled) * inverse_rowsum[...]
    columns = jnp.concatenate(
        [gains[layer], bias[...], jnp.zeros((8 - 4, bias.shape[1]), F32)], axis=0
    ).T
    own = lat[...].astype(F32)

    def normed(value, gain):
        scale = lax.rsqrt(jnp.mean(value * value, axis=0, keepdims=True) + 1e-06)
        return (value * scale * gain).astype(BF16)

    normed_self = normed(own, columns[:, 0:1])
    normed_neighbour = normed(mean, columns[:, 1:2])

    def project(weight, value):
        return lax.dot_general(
            weight, value, (((0,), (0,)), ((), ())), preferred_element_type=F32
        )

    linear = project(w_self[layer], normed_self) + project(w_neighbour[layer], normed_neighbour)
    linear = linear + columns[:, 2 + layer : 3 + layer]
    activated = (linear / (1.0 + jnp.exp(-linear))).astype(BF16)
    return (own + project(w_out[layer], activated)).astype(BF16)


def first_layer(
    a0, a1, a2, a3, local, inverse_rowsum, lat, hits, w_self, w_neighbour, w_out, gains, bias,
    new, s0, s1, s2, s3,
):
    value = layer_step(
        0, (a0, a1, a2, a3), local, inverse_rowsum, lat, hits, w_self, w_neighbour, w_out, gains, bias
    )
    new[...] = value
    send_features(value, hits, (s0, s1, s2, s3))


def last_layer(
    places, a0, a1, a2, a3, local, inverse_rowsum, lat, hits, w_self, w_neighbour, w_out,
    gains, bias, w_decode, guess, s0, s1, s2, s3,
):
    value = layer_step(
        LAYERS - 1, (a0, a1, a2, a3), local, inverse_rowsum, lat, hits, w_self, w_neighbour, w_out,
        gains, bias,
    )
    decode = jnp.broadcast_to(w_decode[...], (8, w_decode.shape[1])).T[:, 0:1]
    row = jnp.sum(value.astype(F32) * decode, axis=0, keepdims=True)
    field = tile_rows_of(row)
    guess[...] = field
    store_sent((s0, s1, s2, s3), pick(field, slot_rows(places)))


def product(matrix, field):
    count = LANES
    width = matrix.shape[1]
    total = jnp.zeros((8, width), F32)
    for t in range(field.shape[0]):
        column = jnp.broadcast_to(field[t : t + 1, :], (count, count)).T
        wide = jnp.concatenate([column] * (width // count), axis=1)
        part = matrix[t * count : (t + 1) * count, :] * wide
        total = total + jnp.sum(part.reshape(count // 8, 8, width), axis=0)
    return tile_rows_of(jnp.sum(total, axis=0, keepdims=True))


def matvec(matrix, vector, out):
    out[...] = product(matrix, vector[...])


def start_basis(places, a0, a1, a2, a3, local, guess, source, diagonal, basis, s0, s1, s2, s3):
    rows = slot_rows(places)
    came = spread_sum(arrived_rows((a0, a1, a2, a3)), rows, guess.shape[0])
    value = (source[...] + local[...] + came) / diagonal[...] - guess[...]
    basis[...] = value
    store_sent((s0, s1, s2, s3), pick(value, rows))


def next_basis(places, a0, a1, a2, a3, local, diagonal, basis, s0, s1, s2, s3):
    rows = slot_rows(places)
    came = spread_sum(arrived_rows((a0, a1, a2, a3)), rows, local.shape[0])
    value = (local[...] + came) / diagonal[...]
    basis[...] = value
    store_sent((s0, s1, s2, s3), pick(value, rows))


def last_basis(places, a0, a1, a2, a3, local, diagonal, b0, b1, matrix, basis, image, packet):
    rows = slot_rows(places)
    came = spread_sum(arrived_rows((a0, a1, a2, a3)), rows, local.shape[0])
    value = (local[...] + came) / diagonal[...]
    basis[...] = value
    mapped = product(matrix, value)
    image[...] = mapped
    held = [b0[...], b1[...], value]
    parts = []
    for k in range(2 * ITERS - 1):
        left, right = held[k // 2], held[(k + 1) // 2]
        parts.append(jnp.sum(left * right * diagonal[...], axis=0, keepdims=True))
    parts.append(jnp.sum(value * mapped, axis=0, keepdims=True))
    parts.append(jnp.zeros((8 - 2 * ITERS, LANES), F32))
    packet[0:8, :] = pick(value, rows)
    packet[8:16, :] = jnp.concatenate(parts, axis=0)


def added(values):
    values = list(values)
    while len(values) > 1:
        values = [sum(values[i : i + 2][1:], values[i]) for i in range(0, len(values), 2)]
    return values[0]


def finish(sizes, where, packets, places, image, guess, diagonal, b0, b1, b2, field, defect):
    doms, subs = sizes

    def block(dom, sub, half):
        at = jnp.bitwise_xor(dom, where[0]) * subs + jnp.bitwise_xor(sub, where[1])
        return packets[pl.ds(pl.multiple_of(at * 16 + half * 8, 8), 8), :]

    slots = [[block(d, s, 0) for s in range(subs)] for d in range(doms)]
    edges = []
    for d in range(doms):
        for s in range(subs):
            for g, (i, j) in ((d % 2, (d + 1, s)), (2 + s % 2, (d, s + 1))):
                if i < doms and j < subs:
                    edges.append((slots[d][s] * slots[i][j])[2 * g : 2 * g + 2, :])
    edges = jnp.sum(added(edges), axis=0, keepdims=True)
    partial = added([block(d, s, 1) for d in range(doms) for s in range(subs)])
    came = []
    for g in range(4):
        mine = block(where[2 + 2 * g], where[3 + 2 * g], 0)
        came += [mine[2 * g : 2 * g + 1, :], mine[2 * g + 1 : 2 * g + 2, :]]
    last = (image[...] + spread_sum(came, slot_rows(places), image.shape[0])) / diagonal[...]

    n = []
    for k in range(2 * ITERS):
        row = partial[k : k + 1, :]
        if k == 2 * ITERS - 1:
            row = row + 2.0 * edges
        n.append(jnp.broadcast_to(jnp.sum(row, axis=1, keepdims=True), (8, LANES)))
    one, zero = jnp.ones((8, LANES), F32), jnp.zeros((8, LANES), F32)

    def paired(left, values):
        total = zero
        for i, a in enumerate(left):
            for j, b in enumerate(left):
                total = total + a * b * values[i + j]
        return total

    gaps = [n[k] - n[k + 1] for k in range(2 * ITERS - 1)]
    residual = [one]
    heading = [one]
    moved = [zero] * ITERS
    size = n[0]
    for step in range(ITERS):
        alpha = size / paired(heading, gaps)
        for i, h in enumerate(heading):
            moved[i] = moved[i] + alpha * h
        change = [
            (heading[i] if i < len(heading) else zero) - (heading[i - 1] if i > 0 else zero)
            for i in range(len(heading) + 1)
        ]
        residual = [
            (residual[i] if i < len(residual) else zero) - alpha * change[i]
            for i in range(len(change))
        ]
        if step + 1 < ITERS:
            following = paired(residual, n)
            beta = following / size
            heading = [
                residual[i] + (beta * heading[i] if i < len(heading) else zero)
                for i in range(len(residual))
            ]
            size = following
    held = [b0[...], b1[...], b2[...], last]
    total = guess[...]
    for c, b in zip(moved, held):
        total = total + c * b
    field[...] = total
    left = zero
    for c, b in zip(residual, held):
        left = left + c * b
    defect[...] = left * diagonal[...]


def matching(sizes, along, first):
    pairs = []
    for dom in range(sizes[0]):
        for sub in range(sizes[1]):
            at = [dom, sub]
            to = [dom, sub]
            other = 1 - along
            mate = (at[along] - first ^ 1) + first
            if at[along] >= first and mate < sizes[along]:
                to[along] = mate
            elif at[other] ^ 1 < sizes[other]:
                to[other] = at[other] ^ 1
            pairs.append((at[0] * sizes[1] + at[1], to[0] * sizes[1] + to[1]))
    return pairs


def sides_of_matchings():
    dom = lax.axis_index("dom") % 2
    sub = lax.axis_index("sub") % 2
    return jnp.stack([1 - dom, dom, 3 - sub, 2 + sub]).astype(jnp.int32)


def exchange(sent):
    axes = ("dom", "sub")
    sizes = [lax.axis_size(axis) for axis in axes]
    return [lax.ppermute(sent[g], axes, matching(sizes, g // 2, g % 2)) for g in range(4)]


def partners():
    at = [lax.axis_index("dom"), lax.axis_index("sub")]
    sizes = [lax.axis_size("dom"), lax.axis_size("sub")]
    out = []
    for g in range(4):
        along, first = g // 2, g % 2
        mate = jnp.bitwise_xor(at[along] - first, 1) + first
        known = (at[along] >= first) & (mate < sizes[along])
        to = list(at)
        to[along] = jnp.where(known, mate, at[along])
        out += to
    return jnp.stack(out).astype(jnp.int32)


def gathered(packet):
    return lax.all_gather(packet, ("dom", "sub"), tiled=True), jnp.zeros((2,), jnp.int32)


def per_device(
    state, tile_values, tile_rows, tile_columns, tile_counts, send_nodes, face_counts, capacity,
    source, w_self, w_neighbour, w_out, gains, bias, w_decode,
):
    nodes, width = state.shape
    slots = send_nodes.shape[2]
    tiles = nodes // LANES
    field = shape((tiles, LANES))
    feature_sent = [shape((width, slots), BF16)] * 4
    vector_sent = [shape((slots // LANES, LANES))] * 4
    weights = (w_self, w_neighbour, w_out, gains, bias)
    capacity = capacity.reshape(tiles, LANES)
    source = source.reshape(tiles, LANES)

    lat, hits, places, *sent = run(
        gather_first,
        [shape((width, nodes), BF16), shape((nodes, 4 * slots), BF16), shape((4 * slots // LANES, LANES), jnp.int32)]
        + feature_sent,
        (send_nodes, state), (sides_of_matchings(), face_counts), flops=2 * nodes * 4 * slots * width,
    )
    arrived = exchange(sent)
    matrix, half, inverse_rowsum, diagonal, local = run(
        build,
        [shape((nodes, nodes)), shape((nodes, nodes), BF16), shape((1, nodes)), field, shape((width, nodes))],
        (places, tile_values, lat, capacity),
        (tile_rows, tile_columns, tile_counts), flops=2 * nodes * nodes * width, moved=6_000_000,
    )
    lat, *sent = run(
        first_layer, [shape((width, nodes), BF16)] + feature_sent,
        (*arrived, local, inverse_rowsum, lat, hits, *weights), flops=6 * nodes * nodes * width,
    )
    arrived = exchange(sent)
    (local,) = run(
        local_features, [shape((width, nodes))], (lat, half), flops=2 * nodes * nodes * width, moved=4_000_000
    )
    guess, *sent = run(
        last_layer, [field] + vector_sent,
        (places, *arrived, local, inverse_rowsum, lat, hits, *weights, w_decode.reshape(1, width)),
        flops=6 * nodes * nodes * width,
    )

    def mapped(vector):
        return run(matvec, [field], (matrix, vector), flops=2 * nodes * nodes, moved=4 * nodes * nodes)[0]

    arrived = exchange(sent)
    local = mapped(guess)
    b0, *sent = run(
        start_basis, [field] + vector_sent, (places, *arrived, local, guess, source, diagonal)
    )
    arrived = exchange(sent)
    local = mapped(b0)
    b1, *sent = run(next_basis, [field] + vector_sent, (places, *arrived, local, diagonal))
    arrived = exchange(sent)
    local = mapped(b1)
    b2, image, packet = run(
        last_basis, [field, field, shape((16, LANES))],
        (places, *arrived, local, diagonal, b0, b1, matrix),
    )
    packets, order = gathered(packet)
    sizes = (lax.axis_size("dom"), lax.axis_size("sub"))
    heat, defect = run(
        functools.partial(finish, sizes), [field, field],
        (packets, places, image, guess, diagonal, b0, b1, b2),
        (jnp.concatenate([order, partners()]),),
    )
    return heat.reshape(nodes), defect.reshape(nodes)


def solution(mesh):
    both = ("dom", "sub")
    return jax.shard_map(
        per_device,
        mesh=mesh,
        in_specs=(
            P(both, None),
            P(both, None, None, None),
            P(both, None),
            P(both, None),
            P(both),
            P(both, None, None),
            P(both, None),
            P(both),
            P(both),
            P(),
            P(),
            P(),
            P(),
            P(),
            P(),
        ),
        out_specs=(P(both), P(both)),
        check_vma=False,
    )
```

```python
import functools

import jax
import jax.numpy as jnp
from jax import lax
from jax.experimental import pallas as pl
from jax.experimental.pallas import tpu as pltpu
from jax.sharding import PartitionSpec as P

LAYERS = 2
ITERS = 3
LANES = 128
VMEM_LIMIT = 24 * 1024 * 1024

F32 = jnp.float32
BF16 = jnp.bfloat16


def shape(dims, dtype=F32):
    return jax.ShapeDtypeStruct(dims, dtype)


def run(body, outs, operands, scalars=(), flops=1_000_000, moved=1_000_000):
    smem = pl.BlockSpec(memory_space=pltpu.SMEM)
    vmem = pl.BlockSpec(memory_space=pltpu.VMEM)
    return pl.pallas_call(
        body,
        out_shape=outs,
        in_specs=[smem] * len(scalars) + [vmem] * len(operands),
        out_specs=[vmem] * len(outs),
        compiler_params=pltpu.CompilerParams(vmem_limit_bytes=VMEM_LIMIT),
        cost_estimate=pl.CostEstimate(flops=flops, bytes_accessed=moved, transcendentals=0),
    )(*scalars, *operands)


def slot_rows(places):
    return [places[r : r + 1, :] for r in range(places.shape[0])]


def pick(vector, rows):
    index = jnp.concatenate(rows, axis=0)
    low = jnp.bitwise_and(index, LANES - 1)
    high = jnp.right_shift(index, 7)
    out = jnp.zeros(index.shape, F32)
    for t in range(vector.shape[0]):
        spread = jnp.broadcast_to(vector[t : t + 1, :], index.shape)
        got = jnp.take_along_axis(spread, low, axis=1, mode="promise_in_bounds")
        out = jnp.where(high == t, got, out)
    return out


def pieces(value):
    first = value.astype(BF16)
    rest = value - first.astype(F32)
    second = rest.astype(BF16)
    third = (rest - second.astype(F32)).astype(BF16)
    return first, second, third


def low_hits(rows):
    lane = lax.broadcasted_iota(jnp.int32, (LANES, LANES), 0)
    return jnp.concatenate(
        [(lane == jnp.bitwise_and(row, LANES - 1)).astype(F32).astype(BF16) for row in rows], axis=1
    )


def spread_sum(values, rows, tiles):
    tile = lax.broadcasted_iota(jnp.int32, (tiles, LANES), 0)
    parts = [
        jnp.where(tile == jnp.right_shift(row, 7), value, 0.0) for value, row in zip(values, rows)
    ]
    held = jnp.concatenate(parts, axis=1)
    stacked = jnp.concatenate([p.astype(F32) for p in pieces(held)], axis=0).astype(BF16)
    out = lax.dot_general(
        stacked, low_hits(rows), (((1,), (1,)), ((), ())), preferred_element_type=F32
    )
    return out[:tiles] + out[tiles : 2 * tiles] + out[2 * tiles :]


def arrived_rows(refs):
    return [ref[h : h + 1, :] for ref in refs for h in range(ref.shape[0])]


def store_sent(refs, sent):
    per = refs[0].shape[0]
    for k, ref in enumerate(refs):
        ref[...] = sent[k * per : (k + 1) * per, :]


def lane_rows(vector):
    return jnp.concatenate([vector[t : t + 1, :] for t in range(vector.shape[0])], axis=1)


def tile_rows_of(row):
    return jnp.concatenate(
        [row[:, t * LANES : (t + 1) * LANES] for t in range(row.shape[1] // LANES)], axis=0
    )


def gather_first(sides, counts, index, state, lat, hits, places, s0, s1, s2, s3):
    per = index.shape[2] // LANES
    for g in range(index.shape[1]):
        side = sides[g]
        for h in range(per):
            low, high = g // 2 * 2, g // 2 * 2 + 1
            span = slice(h * LANES, (h + 1) * LANES)
            row = jnp.where(side == low, index[0, low : low + 1, span], index[0, high : high + 1, span])
            slot = lax.broadcasted_iota(jnp.int32, (1, LANES), 1) + h * LANES
            r = g * per + h
            places[r : r + 1, :] = jnp.where(slot < counts[0, side], row, -1)
    node = lax.broadcasted_iota(jnp.int32, (state.shape[0], LANES), 0)
    for c, row in enumerate(slot_rows(places)):
        hits[:, c * LANES : (c + 1) * LANES] = (node == row).astype(F32).astype(BF16)
    lat[...] = state[...].T
    send_features(lat[...], hits, (s0, s1, s2, s3))


def send_features(lat, hits, outs):
    width = outs[0].shape[1]
    for k, out in enumerate(outs):
        out[...] = jnp.dot(
            lat, hits[:, k * width : (k + 1) * width], preferred_element_type=F32
        ).astype(BF16)


def build(
    tile_rows, tile_columns, tile_counts, places, tiles, lat, capacity,
    matrix, half, inverse_rowsum, diagonal, local,
):
    count = tiles.shape[2]
    node_tiles = matrix.shape[0] // count
    matrix[...] = jnp.zeros(matrix.shape, F32)
    for t in range(node_tiles):
        span = slice(t * count, (t + 1) * count)
        block = tiles[0, t]
        matrix[span, span] = block + block.T

    def add(t, carry):
        r = pl.multiple_of(tile_rows[0, t] * count, count)
        c = pl.multiple_of(tile_columns[0, t] * count, count)
        block = tiles[0, t]
        matrix[pl.ds(r, count), pl.ds(c, count)] += block
        matrix[pl.ds(c, count), pl.ds(r, count)] += block.T
        return carry

    lax.fori_loop(node_tiles, tile_counts[0], add, 0)
    rows = slot_rows(places)
    faces = spread_sum([jnp.ones((1, LANES), F32)] * len(rows), rows, node_tiles)
    total = jnp.sum(matrix[...], axis=0, keepdims=True)
    rowsum = tile_rows_of(total) + faces
    inverse_rowsum[...] = lane_rows(1.0 / rowsum)
    diagonal[...] = capacity[...] + rowsum
    half[...] = matrix[...].astype(BF16)
    local[...] = jnp.dot(lat[...], half[...], preferred_element_type=F32)


def local_features(lat, half, local):
    local[...] = jnp.dot(lat[...], half[...], preferred_element_type=F32)


def layer_step(layer, arrived, local, inverse_rowsum, lat, hits, w_self, w_neighbour, w_out, gains, bias):
    came = jnp.concatenate([a[...] for a in arrived], axis=1)
    coupled = lax.dot_general(
        came, hits[...], (((1,), (1,)), ((), ())), preferred_element_type=F32
    )
    mean = (local[...] + coupled) * inverse_rowsum[...]
    columns = jnp.concatenate(
        [gains[layer], bias[...], jnp.zeros((8 - 4, bias.shape[1]), F32)], axis=0
    ).T
    own = lat[...].astype(F32)

    def normed(value, gain):
        scale = lax.rsqrt(jnp.mean(value * value, axis=0, keepdims=True) + 1e-06)
        return (value * scale * gain).astype(BF16)

    normed_self = normed(own, columns[:, 0:1])
    normed_neighbour = normed(mean, columns[:, 1:2])

    def project(weight, value):
        return lax.dot_general(
            weight, value, (((0,), (0,)), ((), ())), preferred_element_type=F32
        )

    linear = project(w_self[layer], normed_self) + project(w_neighbour[layer], normed_neighbour)
    linear = linear + columns[:, 2 + layer : 3 + layer]
    activated = (linear / (1.0 + jnp.exp(-linear))).astype(BF16)
    return (own + project(w_out[layer], activated)).astype(BF16)


def first_layer(
    a0, a1, a2, a3, local, inverse_rowsum, lat, hits, w_self, w_neighbour, w_out, gains, bias,
    new, s0, s1, s2, s3,
):
    value = layer_step(
        0, (a0, a1, a2, a3), local, inverse_rowsum, lat, hits, w_self, w_neighbour, w_out, gains, bias
    )
    new[...] = value
    send_features(value, hits, (s0, s1, s2, s3))


def last_layer(
    places, a0, a1, a2, a3, local, inverse_rowsum, lat, hits, w_self, w_neighbour, w_out,
    gains, bias, w_decode, guess, s0, s1, s2, s3,
):
    value = layer_step(
        LAYERS - 1, (a0, a1, a2, a3), local, inverse_rowsum, lat, hits, w_self, w_neighbour, w_out,
        gains, bias,
    )
    decode = jnp.broadcast_to(w_decode[...], (8, w_decode.shape[1])).T[:, 0:1]
    row = jnp.sum(value.astype(F32) * decode, axis=0, keepdims=True)
    field = tile_rows_of(row)
    guess[...] = field
    store_sent((s0, s1, s2, s3), pick(field, slot_rows(places)))


def product(matrix, field):
    count = LANES
    width = matrix.shape[1]
    total = jnp.zeros((8, width), F32)
    for t in range(field.shape[0]):
        column = jnp.broadcast_to(field[t : t + 1, :], (count, count)).T
        wide = jnp.concatenate([column] * (width // count), axis=1)
        part = matrix[t * count : (t + 1) * count, :] * wide
        total = total + jnp.sum(part.reshape(count // 8, 8, width), axis=0)
    return tile_rows_of(jnp.sum(total, axis=0, keepdims=True))


def matvec(matrix, vector, out):
    out[...] = product(matrix, vector[...])


def start_basis(places, a0, a1, a2, a3, local, guess, source, diagonal, basis, s0, s1, s2, s3):
    rows = slot_rows(places)
    came = spread_sum(arrived_rows((a0, a1, a2, a3)), rows, guess.shape[0])
    value = (source[...] + local[...] + came) / diagonal[...] - guess[...]
    basis[...] = value
    store_sent((s0, s1, s2, s3), pick(value, rows))


def next_basis(places, a0, a1, a2, a3, local, diagonal, basis, s0, s1, s2, s3):
    rows = slot_rows(places)
    came = spread_sum(arrived_rows((a0, a1, a2, a3)), rows, local.shape[0])
    value = (local[...] + came) / diagonal[...]
    basis[...] = value
    store_sent((s0, s1, s2, s3), pick(value, rows))


def last_basis(places, a0, a1, a2, a3, local, diagonal, b0, b1, matrix, basis, image, packet):
    rows = slot_rows(places)
    came = spread_sum(arrived_rows((a0, a1, a2, a3)), rows, local.shape[0])
    value = (local[...] + came) / diagonal[...]
    basis[...] = value
    mapped = product(matrix, value)
    image[...] = mapped
    held = [b0[...], b1[...], value]
    parts = []
    for k in range(2 * ITERS - 1):
        left, right = held[k // 2], held[(k + 1) // 2]
        parts.append(jnp.sum(left * right * diagonal[...], axis=0, keepdims=True))
    parts.append(jnp.sum(value * mapped, axis=0, keepdims=True))
    parts.append(jnp.zeros((8 - 2 * ITERS, LANES), F32))
    packet[0:8, :] = pick(value, rows)
    packet[8:16, :] = jnp.concatenate(parts, axis=0)


def added(values):
    values = list(values)
    while len(values) > 1:
        values = [sum(values[i : i + 2][1:], values[i]) for i in range(0, len(values), 2)]
    return values[0]


def finish(sizes, where, packets, places, image, guess, diagonal, b0, b1, b2, field, defect):
    doms, subs = sizes

    def block(dom, sub, half):
        at = jnp.bitwise_xor(dom, where[0]) * subs + jnp.bitwise_xor(sub, where[1])
        return packets[pl.ds(pl.multiple_of(at * 16 + half * 8, 8), 8), :]

    slots = [[block(d, s, 0) for s in range(subs)] for d in range(doms)]
    edges = []
    for d in range(doms):
        for s in range(subs):
            for g, (i, j) in ((d % 2, (d + 1, s)), (2 + s % 2, (d, s + 1))):
                if i < doms and j < subs:
                    edges.append((slots[d][s] * slots[i][j])[2 * g : 2 * g + 2, :])
    edges = jnp.sum(added(edges), axis=0, keepdims=True)
    partial = added([block(d, s, 1) for d in range(doms) for s in range(subs)])
    came = []
    for g in range(4):
        mine = block(where[2 + 2 * g], where[3 + 2 * g], 0)
        came += [mine[2 * g : 2 * g + 1, :], mine[2 * g + 1 : 2 * g + 2, :]]
    last = (image[...] + spread_sum(came, slot_rows(places), image.shape[0])) / diagonal[...]

    n = []
    for k in range(2 * ITERS):
        row = partial[k : k + 1, :]
        if k == 2 * ITERS - 1:
            row = row + 2.0 * edges
        n.append(jnp.broadcast_to(jnp.sum(row, axis=1, keepdims=True), (8, LANES)))
    one, zero = jnp.ones((8, LANES), F32), jnp.zeros((8, LANES), F32)

    def paired(left, values):
        total = zero
        for i, a in enumerate(left):
            for j, b in enumerate(left):
                total = total + a * b * values[i + j]
        return total

    gaps = [n[k] - n[k + 1] for k in range(2 * ITERS - 1)]
    residual = [one]
    heading = [one]
    moved = [zero] * ITERS
    size = n[0]
    for step in range(ITERS):
        alpha = size / paired(heading, gaps)
        for i, h in enumerate(heading):
            moved[i] = moved[i] + alpha * h
        change = [
            (heading[i] if i < len(heading) else zero) - (heading[i - 1] if i > 0 else zero)
            for i in range(len(heading) + 1)
        ]
        residual = [
            (residual[i] if i < len(residual) else zero) - alpha * change[i]
            for i in range(len(change))
        ]
        if step + 1 < ITERS:
            following = paired(residual, n)
            beta = following / size
            heading = [
                residual[i] + (beta * heading[i] if i < len(heading) else zero)
                for i in range(len(residual))
            ]
            size = following
    held = [b0[...], b1[...], b2[...], last]
    total = guess[...]
    for c, b in zip(moved, held):
        total = total + c * b
    field[...] = total
    left = zero
    for c, b in zip(residual, held):
        left = left + c * b
    defect[...] = left * diagonal[...]


def matching(sizes, along, first):
    pairs = []
    for dom in range(sizes[0]):
        for sub in range(sizes[1]):
            at = [dom, sub]
            to = [dom, sub]
            other = 1 - along
            mate = (at[along] - first ^ 1) + first
            if at[along] >= first and mate < sizes[along]:
                to[along] = mate
            elif at[other] ^ 1 < sizes[other]:
                to[other] = at[other] ^ 1
            pairs.append((at[0] * sizes[1] + at[1], to[0] * sizes[1] + to[1]))
    return pairs


def sides_of_matchings():
    dom = lax.axis_index("dom") % 2
    sub = lax.axis_index("sub") % 2
    return jnp.stack([1 - dom, dom, 3 - sub, 2 + sub]).astype(jnp.int32)


def exchange(sent):
    axes = ("dom", "sub")
    sizes = [lax.axis_size(axis) for axis in axes]
    return [lax.ppermute(sent[g], axes, matching(sizes, g // 2, g % 2)) for g in range(4)]


def partners():
    at = [lax.axis_index("dom"), lax.axis_index("sub")]
    sizes = [lax.axis_size("dom"), lax.axis_size("sub")]
    out = []
    for g in range(4):
        along, first = g // 2, g % 2
        mate = jnp.bitwise_xor(at[along] - first, 1) + first
        known = (at[along] >= first) & (mate < sizes[along])
        to = list(at)
        to[along] = jnp.where(known, mate, at[along])
        out += to
    return jnp.stack(out).astype(jnp.int32)


def gathered(packet):
    sizes = {axis: lax.axis_size(axis) for axis in ("sub", "dom")}
    if any(size & (size - 1) for size in sizes.values()):
        return lax.all_gather(packet, ("dom", "sub"), tiled=True), jnp.zeros((2,), jnp.int32)
    for axis, size in sizes.items():
        step = 1
        while step < size:
            came = lax.ppermute(packet, axis, [(i, i ^ step) for i in range(size)])
            packet = jnp.concatenate([packet, came], axis=0)
            step *= 2
    order = jnp.stack([lax.axis_index("dom"), lax.axis_index("sub")])
    return packet, order.astype(jnp.int32)


def per_device(
    state, tile_values, tile_rows, tile_columns, tile_counts, send_nodes, face_counts, capacity,
    source, w_self, w_neighbour, w_out, gains, bias, w_decode,
):
    nodes, width = state.shape
    slots = send_nodes.shape[2]
    tiles = nodes // LANES
    field = shape((tiles, LANES))
    feature_sent = [shape((width, slots), BF16)] * 4
    vector_sent = [shape((slots // LANES, LANES))] * 4
    weights = (w_self, w_neighbour, w_out, gains, bias)
    capacity = capacity.reshape(tiles, LANES)
    source = source.reshape(tiles, LANES)

    lat, hits, places, *sent = run(
        gather_first,
        [shape((width, nodes), BF16), shape((nodes, 4 * slots), BF16), shape((4 * slots // LANES, LANES), jnp.int32)]
        + feature_sent,
        (send_nodes, state), (sides_of_matchings(), face_counts), flops=2 * nodes * 4 * slots * width,
    )
    arrived = exchange(sent)
    matrix, half, inverse_rowsum, diagonal, local = run(
        build,
        [shape((nodes, nodes)), shape((nodes, nodes), BF16), shape((1, nodes)), field, shape((width, nodes))],
        (places, tile_values, lat, capacity),
        (tile_rows, tile_columns, tile_counts), flops=2 * nodes * nodes * width, moved=6_000_000,
    )
    lat, *sent = run(
        first_layer, [shape((width, nodes), BF16)] + feature_sent,
        (*arrived, local, inverse_rowsum, lat, hits, *weights), flops=6 * nodes * nodes * width,
    )
    arrived = exchange(sent)
    (local,) = run(
        local_features, [shape((width, nodes))], (lat, half), flops=2 * nodes * nodes * width, moved=4_000_000
    )
    guess, *sent = run(
        last_layer, [field] + vector_sent,
        (places, *arrived, local, inverse_rowsum, lat, hits, *weights, w_decode.reshape(1, width)),
        flops=6 * nodes * nodes * width,
    )

    def mapped(vector):
        return run(matvec, [field], (matrix, vector), flops=2 * nodes * nodes, moved=4 * nodes * nodes)[0]

    arrived = exchange(sent)
    local = mapped(guess)
    b0, *sent = run(
        start_basis, [field] + vector_sent, (places, *arrived, local, guess, source, diagonal)
    )
    arrived = exchange(sent)
    local = mapped(b0)
    b1, *sent = run(next_basis, [field] + vector_sent, (places, *arrived, local, diagonal))
    arrived = exchange(sent)
    local = mapped(b1)
    b2, image, packet = run(
        last_basis, [field, field, shape((16, LANES))],
        (places, *arrived, local, diagonal, b0, b1, matrix),
    )
    packets, order = gathered(packet)
    sizes = (lax.axis_size("dom"), lax.axis_size("sub"))
    heat, defect = run(
        functools.partial(finish, sizes), [field, field],
        (packets, places, image, guess, diagonal, b0, b1, b2),
        (jnp.concatenate([order, partners()]),),
    )
    return heat.reshape(nodes), defect.reshape(nodes)


def solution(mesh):
    both = ("dom", "sub")
    return jax.shard_map(
        per_device,
        mesh=mesh,
        in_specs=(
            P(both, None),
            P(both, None, None, None),
            P(both, None),
            P(both, None),
            P(both),
            P(both, None, None),
            P(both, None),
            P(both),
            P(both),
            P(),
            P(),
            P(),
            P(),
            P(),
            P(),
        ),
        out_specs=(P(both), P(both)),
        check_vma=False,
    )
```

```python
import functools

import jax
import jax.numpy as jnp
from jax import lax
from jax.experimental import pallas as pl
from jax.experimental.pallas import tpu as pltpu
from jax.sharding import PartitionSpec as P

LAYERS = 2
ITERS = 3
LANES = 128
VMEM_LIMIT = 24 * 1024 * 1024

F32 = jnp.float32
BF16 = jnp.bfloat16


def shape(dims, dtype=F32):
    return jax.ShapeDtypeStruct(dims, dtype)


def run(body, outs, operands, scalars=(), flops=1_000_000, moved=1_000_000):
    smem = pl.BlockSpec(memory_space=pltpu.SMEM)
    vmem = pl.BlockSpec(memory_space=pltpu.VMEM)
    return pl.pallas_call(
        body,
        out_shape=outs,
        in_specs=[smem] * len(scalars) + [vmem] * len(operands),
        out_specs=[vmem] * len(outs),
        compiler_params=pltpu.CompilerParams(vmem_limit_bytes=VMEM_LIMIT),
        cost_estimate=pl.CostEstimate(flops=flops, bytes_accessed=moved, transcendentals=0),
    )(*scalars, *operands)


def slot_rows(places):
    return [places[r : r + 1, :] for r in range(places.shape[0])]


def pick(vector, rows):
    index = jnp.concatenate(rows, axis=0)
    low = jnp.bitwise_and(index, LANES - 1)
    high = jnp.right_shift(index, 7)
    out = jnp.zeros(index.shape, F32)
    for t in range(vector.shape[0]):
        spread = jnp.broadcast_to(vector[t : t + 1, :], index.shape)
        got = jnp.take_along_axis(spread, low, axis=1, mode="promise_in_bounds")
        out = jnp.where(high == t, got, out)
    return out


def pieces(value):
    first = value.astype(BF16)
    rest = value - first.astype(F32)
    second = rest.astype(BF16)
    third = (rest - second.astype(F32)).astype(BF16)
    return first, second, third


def low_hits(rows):
    lane = lax.broadcasted_iota(jnp.int32, (LANES, LANES), 0)
    return jnp.concatenate(
        [(lane == jnp.bitwise_and(row, LANES - 1)).astype(F32).astype(BF16) for row in rows], axis=1
    )


def spread_sum(values, rows, tiles):
    tile = lax.broadcasted_iota(jnp.int32, (tiles, LANES), 0)
    parts = [
        jnp.where(tile == jnp.right_shift(row, 7), value, 0.0) for value, row in zip(values, rows)
    ]
    held = jnp.concatenate(parts, axis=1)
    stacked = jnp.concatenate([p.astype(F32) for p in pieces(held)], axis=0).astype(BF16)
    out = lax.dot_general(
        stacked, low_hits(rows), (((1,), (1,)), ((), ())), preferred_element_type=F32
    )
    return out[:tiles] + out[tiles : 2 * tiles] + out[2 * tiles :]


def arrived_rows(refs):
    return [ref[h : h + 1, :] for ref in refs for h in range(ref.shape[0])]


def store_sent(refs, sent):
    per = refs[0].shape[0]
    for k, ref in enumerate(refs):
        ref[...] = sent[k * per : (k + 1) * per, :]


def lane_rows(vector):
    return jnp.concatenate([vector[t : t + 1, :] for t in range(vector.shape[0])], axis=1)


def tile_rows_of(row):
    return jnp.concatenate(
        [row[:, t * LANES : (t + 1) * LANES] for t in range(row.shape[1] // LANES)], axis=0
    )


def gather_first(sides, counts, index, state, lat, hits, places, s0, s1, s2, s3):
    per = index.shape[2] // LANES
    for g in range(index.shape[1]):
        side = sides[g]
        for h in range(per):
            low, high = g // 2 * 2, g // 2 * 2 + 1
            span = slice(h * LANES, (h + 1) * LANES)
            row = jnp.where(side == low, index[0, low : low + 1, span], index[0, high : high + 1, span])
            slot = lax.broadcasted_iota(jnp.int32, (1, LANES), 1) + h * LANES
            r = g * per + h
            places[r : r + 1, :] = jnp.where(slot < counts[0, side], row, -1)
    node = lax.broadcasted_iota(jnp.int32, (state.shape[0], LANES), 0)
    for c, row in enumerate(slot_rows(places)):
        hits[:, c * LANES : (c + 1) * LANES] = (node == row).astype(F32).astype(BF16)
    lat[...] = state[...].T
    send_features(lat[...], hits, (s0, s1, s2, s3))


def send_features(lat, hits, outs):
    width = outs[0].shape[1]
    for k, out in enumerate(outs):
        out[...] = jnp.dot(
            lat, hits[:, k * width : (k + 1) * width], preferred_element_type=F32
        ).astype(BF16)


def build(
    tile_rows, tile_columns, tile_counts, places, tiles, lat, capacity,
    matrix, half, inverse_rowsum, diagonal, local,
):
    count = tiles.shape[2]
    node_tiles = matrix.shape[0] // count
    matrix[...] = jnp.zeros(matrix.shape, F32)
    for t in range(node_tiles):
        span = slice(t * count, (t + 1) * count)
        block = tiles[0, t]
        matrix[span, span] = block + block.T

    def add(t, carry):
        r = pl.multiple_of(tile_rows[0, t] * count, count)
        c = pl.multiple_of(tile_columns[0, t] * count, count)
        block = tiles[0, t]
        matrix[pl.ds(r, count), pl.ds(c, count)] += block
        matrix[pl.ds(c, count), pl.ds(r, count)] += block.T
        return carry

    lax.fori_loop(node_tiles, tile_counts[0], add, 0)
    rows = slot_rows(places)
    faces = spread_sum([jnp.ones((1, LANES), F32)] * len(rows), rows, node_tiles)
    total = jnp.sum(matrix[...], axis=0, keepdims=True)
    rowsum = tile_rows_of(total) + faces
    inverse_rowsum[...] = lane_rows(1.0 / rowsum)
    diagonal[...] = capacity[...] + rowsum
    half[...] = matrix[...].astype(BF16)
    local[...] = jnp.dot(lat[...], half[...], preferred_element_type=F32)


def local_features(lat, half, local):
    local[...] = jnp.dot(lat[...], half[...], preferred_element_type=F32)


def layer_step(layer, arrived, local, inverse_rowsum, lat, hits, w_self, w_neighbour, w_out, gains, bias):
    came = jnp.concatenate([a[...] for a in arrived], axis=1)
    coupled = lax.dot_general(
        came, hits[...], (((1,), (1,)), ((), ())), preferred_element_type=F32
    )
    mean = (local[...] + coupled) * inverse_rowsum[...]
    columns = jnp.concatenate(
        [gains[layer], bias[...], jnp.zeros((8 - 4, bias.shape[1]), F32)], axis=0
    ).T
    own = lat[...].astype(F32)

    def normed(value, gain):
        scale = lax.rsqrt(jnp.mean(value * value, axis=0, keepdims=True) + 1e-06)
        return (value * scale * gain).astype(BF16)

    normed_self = normed(own, columns[:, 0:1])
    normed_neighbour = normed(mean, columns[:, 1:2])

    def project(weight, value):
        return lax.dot_general(
            weight, value, (((0,), (0,)), ((), ())), preferred_element_type=F32
        )

    linear = project(w_self[layer], normed_self) + project(w_neighbour[layer], normed_neighbour)
    linear = linear + columns[:, 2 + layer : 3 + layer]
    activated = (linear / (1.0 + jnp.exp(-linear))).astype(BF16)
    return (own + project(w_out[layer], activated)).astype(BF16)


def first_layer(
    a0, a1, a2, a3, local, inverse_rowsum, lat, hits, w_self, w_neighbour, w_out, gains, bias,
    new, s0, s1, s2, s3,
):
    value = layer_step(
        0, (a0, a1, a2, a3), local, inverse_rowsum, lat, hits, w_self, w_neighbour, w_out, gains, bias
    )
    new[...] = value
    send_features(value, hits, (s0, s1, s2, s3))


def last_layer(
    places, a0, a1, a2, a3, local, inverse_rowsum, lat, hits, w_self, w_neighbour, w_out,
    gains, bias, w_decode, guess, s0, s1, s2, s3,
):
    value = layer_step(
        LAYERS - 1, (a0, a1, a2, a3), local, inverse_rowsum, lat, hits, w_self, w_neighbour, w_out,
        gains, bias,
    )
    decode = jnp.broadcast_to(w_decode[...], (8, w_decode.shape[1])).T[:, 0:1]
    row = jnp.sum(value.astype(F32) * decode, axis=0, keepdims=True)
    field = tile_rows_of(row)
    guess[...] = field
    store_sent((s0, s1, s2, s3), pick(field, slot_rows(places)))


def product(matrix, field):
    count = LANES
    width = matrix.shape[1]
    total = jnp.zeros((8, width), F32)
    for t in range(field.shape[0]):
        column = jnp.broadcast_to(field[t : t + 1, :], (count, count)).T
        wide = jnp.concatenate([column] * (width // count), axis=1)
        part = matrix[t * count : (t + 1) * count, :] * wide
        total = total + jnp.sum(part.reshape(count // 8, 8, width), axis=0)
    return tile_rows_of(jnp.sum(total, axis=0, keepdims=True))


def matvec(matrix, vector, out):
    out[...] = product(matrix, vector[...])


def start_basis(places, a0, a1, a2, a3, local, guess, source, diagonal, basis, s0, s1, s2, s3):
    rows = slot_rows(places)
    came = spread_sum(arrived_rows((a0, a1, a2, a3)), rows, guess.shape[0])
    value = (source[...] + local[...] + came) / diagonal[...] - guess[...]
    basis[...] = value
    store_sent((s0, s1, s2, s3), pick(value, rows))


def next_basis(places, a0, a1, a2, a3, local, diagonal, basis, s0, s1, s2, s3):
    rows = slot_rows(places)
    came = spread_sum(arrived_rows((a0, a1, a2, a3)), rows, local.shape[0])
    value = (local[...] + came) / diagonal[...]
    basis[...] = value
    store_sent((s0, s1, s2, s3), pick(value, rows))


def last_basis(places, a0, a1, a2, a3, local, diagonal, b0, b1, matrix, basis, image, packet):
    rows = slot_rows(places)
    came = spread_sum(arrived_rows((a0, a1, a2, a3)), rows, local.shape[0])
    value = (local[...] + came) / diagonal[...]
    basis[...] = value
    mapped = product(matrix, value)
    image[...] = mapped
    held = [b0[...], b1[...], value]
    parts = []
    for k in range(2 * ITERS - 1):
        left, right = held[k // 2], held[(k + 1) // 2]
        parts.append(jnp.sum(left * right * diagonal[...], axis=0, keepdims=True))
    parts.append(jnp.sum(value * mapped, axis=0, keepdims=True))
    parts.append(jnp.zeros((8 - 2 * ITERS, LANES), F32))
    packet[0:8, :] = pick(value, rows)
    packet[8:16, :] = jnp.concatenate(parts, axis=0)


def added(values):
    values = list(values)
    while len(values) > 1:
        values = [sum(values[i : i + 2][1:], values[i]) for i in range(0, len(values), 2)]
    return values[0]


def finish(sizes, where, packets, places, image, guess, diagonal, b0, b1, b2, field, defect):
    doms, subs = sizes

    def block(dom, sub, half):
        at = jnp.bitwise_xor(dom, where[0]) * subs + jnp.bitwise_xor(sub, where[1])
        return packets[pl.ds(pl.multiple_of(at * 16 + half * 8, 8), 8), :]

    slots = [[block(d, s, 0) for s in range(subs)] for d in range(doms)]
    edges = []
    for d in range(doms):
        for s in range(subs):
            for g, (i, j) in ((d % 2, (d + 1, s)), (2 + s % 2, (d, s + 1))):
                if i < doms and j < subs:
                    edges.append((slots[d][s] * slots[i][j])[2 * g : 2 * g + 2, :])
    edges = jnp.sum(added(edges), axis=0, keepdims=True)
    partial = added([block(d, s, 1) for d in range(doms) for s in range(subs)])
    came = []
    for g in range(4):
        mine = block(where[2 + 2 * g], where[3 + 2 * g], 0)
        came += [mine[2 * g : 2 * g + 1, :], mine[2 * g + 1 : 2 * g + 2, :]]
    last = (image[...] + spread_sum(came, slot_rows(places), image.shape[0])) / diagonal[...]

    n = []
    for k in range(2 * ITERS):
        row = partial[k : k + 1, :]
        if k == 2 * ITERS - 1:
            row = row + 2.0 * edges
        n.append(jnp.broadcast_to(jnp.sum(row, axis=1, keepdims=True), (8, LANES)))
    one, zero = jnp.ones((8, LANES), F32), jnp.zeros((8, LANES), F32)

    def paired(left, values):
        total = zero
        for i, a in enumerate(left):
            for j, b in enumerate(left):
                total = total + a * b * values[i + j]
        return total

    gaps = [n[k] - n[k + 1] for k in range(2 * ITERS - 1)]
    residual = [one]
    heading = [one]
    moved = [zero] * ITERS
    size = n[0]
    for step in range(ITERS):
        alpha = size / paired(heading, gaps)
        for i, h in enumerate(heading):
            moved[i] = moved[i] + alpha * h
        change = [
            (heading[i] if i < len(heading) else zero) - (heading[i - 1] if i > 0 else zero)
            for i in range(len(heading) + 1)
        ]
        residual = [
            (residual[i] if i < len(residual) else zero) - alpha * change[i]
            for i in range(len(change))
        ]
        if step + 1 < ITERS:
            following = paired(residual, n)
            beta = following / size
            heading = [
                residual[i] + (beta * heading[i] if i < len(heading) else zero)
                for i in range(len(residual))
            ]
            size = following
    held = [b0[...], b1[...], b2[...], last]
    total = guess[...]
    for c, b in zip(moved, held):
        total = total + c * b
    field[...] = total
    left = zero
    for c, b in zip(residual, held):
        left = left + c * b
    defect[...] = left * diagonal[...]


def matching(sizes, along, first):
    pairs = []
    for dom in range(sizes[0]):
        for sub in range(sizes[1]):
            at = [dom, sub]
            to = [dom, sub]
            other = 1 - along
            mate = (at[along] - first ^ 1) + first
            if at[along] >= first and mate < sizes[along]:
                to[along] = mate
            elif at[other] ^ 1 < sizes[other]:
                to[other] = at[other] ^ 1
            pairs.append((at[0] * sizes[1] + at[1], to[0] * sizes[1] + to[1]))
    return pairs


def sides_of_matchings():
    dom = lax.axis_index("dom") % 2
    sub = lax.axis_index("sub") % 2
    return jnp.stack([1 - dom, dom, 3 - sub, 2 + sub]).astype(jnp.int32)


def exchange(sent):
    axes = ("dom", "sub")
    sizes = [lax.axis_size(axis) for axis in axes]
    return [lax.ppermute(sent[g], axes, matching(sizes, g // 2, g % 2)) for g in range(4)]


def partners():
    at = [lax.axis_index("dom"), lax.axis_index("sub")]
    sizes = [lax.axis_size("dom"), lax.axis_size("sub")]
    out = []
    for g in range(4):
        along, first = g // 2, g % 2
        mate = jnp.bitwise_xor(at[along] - first, 1) + first
        known = (at[along] >= first) & (mate < sizes[along])
        to = list(at)
        to[along] = jnp.where(known, mate, at[along])
        out += to
    return jnp.stack(out).astype(jnp.int32)


def gathered(packet):
    axes = ("dom", "sub")
    devices = lax.axis_size("dom") * lax.axis_size("sub")
    copies = jnp.broadcast_to(packet[None], (devices,) + packet.shape)
    came = lax.all_to_all(copies, axes, split_axis=0, concat_axis=0, tiled=True)
    return came.reshape(devices * packet.shape[0], packet.shape[1]), jnp.zeros((2,), jnp.int32)


def per_device(
    state, tile_values, tile_rows, tile_columns, tile_counts, send_nodes, face_counts, capacity,
    source, w_self, w_neighbour, w_out, gains, bias, w_decode,
):
    nodes, width = state.shape
    slots = send_nodes.shape[2]
    tiles = nodes // LANES
    field = shape((tiles, LANES))
    feature_sent = [shape((width, slots), BF16)] * 4
    vector_sent = [shape((slots // LANES, LANES))] * 4
    weights = (w_self, w_neighbour, w_out, gains, bias)
    capacity = capacity.reshape(tiles, LANES)
    source = source.reshape(tiles, LANES)

    lat, hits, places, *sent = run(
        gather_first,
        [shape((width, nodes), BF16), shape((nodes, 4 * slots), BF16), shape((4 * slots // LANES, LANES), jnp.int32)]
        + feature_sent,
        (send_nodes, state), (sides_of_matchings(), face_counts), flops=2 * nodes * 4 * slots * width,
    )
    arrived = exchange(sent)
    matrix, half, inverse_rowsum, diagonal, local = run(
        build,
        [shape((nodes, nodes)), shape((nodes, nodes), BF16), shape((1, nodes)), field, shape((width, nodes))],
        (places, tile_values, lat, capacity),
        (tile_rows, tile_columns, tile_counts), flops=2 * nodes * nodes * width, moved=6_000_000,
    )
    lat, *sent = run(
        first_layer, [shape((width, nodes), BF16)] + feature_sent,
        (*arrived, local, inverse_rowsum, lat, hits, *weights), flops=6 * nodes * nodes * width,
    )
    arrived = exchange(sent)
    (local,) = run(
        local_features, [shape((width, nodes))], (lat, half), flops=2 * nodes * nodes * width, moved=4_000_000
    )
    guess, *sent = run(
        last_layer, [field] + vector_sent,
        (places, *arrived, local, inverse_rowsum, lat, hits, *weights, w_decode.reshape(1, width)),
        flops=6 * nodes * nodes * width,
    )

    def mapped(vector):
        return run(matvec, [field], (matrix, vector), flops=2 * nodes * nodes, moved=4 * nodes * nodes)[0]

    arrived = exchange(sent)
    local = mapped(guess)
    b0, *sent = run(
        start_basis, [field] + vector_sent, (places, *arrived, local, guess, source, diagonal)
    )
    arrived = exchange(sent)
    local = mapped(b0)
    b1, *sent = run(next_basis, [field] + vector_sent, (places, *arrived, local, diagonal))
    arrived = exchange(sent)
    local = mapped(b1)
    b2, image, packet = run(
        last_basis, [field, field, shape((16, LANES))],
        (places, *arrived, local, diagonal, b0, b1, matrix),
    )
    packets, order = gathered(packet)
    sizes = (lax.axis_size("dom"), lax.axis_size("sub"))
    heat, defect = run(
        functools.partial(finish, sizes), [field, field],
        (packets, places, image, guess, diagonal, b0, b1, b2),
        (jnp.concatenate([order, partners()]),),
    )
    return heat.reshape(nodes), defect.reshape(nodes)


def solution(mesh):
    both = ("dom", "sub")
    return jax.shard_map(
        per_device,
        mesh=mesh,
        in_specs=(
            P(both, None),
            P(both, None, None, None),
            P(both, None),
            P(both, None),
            P(both),
            P(both, None, None),
            P(both, None),
            P(both),
            P(both),
            P(),
            P(),
            P(),
            P(),
            P(),
            P(),
        ),
        out_specs=(P(both), P(both)),
        check_vma=False,
    )
```

```python
import functools

import jax
import jax.numpy as jnp
from jax import lax
from jax.experimental import pallas as pl
from jax.experimental.pallas import tpu as pltpu
from jax.sharding import PartitionSpec as P

LAYERS = 2
ITERS = 3
LANES = 128
VMEM_LIMIT = 24 * 1024 * 1024

F32 = jnp.float32
BF16 = jnp.bfloat16


def shape(dims, dtype=F32):
    return jax.ShapeDtypeStruct(dims, dtype)


def run(body, outs, operands, scalars=(), flops=1_000_000, moved=1_000_000):
    smem = pl.BlockSpec(memory_space=pltpu.SMEM)
    vmem = pl.BlockSpec(memory_space=pltpu.VMEM)
    return pl.pallas_call(
        body,
        out_shape=outs,
        in_specs=[smem] * len(scalars) + [vmem] * len(operands),
        out_specs=[vmem] * len(outs),
        compiler_params=pltpu.CompilerParams(vmem_limit_bytes=VMEM_LIMIT),
        cost_estimate=pl.CostEstimate(flops=flops, bytes_accessed=moved, transcendentals=0),
    )(*scalars, *operands)


def slot_rows(places):
    return [places[r : r + 1, :] for r in range(places.shape[0])]


def pick(vector, rows):
    index = jnp.concatenate(rows, axis=0)
    low = jnp.bitwise_and(index, LANES - 1)
    high = jnp.right_shift(index, 7)
    out = jnp.zeros(index.shape, F32)
    for t in range(vector.shape[0]):
        spread = jnp.broadcast_to(vector[t : t + 1, :], index.shape)
        got = jnp.take_along_axis(spread, low, axis=1, mode="promise_in_bounds")
        out = jnp.where(high == t, got, out)
    return out


def pieces(value):
    first = value.astype(BF16)
    rest = value - first.astype(F32)
    second = rest.astype(BF16)
    third = (rest - second.astype(F32)).astype(BF16)
    return first, second, third


def low_hits(rows):
    lane = lax.broadcasted_iota(jnp.int32, (LANES, LANES), 0)
    return jnp.concatenate(
        [(lane == jnp.bitwise_and(row, LANES - 1)).astype(F32).astype(BF16) for row in rows], axis=1
    )


def spread_sum(values, rows, tiles):
    tile = lax.broadcasted_iota(jnp.int32, (tiles, LANES), 0)
    parts = [
        jnp.where(tile == jnp.right_shift(row, 7), value, 0.0) for value, row in zip(values, rows)
    ]
    held = jnp.concatenate(parts, axis=1)
    stacked = jnp.concatenate([p.astype(F32) for p in pieces(held)], axis=0).astype(BF16)
    out = lax.dot_general(
        stacked, low_hits(rows), (((1,), (1,)), ((), ())), preferred_element_type=F32
    )
    return out[:tiles] + out[tiles : 2 * tiles] + out[2 * tiles :]


def arrived_rows(partner, came):
    rows = []
    for g in range(4):
        message = came[partner[g]]
        rows += [message[:, h : h + LANES] for h in range(0, message.shape[1], LANES)]
    return rows


def store_sent(partner, out, sent):
    out[...] = jnp.zeros(out.shape, F32)
    per = out.shape[2] // LANES
    for g in range(4):
        out[partner[g]] = lane_rows(sent[g * per : (g + 1) * per, :])


def lane_rows(vector):
    return jnp.concatenate([vector[t : t + 1, :] for t in range(vector.shape[0])], axis=1)


def tile_rows_of(row):
    return jnp.concatenate(
        [row[:, t * LANES : (t + 1) * LANES] for t in range(row.shape[1] // LANES)], axis=0
    )


def gather_first(sides, counts, index, state, lat, hits, places, s0, s1, s2, s3):
    per = index.shape[2] // LANES
    for g in range(index.shape[1]):
        side = sides[g]
        for h in range(per):
            low, high = g // 2 * 2, g // 2 * 2 + 1
            span = slice(h * LANES, (h + 1) * LANES)
            row = jnp.where(side == low, index[0, low : low + 1, span], index[0, high : high + 1, span])
            slot = lax.broadcasted_iota(jnp.int32, (1, LANES), 1) + h * LANES
            r = g * per + h
            places[r : r + 1, :] = jnp.where(slot < counts[0, side], row, -1)
    node = lax.broadcasted_iota(jnp.int32, (state.shape[0], LANES), 0)
    for c, row in enumerate(slot_rows(places)):
        hits[:, c * LANES : (c + 1) * LANES] = (node == row).astype(F32).astype(BF16)
    lat[...] = state[...].T
    send_features(lat[...], hits, (s0, s1, s2, s3))


def send_features(lat, hits, outs):
    width = outs[0].shape[1]
    for k, out in enumerate(outs):
        out[...] = jnp.dot(
            lat, hits[:, k * width : (k + 1) * width], preferred_element_type=F32
        ).astype(BF16)


def build(
    tile_rows, tile_columns, tile_counts, places, tiles, lat, capacity,
    matrix, half, inverse_rowsum, diagonal, local,
):
    count = tiles.shape[2]
    node_tiles = matrix.shape[0] // count
    matrix[...] = jnp.zeros(matrix.shape, F32)
    for t in range(node_tiles):
        span = slice(t * count, (t + 1) * count)
        block = tiles[0, t]
        matrix[span, span] = block + block.T

    def add(t, carry):
        r = pl.multiple_of(tile_rows[0, t] * count, count)
        c = pl.multiple_of(tile_columns[0, t] * count, count)
        block = tiles[0, t]
        matrix[pl.ds(r, count), pl.ds(c, count)] += block
        matrix[pl.ds(c, count), pl.ds(r, count)] += block.T
        return carry

    lax.fori_loop(node_tiles, tile_counts[0], add, 0)
    rows = slot_rows(places)
    faces = spread_sum([jnp.ones((1, LANES), F32)] * len(rows), rows, node_tiles)
    total = jnp.sum(matrix[...], axis=0, keepdims=True)
    rowsum = tile_rows_of(total) + faces
    inverse_rowsum[...] = lane_rows(1.0 / rowsum)
    diagonal[...] = capacity[...] + rowsum
    half[...] = matrix[...].astype(BF16)
    local[...] = jnp.dot(lat[...], half[...], preferred_element_type=F32)


def local_features(lat, half, local):
    local[...] = jnp.dot(lat[...], half[...], preferred_element_type=F32)


def layer_step(layer, arrived, local, inverse_rowsum, lat, hits, w_self, w_neighbour, w_out, gains, bias):
    came = jnp.concatenate([a[...] for a in arrived], axis=1)
    coupled = lax.dot_general(
        came, hits[...], (((1,), (1,)), ((), ())), preferred_element_type=F32
    )
    mean = (local[...] + coupled) * inverse_rowsum[...]
    columns = jnp.concatenate(
        [gains[layer], bias[...], jnp.zeros((8 - 4, bias.shape[1]), F32)], axis=0
    ).T
    own = lat[...].astype(F32)

    def normed(value, gain):
        scale = lax.rsqrt(jnp.mean(value * value, axis=0, keepdims=True) + 1e-06)
        return (value * scale * gain).astype(BF16)

    normed_self = normed(own, columns[:, 0:1])
    normed_neighbour = normed(mean, columns[:, 1:2])

    def project(weight, value):
        return lax.dot_general(
            weight, value, (((0,), (0,)), ((), ())), preferred_element_type=F32
        )

    linear = project(w_self[layer], normed_self) + project(w_neighbour[layer], normed_neighbour)
    linear = linear + columns[:, 2 + layer : 3 + layer]
    activated = (linear / (1.0 + jnp.exp(-linear))).astype(BF16)
    return (own + project(w_out[layer], activated)).astype(BF16)


def first_layer(
    a0, a1, a2, a3, local, inverse_rowsum, lat, hits, w_self, w_neighbour, w_out, gains, bias,
    new, s0, s1, s2, s3,
):
    value = layer_step(
        0, (a0, a1, a2, a3), local, inverse_rowsum, lat, hits, w_self, w_neighbour, w_out, gains, bias
    )
    new[...] = value
    send_features(value, hits, (s0, s1, s2, s3))


def last_layer(
    partner, places, a0, a1, a2, a3, local, inverse_rowsum, lat, hits, w_self, w_neighbour, w_out,
    gains, bias, w_decode, guess, sent,
):
    value = layer_step(
        LAYERS - 1, (a0, a1, a2, a3), local, inverse_rowsum, lat, hits, w_self, w_neighbour, w_out,
        gains, bias,
    )
    decode = jnp.broadcast_to(w_decode[...], (8, w_decode.shape[1])).T[:, 0:1]
    row = jnp.sum(value.astype(F32) * decode, axis=0, keepdims=True)
    field = tile_rows_of(row)
    guess[...] = field
    store_sent(partner, sent, pick(field, slot_rows(places)))


def product(matrix, field):
    count = LANES
    width = matrix.shape[1]
    total = jnp.zeros((8, width), F32)
    for t in range(field.shape[0]):
        column = jnp.broadcast_to(field[t : t + 1, :], (count, count)).T
        wide = jnp.concatenate([column] * (width // count), axis=1)
        part = matrix[t * count : (t + 1) * count, :] * wide
        total = total + jnp.sum(part.reshape(count // 8, 8, width), axis=0)
    return tile_rows_of(jnp.sum(total, axis=0, keepdims=True))


def matvec(matrix, vector, out):
    out[...] = product(matrix, vector[...])


def start_basis(partner, places, arrived, local, guess, source, diagonal, basis, sent):
    rows = slot_rows(places)
    came = spread_sum(arrived_rows(partner, arrived), rows, guess.shape[0])
    value = (source[...] + local[...] + came) / diagonal[...] - guess[...]
    basis[...] = value
    store_sent(partner, sent, pick(value, rows))


def next_basis(partner, places, arrived, local, diagonal, basis, sent):
    rows = slot_rows(places)
    came = spread_sum(arrived_rows(partner, arrived), rows, local.shape[0])
    value = (local[...] + came) / diagonal[...]
    basis[...] = value
    store_sent(partner, sent, pick(value, rows))


def diagonal_mask():
    return lax.broadcasted_iota(jnp.int32, (8, LANES), 0) == lax.broadcasted_iota(jnp.int32, (8, LANES), 1)


def last_basis(partner, places, arrived, local, diagonal, b0, b1, matrix, basis, image, packets):
    rows = slot_rows(places)
    came = spread_sum(arrived_rows(partner, arrived), rows, local.shape[0])
    value = (local[...] + came) / diagonal[...]
    basis[...] = value
    mapped = product(matrix, value)
    image[...] = mapped
    held = [b0[...], b1[...], value]
    parts = []
    for k in range(2 * ITERS - 1):
        left, right = held[k // 2], held[(k + 1) // 2]
        parts.append(jnp.sum(left * right * diagonal[...], axis=0, keepdims=True))
    parts.append(jnp.sum(value * mapped, axis=0, keepdims=True))
    parts.append(jnp.zeros((8 - 2 * ITERS, LANES), F32))
    sums = jnp.sum(jnp.concatenate(parts, axis=0), axis=1, keepdims=True)
    row = jnp.sum(jnp.where(diagonal_mask(), sums, 0.0), axis=0, keepdims=True)
    packet = jnp.concatenate([lane_rows(pick(value, rows)), row], axis=1)
    for device in range(packets.shape[0]):
        packets[device] = packet


def added(values):
    values = list(values)
    while len(values) > 1:
        values = [sum(values[i : i + 2][1:], values[i]) for i in range(0, len(values), 2)]
    return values[0]


def finish(sizes, partner, packets, places, image, guess, diagonal, b0, b1, b2, field, defect):
    doms, subs = sizes
    width = packets.shape[2] - LANES
    per = width // 4

    def slots(device, g):
        return packets[device, :, g * per : (g + 1) * per]

    edges = []
    for d in range(doms):
        for s in range(subs):
            for g, (i, j) in ((d % 2, (d + 1, s)), (2 + s % 2, (d, s + 1))):
                if i < doms and j < subs:
                    edges.append(slots(d * subs + s, g) * slots(i * subs + j, g))
    edges = added(edges)
    edges = added([edges[:, h : h + LANES] for h in range(0, per, LANES)])
    sums = added([packets[e, :, width : width + LANES] for e in range(doms * subs)])
    lane = lax.broadcasted_iota(jnp.int32, (1, LANES), 1)
    sums = sums + jnp.where(lane == 2 * ITERS - 1, 2.0 * jnp.sum(edges, axis=1, keepdims=True), 0.0)
    columns = jnp.sum(
        jnp.where(diagonal_mask(), jnp.broadcast_to(sums, (8, LANES)), 0.0), axis=1, keepdims=True
    )
    n = [jnp.broadcast_to(columns[k : k + 1, :], (8, LANES)) for k in range(2 * ITERS)]
    came = []
    for g in range(4):
        mine = slots(partner[g], g)
        came += [mine[:, h : h + LANES] for h in range(0, per, LANES)]
    last = (image[...] + spread_sum(came, slot_rows(places), image.shape[0])) / diagonal[...]
    one, zero = jnp.ones((8, LANES), F32), jnp.zeros((8, LANES), F32)

    def paired(left, values):
        total = zero
        for i, a in enumerate(left):
            for j, b in enumerate(left):
                total = total + a * b * values[i + j]
        return total

    gaps = [n[k] - n[k + 1] for k in range(2 * ITERS - 1)]
    residual = [one]
    heading = [one]
    moved = [zero] * ITERS
    size = n[0]
    for step in range(ITERS):
        alpha = size / paired(heading, gaps)
        for i, h in enumerate(heading):
            moved[i] = moved[i] + alpha * h
        change = [
            (heading[i] if i < len(heading) else zero) - (heading[i - 1] if i > 0 else zero)
            for i in range(len(heading) + 1)
        ]
        residual = [
            (residual[i] if i < len(residual) else zero) - alpha * change[i]
            for i in range(len(change))
        ]
        if step + 1 < ITERS:
            following = paired(residual, n)
            beta = following / size
            heading = [
                residual[i] + (beta * heading[i] if i < len(heading) else zero)
                for i in range(len(residual))
            ]
            size = following
    held = [b0[...], b1[...], b2[...], last]
    total = guess[...]
    for c, b in zip(moved, held):
        total = total + c * b
    field[...] = total
    left = zero
    for c, b in zip(residual, held):
        left = left + c * b
    defect[...] = left * diagonal[...]


def matching(sizes, along, first):
    pairs = []
    for dom in range(sizes[0]):
        for sub in range(sizes[1]):
            at = [dom, sub]
            to = [dom, sub]
            other = 1 - along
            mate = (at[along] - first ^ 1) + first
            if at[along] >= first and mate < sizes[along]:
                to[along] = mate
            elif at[other] ^ 1 < sizes[other]:
                to[other] = at[other] ^ 1
            pairs.append((at[0] * sizes[1] + at[1], to[0] * sizes[1] + to[1]))
    return pairs


def sides_of_matchings():
    dom = lax.axis_index("dom") % 2
    sub = lax.axis_index("sub") % 2
    return jnp.stack([1 - dom, dom, 3 - sub, 2 + sub]).astype(jnp.int32)


def exchange(sent):
    axes = ("dom", "sub")
    sizes = [lax.axis_size(axis) for axis in axes]
    return [lax.ppermute(sent[g], axes, matching(sizes, g // 2, g % 2)) for g in range(4)]


def partners():
    at = [lax.axis_index("dom"), lax.axis_index("sub")]
    sizes = [lax.axis_size("dom"), lax.axis_size("sub")]
    out = []
    for g in range(4):
        along, first = g // 2, g % 2
        mate = jnp.bitwise_xor(at[along] - first, 1) + first
        known = (at[along] >= first) & (mate < sizes[along])
        to = list(at)
        to[along] = jnp.where(known, mate, at[along])
        out.append(to[0] * sizes[1] + to[1])
    return jnp.stack(out).astype(jnp.int32)


def all_to_all(messages):
    return lax.all_to_all(messages, ("dom", "sub"), split_axis=0, concat_axis=0, tiled=True)


def per_device(
    state, tile_values, tile_rows, tile_columns, tile_counts, send_nodes, face_counts, capacity,
    source, w_self, w_neighbour, w_out, gains, bias, w_decode,
):
    nodes, width = state.shape
    slots = send_nodes.shape[2]
    tiles = nodes // LANES
    field = shape((tiles, LANES))
    feature_sent = [shape((width, slots), BF16)] * 4
    sizes = (lax.axis_size("dom"), lax.axis_size("sub"))
    devices = sizes[0] * sizes[1]
    vector_sent = [shape((devices, 1, slots))]
    partner = (partners(),)
    weights = (w_self, w_neighbour, w_out, gains, bias)
    capacity = capacity.reshape(tiles, LANES)
    source = source.reshape(tiles, LANES)

    lat, hits, places, *sent = run(
        gather_first,
        [shape((width, nodes), BF16), shape((nodes, 4 * slots), BF16), shape((4 * slots // LANES, LANES), jnp.int32)]
        + feature_sent,
        (send_nodes, state), (sides_of_matchings(), face_counts), flops=2 * nodes * 4 * slots * width,
    )
    arrived = exchange(sent)
    matrix, half, inverse_rowsum, diagonal, local = run(
        build,
        [shape((nodes, nodes)), shape((nodes, nodes), BF16), shape((1, nodes)), field, shape((width, nodes))],
        (places, tile_values, lat, capacity),
        (tile_rows, tile_columns, tile_counts), flops=2 * nodes * nodes * width, moved=6_000_000,
    )
    lat, *sent = run(
        first_layer, [shape((width, nodes), BF16)] + feature_sent,
        (*arrived, local, inverse_rowsum, lat, hits, *weights), flops=6 * nodes * nodes * width,
    )
    arrived = exchange(sent)
    (local,) = run(
        local_features, [shape((width, nodes))], (lat, half), flops=2 * nodes * nodes * width, moved=4_000_000
    )
    guess, sent = run(
        last_layer, [field] + vector_sent,
        (places, *arrived, local, inverse_rowsum, lat, hits, *weights, w_decode.reshape(1, width)),
        partner, flops=6 * nodes * nodes * width,
    )

    def mapped(vector):
        return run(matvec, [field], (matrix, vector), flops=2 * nodes * nodes, moved=4 * nodes * nodes)[0]

    arrived = all_to_all(sent)
    local = mapped(guess)
    b0, sent = run(
        start_basis, [field] + vector_sent, (places, arrived, local, guess, source, diagonal), partner
    )
    arrived = all_to_all(sent)
    local = mapped(b0)
    b1, sent = run(next_basis, [field] + vector_sent, (places, arrived, local, diagonal), partner)
    arrived = all_to_all(sent)
    local = mapped(b1)
    b2, image, packets = run(
        last_basis, [field, field, shape((devices, 1, 4 * slots + LANES))],
        (places, arrived, local, diagonal, b0, b1, matrix), partner,
    )
    packets = all_to_all(packets)
    heat, defect = run(
        functools.partial(finish, sizes), [field, field],
        (packets, places, image, guess, diagonal, b0, b1, b2), partner,
    )
    return heat.reshape(nodes), defect.reshape(nodes)


def solution(mesh):
    both = ("dom", "sub")
    return jax.shard_map(
        per_device,
        mesh=mesh,
        in_specs=(
            P(both, None),
            P(both, None, None, None),
            P(both, None),
            P(both, None),
            P(both),
            P(both, None, None),
            P(both, None),
            P(both),
            P(both),
            P(),
            P(),
            P(),
            P(),
            P(),
            P(),
        ),
        out_specs=(P(both), P(both)),
        check_vma=False,
    )
```

```python
import functools

import jax
import jax.numpy as jnp
from jax import lax
from jax.experimental import pallas as pl
from jax.experimental.pallas import tpu as pltpu
from jax.sharding import PartitionSpec as P

LAYERS = 2
ITERS = 3
LANES = 128
VMEM_LIMIT = 24 * 1024 * 1024

F32 = jnp.float32
BF16 = jnp.bfloat16


def shape(dims, dtype=F32):
    return jax.ShapeDtypeStruct(dims, dtype)


def run(body, outs, operands, scalars=(), raw=(), scratch=(), flops=1_000_000, moved=1_000_000):
    smem = pl.BlockSpec(memory_space=pltpu.SMEM)
    vmem = pl.BlockSpec(memory_space=pltpu.VMEM)
    anywhere = pl.BlockSpec(memory_space=pltpu.HBM)
    scratch = list(scratch) + [pltpu.SemaphoreType.DMA((len(raw),))] * bool(raw)
    return pl.pallas_call(
        body,
        out_shape=outs,
        in_specs=[smem] * len(scalars) + [vmem] * len(operands) + [anywhere] * len(raw),
        out_specs=[vmem] * len(outs),
        scratch_shapes=scratch,
        compiler_params=pltpu.CompilerParams(vmem_limit_bytes=VMEM_LIMIT),
        cost_estimate=pl.CostEstimate(flops=flops, bytes_accessed=moved, transcendentals=0),
    )(*scalars, *operands, *(pltpu.with_memory_space_constraint(r, pltpu.HBM) for r in raw))


def copies(pairs, semaphores):
    started = [pltpu.make_async_copy(*pair, semaphores.at[i]) for i, pair in enumerate(pairs)]
    for copy in started:
        copy.start()
    return started


def slot_rows(places):
    return [places[r : r + 1, :] for r in range(places.shape[0])]


def pick(vector, rows):
    index = jnp.concatenate(rows, axis=0)
    low = jnp.bitwise_and(index, LANES - 1)
    high = jnp.right_shift(index, 7)
    out = jnp.zeros(index.shape, F32)
    for t in range(vector.shape[0]):
        spread = jnp.broadcast_to(vector[t : t + 1, :], index.shape)
        got = jnp.take_along_axis(spread, low, axis=1, mode="promise_in_bounds")
        out = jnp.where(high == t, got, out)
    return out


def pieces(value):
    first = value.astype(BF16)
    rest = value - first.astype(F32)
    second = rest.astype(BF16)
    third = (rest - second.astype(F32)).astype(BF16)
    return first, second, third


def low_hits(rows):
    lane = lax.broadcasted_iota(jnp.int32, (LANES, LANES), 0)
    return jnp.concatenate(
        [(lane == jnp.bitwise_and(row, LANES - 1)).astype(F32).astype(BF16) for row in rows], axis=1
    )


def spread_sum(values, rows, tiles):
    tile = lax.broadcasted_iota(jnp.int32, (tiles, LANES), 0)
    parts = [
        jnp.where(tile == jnp.right_shift(row, 7), value, 0.0) for value, row in zip(values, rows)
    ]
    held = jnp.concatenate(parts, axis=1)
    stacked = jnp.concatenate([p.astype(F32) for p in pieces(held)], axis=0).astype(BF16)
    out = lax.dot_general(
        stacked, low_hits(rows), (((1,), (1,)), ((), ())), preferred_element_type=F32
    )
    return out[:tiles] + out[tiles : 2 * tiles] + out[2 * tiles :]


def arrived_rows(refs):
    return [ref[h : h + 1, :] for ref in refs for h in range(ref.shape[0])]


def store_sent(refs, sent):
    per = refs[0].shape[0]
    for k, ref in enumerate(refs):
        ref[...] = sent[k * per : (k + 1) * per, :]


def lane_rows(vector):
    return jnp.concatenate([vector[t : t + 1, :] for t in range(vector.shape[0])], axis=1)


def tile_rows_of(row):
    return jnp.concatenate(
        [row[:, t * LANES : (t + 1) * LANES] for t in range(row.shape[1] // LANES)], axis=0
    )


def gather_first(
    sides, index_in, counts_in, state_in, gains_in, bias_in, decode_in,
    lat, hits, places, columns, s0, s1, s2, s3,
    index, counts, state, gains, bias, decode, sems,
):
    first, second, third, *others = copies(
        (
            (index_in, index), (counts_in, counts), (state_in, state), (gains_in, gains), (bias_in, bias),
            (decode_in, decode),
        ),
        sems,
    )
    per = index.shape[2] // LANES
    first.wait()
    second.wait()
    for g in range(index.shape[1]):
        side = sides[g]
        for h in range(per):
            low, high = g // 2 * 2, g // 2 * 2 + 1
            span = slice(h * LANES, (h + 1) * LANES)
            row = jnp.where(side == low, index[0, low : low + 1, span], index[0, high : high + 1, span])
            slot = lax.broadcasted_iota(jnp.int32, (1, LANES), 1) + h * LANES
            r = g * per + h
            places[r : r + 1, :] = jnp.where(slot < counts[0, side], row, -1)
    node = lax.broadcasted_iota(jnp.int32, (state.shape[0], LANES), 0)
    for c, row in enumerate(slot_rows(places)):
        hits[:, c * LANES : (c + 1) * LANES] = (node == row).astype(F32).astype(BF16)
    third.wait()
    lat[...] = state[...].T
    send_features(lat[...], hits, (s0, s1, s2, s3))
    for copy in others:
        copy.wait()
    rows = [gains[layer] for layer in range(LAYERS)] + [bias[...], decode[...]]
    rows.append(jnp.zeros((8 - 3 * LAYERS - 1, bias.shape[1]), F32))
    columns[...] = jnp.concatenate(rows, axis=0).T


def send_features(lat, hits, outs):
    width = outs[0].shape[1]
    for k, out in enumerate(outs):
        out[...] = jnp.dot(
            lat, hits[:, k * width : (k + 1) * width], preferred_element_type=F32
        ).astype(BF16)


def build(
    tile_counts, places, tiles, lat, w_self, columns, rows_in, columns_in, capacity_in,
    matrix, half, inverse_rowsum, diagonal, local, own,
    tile_rows, tile_columns, capacity, sems,
):
    waits = copies(((rows_in, tile_rows), (columns_in, tile_columns), (capacity_in, capacity)), sems)
    count = tiles.shape[2]
    node_tiles = matrix.shape[0] // count
    matrix[...] = jnp.zeros(matrix.shape, F32)
    for t in range(node_tiles):
        span = slice(t * count, (t + 1) * count)
        block = tiles[0, t]
        matrix[span, span] = block + block.T
    own[...] = own_part(0, lat[...], w_self, columns)
    for copy in waits:
        copy.wait()

    def add(t, carry):
        r = pl.multiple_of(tile_rows[0, t] * count, count)
        c = pl.multiple_of(tile_columns[0, t] * count, count)
        block = tiles[0, t]
        matrix[pl.ds(r, count), pl.ds(c, count)] += block
        matrix[pl.ds(c, count), pl.ds(r, count)] += block.T
        return carry

    lax.fori_loop(node_tiles, tile_counts[0], add, 0)
    rows = slot_rows(places)
    faces = spread_sum([jnp.ones((1, LANES), F32)] * len(rows), rows, node_tiles)
    total = jnp.sum(matrix[...], axis=0, keepdims=True)
    rowsum = tile_rows_of(total) + faces
    inverse_rowsum[...] = lane_rows(1.0 / rowsum)
    diagonal[...] = capacity[...] + rowsum
    half[...] = matrix[...].astype(BF16)
    local[...] = jnp.dot(lat[...], half[...], preferred_element_type=F32)


def normed(value, gain):
    scale = lax.rsqrt(jnp.mean(value * value, axis=0, keepdims=True) + 1e-06)
    return (value * scale * gain).astype(BF16)


def project(weight, value):
    return lax.dot_general(weight, value, (((0,), (0,)), ((), ())), preferred_element_type=F32)


def own_part(layer, lat, w_self, columns):
    gain = columns[:, 2 * layer : 2 * layer + 1]
    bias = columns[:, 2 * LAYERS + layer : 2 * LAYERS + layer + 1]
    return project(w_self[layer], normed(lat.astype(F32), gain)) + bias


def local_features(layer, lat, half, w_self, columns, local, own):
    local[...] = jnp.dot(lat[...], half[...], preferred_element_type=F32)
    own[...] = own_part(layer, lat[...], w_self, columns)


def layer_step(layer, arrived, local, own, inverse_rowsum, lat, hits, w_neighbour, w_out, columns):
    came = jnp.concatenate([a[...] for a in arrived], axis=1)
    coupled = lax.dot_general(
        came, hits[...], (((1,), (1,)), ((), ())), preferred_element_type=F32
    )
    mean = (local[...] + coupled) * inverse_rowsum[...]
    gain = columns[:, 2 * layer + 1 : 2 * layer + 2]
    linear = own[...] + project(w_neighbour[layer], normed(mean, gain))
    activated = (linear / (1.0 + jnp.exp(-linear))).astype(BF16)
    return (lat[...].astype(F32) + project(w_out[layer], activated)).astype(BF16)


def first_layer(
    a0, a1, a2, a3, local, own, inverse_rowsum, lat, hits, w_neighbour, w_out, columns,
    new, s0, s1, s2, s3,
):
    value = layer_step(
        0, (a0, a1, a2, a3), local, own, inverse_rowsum, lat, hits, w_neighbour, w_out, columns
    )
    new[...] = value
    send_features(value, hits, (s0, s1, s2, s3))


def last_layer(
    places, a0, a1, a2, a3, local, own, inverse_rowsum, lat, hits, w_neighbour, w_out, columns,
    guess, s0, s1, s2, s3,
):
    value = layer_step(
        LAYERS - 1, (a0, a1, a2, a3), local, own, inverse_rowsum, lat, hits, w_neighbour, w_out, columns
    )
    decode = columns[:, 3 * LAYERS : 3 * LAYERS + 1]
    row = jnp.sum(value.astype(F32) * decode, axis=0, keepdims=True)
    field = tile_rows_of(row)
    guess[...] = field
    store_sent((s0, s1, s2, s3), pick(field, slot_rows(places)))


def product(matrix, field):
    count = LANES
    width = matrix.shape[1]
    total = jnp.zeros((8, width), F32)
    for t in range(field.shape[0]):
        column = jnp.broadcast_to(field[t : t + 1, :], (count, count)).T
        wide = jnp.concatenate([column] * (width // count), axis=1)
        part = matrix[t * count : (t + 1) * count, :] * wide
        total = total + jnp.sum(part.reshape(count // 8, 8, width), axis=0)
    return tile_rows_of(jnp.sum(total, axis=0, keepdims=True))


def matvec(matrix, vector, out):
    out[...] = product(matrix, vector[...])


def start_basis(places, a0, a1, a2, a3, local, guess, source, diagonal, basis, s0, s1, s2, s3):
    rows = slot_rows(places)
    came = spread_sum(arrived_rows((a0, a1, a2, a3)), rows, guess.shape[0])
    value = (source[...] + local[...] + came) / diagonal[...] - guess[...]
    basis[...] = value
    store_sent((s0, s1, s2, s3), pick(value, rows))


def next_basis(places, a0, a1, a2, a3, local, diagonal, basis, s0, s1, s2, s3):
    rows = slot_rows(places)
    came = spread_sum(arrived_rows((a0, a1, a2, a3)), rows, local.shape[0])
    value = (local[...] + came) / diagonal[...]
    basis[...] = value
    store_sent((s0, s1, s2, s3), pick(value, rows))


def diagonal_mask():
    return lax.broadcasted_iota(jnp.int32, (8, LANES), 0) == lax.broadcasted_iota(jnp.int32, (8, LANES), 1)


def last_basis(places, a0, a1, a2, a3, local, diagonal, b0, b1, matrix, basis, image, packets):
    rows = slot_rows(places)
    came = spread_sum(arrived_rows((a0, a1, a2, a3)), rows, local.shape[0])
    value = (local[...] + came) / diagonal[...]
    basis[...] = value
    mapped = product(matrix, value)
    image[...] = mapped
    held = [b0[...], b1[...], value]
    parts = []
    for k in range(2 * ITERS - 1):
        left, right = held[k // 2], held[(k + 1) // 2]
        parts.append(jnp.sum(left * right * diagonal[...], axis=0, keepdims=True))
    parts.append(jnp.sum(value * mapped, axis=0, keepdims=True))
    parts.append(jnp.zeros((8 - 2 * ITERS, LANES), F32))
    sums = jnp.sum(jnp.concatenate(parts, axis=0), axis=1, keepdims=True)
    row = jnp.sum(jnp.where(diagonal_mask(), sums, 0.0), axis=0, keepdims=True)
    packet = jnp.concatenate([lane_rows(pick(value, rows)), row], axis=1)
    for device in range(packets.shape[0]):
        packets[device] = packet


def added(values):
    values = list(values)
    while len(values) > 1:
        values = [sum(values[i : i + 2][1:], values[i]) for i in range(0, len(values), 2)]
    return values[0]


def finish(sizes, partner, packets, places, image, guess, diagonal, b0, b1, b2, field, defect):
    doms, subs = sizes
    width = packets.shape[2] - LANES
    per = width // 4

    def slots(device, g):
        return packets[device, :, g * per : (g + 1) * per]

    edges = []
    for d in range(doms):
        for s in range(subs):
            for g, (i, j) in ((d % 2, (d + 1, s)), (2 + s % 2, (d, s + 1))):
                if i < doms and j < subs:
                    edges.append(slots(d * subs + s, g) * slots(i * subs + j, g))
    edges = added(edges)
    edges = added([edges[:, h : h + LANES] for h in range(0, per, LANES)])
    sums = added([packets[e, :, width : width + LANES] for e in range(doms * subs)])
    lane = lax.broadcasted_iota(jnp.int32, (1, LANES), 1)
    sums = sums + jnp.where(lane == 2 * ITERS - 1, 2.0 * jnp.sum(edges, axis=1, keepdims=True), 0.0)
    columns = jnp.sum(
        jnp.where(diagonal_mask(), jnp.broadcast_to(sums, (8, LANES)), 0.0), axis=1, keepdims=True
    )
    n = [jnp.broadcast_to(columns[k : k + 1, :], (8, LANES)) for k in range(2 * ITERS)]
    came = []
    for g in range(4):
        mine = slots(partner[g], g)
        came += [mine[:, h : h + LANES] for h in range(0, per, LANES)]
    last = (image[...] + spread_sum(came, slot_rows(places), image.shape[0])) / diagonal[...]
    one, zero = jnp.ones((8, LANES), F32), jnp.zeros((8, LANES), F32)

    def paired(left, values):
        total = zero
        for i, a in enumerate(left):
            for j, b in enumerate(left):
                total = total + a * b * values[i + j]
        return total

    gaps = [n[k] - n[k + 1] for k in range(2 * ITERS - 1)]
    residual = [one]
    heading = [one]
    moved = [zero] * ITERS
    size = n[0]
    for step in range(ITERS):
        alpha = size / paired(heading, gaps)
        for i, h in enumerate(heading):
            moved[i] = moved[i] + alpha * h
        change = [
            (heading[i] if i < len(heading) else zero) - (heading[i - 1] if i > 0 else zero)
            for i in range(len(heading) + 1)
        ]
        residual = [
            (residual[i] if i < len(residual) else zero) - alpha * change[i]
            for i in range(len(change))
        ]
        if step + 1 < ITERS:
            following = paired(residual, n)
            beta = following / size
            heading = [
                residual[i] + (beta * heading[i] if i < len(heading) else zero)
                for i in range(len(residual))
            ]
            size = following
    held = [b0[...], b1[...], b2[...], last]
    total = guess[...]
    for c, b in zip(moved, held):
        total = total + c * b
    field[...] = total
    left = zero
    for c, b in zip(residual, held):
        left = left + c * b
    defect[...] = left * diagonal[...]


def matching(sizes, along, first):
    pairs = []
    for dom in range(sizes[0]):
        for sub in range(sizes[1]):
            at = [dom, sub]
            to = [dom, sub]
            other = 1 - along
            mate = (at[along] - first ^ 1) + first
            if at[along] >= first and mate < sizes[along]:
                to[along] = mate
            elif at[other] ^ 1 < sizes[other]:
                to[other] = at[other] ^ 1
            pairs.append((at[0] * sizes[1] + at[1], to[0] * sizes[1] + to[1]))
    return pairs


def sides_of_matchings():
    dom = lax.axis_index("dom") % 2
    sub = lax.axis_index("sub") % 2
    return jnp.stack([1 - dom, dom, 3 - sub, 2 + sub]).astype(jnp.int32)


def exchange(sent):
    axes = ("dom", "sub")
    sizes = [lax.axis_size(axis) for axis in axes]
    arrived = {}
    for g in (3, 2, 1, 0):
        arrived[g] = lax.ppermute(sent[g], axes, matching(sizes, g // 2, g % 2))
    return [arrived[g] for g in range(4)]


def partners():
    at = [lax.axis_index("dom"), lax.axis_index("sub")]
    sizes = [lax.axis_size("dom"), lax.axis_size("sub")]
    out = []
    for g in range(4):
        along, first = g // 2, g % 2
        mate = jnp.bitwise_xor(at[along] - first, 1) + first
        known = (at[along] >= first) & (mate < sizes[along])
        to = list(at)
        to[along] = jnp.where(known, mate, at[along])
        out.append(to[0] * sizes[1] + to[1])
    return jnp.stack(out).astype(jnp.int32)


def all_to_all(messages):
    return lax.all_to_all(messages, ("dom", "sub"), split_axis=0, concat_axis=0, tiled=True)


def per_device(
    state, tile_values, tile_rows, tile_columns, tile_counts, send_nodes, face_counts, capacity,
    source, w_self, w_neighbour, w_out, gains, bias, w_decode,
):
    nodes, width = state.shape
    slots = send_nodes.shape[2]
    tiles = nodes // LANES
    sizes = (lax.axis_size("dom"), lax.axis_size("sub"))
    devices = sizes[0] * sizes[1]
    field = shape((tiles, LANES))
    features = shape((width, nodes))
    feature_sent = [shape((width, slots), BF16)] * 4
    vector_sent = [shape((slots // LANES, LANES))] * 4
    decode = w_decode.reshape(1, width)
    capacity = capacity.reshape(tiles, LANES)
    source = source.reshape(tiles, LANES)

    lat, hits, places, columns, *sent = run(
        gather_first,
        [shape((width, nodes), BF16), shape((nodes, 4 * slots), BF16), shape((4 * slots // LANES, LANES), jnp.int32),
         shape((width, 8))]
        + feature_sent,
        (), (sides_of_matchings(),), (send_nodes, face_counts, state, gains, bias, decode),
        (
            pltpu.VMEM(send_nodes.shape, jnp.int32),
            pltpu.SMEM(face_counts.shape, jnp.int32),
            pltpu.VMEM(state.shape, BF16),
            pltpu.VMEM(gains.shape, F32),
            pltpu.VMEM(bias.shape, F32),
            pltpu.VMEM(decode.shape, F32),
        ),
        flops=2 * nodes * 4 * slots * width,
    )
    arrived = exchange(sent)
    matrix, half, inverse_rowsum, diagonal, local, own = run(
        build,
        [shape((nodes, nodes)), shape((nodes, nodes), BF16), shape((1, nodes)), field, features, features],
        (places, tile_values, lat, w_self, columns),
        (tile_counts,), (tile_rows, tile_columns, capacity),
        (
            pltpu.SMEM(tile_rows.shape, jnp.int32),
            pltpu.SMEM(tile_columns.shape, jnp.int32),
            pltpu.VMEM(capacity.shape, F32),
        ),
        flops=2 * nodes * nodes * width, moved=6_000_000,
    )
    lat, *sent = run(
        first_layer, [shape((width, nodes), BF16)] + feature_sent,
        (*arrived, local, own, inverse_rowsum, lat, hits, w_neighbour, w_out, columns), flops=6 * nodes * nodes * width,
    )
    arrived = exchange(sent)
    local, own = run(
        functools.partial(local_features, LAYERS - 1), [features, features],
        (lat, half, w_self, columns), flops=2 * nodes * nodes * width, moved=4_000_000,
    )
    guess, *sent = run(
        last_layer, [field] + vector_sent,
        (places, *arrived, local, own, inverse_rowsum, lat, hits, w_neighbour, w_out, columns),
        flops=6 * nodes * nodes * width,
    )

    def mapped(vector):
        return run(matvec, [field], (matrix, vector), flops=2 * nodes * nodes, moved=4 * nodes * nodes)[0]

    arrived = exchange(sent)
    local = mapped(guess)
    b0, *sent = run(
        start_basis, [field] + vector_sent, (places, *arrived, local, guess, source, diagonal)
    )
    arrived = exchange(sent)
    local = mapped(b0)
    b1, *sent = run(next_basis, [field] + vector_sent, (places, *arrived, local, diagonal))
    arrived = exchange(sent)
    local = mapped(b1)
    b2, image, packets = run(
        last_basis, [field, field, shape((devices, 1, 4 * slots + LANES))],
        (places, *arrived, local, diagonal, b0, b1, matrix),
    )
    packets = all_to_all(packets)
    heat, defect = run(
        functools.partial(finish, sizes), [field, field],
        (packets, places, image, guess, diagonal, b0, b1, b2), (partners(),),
    )
    return heat.reshape(nodes), defect.reshape(nodes)


def solution(mesh):
    both = ("dom", "sub")
    return jax.shard_map(
        per_device,
        mesh=mesh,
        in_specs=(
            P(both, None),
            P(both, None, None, None),
            P(both, None),
            P(both, None),
            P(both),
            P(both, None, None),
            P(both, None),
            P(both),
            P(both),
            P(),
            P(),
            P(),
            P(),
            P(),
            P(),
        ),
        out_specs=(P(both), P(both)),
        check_vma=False,
    )
```

```python
import functools

import jax
import jax.numpy as jnp
from jax import lax
from jax.experimental import pallas as pl
from jax.experimental.pallas import tpu as pltpu
from jax.sharding import PartitionSpec as P

LAYERS = 2
ITERS = 3
LANES = 128
MATCHINGS = ((1, 1), (1, 0), (0, 1), (0, 0))
VMEM_LIMIT = 24 * 1024 * 1024

F32 = jnp.float32
BF16 = jnp.bfloat16


def shape(dims, dtype=F32):
    return jax.ShapeDtypeStruct(dims, dtype)


def run(body, outs, operands, scalars=(), raw=(), scratch=(), flops=1_000_000, moved=1_000_000):
    smem = pl.BlockSpec(memory_space=pltpu.SMEM)
    vmem = pl.BlockSpec(memory_space=pltpu.VMEM)
    anywhere = pl.BlockSpec(memory_space=pltpu.HBM)
    scratch = list(scratch) + [pltpu.SemaphoreType.DMA((len(raw),))] * bool(raw)
    return pl.pallas_call(
        body,
        out_shape=outs,
        in_specs=[smem] * len(scalars) + [vmem] * len(operands) + [anywhere] * len(raw),
        out_specs=[vmem] * len(outs),
        scratch_shapes=scratch,
        compiler_params=pltpu.CompilerParams(vmem_limit_bytes=VMEM_LIMIT),
        cost_estimate=pl.CostEstimate(flops=flops, bytes_accessed=moved, transcendentals=0),
    )(*scalars, *operands, *(pltpu.with_memory_space_constraint(r, pltpu.HBM) for r in raw))


def copies(pairs, semaphores):
    started = [pltpu.make_async_copy(*pair, semaphores.at[i]) for i, pair in enumerate(pairs)]
    for copy in started:
        copy.start()
    return started


def slot_rows(places):
    return [places[r : r + 1, :] for r in range(places.shape[0])]


def pick(vector, rows):
    index = jnp.concatenate(rows, axis=0)
    low = jnp.bitwise_and(index, LANES - 1)
    high = jnp.right_shift(index, 7)
    out = jnp.zeros(index.shape, F32)
    for t in range(vector.shape[0]):
        spread = jnp.broadcast_to(vector[t : t + 1, :], index.shape)
        got = jnp.take_along_axis(spread, low, axis=1, mode="promise_in_bounds")
        out = jnp.where(high == t, got, out)
    return out


def pieces(value):
    first = value.astype(BF16)
    rest = value - first.astype(F32)
    second = rest.astype(BF16)
    third = (rest - second.astype(F32)).astype(BF16)
    return first, second, third


def low_hits(rows):
    lane = lax.broadcasted_iota(jnp.int32, (LANES, LANES), 0)
    return jnp.concatenate(
        [(lane == jnp.bitwise_and(row, LANES - 1)).astype(F32).astype(BF16) for row in rows], axis=1
    )


def spread_sum(values, rows, tiles):
    tile = lax.broadcasted_iota(jnp.int32, (tiles, LANES), 0)
    parts = [
        jnp.where(tile == jnp.right_shift(row, 7), value, 0.0) for value, row in zip(values, rows)
    ]
    held = jnp.concatenate(parts, axis=1)
    stacked = jnp.concatenate([p.astype(F32) for p in pieces(held)], axis=0).astype(BF16)
    out = lax.dot_general(
        stacked, low_hits(rows), (((1,), (1,)), ((), ())), preferred_element_type=F32
    )
    return out[:tiles] + out[tiles : 2 * tiles] + out[2 * tiles :]


def arrived_rows(refs):
    return [ref[h : h + 1, :] for ref in refs for h in range(ref.shape[0])]


def store_sent(refs, sent):
    per = refs[0].shape[0]
    for k, ref in enumerate(refs):
        ref[...] = sent[k * per : (k + 1) * per, :]


def lane_rows(vector):
    return jnp.concatenate([vector[t : t + 1, :] for t in range(vector.shape[0])], axis=1)


def tile_rows_of(row):
    return jnp.concatenate(
        [row[:, t * LANES : (t + 1) * LANES] for t in range(row.shape[1] // LANES)], axis=0
    )


def gather_first(
    where, index_in, counts_in, state_in, gains_in, bias_in, decode_in,
    lat, hits, places, columns, s0, s1, s2, s3,
    index, counts, state, gains, bias, decode, sems,
):
    first, second, third, *others = copies(
        (
            (index_in, index), (counts_in, counts), (state_in, state), (gains_in, gains), (bias_in, bias),
            (decode_in, decode),
        ),
        sems,
    )
    per = index.shape[2] // LANES
    first.wait()
    second.wait()
    for g in range(index.shape[1]):
        side = where[g]
        for h in range(per):
            low, high = 2 * MATCHINGS[g][0], 2 * MATCHINGS[g][0] + 1
            span = slice(h * LANES, (h + 1) * LANES)
            row = jnp.where(side == low, index[0, low : low + 1, span], index[0, high : high + 1, span])
            slot = lax.broadcasted_iota(jnp.int32, (1, LANES), 1) + h * LANES
            r = g * per + h
            places[r : r + 1, :] = jnp.where(slot < counts[0, side], row, -1)
    node = lax.broadcasted_iota(jnp.int32, (state.shape[0], LANES), 0)
    for c, row in enumerate(slot_rows(places)):
        hits[:, c * LANES : (c + 1) * LANES] = (node == row).astype(F32).astype(BF16)
    third.wait()
    lat[...] = state[...].T
    send_features(lat[...], hits, (s0, s1, s2, s3))
    for copy in others:
        copy.wait()
    rows = [gains[layer] for layer in range(LAYERS)] + [bias[...], decode[...]]
    rows.append(jnp.zeros((8 - 3 * LAYERS - 1, bias.shape[1]), F32))
    columns[...] = jnp.concatenate(rows, axis=0).T


def send_features(lat, hits, outs):
    width = outs[0].shape[1]
    for k, out in enumerate(outs):
        out[...] = jnp.dot(
            lat, hits[:, k * width : (k + 1) * width], preferred_element_type=F32
        ).astype(BF16)


def build(
    tile_counts, places, tiles, lat, w_self, columns, rows_in, columns_in, capacity_in,
    matrix, half, inverse_rowsum, diagonal, local, own,
    tile_rows, tile_columns, capacity, sems,
):
    waits = copies(((rows_in, tile_rows), (columns_in, tile_columns), (capacity_in, capacity)), sems)
    count = tiles.shape[2]
    node_tiles = matrix.shape[0] // count
    matrix[...] = jnp.zeros(matrix.shape, F32)
    for t in range(node_tiles):
        span = slice(t * count, (t + 1) * count)
        block = tiles[0, t]
        matrix[span, span] = block + block.T
    own[...] = own_part(0, lat[...], w_self, columns)
    for copy in waits:
        copy.wait()

    def add(t, carry):
        r = pl.multiple_of(tile_rows[0, t] * count, count)
        c = pl.multiple_of(tile_columns[0, t] * count, count)
        block = tiles[0, t]
        matrix[pl.ds(r, count), pl.ds(c, count)] += block
        matrix[pl.ds(c, count), pl.ds(r, count)] += block.T
        return carry

    lax.fori_loop(node_tiles, tile_counts[0], add, 0)
    rows = slot_rows(places)
    faces = spread_sum([jnp.ones((1, LANES), F32)] * len(rows), rows, node_tiles)
    total = jnp.sum(matrix[...], axis=0, keepdims=True)
    rowsum = tile_rows_of(total) + faces
    inverse_rowsum[...] = lane_rows(1.0 / rowsum)
    diagonal[...] = capacity[...] + rowsum
    half[...] = matrix[...].astype(BF16)
    local[...] = jnp.dot(lat[...], half[...], preferred_element_type=F32)


def normed(value, gain):
    scale = lax.rsqrt(jnp.mean(value * value, axis=0, keepdims=True) + 1e-06)
    return (value * scale * gain).astype(BF16)


def project(weight, value):
    return lax.dot_general(weight, value, (((0,), (0,)), ((), ())), preferred_element_type=F32)


def own_part(layer, lat, w_self, columns):
    gain = columns[:, 2 * layer : 2 * layer + 1]
    bias = columns[:, 2 * LAYERS + layer : 2 * LAYERS + layer + 1]
    return project(w_self[layer], normed(lat.astype(F32), gain)) + bias


def local_features(layer, lat, half, w_self, columns, local, own):
    local[...] = jnp.dot(lat[...], half[...], preferred_element_type=F32)
    own[...] = own_part(layer, lat[...], w_self, columns)


def layer_step(layer, arrived, local, own, inverse_rowsum, lat, hits, w_neighbour, w_out, columns):
    came = jnp.concatenate([a[...] for a in arrived], axis=1)
    coupled = lax.dot_general(
        came, hits[...], (((1,), (1,)), ((), ())), preferred_element_type=F32
    )
    mean = (local[...] + coupled) * inverse_rowsum[...]
    gain = columns[:, 2 * layer + 1 : 2 * layer + 2]
    linear = own[...] + project(w_neighbour[layer], normed(mean, gain))
    activated = (linear / (1.0 + jnp.exp(-linear))).astype(BF16)
    return (lat[...].astype(F32) + project(w_out[layer], activated)).astype(BF16)


def first_layer(
    a0, a1, a2, a3, local, own, inverse_rowsum, lat, hits, w_neighbour, w_out, columns,
    new, s0, s1, s2, s3,
):
    value = layer_step(
        0, (a0, a1, a2, a3), local, own, inverse_rowsum, lat, hits, w_neighbour, w_out, columns
    )
    new[...] = value
    send_features(value, hits, (s0, s1, s2, s3))


def last_layer(
    places, a0, a1, a2, a3, local, own, inverse_rowsum, lat, hits, w_neighbour, w_out, columns,
    guess, s0, s1, s2, s3,
):
    value = layer_step(
        LAYERS - 1, (a0, a1, a2, a3), local, own, inverse_rowsum, lat, hits, w_neighbour, w_out, columns
    )
    decode = columns[:, 3 * LAYERS : 3 * LAYERS + 1]
    row = jnp.sum(value.astype(F32) * decode, axis=0, keepdims=True)
    field = tile_rows_of(row)
    guess[...] = field
    store_sent((s0, s1, s2, s3), pick(field, slot_rows(places)))


def product(matrix, field):
    count = LANES
    width = matrix.shape[1]
    total = jnp.zeros((8, width), F32)
    for t in range(field.shape[0]):
        column = jnp.broadcast_to(field[t : t + 1, :], (count, count)).T
        wide = jnp.concatenate([column] * (width // count), axis=1)
        part = matrix[t * count : (t + 1) * count, :] * wide
        total = total + jnp.sum(part.reshape(count // 8, 8, width), axis=0)
    return tile_rows_of(jnp.sum(total, axis=0, keepdims=True))


def matvec(matrix, vector, out):
    out[...] = product(matrix, vector[...])


def start_basis(places, a0, a1, a2, a3, local, guess, source, diagonal, basis, s0, s1, s2, s3):
    rows = slot_rows(places)
    came = spread_sum(arrived_rows((a0, a1, a2, a3)), rows, guess.shape[0])
    value = (source[...] + local[...] + came) / diagonal[...] - guess[...]
    basis[...] = value
    store_sent((s0, s1, s2, s3), pick(value, rows))


def next_basis(places, a0, a1, a2, a3, local, diagonal, basis, s0, s1, s2, s3):
    rows = slot_rows(places)
    came = spread_sum(arrived_rows((a0, a1, a2, a3)), rows, local.shape[0])
    value = (local[...] + came) / diagonal[...]
    basis[...] = value
    store_sent((s0, s1, s2, s3), pick(value, rows))


def diagonal_mask():
    return lax.broadcasted_iota(jnp.int32, (8, LANES), 0) == lax.broadcasted_iota(jnp.int32, (8, LANES), 1)


def last_basis(places, a0, a1, a2, a3, local, diagonal, b0, b1, matrix, basis, image, packets):
    rows = slot_rows(places)
    came = spread_sum(arrived_rows((a0, a1, a2, a3)), rows, local.shape[0])
    value = (local[...] + came) / diagonal[...]
    basis[...] = value
    mapped = product(matrix, value)
    image[...] = mapped
    held = [b0[...], b1[...], value]
    parts = []
    for k in range(2 * ITERS - 1):
        left, right = held[k // 2], held[(k + 1) // 2]
        parts.append(jnp.sum(left * right * diagonal[...], axis=0, keepdims=True))
    parts.append(jnp.sum(value * mapped, axis=0, keepdims=True))
    parts.append(jnp.zeros((8 - 2 * ITERS, LANES), F32))
    sums = jnp.sum(jnp.concatenate(parts, axis=0), axis=1, keepdims=True)
    row = jnp.sum(jnp.where(diagonal_mask(), sums, 0.0), axis=0, keepdims=True)
    packet = jnp.concatenate([lane_rows(pick(value, rows)), row], axis=1)
    for device in range(packets.shape[0]):
        packets[device] = packet


def added(values):
    values = list(values)
    while len(values) > 1:
        values = [sum(values[i : i + 2][1:], values[i]) for i in range(0, len(values), 2)]
    return values[0]


def finish(sizes, where, packets, places, image, guess, diagonal, b0, b1, b2, field, defect):
    doms, subs = sizes
    width = packets.shape[2] - LANES
    per = width // 4

    def slots(device, g):
        return packets[device, :, g * per : (g + 1) * per]

    edges = []
    for d in range(doms):
        for s in range(subs):
            for m, (i, j) in (((0, d % 2), (d + 1, s)), ((1, s % 2), (d, s + 1))):
                g = MATCHINGS.index(m)
                if i < doms and j < subs:
                    edges.append(slots(d * subs + s, g) * slots(i * subs + j, g))
    edges = added(edges)
    edges = added([edges[:, h : h + LANES] for h in range(0, per, LANES)])
    sums = added([packets[e, :, width : width + LANES] for e in range(doms * subs)])
    lane = lax.broadcasted_iota(jnp.int32, (1, LANES), 1)
    sums = sums + jnp.where(lane == 2 * ITERS - 1, 2.0 * jnp.sum(edges, axis=1, keepdims=True), 0.0)
    columns = jnp.sum(
        jnp.where(diagonal_mask(), jnp.broadcast_to(sums, (8, LANES)), 0.0), axis=1, keepdims=True
    )
    n = [jnp.broadcast_to(columns[k : k + 1, :], (8, LANES)) for k in range(2 * ITERS)]
    came = []
    for g in range(4):
        mine = slots(where[4 + g], g)
        came += [mine[:, h : h + LANES] for h in range(0, per, LANES)]
    last = (image[...] + spread_sum(came, slot_rows(places), image.shape[0])) / diagonal[...]
    one, zero = jnp.ones((8, LANES), F32), jnp.zeros((8, LANES), F32)

    def paired(left, values):
        total = zero
        for i, a in enumerate(left):
            for j, b in enumerate(left):
                total = total + a * b * values[i + j]
        return total

    gaps = [n[k] - n[k + 1] for k in range(2 * ITERS - 1)]
    residual = [one]
    heading = [one]
    moved = [zero] * ITERS
    size = n[0]
    for step in range(ITERS):
        alpha = size / paired(heading, gaps)
        for i, h in enumerate(heading):
            moved[i] = moved[i] + alpha * h
        change = [
            (heading[i] if i < len(heading) else zero) - (heading[i - 1] if i > 0 else zero)
            for i in range(len(heading) + 1)
        ]
        residual = [
            (residual[i] if i < len(residual) else zero) - alpha * change[i]
            for i in range(len(change))
        ]
        if step + 1 < ITERS:
            following = paired(residual, n)
            beta = following / size
            heading = [
                residual[i] + (beta * heading[i] if i < len(heading) else zero)
                for i in range(len(residual))
            ]
            size = following
    held = [b0[...], b1[...], b2[...], last]
    total = guess[...]
    for c, b in zip(moved, held):
        total = total + c * b
    field[...] = total
    left = zero
    for c, b in zip(residual, held):
        left = left + c * b
    defect[...] = left * diagonal[...]


def matching(sizes, along, first):
    pairs = []
    for dom in range(sizes[0]):
        for sub in range(sizes[1]):
            at = [dom, sub]
            to = [dom, sub]
            other = 1 - along
            mate = (at[along] - first ^ 1) + first
            if at[along] >= first and mate < sizes[along]:
                to[along] = mate
            elif at[other] ^ 1 < sizes[other]:
                to[other] = at[other] ^ 1
            pairs.append((at[0] * sizes[1] + at[1], to[0] * sizes[1] + to[1]))
    return pairs


def sides_of_matchings():
    odd = [lax.axis_index("dom") % 2, lax.axis_index("sub") % 2]
    return [2 * along + (odd[along] if first else 1 - odd[along]) for along, first in MATCHINGS]


def exchange(sent):
    axes = ("dom", "sub")
    sizes = [lax.axis_size(axis) for axis in axes]
    return [lax.ppermute(s, axes, matching(sizes, *m)) for s, m in zip(sent, MATCHINGS)]


def partners():
    at = [lax.axis_index("dom"), lax.axis_index("sub")]
    sizes = [lax.axis_size("dom"), lax.axis_size("sub")]
    out = []
    for along, first in MATCHINGS:
        mate = jnp.bitwise_xor(at[along] - first, 1) + first
        known = (at[along] >= first) & (mate < sizes[along])
        to = list(at)
        to[along] = jnp.where(known, mate, at[along])
        out.append(to[0] * sizes[1] + to[1])
    return out


def all_to_all(messages):
    return lax.all_to_all(messages, ("dom", "sub"), split_axis=0, concat_axis=0, tiled=True)


def per_device(
    state, tile_values, tile_rows, tile_columns, tile_counts, send_nodes, face_counts, capacity,
    source, w_self, w_neighbour, w_out, gains, bias, w_decode,
):
    nodes, width = state.shape
    slots = send_nodes.shape[2]
    tiles = nodes // LANES
    sizes = (lax.axis_size("dom"), lax.axis_size("sub"))
    devices = sizes[0] * sizes[1]
    field = shape((tiles, LANES))
    features = shape((width, nodes))
    feature_sent = [shape((width, slots), BF16)] * 4
    vector_sent = [shape((slots // LANES, LANES))] * 4
    decode = w_decode.reshape(1, width)
    where = jnp.stack(sides_of_matchings() + partners()).astype(jnp.int32)
    capacity = capacity.reshape(tiles, LANES)
    source = source.reshape(tiles, LANES)

    lat, hits, places, columns, *sent = run(
        gather_first,
        [shape((width, nodes), BF16), shape((nodes, 4 * slots), BF16), shape((4 * slots // LANES, LANES), jnp.int32),
         shape((width, 8))]
        + feature_sent,
        (), (where,), (send_nodes, face_counts, state, gains, bias, decode),
        (
            pltpu.VMEM(send_nodes.shape, jnp.int32),
            pltpu.SMEM(face_counts.shape, jnp.int32),
            pltpu.VMEM(state.shape, BF16),
            pltpu.VMEM(gains.shape, F32),
            pltpu.VMEM(bias.shape, F32),
            pltpu.VMEM(decode.shape, F32),
        ),
        flops=2 * nodes * 4 * slots * width,
    )
    arrived = exchange(sent)
    matrix, half, inverse_rowsum, diagonal, local, own = run(
        build,
        [shape((nodes, nodes)), shape((nodes, nodes), BF16), shape((1, nodes)), field, features, features],
        (places, tile_values, lat, w_self, columns),
        (tile_counts,), (tile_rows, tile_columns, capacity),
        (
            pltpu.SMEM(tile_rows.shape, jnp.int32),
            pltpu.SMEM(tile_columns.shape, jnp.int32),
            pltpu.VMEM(capacity.shape, F32),
        ),
        flops=2 * nodes * nodes * width, moved=6_000_000,
    )
    lat, *sent = run(
        first_layer, [shape((width, nodes), BF16)] + feature_sent,
        (*arrived, local, own, inverse_rowsum, lat, hits, w_neighbour, w_out, columns), flops=6 * nodes * nodes * width,
    )
    arrived = exchange(sent)
    local, own = run(
        functools.partial(local_features, LAYERS - 1), [features, features],
        (lat, half, w_self, columns), flops=2 * nodes * nodes * width, moved=4_000_000,
    )
    guess, *sent = run(
        last_layer, [field] + vector_sent,
        (places, *arrived, local, own, inverse_rowsum, lat, hits, w_neighbour, w_out, columns),
        flops=6 * nodes * nodes * width,
    )

    def mapped(vector):
        return run(matvec, [field], (matrix, vector), flops=2 * nodes * nodes, moved=4 * nodes * nodes)[0]

    arrived = exchange(sent)
    local = mapped(guess)
    b0, *sent = run(
        start_basis, [field] + vector_sent, (places, *arrived, local, guess, source, diagonal)
    )
    arrived = exchange(sent)
    local = mapped(b0)
    b1, *sent = run(next_basis, [field] + vector_sent, (places, *arrived, local, diagonal))
    arrived = exchange(sent)
    local = mapped(b1)
    b2, image, packets = run(
        last_basis, [field, field, shape((devices, 1, 4 * slots + LANES))],
        (places, *arrived, local, diagonal, b0, b1, matrix),
    )
    packets = all_to_all(packets)
    heat, defect = run(
        functools.partial(finish, sizes), [field, field],
        (packets, places, image, guess, diagonal, b0, b1, b2), (where,),
    )
    return heat.reshape(nodes), defect.reshape(nodes)


def solution(mesh):
    both = ("dom", "sub")
    return jax.shard_map(
        per_device,
        mesh=mesh,
        in_specs=(
            P(both, None),
            P(both, None, None, None),
            P(both, None),
            P(both, None),
            P(both),
            P(both, None, None),
            P(both, None),
            P(both),
            P(both),
            P(),
            P(),
            P(),
            P(),
            P(),
            P(),
        ),
        out_specs=(P(both), P(both)),
        check_vma=False,
    )
```

```python
import functools

import jax
import jax.numpy as jnp
from jax import lax
from jax.experimental import pallas as pl
from jax.experimental.pallas import tpu as pltpu
from jax.sharding import PartitionSpec as P

LAYERS = 2
ITERS = 3
LANES = 128
MATCHINGS = ((1, 1), (1, 0), (0, 1), (0, 0))
VMEM_LIMIT = 24 * 1024 * 1024

F32 = jnp.float32
BF16 = jnp.bfloat16


def shape(dims, dtype=F32):
    return jax.ShapeDtypeStruct(dims, dtype)


def run(body, outs, operands, scalars=(), raw=(), scratch=(), flops=1_000_000, moved=1_000_000):
    smem = pl.BlockSpec(memory_space=pltpu.SMEM)
    vmem = pl.BlockSpec(memory_space=pltpu.VMEM)
    anywhere = pl.BlockSpec(memory_space=pltpu.HBM)
    scratch = list(scratch) + [pltpu.SemaphoreType.DMA((len(raw),))] * bool(raw)
    return pl.pallas_call(
        body,
        out_shape=outs,
        in_specs=[smem] * len(scalars) + [vmem] * len(operands) + [anywhere] * len(raw),
        out_specs=[vmem] * len(outs),
        scratch_shapes=scratch,
        compiler_params=pltpu.CompilerParams(vmem_limit_bytes=VMEM_LIMIT),
        cost_estimate=pl.CostEstimate(flops=flops, bytes_accessed=moved, transcendentals=0),
    )(*scalars, *operands, *(pltpu.with_memory_space_constraint(r, pltpu.HBM) for r in raw))


def copies(pairs, semaphores):
    started = [pltpu.make_async_copy(*pair, semaphores.at[i]) for i, pair in enumerate(pairs)]
    for copy in started:
        copy.start()
    return started


def slot_rows(places):
    return [places[r : r + 1, :] for r in range(places.shape[0])]


def pick(vector, rows):
    index = jnp.concatenate(rows, axis=0)
    low = jnp.bitwise_and(index, LANES - 1)
    high = jnp.right_shift(index, 7)
    out = jnp.zeros(index.shape, F32)
    for t in range(vector.shape[0]):
        spread = jnp.broadcast_to(vector[t : t + 1, :], index.shape)
        got = jnp.take_along_axis(spread, low, axis=1, mode="promise_in_bounds")
        out = jnp.where(high == t, got, out)
    return out


def pieces(value):
    first = value.astype(BF16)
    rest = value - first.astype(F32)
    second = rest.astype(BF16)
    third = (rest - second.astype(F32)).astype(BF16)
    return first, second, third


def low_hits(rows):
    lane = lax.broadcasted_iota(jnp.int32, (LANES, LANES), 0)
    return jnp.concatenate(
        [(lane == jnp.bitwise_and(row, LANES - 1)).astype(F32).astype(BF16) for row in rows], axis=1
    )


def spread_sum(values, rows, tiles):
    tile = lax.broadcasted_iota(jnp.int32, (tiles, LANES), 0)
    parts = [
        jnp.where(tile == jnp.right_shift(row, 7), value, 0.0) for value, row in zip(values, rows)
    ]
    held = jnp.concatenate(parts, axis=1)
    stacked = jnp.concatenate([p.astype(F32) for p in pieces(held)], axis=0).astype(BF16)
    out = lax.dot_general(
        stacked, low_hits(rows), (((1,), (1,)), ((), ())), preferred_element_type=F32
    )
    return out[:tiles] + out[tiles : 2 * tiles] + out[2 * tiles :]


def arrived_rows(refs):
    return [ref[h : h + 1, :] for ref in refs for h in range(ref.shape[0])]


def store_sent(refs, sent):
    per = refs[0].shape[0]
    for k, ref in enumerate(refs):
        ref[...] = sent[k * per : (k + 1) * per, :]


def lane_rows(vector):
    return jnp.concatenate([vector[t : t + 1, :] for t in range(vector.shape[0])], axis=1)


def tile_rows_of(row):
    return jnp.concatenate(
        [row[:, t * LANES : (t + 1) * LANES] for t in range(row.shape[1] // LANES)], axis=0
    )


def gather_first(
    where, index_in, counts_in, state_in, gains_in, bias_in, decode_in,
    lat, hits, places, columns, s0, s1, s2, s3,
    index, counts, state, gains, bias, decode, sems,
):
    first, second, third, *others = copies(
        (
            (index_in, index), (counts_in, counts), (state_in, state), (gains_in, gains), (bias_in, bias),
            (decode_in, decode),
        ),
        sems,
    )
    per = index.shape[2] // LANES
    first.wait()
    second.wait()
    for g in range(index.shape[1]):
        side = where[g]
        for h in range(per):
            low, high = 2 * MATCHINGS[g][0], 2 * MATCHINGS[g][0] + 1
            span = slice(h * LANES, (h + 1) * LANES)
            row = jnp.where(side == low, index[0, low : low + 1, span], index[0, high : high + 1, span])
            slot = lax.broadcasted_iota(jnp.int32, (1, LANES), 1) + h * LANES
            r = g * per + h
            places[r : r + 1, :] = jnp.where(slot < counts[0, side], row, -1)
    node = lax.broadcasted_iota(jnp.int32, (state.shape[0], LANES), 0).astype(jnp.int16)
    one, zero = jnp.ones(node.shape, BF16), jnp.zeros(node.shape, BF16)
    for c, row in enumerate(slot_rows(places)):
        wide = jnp.broadcast_to(row, node.shape).astype(jnp.int16)
        hits[:, c * LANES : (c + 1) * LANES] = jnp.where(node == wide, one, zero)
    third.wait()
    lat[...] = state[...].T
    send_features(lat[...], hits, (s0, s1, s2, s3))
    for copy in others:
        copy.wait()
    rows = [gains[layer] for layer in range(LAYERS)] + [bias[...], decode[...]]
    rows.append(jnp.zeros((8 - 3 * LAYERS - 1, bias.shape[1]), F32))
    columns[...] = jnp.concatenate(rows, axis=0).T


def send_features(lat, hits, outs):
    width = outs[0].shape[1]
    for k, out in enumerate(outs):
        out[...] = jnp.dot(
            lat, hits[:, k * width : (k + 1) * width], preferred_element_type=F32
        ).astype(BF16)


def build(
    tile_counts, places, tiles, lat, w_self, columns, rows_in, columns_in, capacity_in,
    matrix, half, inverse_rowsum, diagonal, local, own,
    tile_rows, tile_columns, capacity, sems,
):
    waits = copies(((rows_in, tile_rows), (columns_in, tile_columns), (capacity_in, capacity)), sems)
    count = tiles.shape[2]
    node_tiles = matrix.shape[0] // count
    matrix[...] = jnp.zeros(matrix.shape, F32)
    for t in range(node_tiles):
        span = slice(t * count, (t + 1) * count)
        block = tiles[0, t]
        matrix[span, span] = block + block.T
    for copy in waits:
        copy.wait()

    def add(t, carry):
        r = pl.multiple_of(tile_rows[0, t] * count, count)
        c = pl.multiple_of(tile_columns[0, t] * count, count)
        block = tiles[0, t]
        matrix[pl.ds(r, count), pl.ds(c, count)] += block
        matrix[pl.ds(c, count), pl.ds(r, count)] += block.T
        return carry

    lax.fori_loop(node_tiles, tile_counts[0], add, 0)
    rows = slot_rows(places)
    faces = spread_sum([jnp.ones((1, LANES), F32)] * len(rows), rows, node_tiles)
    total = jnp.zeros((8, matrix.shape[1]), F32)
    for t in range(node_tiles):
        block = matrix[t * count : (t + 1) * count, :]
        half[t * count : (t + 1) * count, :] = block.astype(BF16)
        total = total + jnp.sum(block.reshape(count // 8, 8, matrix.shape[1]), axis=0)
    rowsum = tile_rows_of(jnp.sum(total, axis=0, keepdims=True)) + faces
    inverse_rowsum[...] = lane_rows(1.0 / rowsum)
    diagonal[...] = capacity[...] + rowsum
    local[...] = jnp.dot(lat[...], half[...], preferred_element_type=F32)
    own[...] = own_part(0, lat[...], w_self, columns)


def normed(value, gain):
    scale = lax.rsqrt(jnp.mean(value * value, axis=0, keepdims=True) + 1e-06)
    return (value * scale * gain).astype(BF16)


def project(weight, value):
    return lax.dot_general(weight, value, (((0,), (0,)), ((), ())), preferred_element_type=F32)


def own_part(layer, lat, w_self, columns):
    gain = columns[:, 2 * layer : 2 * layer + 1]
    bias = columns[:, 2 * LAYERS + layer : 2 * LAYERS + layer + 1]
    return project(w_self[layer], normed(lat.astype(F32), gain)) + bias


def local_features(layer, lat, half, w_self, columns, local, own):
    local[...] = jnp.dot(lat[...], half[...], preferred_element_type=F32)
    own[...] = own_part(layer, lat[...], w_self, columns)


def layer_step(layer, arrived, local, own, inverse_rowsum, lat, hits, w_neighbour, w_out, columns):
    came = jnp.concatenate([a[...] for a in arrived], axis=1)
    coupled = lax.dot_general(
        came, hits[...], (((1,), (1,)), ((), ())), preferred_element_type=F32
    )
    mean = (local[...] + coupled) * inverse_rowsum[...]
    gain = columns[:, 2 * layer + 1 : 2 * layer + 2]
    linear = own[...] + project(w_neighbour[layer], normed(mean, gain))
    activated = (linear / (1.0 + jnp.exp(-linear))).astype(BF16)
    return (lat[...].astype(F32) + project(w_out[layer], activated)).astype(BF16)


def first_layer(
    a0, a1, a2, a3, local, own, inverse_rowsum, lat, hits, w_neighbour, w_out, columns,
    new, s0, s1, s2, s3,
):
    value = layer_step(
        0, (a0, a1, a2, a3), local, own, inverse_rowsum, lat, hits, w_neighbour, w_out, columns
    )
    new[...] = value
    send_features(value, hits, (s0, s1, s2, s3))


def last_layer(
    places, a0, a1, a2, a3, local, own, inverse_rowsum, lat, hits, w_neighbour, w_out, columns,
    guess, s0, s1, s2, s3,
):
    value = layer_step(
        LAYERS - 1, (a0, a1, a2, a3), local, own, inverse_rowsum, lat, hits, w_neighbour, w_out, columns
    )
    decode = columns[:, 3 * LAYERS : 3 * LAYERS + 1]
    row = jnp.sum(value.astype(F32) * decode, axis=0, keepdims=True)
    field = tile_rows_of(row)
    guess[...] = field
    store_sent((s0, s1, s2, s3), pick(field, slot_rows(places)))


def product(matrix, field):
    count = LANES
    width = matrix.shape[1]
    total = jnp.zeros((8, width), F32)
    for t in range(field.shape[0]):
        column = jnp.broadcast_to(field[t : t + 1, :], (count, count)).T
        wide = jnp.concatenate([column] * (width // count), axis=1)
        part = matrix[t * count : (t + 1) * count, :] * wide
        total = total + jnp.sum(part.reshape(count // 8, 8, width), axis=0)
    return tile_rows_of(jnp.sum(total, axis=0, keepdims=True))


def matvec(matrix, vector, out):
    out[...] = product(matrix, vector[...])


def start_basis(places, a0, a1, a2, a3, local, guess, source, diagonal, basis, s0, s1, s2, s3):
    rows = slot_rows(places)
    came = spread_sum(arrived_rows((a0, a1, a2, a3)), rows, guess.shape[0])
    value = (source[...] + local[...] + came) / diagonal[...] - guess[...]
    basis[...] = value
    store_sent((s0, s1, s2, s3), pick(value, rows))


def next_basis(places, a0, a1, a2, a3, local, diagonal, basis, s0, s1, s2, s3):
    rows = slot_rows(places)
    came = spread_sum(arrived_rows((a0, a1, a2, a3)), rows, local.shape[0])
    value = (local[...] + came) / diagonal[...]
    basis[...] = value
    store_sent((s0, s1, s2, s3), pick(value, rows))


def diagonal_mask():
    return lax.broadcasted_iota(jnp.int32, (8, LANES), 0) == lax.broadcasted_iota(jnp.int32, (8, LANES), 1)


def last_basis(places, a0, a1, a2, a3, local, diagonal, b0, b1, matrix, basis, image, packets):
    rows = slot_rows(places)
    came = spread_sum(arrived_rows((a0, a1, a2, a3)), rows, local.shape[0])
    value = (local[...] + came) / diagonal[...]
    basis[...] = value
    mapped = product(matrix, value)
    image[...] = mapped
    held = [b0[...], b1[...], value]
    parts = []
    for k in range(2 * ITERS - 1):
        left, right = held[k // 2], held[(k + 1) // 2]
        parts.append(jnp.sum(left * right * diagonal[...], axis=0, keepdims=True))
    parts.append(jnp.sum(value * mapped, axis=0, keepdims=True))
    parts.append(jnp.zeros((8 - 2 * ITERS, LANES), F32))
    sums = jnp.sum(jnp.concatenate(parts, axis=0), axis=1, keepdims=True)
    row = jnp.sum(jnp.where(diagonal_mask(), sums, 0.0), axis=0, keepdims=True)
    packet = jnp.concatenate([lane_rows(pick(value, rows)), row], axis=1)
    for device in range(packets.shape[0]):
        packets[device] = packet


def added(values):
    values = list(values)
    while len(values) > 1:
        values = [sum(values[i : i + 2][1:], values[i]) for i in range(0, len(values), 2)]
    return values[0]


def near_sums(group, far):
    subs = group.shape[0]
    width = group.shape[2] - LANES
    per = width // 4
    edges = []
    for s in range(subs - 1):
        g = MATCHINGS.index((1, s % 2))
        span = slice(g * per, (g + 1) * per)
        edges.append(group[s, :, span] * group[s + 1, :, span])
    sums = added([group[s, :, width : width + LANES] for s in range(subs)])
    packet = [
        group[s, :, g * per : (g + 1) * per]
        for g in (MATCHINGS.index((0, 0)), MATCHINGS.index((0, 1)))
        for s in range(subs)
    ]
    packet = jnp.concatenate(packet + [with_edges(sums, edges)], axis=1)
    for device in range(far.shape[0]):
        far[device] = packet


def with_edges(sums, edges):
    if not edges:
        return sums
    edges = added(edges)
    edges = added([edges[:, h : h + LANES] for h in range(0, edges.shape[1], LANES)])
    lane = lax.broadcasted_iota(jnp.int32, (1, LANES), 1)
    return sums + jnp.where(lane == 2 * ITERS - 1, 2.0 * jnp.sum(edges, axis=1, keepdims=True), 0.0)


def finish(where, group, far, places, image, guess, diagonal, b0, b1, b2, field, defect):
    subs, doms = group.shape[0], far.shape[0]
    per = (group.shape[2] - LANES) // 4
    wide = subs * per
    edges = []
    for d in range(doms - 1):
        span = slice(d % 2 * wide, (d % 2 + 1) * wide)
        edges.append(far[d, :, span] * far[d + 1, :, span])
    sums = with_edges(added([far[d, :, 2 * wide : 2 * wide + LANES] for d in range(doms)]), edges)
    columns = jnp.sum(
        jnp.where(diagonal_mask(), jnp.broadcast_to(sums, (8, LANES)), 0.0), axis=1, keepdims=True
    )
    n = [jnp.broadcast_to(columns[k : k + 1, :], (8, LANES)) for k in range(2 * ITERS)]
    came = []
    for g, (along, first) in enumerate(MATCHINGS):
        if along:
            mine = group[where[4 + g], :, g * per : (g + 1) * per]
        else:
            at = pl.multiple_of(where[8] * per, LANES) + first * wide
            mine = far[where[4 + g], :, pl.ds(pl.multiple_of(at, LANES), per)]
        came += [mine[:, h : h + LANES] for h in range(0, per, LANES)]
    last = (image[...] + spread_sum(came, slot_rows(places), image.shape[0])) / diagonal[...]
    one, zero = jnp.ones((8, LANES), F32), jnp.zeros((8, LANES), F32)

    def paired(left, values):
        total = zero
        for i, a in enumerate(left):
            for j, b in enumerate(left):
                total = total + a * b * values[i + j]
        return total

    gaps = [n[k] - n[k + 1] for k in range(2 * ITERS - 1)]
    residual = [one]
    heading = [one]
    moved = [zero] * ITERS
    size = n[0]
    for step in range(ITERS):
        alpha = size / paired(heading, gaps)
        for i, h in enumerate(heading):
            moved[i] = moved[i] + alpha * h
        change = [
            (heading[i] if i < len(heading) else zero) - (heading[i - 1] if i > 0 else zero)
            for i in range(len(heading) + 1)
        ]
        residual = [
            (residual[i] if i < len(residual) else zero) - alpha * change[i]
            for i in range(len(change))
        ]
        if step + 1 < ITERS:
            following = paired(residual, n)
            beta = following / size
            heading = [
                residual[i] + (beta * heading[i] if i < len(heading) else zero)
                for i in range(len(residual))
            ]
            size = following
    held = [b0[...], b1[...], b2[...], last]
    total = guess[...]
    for c, b in zip(moved, held):
        total = total + c * b
    field[...] = total
    left = zero
    for c, b in zip(residual, held):
        left = left + c * b
    defect[...] = left * diagonal[...]


def matching(sizes, along, first):
    pairs = []
    for dom in range(sizes[0]):
        for sub in range(sizes[1]):
            at = [dom, sub]
            to = [dom, sub]
            other = 1 - along
            mate = (at[along] - first ^ 1) + first
            if at[along] >= first and mate < sizes[along]:
                to[along] = mate
            elif at[other] ^ 1 < sizes[other]:
                to[other] = at[other] ^ 1
            pairs.append((at[0] * sizes[1] + at[1], to[0] * sizes[1] + to[1]))
    return pairs


def sides_of_matchings():
    odd = [lax.axis_index("dom") % 2, lax.axis_index("sub") % 2]
    return [2 * along + (odd[along] if first else 1 - odd[along]) for along, first in MATCHINGS]


def exchange(sent):
    axes = ("dom", "sub")
    sizes = [lax.axis_size(axis) for axis in axes]
    return [lax.ppermute(s, axes, matching(sizes, *m)) for s, m in zip(sent, MATCHINGS)]


def partners():
    out = []
    for along, first in MATCHINGS:
        axis = ("dom", "sub")[along]
        at = lax.axis_index(axis)
        mate = jnp.bitwise_xor(at - first, 1) + first
        out.append(jnp.where((at >= first) & (mate < lax.axis_size(axis)), mate, at))
    return out


def all_to_all(messages, axis):
    return lax.all_to_all(messages, axis, split_axis=0, concat_axis=0, tiled=True)


def per_device(
    state, tile_values, tile_rows, tile_columns, tile_counts, send_nodes, face_counts, capacity,
    source, w_self, w_neighbour, w_out, gains, bias, w_decode,
):
    nodes, width = state.shape
    slots = send_nodes.shape[2]
    tiles = nodes // LANES
    doms, subs = lax.axis_size("dom"), lax.axis_size("sub")
    field = shape((tiles, LANES))
    features = shape((width, nodes))
    feature_sent = [shape((width, slots), BF16)] * 4
    vector_sent = [shape((slots // LANES, LANES))] * 4
    decode = w_decode.reshape(1, width)
    where = jnp.stack(sides_of_matchings() + partners() + [lax.axis_index("sub")]).astype(jnp.int32)
    capacity = capacity.reshape(tiles, LANES)
    source = source.reshape(tiles, LANES)

    lat, hits, places, columns, *sent = run(
        gather_first,
        [shape((width, nodes), BF16), shape((nodes, 4 * slots), BF16), shape((4 * slots // LANES, LANES), jnp.int32),
         shape((width, 8))]
        + feature_sent,
        (), (where,), (send_nodes, face_counts, state, gains, bias, decode),
        (
            pltpu.VMEM(send_nodes.shape, jnp.int32),
            pltpu.SMEM(face_counts.shape, jnp.int32),
            pltpu.VMEM(state.shape, BF16),
            pltpu.VMEM(gains.shape, F32),
            pltpu.VMEM(bias.shape, F32),
            pltpu.VMEM(decode.shape, F32),
        ),
        flops=2 * nodes * 4 * slots * width,
    )
    arrived = exchange(sent)
    matrix, half, inverse_rowsum, diagonal, local, own = run(
        build,
        [shape((nodes, nodes)), shape((nodes, nodes), BF16), shape((1, nodes)), field, features, features],
        (places, tile_values, lat, w_self, columns),
        (tile_counts,), (tile_rows, tile_columns, capacity),
        (
            pltpu.SMEM(tile_rows.shape, jnp.int32),
            pltpu.SMEM(tile_columns.shape, jnp.int32),
            pltpu.VMEM(capacity.shape, F32),
        ),
        flops=2 * nodes * nodes * width, moved=6_000_000,
    )
    lat, *sent = run(
        first_layer, [shape((width, nodes), BF16)] + feature_sent,
        (*arrived, local, own, inverse_rowsum, lat, hits, w_neighbour, w_out, columns), flops=6 * nodes * nodes * width,
    )
    arrived = exchange(sent)
    local, own = run(
        functools.partial(local_features, LAYERS - 1), [features, features],
        (lat, half, w_self, columns), flops=2 * nodes * nodes * width, moved=4_000_000,
    )
    guess, *sent = run(
        last_layer, [field] + vector_sent,
        (places, *arrived, local, own, inverse_rowsum, lat, hits, w_neighbour, w_out, columns),
        flops=6 * nodes * nodes * width,
    )

    def mapped(vector):
        return run(matvec, [field], (matrix, vector), flops=2 * nodes * nodes, moved=4 * nodes * nodes)[0]

    arrived = exchange(sent)
    local = mapped(guess)
    b0, *sent = run(
        start_basis, [field] + vector_sent, (places, *arrived, local, guess, source, diagonal)
    )
    arrived = exchange(sent)
    local = mapped(b0)
    b1, *sent = run(next_basis, [field] + vector_sent, (places, *arrived, local, diagonal))
    arrived = exchange(sent)
    local = mapped(b1)
    b2, image, packets = run(
        last_basis, [field, field, shape((subs, 1, 4 * slots + LANES))],
        (places, *arrived, local, diagonal, b0, b1, matrix),
    )
    group = all_to_all(packets, "sub")
    (far,) = run(near_sums, [shape((doms, 1, 2 * subs * slots + LANES))], (group,))
    far = all_to_all(far, "dom")
    heat, defect = run(
        finish, [field, field],
        (group, far, places, image, guess, diagonal, b0, b1, b2), (where,),
    )
    return heat.reshape(nodes), defect.reshape(nodes)


def solution(mesh):
    both = ("dom", "sub")
    return jax.shard_map(
        per_device,
        mesh=mesh,
        in_specs=(
            P(both, None),
            P(both, None, None, None),
            P(both, None),
            P(both, None),
            P(both),
            P(both, None, None),
            P(both, None),
            P(both),
            P(both),
            P(),
            P(),
            P(),
            P(),
            P(),
            P(),
        ),
        out_specs=(P(both), P(both)),
        check_vma=False,
    )
```

```python
import functools

import jax
import jax.numpy as jnp
from jax import lax
from jax.experimental import pallas as pl
from jax.experimental.pallas import tpu as pltpu
from jax.sharding import PartitionSpec as P

LAYERS = 2
ITERS = 3
LANES = 128
MATCHINGS = ((1, 1), (1, 0), (0, 1), (0, 0))
VMEM_LIMIT = 24 * 1024 * 1024

F32 = jnp.float32
BF16 = jnp.bfloat16


def shape(dims, dtype=F32):
    return jax.ShapeDtypeStruct(dims, dtype)


def run(body, outs, operands, scalars=(), raw=(), scratch=(), flops=1_000_000, moved=1_000_000):
    smem = pl.BlockSpec(memory_space=pltpu.SMEM)
    vmem = pl.BlockSpec(memory_space=pltpu.VMEM)
    anywhere = pl.BlockSpec(memory_space=pltpu.HBM)
    scratch = list(scratch) + [pltpu.SemaphoreType.DMA((len(raw),))] * bool(raw)
    return pl.pallas_call(
        body,
        out_shape=outs,
        in_specs=[smem] * len(scalars) + [vmem] * len(operands) + [anywhere] * len(raw),
        out_specs=[vmem] * len(outs),
        scratch_shapes=scratch,
        compiler_params=pltpu.CompilerParams(vmem_limit_bytes=VMEM_LIMIT),
        cost_estimate=pl.CostEstimate(flops=flops, bytes_accessed=moved, transcendentals=0),
    )(*scalars, *operands, *(pltpu.with_memory_space_constraint(r, pltpu.HBM) for r in raw))


def copies(pairs, semaphores):
    started = [pltpu.make_async_copy(*pair, semaphores.at[i]) for i, pair in enumerate(pairs)]
    for copy in started:
        copy.start()
    return started


def slot_rows(places):
    return [places[r : r + 1, :] for r in range(places.shape[0])]


def pick(vector, rows):
    index = jnp.concatenate(rows, axis=0)
    low = jnp.bitwise_and(index, LANES - 1)
    high = jnp.right_shift(index, 7)
    out = jnp.zeros(index.shape, F32)
    for t in range(vector.shape[0]):
        spread = jnp.broadcast_to(vector[t : t + 1, :], index.shape)
        got = jnp.take_along_axis(spread, low, axis=1, mode="promise_in_bounds")
        out = jnp.where(high == t, got, out)
    return out


def pieces(value):
    first = value.astype(BF16)
    rest = value - first.astype(F32)
    second = rest.astype(BF16)
    third = (rest - second.astype(F32)).astype(BF16)
    return first, second, third


def low_hits(rows):
    lane = lax.broadcasted_iota(jnp.int32, (LANES, LANES), 0)
    return jnp.concatenate(
        [(lane == jnp.bitwise_and(row, LANES - 1)).astype(F32).astype(BF16) for row in rows], axis=1
    )


def spread_sum(values, rows, tiles):
    tile = lax.broadcasted_iota(jnp.int32, (tiles, LANES), 0)
    parts = [
        jnp.where(tile == jnp.right_shift(row, 7), value, 0.0) for value, row in zip(values, rows)
    ]
    held = jnp.concatenate(parts, axis=1)
    stacked = jnp.concatenate([p.astype(F32) for p in pieces(held)], axis=0).astype(BF16)
    out = lax.dot_general(
        stacked, low_hits(rows), (((1,), (1,)), ((), ())), preferred_element_type=F32
    )
    return out[:tiles] + out[tiles : 2 * tiles] + out[2 * tiles :]


def arrived_rows(refs):
    return [ref[h : h + 1, :] for ref in refs for h in range(ref.shape[0])]


def store_sent(refs, sent):
    per = refs[0].shape[0]
    for k, ref in enumerate(refs):
        ref[...] = sent[k * per : (k + 1) * per, :]


def lane_rows(vector):
    return jnp.concatenate([vector[t : t + 1, :] for t in range(vector.shape[0])], axis=1)


def tile_rows_of(row):
    return jnp.concatenate(
        [row[:, t * LANES : (t + 1) * LANES] for t in range(row.shape[1] // LANES)], axis=0
    )


def fill_hits(hits, rows, first, last):
    node = lax.broadcasted_iota(jnp.int32, (hits.shape[0], LANES), 0).astype(jnp.int16)
    one, zero = jnp.ones(node.shape, BF16), jnp.zeros(node.shape, BF16)
    for c in range(first, last):
        wide = jnp.broadcast_to(rows[c], node.shape).astype(jnp.int16)
        at = (c - first) * LANES
        hits[:, at : at + LANES] = jnp.where(node == wide, one, zero)


def gather_first(
    where, index_in, counts_in, state_in, lat, hits, places, sent, index, counts, state, sems
):
    first, second, third = copies(((index_in, index), (counts_in, counts), (state_in, state)), sems)
    per = index.shape[2] // LANES
    first.wait()
    second.wait()
    for g in range(index.shape[1]):
        side = where[g]
        for h in range(per):
            low, high = 2 * MATCHINGS[g][0], 2 * MATCHINGS[g][0] + 1
            span = slice(h * LANES, (h + 1) * LANES)
            row = jnp.where(side == low, index[0, low : low + 1, span], index[0, high : high + 1, span])
            slot = lax.broadcasted_iota(jnp.int32, (1, LANES), 1) + h * LANES
            r = g * per + h
            places[r : r + 1, :] = jnp.where(slot < counts[0, side], row, -1)
    fill_hits(hits, slot_rows(places), 0, per)
    third.wait()
    lat[...] = state[...].T
    send_features(lat[...], hits, (sent,))


def gather_rest(places, lat, gains_in, bias_in, decode_in, hits, columns, s1, s2, s3, gains, bias, decode, sems):
    waits = copies(((gains_in, gains), (bias_in, bias), (decode_in, decode)), sems)
    rows = slot_rows(places)
    fill_hits(hits, rows, len(rows) // 4, len(rows))
    send_features(lat[...], hits, (s1, s2, s3))
    for copy in waits:
        copy.wait()
    lines = [gains[layer] for layer in range(LAYERS)] + [bias[...], decode[...]]
    lines.append(jnp.zeros((8 - 3 * LAYERS - 1, bias.shape[1]), F32))
    columns[...] = jnp.concatenate(lines, axis=0).T


def send_features(lat, hits, outs):
    width = outs[0].shape[1]
    for k, out in enumerate(outs):
        out[...] = jnp.dot(
            lat, hits[:, k * width : (k + 1) * width], preferred_element_type=F32
        ).astype(BF16)


def send_rest(lat, hits, s1, s2, s3):
    send_features(lat[...], hits, (s1, s2, s3))


def build(
    tile_counts, places, tiles, lat, w_self, columns, rows_in, columns_in, capacity_in,
    matrix, half, inverse_rowsum, diagonal, local, own,
    tile_rows, tile_columns, capacity, sems,
):
    waits = copies(((rows_in, tile_rows), (columns_in, tile_columns), (capacity_in, capacity)), sems)
    count = tiles.shape[2]
    node_tiles = matrix.shape[0] // count
    matrix[...] = jnp.zeros(matrix.shape, F32)
    for t in range(node_tiles):
        span = slice(t * count, (t + 1) * count)
        block = tiles[0, t]
        matrix[span, span] = block + block.T
    for copy in waits:
        copy.wait()

    def add(t, carry):
        r = pl.multiple_of(tile_rows[0, t] * count, count)
        c = pl.multiple_of(tile_columns[0, t] * count, count)
        block = tiles[0, t]
        matrix[pl.ds(r, count), pl.ds(c, count)] += block
        matrix[pl.ds(c, count), pl.ds(r, count)] += block.T
        return carry

    lax.fori_loop(node_tiles, tile_counts[0], add, 0)
    rows = slot_rows(places)
    faces = spread_sum([jnp.ones((1, LANES), F32)] * len(rows), rows, node_tiles)
    total = jnp.zeros((8, matrix.shape[1]), F32)
    for t in range(node_tiles):
        block = matrix[t * count : (t + 1) * count, :]
        half[t * count : (t + 1) * count, :] = block.astype(BF16)
        total = total + jnp.sum(block.reshape(count // 8, 8, matrix.shape[1]), axis=0)
    rowsum = tile_rows_of(jnp.sum(total, axis=0, keepdims=True)) + faces
    inverse_rowsum[...] = lane_rows(1.0 / rowsum)
    diagonal[...] = capacity[...] + rowsum
    local[...] = jnp.dot(lat[...], half[...], preferred_element_type=F32)
    own[...] = own_part(0, lat[...], w_self, columns)


def normed(value, gain):
    scale = lax.rsqrt(jnp.mean(value * value, axis=0, keepdims=True) + 1e-06)
    return (value * scale * gain).astype(BF16)


def project(weight, value):
    return lax.dot_general(weight, value, (((0,), (0,)), ((), ())), preferred_element_type=F32)


def own_part(layer, lat, w_self, columns):
    gain = columns[:, 2 * layer : 2 * layer + 1]
    bias = columns[:, 2 * LAYERS + layer : 2 * LAYERS + layer + 1]
    return project(w_self[layer], normed(lat.astype(F32), gain)) + bias


def local_features(layer, lat, half, w_self, columns, local, own):
    local[...] = jnp.dot(lat[...], half[...], preferred_element_type=F32)
    own[...] = own_part(layer, lat[...], w_self, columns)


def with_slots(local, came, hits):
    return local + lax.dot_general(came, hits, (((1,), (1,)), ((), ())), preferred_element_type=F32)


def layer_step(layer, arrived, local, own, inverse_rowsum, lat, first_hits, hits, w_neighbour, w_out, columns):
    total = with_slots(local[...], arrived[0][...], first_hits[...])
    total = with_slots(total, jnp.concatenate([a[...] for a in arrived[1:]], axis=1), hits[...])
    mean = total * inverse_rowsum[...]
    gain = columns[:, 2 * layer + 1 : 2 * layer + 2]
    linear = own[...] + project(w_neighbour[layer], normed(mean, gain))
    activated = (linear / (1.0 + jnp.exp(-linear))).astype(BF16)
    return (lat[...].astype(F32) + project(w_out[layer], activated)).astype(BF16)


def first_layer(
    a0, a1, a2, a3, local, own, inverse_rowsum, lat, first_hits, hits, w_neighbour, w_out, columns, new, sent
):
    value = layer_step(
        0, (a0, a1, a2, a3), local, own, inverse_rowsum, lat, first_hits, hits, w_neighbour, w_out, columns
    )
    new[...] = value
    send_features(value, first_hits, (sent,))


def last_layer(
    places, a0, a1, a2, a3, local, own, inverse_rowsum, lat, first_hits, hits, w_neighbour, w_out, columns,
    guess, s0, s1, s2, s3,
):
    value = layer_step(
        LAYERS - 1, (a0, a1, a2, a3), local, own, inverse_rowsum, lat, first_hits, hits, w_neighbour, w_out, columns
    )
    decode = columns[:, 3 * LAYERS : 3 * LAYERS + 1]
    row = jnp.sum(value.astype(F32) * decode, axis=0, keepdims=True)
    field = tile_rows_of(row)
    guess[...] = field
    store_sent((s0, s1, s2, s3), pick(field, slot_rows(places)))


def product(matrix, field):
    count = LANES
    width = matrix.shape[1]
    total = jnp.zeros((8, width), F32)
    for t in range(field.shape[0]):
        column = jnp.broadcast_to(field[t : t + 1, :], (count, count)).T
        wide = jnp.concatenate([column] * (width // count), axis=1)
        part = matrix[t * count : (t + 1) * count, :] * wide
        total = total + jnp.sum(part.reshape(count // 8, 8, width), axis=0)
    return tile_rows_of(jnp.sum(total, axis=0, keepdims=True))


def matvec(matrix, vector, out):
    out[...] = product(matrix, vector[...])


def start_basis(places, a0, a1, a2, a3, local, guess, source, diagonal, basis, s0, s1, s2, s3):
    rows = slot_rows(places)
    came = spread_sum(arrived_rows((a0, a1, a2, a3)), rows, guess.shape[0])
    value = (source[...] + local[...] + came) / diagonal[...] - guess[...]
    basis[...] = value
    store_sent((s0, s1, s2, s3), pick(value, rows))


def next_basis(places, a0, a1, a2, a3, local, diagonal, basis, s0, s1, s2, s3):
    rows = slot_rows(places)
    came = spread_sum(arrived_rows((a0, a1, a2, a3)), rows, local.shape[0])
    value = (local[...] + came) / diagonal[...]
    basis[...] = value
    store_sent((s0, s1, s2, s3), pick(value, rows))


def diagonal_mask():
    return lax.broadcasted_iota(jnp.int32, (8, LANES), 0) == lax.broadcasted_iota(jnp.int32, (8, LANES), 1)


def last_basis(places, a0, a1, a2, a3, local, diagonal, b0, b1, matrix, basis, image, packets):
    rows = slot_rows(places)
    came = spread_sum(arrived_rows((a0, a1, a2, a3)), rows, local.shape[0])
    value = (local[...] + came) / diagonal[...]
    basis[...] = value
    mapped = product(matrix, value)
    image[...] = mapped
    held = [b0[...], b1[...], value]
    parts = []
    for k in range(2 * ITERS - 1):
        left, right = held[k // 2], held[(k + 1) // 2]
        parts.append(jnp.sum(left * right * diagonal[...], axis=0, keepdims=True))
    parts.append(jnp.sum(value * mapped, axis=0, keepdims=True))
    parts.append(jnp.zeros((8 - 2 * ITERS, LANES), F32))
    sums = jnp.sum(jnp.concatenate(parts, axis=0), axis=1, keepdims=True)
    row = jnp.sum(jnp.where(diagonal_mask(), sums, 0.0), axis=0, keepdims=True)
    packet = jnp.concatenate([lane_rows(pick(value, rows)), row], axis=1)
    for device in range(packets.shape[0]):
        packets[device] = packet


def added(values):
    values = list(values)
    while len(values) > 1:
        values = [sum(values[i : i + 2][1:], values[i]) for i in range(0, len(values), 2)]
    return values[0]


def finish(sizes, where, packets, places, image, guess, diagonal, b0, b1, b2, field, defect):
    doms, subs = sizes
    width = packets.shape[2] - LANES
    per = width // 4

    def slots(device, g):
        return packets[device, :, g * per : (g + 1) * per]

    edges = []
    for d in range(doms):
        for s in range(subs):
            for m, (i, j) in (((0, d % 2), (d + 1, s)), ((1, s % 2), (d, s + 1))):
                g = MATCHINGS.index(m)
                if i < doms and j < subs:
                    edges.append(slots(d * subs + s, g) * slots(i * subs + j, g))
    edges = added(edges)
    edges = added([edges[:, h : h + LANES] for h in range(0, per, LANES)])
    sums = added([packets[e, :, width : width + LANES] for e in range(doms * subs)])
    lane = lax.broadcasted_iota(jnp.int32, (1, LANES), 1)
    sums = sums + jnp.where(lane == 2 * ITERS - 1, 2.0 * jnp.sum(edges, axis=1, keepdims=True), 0.0)
    columns = jnp.sum(
        jnp.where(diagonal_mask(), jnp.broadcast_to(sums, (8, LANES)), 0.0), axis=1, keepdims=True
    )
    n = [jnp.broadcast_to(columns[k : k + 1, :], (8, LANES)) for k in range(2 * ITERS)]
    came = []
    for g in range(4):
        mine = slots(where[4 + g], g)
        came += [mine[:, h : h + LANES] for h in range(0, per, LANES)]
    last = (image[...] + spread_sum(came, slot_rows(places), image.shape[0])) / diagonal[...]
    one, zero = jnp.ones((8, LANES), F32), jnp.zeros((8, LANES), F32)

    def paired(left, values):
        total = zero
        for i, a in enumerate(left):
            for j, b in enumerate(left):
                total = total + a * b * values[i + j]
        return total

    gaps = [n[k] - n[k + 1] for k in range(2 * ITERS - 1)]
    residual = [one]
    heading = [one]
    moved = [zero] * ITERS
    size = n[0]
    for step in range(ITERS):
        alpha = size / paired(heading, gaps)
        for i, h in enumerate(heading):
            moved[i] = moved[i] + alpha * h
        change = [
            (heading[i] if i < len(heading) else zero) - (heading[i - 1] if i > 0 else zero)
            for i in range(len(heading) + 1)
        ]
        residual = [
            (residual[i] if i < len(residual) else zero) - alpha * change[i]
            for i in range(len(change))
        ]
        if step + 1 < ITERS:
            following = paired(residual, n)
            beta = following / size
            heading = [
                residual[i] + (beta * heading[i] if i < len(heading) else zero)
                for i in range(len(residual))
            ]
            size = following
    held = [b0[...], b1[...], b2[...], last]
    total = guess[...]
    for c, b in zip(moved, held):
        total = total + c * b
    field[...] = total
    left = zero
    for c, b in zip(residual, held):
        left = left + c * b
    defect[...] = left * diagonal[...]


def matching(sizes, along, first):
    pairs = []
    for dom in range(sizes[0]):
        for sub in range(sizes[1]):
            at = [dom, sub]
            to = [dom, sub]
            other = 1 - along
            mate = (at[along] - first ^ 1) + first
            if at[along] >= first and mate < sizes[along]:
                to[along] = mate
            elif at[other] ^ 1 < sizes[other]:
                to[other] = at[other] ^ 1
            pairs.append((at[0] * sizes[1] + at[1], to[0] * sizes[1] + to[1]))
    return pairs


def sides_of_matchings():
    odd = [lax.axis_index("dom") % 2, lax.axis_index("sub") % 2]
    return [2 * along + (odd[along] if first else 1 - odd[along]) for along, first in MATCHINGS]


def swap(sent, matching_at):
    axes = ("dom", "sub")
    sizes = [lax.axis_size(axis) for axis in axes]
    return lax.ppermute(sent, axes, matching(sizes, *MATCHINGS[matching_at]))


def exchange(sent, first=0):
    return [swap(s, first + i) for i, s in enumerate(sent)]


def partners():
    at = [lax.axis_index("dom"), lax.axis_index("sub")]
    sizes = [lax.axis_size("dom"), lax.axis_size("sub")]
    out = []
    for along, first in MATCHINGS:
        mate = jnp.bitwise_xor(at[along] - first, 1) + first
        known = (at[along] >= first) & (mate < sizes[along])
        to = list(at)
        to[along] = jnp.where(known, mate, at[along])
        out.append(to[0] * sizes[1] + to[1])
    return out


def all_to_all(messages):
    return lax.all_to_all(messages, ("dom", "sub"), split_axis=0, concat_axis=0, tiled=True)


def per_device(
    state, tile_values, tile_rows, tile_columns, tile_counts, send_nodes, face_counts, capacity,
    source, w_self, w_neighbour, w_out, gains, bias, w_decode,
):
    nodes, width = state.shape
    slots = send_nodes.shape[2]
    tiles = nodes // LANES
    sizes = (lax.axis_size("dom"), lax.axis_size("sub"))
    devices = sizes[0] * sizes[1]
    field = shape((tiles, LANES))
    features = shape((width, nodes))
    vector_sent = [shape((slots // LANES, LANES))] * 4
    decode = w_decode.reshape(1, width)
    where = jnp.stack(sides_of_matchings() + partners()).astype(jnp.int32)
    capacity = capacity.reshape(tiles, LANES)
    source = source.reshape(tiles, LANES)

    one_sent = [shape((width, slots), BF16)]
    gather_flops = 2 * nodes * slots * width
    lat, first_hits, places, sent = run(
        gather_first,
        [shape((width, nodes), BF16), shape((nodes, slots), BF16), shape((4 * slots // LANES, LANES), jnp.int32)]
        + one_sent,
        (), (where,), (send_nodes, face_counts, state),
        (
            pltpu.VMEM(send_nodes.shape, jnp.int32),
            pltpu.SMEM(face_counts.shape, jnp.int32),
            pltpu.VMEM(state.shape, BF16),
        ),
        flops=gather_flops,
    )
    a0 = swap(sent, 0)
    hits, columns, *sent = run(
        gather_rest, [shape((nodes, 3 * slots), BF16), shape((width, 8))] + one_sent * 3,
        (places, lat), (), (gains, bias, decode),
        (pltpu.VMEM(gains.shape, F32), pltpu.VMEM(bias.shape, F32), pltpu.VMEM(decode.shape, F32)),
        flops=3 * gather_flops,
    )
    a1, a2, a3 = exchange(sent, 1)
    matrix, half, inverse_rowsum, diagonal, local, own = run(
        build,
        [shape((nodes, nodes)), shape((nodes, nodes), BF16), shape((1, nodes)), field, features, features],
        (places, tile_values, lat, w_self, columns),
        (tile_counts,), (tile_rows, tile_columns, capacity),
        (
            pltpu.SMEM(tile_rows.shape, jnp.int32),
            pltpu.SMEM(tile_columns.shape, jnp.int32),
            pltpu.VMEM(capacity.shape, F32),
        ),
        flops=0, moved=0,
    )
    lat, sent = run(
        first_layer, [shape((width, nodes), BF16)] + one_sent,
        (a0, a1, a2, a3, local, own, inverse_rowsum, lat, first_hits, hits, w_neighbour, w_out, columns),
        flops=3 * nodes * nodes * width,
    )
    a0 = swap(sent, 0)
    sent = run(send_rest, one_sent * 3, (lat, hits), flops=3 * gather_flops)
    a1, a2, a3 = exchange(sent, 1)
    local, own = run(
        functools.partial(local_features, LAYERS - 1), [features, features],
        (lat, half, w_self, columns), flops=0, moved=0,
    )
    guess, *sent = run(
        last_layer, [field] + vector_sent,
        (places, a0, a1, a2, a3, local, own, inverse_rowsum, lat, first_hits, hits, w_neighbour, w_out, columns),
        flops=3 * nodes * nodes * width,
    )

    def mapped(vector):
        return run(matvec, [field], (matrix, vector), flops=2 * nodes * nodes, moved=4 * nodes * nodes)[0]

    arrived = exchange(sent)
    local = mapped(guess)
    b0, *sent = run(
        start_basis, [field] + vector_sent, (places, *arrived, local, guess, source, diagonal)
    )
    arrived = exchange(sent)
    local = mapped(b0)
    b1, *sent = run(next_basis, [field] + vector_sent, (places, *arrived, local, diagonal))
    arrived = exchange(sent)
    local = mapped(b1)
    b2, image, packets = run(
        last_basis, [field, field, shape((devices, 1, 4 * slots + LANES))],
        (places, *arrived, local, diagonal, b0, b1, matrix),
    )
    packets = all_to_all(packets)
    heat, defect = run(
        functools.partial(finish, sizes), [field, field],
        (packets, places, image, guess, diagonal, b0, b1, b2), (where,),
    )
    return heat.reshape(nodes), defect.reshape(nodes)


def solution(mesh):
    both = ("dom", "sub")
    return jax.shard_map(
        per_device,
        mesh=mesh,
        in_specs=(
            P(both, None),
            P(both, None, None, None),
            P(both, None),
            P(both, None),
            P(both),
            P(both, None, None),
            P(both, None),
            P(both),
            P(both),
            P(),
            P(),
            P(),
            P(),
            P(),
            P(),
        ),
        out_specs=(P(both), P(both)),
        check_vma=False,
    )
```

```python
import functools

import jax
import jax.numpy as jnp
from jax import lax
from jax.experimental import pallas as pl
from jax.experimental.pallas import tpu as pltpu
from jax.sharding import PartitionSpec as P

LAYERS = 2
ITERS = 3
LANES = 128
INNER = ((1, 1), (1, 0), (0, 1), (0, 0))
OUTER = ((0, 1), (1, 0), (0, 0), (1, 1))
VMEM_LIMIT = 24 * 1024 * 1024

F32 = jnp.float32
BF16 = jnp.bfloat16


def shape(dims, dtype=F32):
    return jax.ShapeDtypeStruct(dims, dtype)


def run(body, outs, operands, scalars=(), raw=(), scratch=(), waits=0, flops=1_000_000, moved=1_000_000):
    smem = pl.BlockSpec(memory_space=pltpu.SMEM)
    vmem = pl.BlockSpec(memory_space=pltpu.VMEM)
    anywhere = pl.BlockSpec(memory_space=pltpu.HBM)
    scratch = list(scratch) + [pltpu.SemaphoreType.DMA((waits,))] * bool(waits)
    return pl.pallas_call(
        body,
        out_shape=outs,
        in_specs=[smem] * len(scalars) + [vmem] * len(operands) + [anywhere] * len(raw),
        out_specs=[vmem] * len(outs),
        scratch_shapes=scratch,
        compiler_params=pltpu.CompilerParams(vmem_limit_bytes=VMEM_LIMIT),
        cost_estimate=pl.CostEstimate(flops=flops, bytes_accessed=moved, transcendentals=0),
    )(*scalars, *operands, *(pltpu.with_memory_space_constraint(r, pltpu.HBM) for r in raw))


def copies(pairs, semaphores):
    started = [pltpu.make_async_copy(*pair, semaphores.at[i]) for i, pair in enumerate(pairs)]
    for copy in started:
        copy.start()
    return started


def slot_rows(places):
    return [places[r : r + 1, :] for r in range(places.shape[0])]


def pick(vector, rows):
    index = jnp.concatenate(rows, axis=0)
    low = jnp.bitwise_and(index, LANES - 1)
    high = jnp.right_shift(index, 7)
    out = jnp.zeros(index.shape, F32)
    for t in range(vector.shape[0]):
        spread = jnp.broadcast_to(vector[t : t + 1, :], index.shape)
        got = jnp.take_along_axis(spread, low, axis=1, mode="promise_in_bounds")
        out = jnp.where(high == t, got, out)
    return out


def pieces(value):
    first = value.astype(BF16)
    rest = value - first.astype(F32)
    second = rest.astype(BF16)
    third = (rest - second.astype(F32)).astype(BF16)
    return first, second, third


def low_hits(rows):
    lane = lax.broadcasted_iota(jnp.int32, (LANES, LANES), 0)
    return jnp.concatenate(
        [(lane == jnp.bitwise_and(row, LANES - 1)).astype(F32).astype(BF16) for row in rows], axis=1
    )


def spread_sum(values, rows, tiles):
    tile = lax.broadcasted_iota(jnp.int32, (tiles, LANES), 0)
    parts = [
        jnp.where(tile == jnp.right_shift(row, 7), value, 0.0) for value, row in zip(values, rows)
    ]
    held = jnp.concatenate(parts, axis=1)
    stacked = jnp.concatenate([p.astype(F32) for p in pieces(held)], axis=0).astype(BF16)
    out = lax.dot_general(
        stacked, low_hits(rows), (((1,), (1,)), ((), ())), preferred_element_type=F32
    )
    return out[:tiles] + out[tiles : 2 * tiles] + out[2 * tiles :]


def arrived_rows(refs):
    return [ref[h : h + 1, :] for ref in refs for h in range(ref.shape[0])]


def store_sent(refs, sent):
    per = refs[0].shape[0]
    for k, ref in enumerate(refs):
        ref[...] = sent[k * per : (k + 1) * per, :]


def lane_rows(vector):
    return jnp.concatenate([vector[t : t + 1, :] for t in range(vector.shape[0])], axis=1)


def tile_rows_of(row):
    return jnp.concatenate(
        [row[:, t * LANES : (t + 1) * LANES] for t in range(row.shape[1] // LANES)], axis=0
    )


def fill_hits(hits, rows, first, last):
    node = lax.broadcasted_iota(jnp.int32, (hits.shape[0], LANES), 0).astype(jnp.int16)
    one, zero = jnp.ones(node.shape, BF16), jnp.zeros(node.shape, BF16)
    for c in range(first, last):
        wide = jnp.broadcast_to(rows[c], node.shape).astype(jnp.int16)
        at = (c - first) * LANES
        hits[:, at : at + LANES] = jnp.where(node == wide, one, zero)


def gather_first(
    where, index_in, counts_in, state_in, lat, hits, places, sent, index, counts, state, sems
):
    parts = 4
    part = state.shape[0] // parts
    spans = [slice(p * part, (p + 1) * part) for p in range(parts)]
    first, second, *others = copies(
        [(index_in, index), (counts_in, counts)]
        + [(state_in.at[span, :], state.at[span, :]) for span in spans],
        sems,
    )
    per = index.shape[2] // LANES
    first.wait()
    second.wait()
    for g in range(index.shape[1]):
        side = where[g]
        for h in range(per):
            span = slice(h * LANES, (h + 1) * LANES)
            row = index[0, 0:1, span]
            for k in range(1, index.shape[1]):
                row = jnp.where(side == k, index[0, k : k + 1, span], row)
            slot = lax.broadcasted_iota(jnp.int32, (1, LANES), 1) + h * LANES
            r = g * per + h
            places[r : r + 1, :] = jnp.where(slot < counts[0, side], row, -1)
    fill_hits(hits, slot_rows(places), 0, per)
    for copy, span in zip(others, spans):
        copy.wait()
        lat[:, span] = state[span, :].T
    send_features(lat[...], hits, (sent,))


def gather_rest(places, lat, gains_in, bias_in, decode_in, hits, columns, s1, s2, s3, gains, bias, decode, sems):
    waits = copies(((gains_in, gains), (bias_in, bias), (decode_in, decode)), sems)
    rows = slot_rows(places)
    fill_hits(hits, rows, len(rows) // 4, len(rows))
    send_features(lat[...], hits, (s1, s2, s3))
    for copy in waits:
        copy.wait()
    lines = [gains[layer] for layer in range(LAYERS)] + [bias[...], decode[...]]
    lines.append(jnp.zeros((8 - 3 * LAYERS - 1, bias.shape[1]), F32))
    columns[...] = jnp.concatenate(lines, axis=0).T


def send_features(lat, hits, outs):
    width = outs[0].shape[1]
    for k, out in enumerate(outs):
        out[...] = jnp.dot(
            lat, hits[:, k * width : (k + 1) * width], preferred_element_type=F32
        ).astype(BF16)


def send_rest(lat, hits, s1, s2, s3):
    send_features(lat[...], hits, (s1, s2, s3))


def build(
    places, tiles, lat, w_self, columns, counts_in, rows_in, columns_in, capacity_in,
    matrix, half, inverse_rowsum, diagonal, local, own,
    tile_rows, tile_columns, tile_counts, capacity, sems,
):
    waits = copies(
        ((rows_in, tile_rows), (columns_in, tile_columns), (counts_in, tile_counts), (capacity_in, capacity)), sems
    )
    count = tiles.shape[2]
    node_tiles = matrix.shape[0] // count
    matrix[...] = jnp.zeros(matrix.shape, F32)
    for t in range(node_tiles):
        span = slice(t * count, (t + 1) * count)
        block = tiles[0, t]
        matrix[span, span] = block + block.T
    for copy in waits:
        copy.wait()

    def add(t, carry):
        r = pl.multiple_of(tile_rows[0, t] * count, count)
        c = pl.multiple_of(tile_columns[0, t] * count, count)
        block = tiles[0, t]
        matrix[pl.ds(r, count), pl.ds(c, count)] += block
        matrix[pl.ds(c, count), pl.ds(r, count)] += block.T
        return carry

    lax.fori_loop(node_tiles, tile_counts[0, 0], add, 0)
    rows = slot_rows(places)
    faces = spread_sum([jnp.ones((1, LANES), F32)] * len(rows), rows, node_tiles)
    total = jnp.zeros((8, matrix.shape[1]), F32)
    for t in range(node_tiles):
        block = matrix[t * count : (t + 1) * count, :]
        half[t * count : (t + 1) * count, :] = block.astype(BF16)
        total = total + jnp.sum(block.reshape(count // 8, 8, matrix.shape[1]), axis=0)
    rowsum = tile_rows_of(jnp.sum(total, axis=0, keepdims=True)) + faces
    inverse_rowsum[...] = lane_rows(1.0 / rowsum)
    diagonal[...] = capacity[...] + rowsum
    local[...] = jnp.dot(lat[...], half[...], preferred_element_type=F32)
    own[...] = own_part(0, lat[...], w_self, columns)


def normed(value, gain):
    scale = lax.rsqrt(jnp.mean(value * value, axis=0, keepdims=True) + 1e-06)
    return (value * scale * gain).astype(BF16)


def project(weight, value):
    return lax.dot_general(weight, value, (((0,), (0,)), ((), ())), preferred_element_type=F32)


def own_part(layer, lat, w_self, columns):
    gain = columns[:, 2 * layer : 2 * layer + 1]
    bias = columns[:, 2 * LAYERS + layer : 2 * LAYERS + layer + 1]
    return project(w_self[layer], normed(lat.astype(F32), gain)) + bias


def local_features(layer, lat, half, w_self, w_out, columns, local, own, before, decoder):
    local[...] = jnp.dot(lat[...], half[...], preferred_element_type=F32)
    own[...] = own_part(layer, lat[...], w_self, columns)
    decode = columns[:, 3 * LAYERS : 3 * LAYERS + 1]
    before[...] = jnp.sum(lat[...].astype(F32) * decode, axis=0, keepdims=True)
    line = jnp.broadcast_to(decode, (decode.shape[0], LANES)).T[0:1, :]
    decoder[...] = jnp.sum(w_out[layer].astype(F32) * line, axis=1, keepdims=True)


def with_slots(local, came, hits):
    return local + lax.dot_general(came, hits, (((1,), (1,)), ((), ())), preferred_element_type=F32)


def activation(layer, arrived, local, own, inverse_rowsum, first_hits, hits, w_neighbour, columns):
    total = with_slots(local[...], arrived[0][...], first_hits[...])
    total = with_slots(total, jnp.concatenate([a[...] for a in arrived[1:]], axis=1), hits[...])
    inverse = inverse_rowsum[...]
    square = jnp.mean(total * total, axis=0, keepdims=True) * inverse * inverse
    gain = columns[:, 2 * layer + 1 : 2 * layer + 2]
    neighbour = (total * (inverse * lax.rsqrt(square + 1e-06)) * gain).astype(BF16)
    half = 0.5 * (own[...] + project(w_neighbour[layer], neighbour))
    return half + half * jnp.tanh(half)


def first_layer(
    a0, a1, a2, a3, local, own, inverse_rowsum, lat, first_hits, hits, w_neighbour, w_out, columns, new, sent
):
    activated = activation(
        0, (a0, a1, a2, a3), local, own, inverse_rowsum, first_hits, hits, w_neighbour, columns
    ).astype(BF16)
    value = (lat[...].astype(F32) + project(w_out[0], activated)).astype(BF16)
    new[...] = value
    send_features(value, first_hits, (sent,))


def last_layer(
    places, a0, a1, a2, a3, local, own, inverse_rowsum, lat, first_hits, hits, w_neighbour, columns, before, decoder,
    guess, s0, s1, s2, s3,
):
    activated = activation(
        LAYERS - 1, (a0, a1, a2, a3), local, own, inverse_rowsum, first_hits, hits, w_neighbour, columns
    ).astype(BF16)
    row = before[...] + jnp.sum(activated.astype(F32) * decoder[...], axis=0, keepdims=True)
    field = tile_rows_of(row)
    guess[...] = field
    store_sent((s0, s1, s2, s3), pick(field, slot_rows(places)))


def product(matrix, field):
    count = LANES
    width = matrix.shape[1]
    total = jnp.zeros((8, width), F32)
    for t in range(field.shape[0]):
        column = jnp.broadcast_to(field[t : t + 1, :], (count, count)).T
        wide = jnp.concatenate([column] * (width // count), axis=1)
        part = matrix[t * count : (t + 1) * count, :] * wide
        total = total + jnp.sum(part.reshape(count // 8, 8, width), axis=0)
    return tile_rows_of(jnp.sum(total, axis=0, keepdims=True))


def matvec(matrix, vector, out):
    out[...] = product(matrix, vector[...])


def start_basis(places, a0, a1, a2, a3, local, guess, source, diagonal, basis, s0, s1, s2, s3):
    rows = slot_rows(places)
    came = spread_sum(arrived_rows((a0, a1, a2, a3)), rows, guess.shape[0])
    value = (source[...] + local[...] + came) / diagonal[...] - guess[...]
    basis[...] = value
    store_sent((s0, s1, s2, s3), pick(value, rows))


def next_basis(places, a0, a1, a2, a3, local, diagonal, basis, s0, s1, s2, s3):
    rows = slot_rows(places)
    came = spread_sum(arrived_rows((a0, a1, a2, a3)), rows, local.shape[0])
    value = (local[...] + came) / diagonal[...]
    basis[...] = value
    store_sent((s0, s1, s2, s3), pick(value, rows))


def diagonal_mask():
    return lax.broadcasted_iota(jnp.int32, (8, LANES), 0) == lax.broadcasted_iota(jnp.int32, (8, LANES), 1)


def last_basis(places, a0, a1, a2, a3, local, diagonal, b0, b1, matrix, basis, image, packets):
    rows = slot_rows(places)
    came = spread_sum(arrived_rows((a0, a1, a2, a3)), rows, local.shape[0])
    value = (local[...] + came) / diagonal[...]
    basis[...] = value
    mapped = product(matrix, value)
    image[...] = mapped
    held = [b0[...], b1[...], value]
    parts = []
    for k in range(2 * ITERS - 1):
        left, right = held[k // 2], held[(k + 1) // 2]
        parts.append(jnp.sum(left * right * diagonal[...], axis=0, keepdims=True))
    parts.append(jnp.sum(value * mapped, axis=0, keepdims=True))
    parts.append(jnp.zeros((8 - 2 * ITERS, LANES), F32))
    sums = jnp.sum(jnp.concatenate(parts, axis=0), axis=1, keepdims=True)
    row = jnp.sum(jnp.where(diagonal_mask(), sums, 0.0), axis=0, keepdims=True)
    packet = jnp.concatenate([lane_rows(pick(value, rows)), row], axis=1)
    for device in range(packets.shape[0]):
        packets[device] = packet


def added(values):
    values = list(values)
    while len(values) > 1:
        values = [sum(values[i : i + 2][1:], values[i]) for i in range(0, len(values), 2)]
    return values[0]


def finish(sizes, where, packets, places, image, guess, diagonal, b0, b1, b2, field, defect):
    doms, subs = sizes
    width = packets.shape[2] - LANES
    per = width // 4

    def slots(device, g):
        return packets[device, :, g * per : (g + 1) * per]

    edges = []
    for d in range(doms):
        for s in range(subs):
            for m, (i, j) in (((0, d % 2), (d + 1, s)), ((1, s % 2), (d, s + 1))):
                g = turns_of(s, subs).index(m)
                if i < doms and j < subs:
                    edges.append(slots(d * subs + s, g) * slots(i * subs + j, g))
    edges = added(edges)
    edges = added([edges[:, h : h + LANES] for h in range(0, per, LANES)])
    sums = added([packets[e, :, width : width + LANES] for e in range(doms * subs)])
    last_row = lax.broadcasted_iota(jnp.int32, (8, LANES), 0) == 2 * ITERS - 1
    table = jnp.where(diagonal_mask(), jnp.broadcast_to(sums, (8, LANES)), 0.0)
    table = table + jnp.where(last_row, jnp.broadcast_to(2.0 * edges, (8, LANES)), 0.0)
    columns = jnp.sum(table, axis=1, keepdims=True)
    n = [jnp.broadcast_to(columns[k : k + 1, :], (8, LANES)) for k in range(2 * ITERS)]
    came = []
    for g in range(4):
        mine = slots(where[4 + g], g)
        came += [mine[:, h : h + LANES] for h in range(0, per, LANES)]
    last = (image[...] + spread_sum(came, slot_rows(places), image.shape[0])) / diagonal[...]
    one, zero = jnp.ones((8, LANES), F32), jnp.zeros((8, LANES), F32)

    def paired(left, values):
        total = zero
        for i, a in enumerate(left):
            for j, b in enumerate(left):
                total = total + a * b * values[i + j]
        return total

    gaps = [n[k] - n[k + 1] for k in range(2 * ITERS - 1)]
    residual = [one]
    heading = [one]
    moved = [zero] * ITERS
    size = n[0]
    for step in range(ITERS):
        alpha = size / paired(heading, gaps)
        for i, h in enumerate(heading):
            moved[i] = moved[i] + alpha * h
        change = [
            (heading[i] if i < len(heading) else zero) - (heading[i - 1] if i > 0 else zero)
            for i in range(len(heading) + 1)
        ]
        residual = [
            (residual[i] if i < len(residual) else zero) - alpha * change[i]
            for i in range(len(change))
        ]
        if step + 1 < ITERS:
            following = paired(residual, n)
            beta = following / size
            heading = [
                residual[i] + (beta * heading[i] if i < len(heading) else zero)
                for i in range(len(residual))
            ]
            size = following
    held = [b0[...], b1[...], b2[...], last]
    total = guess[...]
    for c, b in zip(moved, held):
        total = total + c * b
    field[...] = total
    left = zero
    for c, b in zip(residual, held):
        left = left + c * b
    defect[...] = left * diagonal[...]


def mate_of(place, first, size):
    mate = ((place - first) ^ 1) + first
    return mate if place >= first and mate < size else None


def turns_of(sub, subs):
    return OUTER if mate_of(sub, 1, subs) is None else INNER


def swaps(sizes, turn):
    doms, subs = sizes
    pairs = []
    for dom in range(doms):
        for sub in range(subs):
            along, first = turns_of(sub, subs)[turn]
            to = [dom, sub]
            mate = mate_of(to[along], first, sizes[along])
            if mate is not None:
                to[along] = mate
            elif along == 0 and turns_of(sub, subs) is INNER:
                to[1] = mate_of(sub, 1, subs)
            elif along == 0 and subs % 2 == 0:
                to[1] = subs - 1 - sub
            elif doms % 2 == 0:
                to[0] = dom ^ 1
            pairs.append((dom * subs + sub, to[0] * subs + to[1]))
    return pairs


def places_of_turns():
    at = [lax.axis_index("dom"), lax.axis_index("sub")]
    sizes = [lax.axis_size("dom"), lax.axis_size("sub")]

    def side(along, first):
        odd = at[along] % 2
        return 2 * along + (odd if first else 1 - odd)

    def partner(along, first):
        mate = jnp.bitwise_xor(at[along] - first, 1) + first
        to = list(at)
        to[along] = jnp.where((at[along] >= first) & (mate < sizes[along]), mate, at[along])
        return to[0] * sizes[1] + to[1]

    outer = (at[1] == 0) | ((at[1] == sizes[1] - 1) & (sizes[1] % 2 == 0))
    out = []
    for value in (side, partner):
        out += [jnp.where(outer, value(*o), value(*i)) for o, i in zip(OUTER, INNER)]
    return jnp.stack(out).astype(jnp.int32)


def swap(sent, turn):
    axes = ("dom", "sub")
    return lax.ppermute(sent, axes, swaps([lax.axis_size(axis) for axis in axes], turn))


def exchange(sent, first=0):
    return [swap(s, first + i) for i, s in enumerate(sent)]


def all_to_all(messages):
    return lax.all_to_all(messages, ("dom", "sub"), split_axis=0, concat_axis=0, tiled=True)


def per_device(
    state, tile_values, tile_rows, tile_columns, tile_counts, send_nodes, face_counts, capacity,
    source, w_self, w_neighbour, w_out, gains, bias, w_decode,
):
    nodes, width = state.shape
    slots = send_nodes.shape[2]
    tiles = nodes // LANES
    sizes = (lax.axis_size("dom"), lax.axis_size("sub"))
    devices = sizes[0] * sizes[1]
    field = shape((tiles, LANES))
    features = shape((width, nodes))
    vector_sent = [shape((slots // LANES, LANES))] * 4
    decode = w_decode.reshape(1, width)
    where = places_of_turns()
    capacity = capacity.reshape(tiles, LANES)
    source = source.reshape(tiles, LANES)

    one_sent = [shape((width, slots), BF16)]
    gather_flops = 2 * nodes * slots * width
    lat, first_hits, places, sent = run(
        gather_first,
        [shape((width, nodes), BF16), shape((nodes, slots), BF16), shape((4 * slots // LANES, LANES), jnp.int32)]
        + one_sent,
        (), (where,), (send_nodes, face_counts, state),
        (
            pltpu.VMEM(send_nodes.shape, jnp.int32),
            pltpu.SMEM(face_counts.shape, jnp.int32),
            pltpu.VMEM(state.shape, BF16),
        ),
        waits=6, flops=gather_flops,
    )
    a0 = swap(sent, 0)
    hits, columns, *sent = run(
        gather_rest, [shape((nodes, 3 * slots), BF16), shape((width, 8))] + one_sent * 3,
        (places, lat), (), (gains, bias, decode),
        (pltpu.VMEM(gains.shape, F32), pltpu.VMEM(bias.shape, F32), pltpu.VMEM(decode.shape, F32)),
        waits=3, flops=3 * gather_flops,
    )
    a1, a2, a3 = exchange(sent, 1)
    matrix, half, inverse_rowsum, diagonal, local, own = run(
        build,
        [shape((nodes, nodes)), shape((nodes, nodes), BF16), shape((1, nodes)), field, features, features],
        (places, tile_values, lat, w_self, columns, tile_counts.reshape(1, 1)),
        (), (tile_rows, tile_columns, capacity),
        (
            pltpu.SMEM(tile_rows.shape, jnp.int32),
            pltpu.SMEM(tile_columns.shape, jnp.int32),
            pltpu.SMEM((1, 1), jnp.int32),
            pltpu.VMEM(capacity.shape, F32),
        ),
        waits=4, flops=0, moved=0,
    )
    lat, sent = run(
        first_layer, [shape((width, nodes), BF16)] + one_sent,
        (a0, a1, a2, a3, local, own, inverse_rowsum, lat, first_hits, hits, w_neighbour, w_out, columns),
        flops=3 * nodes * nodes * width,
    )
    a0 = swap(sent, 0)
    sent = run(send_rest, one_sent * 3, (lat, hits), flops=3 * gather_flops)
    a1, a2, a3 = exchange(sent, 1)
    local, own, before, decoder = run(
        functools.partial(local_features, LAYERS - 1),
        [features, features, shape((1, nodes)), shape((width, 1))],
        (lat, half, w_self, w_out, columns), flops=0, moved=0,
    )
    guess, *sent = run(
        last_layer, [field] + vector_sent,
        (places, a0, a1, a2, a3, local, own, inverse_rowsum, lat, first_hits, hits, w_neighbour, columns, before, decoder),
        flops=3 * nodes * nodes * width,
    )

    def mapped(vector):
        return run(matvec, [field], (matrix, vector), flops=2 * nodes * nodes, moved=4 * nodes * nodes)[0]

    arrived = exchange(sent)
    local = mapped(guess)
    b0, *sent = run(
        start_basis, [field] + vector_sent, (places, *arrived, local, guess, source, diagonal)
    )
    arrived = exchange(sent)
    local = mapped(b0)
    b1, *sent = run(next_basis, [field] + vector_sent, (places, *arrived, local, diagonal))
    arrived = exchange(sent)
    local = mapped(b1)
    b2, image, packets = run(
        last_basis, [field, field, shape((devices, 1, 4 * slots + LANES))],
        (places, *arrived, local, diagonal, b0, b1, matrix),
    )
    packets = all_to_all(packets)
    heat, defect = run(
        functools.partial(finish, sizes), [field, field],
        (packets, places, image, guess, diagonal, b0, b1, b2), (where,),
    )
    return heat.reshape(nodes), defect.reshape(nodes)


def solution(mesh):
    both = ("dom", "sub")
    return jax.shard_map(
        per_device,
        mesh=mesh,
        in_specs=(
            P(both, None),
            P(both, None, None, None),
            P(both, None),
            P(both, None),
            P(both),
            P(both, None, None),
            P(both, None),
            P(both),
            P(both),
            P(),
            P(),
            P(),
            P(),
            P(),
            P(),
        ),
        out_specs=(P(both), P(both)),
        check_vma=False,
    )
```

```python
import functools

import jax
import jax.numpy as jnp
from jax import lax
from jax.experimental import pallas as pl
from jax.experimental.pallas import tpu as pltpu
from jax.sharding import PartitionSpec as P

LAYERS = 2
ITERS = 3
LANES = 128
MATCHINGS = ((1, 1), (1, 0), (0, 1), (0, 0))
VMEM_LIMIT = 24 * 1024 * 1024

F32 = jnp.float32
BF16 = jnp.bfloat16


def shape(dims, dtype=F32):
    return jax.ShapeDtypeStruct(dims, dtype)


def run(body, outs, operands, scalars=(), raw=(), scratch=(), waits=0, flops=1_000_000, moved=1_000_000):
    smem = pl.BlockSpec(memory_space=pltpu.SMEM)
    vmem = pl.BlockSpec(memory_space=pltpu.VMEM)
    anywhere = pl.BlockSpec(memory_space=pltpu.HBM)
    scratch = list(scratch) + [pltpu.SemaphoreType.DMA((waits,))] * bool(waits)
    return pl.pallas_call(
        body,
        out_shape=outs,
        in_specs=[smem] * len(scalars) + [vmem] * len(operands) + [anywhere] * len(raw),
        out_specs=[vmem] * len(outs),
        scratch_shapes=scratch,
        compiler_params=pltpu.CompilerParams(vmem_limit_bytes=VMEM_LIMIT),
        cost_estimate=pl.CostEstimate(flops=flops, bytes_accessed=moved, transcendentals=0),
    )(*scalars, *operands, *(pltpu.with_memory_space_constraint(r, pltpu.HBM) for r in raw))


def copies(pairs, semaphores):
    started = [pltpu.make_async_copy(*pair, semaphores.at[i]) for i, pair in enumerate(pairs)]
    for copy in started:
        copy.start()
    return started


def slot_rows(places):
    return [places[r : r + 1, :] for r in range(places.shape[0])]


def pick(vector, rows):
    index = jnp.concatenate(rows, axis=0)
    low = jnp.bitwise_and(index, LANES - 1)
    high = jnp.right_shift(index, 7)
    out = jnp.zeros(index.shape, F32)
    for t in range(vector.shape[0]):
        spread = jnp.broadcast_to(vector[t : t + 1, :], index.shape)
        got = jnp.take_along_axis(spread, low, axis=1, mode="promise_in_bounds")
        out = jnp.where(high == t, got, out)
    return out


def pieces(value):
    first = value.astype(BF16)
    rest = value - first.astype(F32)
    second = rest.astype(BF16)
    third = (rest - second.astype(F32)).astype(BF16)
    return first, second, third


def low_hits(rows):
    lane = lax.broadcasted_iota(jnp.int32, (LANES, LANES), 0)
    return jnp.concatenate(
        [(lane == jnp.bitwise_and(row, LANES - 1)).astype(F32).astype(BF16) for row in rows], axis=1
    )


def spread_sum(values, rows, tiles):
    tile = lax.broadcasted_iota(jnp.int32, (tiles, LANES), 0)
    parts = [
        jnp.where(tile == jnp.right_shift(row, 7), value, 0.0) for value, row in zip(values, rows)
    ]
    held = jnp.concatenate(parts, axis=1)
    stacked = jnp.concatenate([p.astype(F32) for p in pieces(held)], axis=0).astype(BF16)
    out = lax.dot_general(
        stacked, low_hits(rows), (((1,), (1,)), ((), ())), preferred_element_type=F32
    )
    return out[:tiles] + out[tiles : 2 * tiles] + out[2 * tiles :]


def arrived_rows(refs):
    return [ref[h : h + 1, :] for ref in refs for h in range(ref.shape[0])]


def store_sent(refs, sent):
    per = refs[0].shape[0]
    for k, ref in enumerate(refs):
        ref[...] = sent[k * per : (k + 1) * per, :]


def lane_rows(vector):
    return jnp.concatenate([vector[t : t + 1, :] for t in range(vector.shape[0])], axis=1)


def tile_rows_of(row):
    return jnp.concatenate(
        [row[:, t * LANES : (t + 1) * LANES] for t in range(row.shape[1] // LANES)], axis=0
    )


def fill_hits(hits, rows, first, last):
    node = lax.broadcasted_iota(jnp.int32, (hits.shape[0], LANES), 0).astype(jnp.int16)
    one, zero = jnp.ones(node.shape, BF16), jnp.zeros(node.shape, BF16)
    for c in range(first, last):
        wide = jnp.broadcast_to(rows[c], node.shape).astype(jnp.int16)
        at = (c - first) * LANES
        hits[:, at : at + LANES] = jnp.where(node == wide, one, zero)


def gather_first(
    where, index_in, counts_in, state_in, lat, hits, places, sent, index, counts, state, sems
):
    first, second, third = copies(((index_in, index), (counts_in, counts), (state_in, state)), sems)
    per = index.shape[2] // LANES
    first.wait()
    second.wait()
    for g in range(index.shape[1]):
        side = where[g]
        for h in range(per):
            span = slice(h * LANES, (h + 1) * LANES)
            row = index[0, 0:1, span]
            for k in range(1, index.shape[1]):
                row = jnp.where(side == k, index[0, k : k + 1, span], row)
            slot = lax.broadcasted_iota(jnp.int32, (1, LANES), 1) + h * LANES
            r = g * per + h
            places[r : r + 1, :] = jnp.where(slot < counts[0, side], row, -1)
    fill_hits(hits, slot_rows(places), 0, per)
    third.wait()
    lat[...] = state[...].T
    send_features(lat[...], hits, (sent,))


def gather_rest(places, lat, gains_in, bias_in, decode_in, hits, columns, s1, s2, s3, gains, bias, decode, sems):
    waits = copies(((gains_in, gains), (bias_in, bias), (decode_in, decode)), sems)
    rows = slot_rows(places)
    fill_hits(hits, rows, len(rows) // 4, len(rows))
    send_features(lat[...], hits, (s1, s2, s3))
    for copy in waits:
        copy.wait()
    lines = [gains[layer] for layer in range(LAYERS)] + [bias[...], decode[...]]
    lines.append(jnp.zeros((8 - 3 * LAYERS - 1, bias.shape[1]), F32))
    columns[...] = jnp.concatenate(lines, axis=0).T


def send_features(lat, hits, outs):
    width = outs[0].shape[1]
    for k, out in enumerate(outs):
        out[...] = jnp.dot(
            lat, hits[:, k * width : (k + 1) * width], preferred_element_type=F32
        ).astype(BF16)


def send_rest(lat, hits, s1, s2, s3):
    send_features(lat[...], hits, (s1, s2, s3))


def build(
    tile_counts, places, tiles, lat, w_self, columns, rows_in, columns_in, capacity_in,
    matrix, half, inverse_rowsum, diagonal, local, own,
    tile_rows, tile_columns, capacity, sems,
):
    waits = copies(((rows_in, tile_rows), (columns_in, tile_columns), (capacity_in, capacity)), sems)
    count = tiles.shape[2]
    node_tiles = matrix.shape[0] // count
    matrix[...] = jnp.zeros(matrix.shape, F32)
    for t in range(node_tiles):
        span = slice(t * count, (t + 1) * count)
        block = tiles[0, t]
        matrix[span, span] = block + block.T
    for copy in waits:
        copy.wait()

    known = tile_rows.shape[1]
    live = tile_counts[0]
    together = 4

    def add(step, carry):
        for k in range(together):
            t = node_tiles + step * together + k
            at = jnp.minimum(t, known - 1)
            r = pl.multiple_of(tile_rows[0, at] * count, count)
            c = pl.multiple_of(tile_columns[0, at] * count, count)
            block = jnp.where(t < live, tiles[0, at], 0.0)
            matrix[pl.ds(r, count), pl.ds(c, count)] += block
            matrix[pl.ds(c, count), pl.ds(r, count)] += block.T
        return carry

    lax.fori_loop(0, (live - node_tiles + together - 1) // together, add, 0)
    rows = slot_rows(places)
    faces = spread_sum([jnp.ones((1, LANES), F32)] * len(rows), rows, node_tiles)
    total = jnp.zeros((8, matrix.shape[1]), F32)
    for t in range(node_tiles):
        block = matrix[t * count : (t + 1) * count, :]
        half[t * count : (t + 1) * count, :] = block.astype(BF16)
        total = total + jnp.sum(block.reshape(count // 8, 8, matrix.shape[1]), axis=0)
    rowsum = tile_rows_of(jnp.sum(total, axis=0, keepdims=True)) + faces
    inverse_rowsum[...] = lane_rows(1.0 / rowsum)
    diagonal[...] = capacity[...] + rowsum
    local[...] = jnp.dot(lat[...], half[...], preferred_element_type=F32)
    own[...] = own_part(0, lat[...], w_self, columns)


def normed(value, gain):
    scale = lax.rsqrt(jnp.mean(value * value, axis=0, keepdims=True) + 1e-06)
    return (value * scale * gain).astype(BF16)


def project(weight, value):
    return lax.dot_general(weight, value, (((0,), (0,)), ((), ())), preferred_element_type=F32)


def own_part(layer, lat, w_self, columns):
    gain = columns[:, 2 * layer : 2 * layer + 1]
    bias = columns[:, 2 * LAYERS + layer : 2 * LAYERS + layer + 1]
    return project(w_self[layer], normed(lat.astype(F32), gain)) + bias


def local_features(layer, lat, half, w_self, w_out, columns, local, own, before, decoder):
    local[...] = jnp.dot(lat[...], half[...], preferred_element_type=F32)
    own[...] = own_part(layer, lat[...], w_self, columns)
    decode = columns[:, 3 * LAYERS : 3 * LAYERS + 1]
    before[...] = jnp.sum(lat[...].astype(F32) * decode, axis=0, keepdims=True)
    line = jnp.broadcast_to(decode, (decode.shape[0], LANES)).T[0:1, :]
    decoder[...] = jnp.sum(w_out[layer].astype(F32) * line, axis=1, keepdims=True)


def with_slots(local, came, hits):
    return local + lax.dot_general(came, hits, (((1,), (1,)), ((), ())), preferred_element_type=F32)


def activation(layer, arrived, local, own, inverse_rowsum, first_hits, hits, w_neighbour, columns):
    total = with_slots(local[...], arrived[0][...], first_hits[...])
    total = with_slots(total, jnp.concatenate([a[...] for a in arrived[1:]], axis=1), hits[...])
    inverse = inverse_rowsum[...]
    square = jnp.mean(total * total, axis=0, keepdims=True) * inverse * inverse
    gain = columns[:, 2 * layer + 1 : 2 * layer + 2]
    neighbour = (total * (inverse * lax.rsqrt(square + 1e-06)) * gain).astype(BF16)
    linear = own[...] + project(w_neighbour[layer], neighbour)
    return linear / (1.0 + jnp.exp(-linear))


def first_layer(
    a0, a1, a2, a3, local, own, inverse_rowsum, lat, first_hits, hits, w_neighbour, w_out, columns, new, sent
):
    activated = activation(
        0, (a0, a1, a2, a3), local, own, inverse_rowsum, first_hits, hits, w_neighbour, columns
    ).astype(BF16)
    value = (lat[...].astype(F32) + project(w_out[0], activated)).astype(BF16)
    new[...] = value
    send_features(value, first_hits, (sent,))


def last_layer(
    places, a0, a1, a2, a3, local, own, inverse_rowsum, lat, first_hits, hits, w_neighbour, columns, before, decoder,
    guess, s0, s1, s2, s3,
):
    activated = activation(
        LAYERS - 1, (a0, a1, a2, a3), local, own, inverse_rowsum, first_hits, hits, w_neighbour, columns
    ).astype(BF16)
    row = before[...] + jnp.sum(activated.astype(F32) * decoder[...], axis=0, keepdims=True)
    field = tile_rows_of(row)
    guess[...] = field
    store_sent((s0, s1, s2, s3), pick(field, slot_rows(places)))


def product(matrix, field):
    count = LANES
    width = matrix.shape[1]
    total = jnp.zeros((8, width), F32)
    for t in range(field.shape[0]):
        column = jnp.broadcast_to(field[t : t + 1, :], (count, count)).T
        wide = jnp.concatenate([column] * (width // count), axis=1)
        part = matrix[t * count : (t + 1) * count, :] * wide
        total = total + jnp.sum(part.reshape(count // 8, 8, width), axis=0)
    return tile_rows_of(jnp.sum(total, axis=0, keepdims=True))


def matvec(matrix, vector, out):
    out[...] = product(matrix, vector[...])


def start_basis(places, a0, a1, a2, a3, local, guess, source, diagonal, basis, s0, s1, s2, s3):
    rows = slot_rows(places)
    came = spread_sum(arrived_rows((a0, a1, a2, a3)), rows, guess.shape[0])
    value = (source[...] + local[...] + came) / diagonal[...] - guess[...]
    basis[...] = value
    store_sent((s0, s1, s2, s3), pick(value, rows))


def next_basis(places, a0, a1, a2, a3, local, diagonal, basis, s0, s1, s2, s3):
    rows = slot_rows(places)
    came = spread_sum(arrived_rows((a0, a1, a2, a3)), rows, local.shape[0])
    value = (local[...] + came) / diagonal[...]
    basis[...] = value
    store_sent((s0, s1, s2, s3), pick(value, rows))


def diagonal_mask():
    return lax.broadcasted_iota(jnp.int32, (8, LANES), 0) == lax.broadcasted_iota(jnp.int32, (8, LANES), 1)


def last_basis(places, a0, a1, a2, a3, local, diagonal, b0, b1, matrix, basis, image, packets):
    rows = slot_rows(places)
    came = spread_sum(arrived_rows((a0, a1, a2, a3)), rows, local.shape[0])
    value = (local[...] + came) / diagonal[...]
    basis[...] = value
    mapped = product(matrix, value)
    image[...] = mapped
    held = [b0[...], b1[...], value]
    parts = []
    for k in range(2 * ITERS - 1):
        left, right = held[k // 2], held[(k + 1) // 2]
        parts.append(jnp.sum(left * right * diagonal[...], axis=0, keepdims=True))
    parts.append(jnp.sum(value * mapped, axis=0, keepdims=True))
    parts.append(jnp.zeros((8 - 2 * ITERS, LANES), F32))
    sums = jnp.sum(jnp.concatenate(parts, axis=0), axis=1, keepdims=True)
    row = jnp.sum(jnp.where(diagonal_mask(), sums, 0.0), axis=0, keepdims=True)
    packet = jnp.concatenate([lane_rows(pick(value, rows)), row], axis=1)
    for device in range(packets.shape[0]):
        packets[device] = packet


def added(values):
    values = list(values)
    while len(values) > 1:
        values = [sum(values[i : i + 2][1:], values[i]) for i in range(0, len(values), 2)]
    return values[0]


def finish(sizes, where, packets, places, image, guess, diagonal, b0, b1, b2, field, defect):
    doms, subs = sizes
    width = packets.shape[2] - LANES
    per = width // 4

    def slots(device, g):
        return packets[device, :, g * per : (g + 1) * per]

    edges = []
    for d in range(doms):
        for s in range(subs):
            for m, (i, j) in (((0, d % 2), (d + 1, s)), ((1, s % 2), (d, s + 1))):
                g = MATCHINGS.index(m)
                if i < doms and j < subs:
                    edges.append(slots(d * subs + s, g) * slots(i * subs + j, g))
    edges = added(edges)
    edges = added([edges[:, h : h + LANES] for h in range(0, per, LANES)])
    sums = added([packets[e, :, width : width + LANES] for e in range(doms * subs)])
    last_row = lax.broadcasted_iota(jnp.int32, (8, LANES), 0) == 2 * ITERS - 1
    table = jnp.where(diagonal_mask(), jnp.broadcast_to(sums, (8, LANES)), 0.0)
    table = table + jnp.where(last_row, jnp.broadcast_to(2.0 * edges, (8, LANES)), 0.0)
    columns = jnp.sum(table, axis=1, keepdims=True)
    n = [jnp.broadcast_to(columns[k : k + 1, :], (8, LANES)) for k in range(2 * ITERS)]
    came = []
    for g in range(4):
        mine = slots(where[4 + g], g)
        came += [mine[:, h : h + LANES] for h in range(0, per, LANES)]
    last = (image[...] + spread_sum(came, slot_rows(places), image.shape[0])) / diagonal[...]
    one, zero = jnp.ones((8, LANES), F32), jnp.zeros((8, LANES), F32)

    def paired(left, values):
        total = zero
        for i, a in enumerate(left):
            for j, b in enumerate(left):
                total = total + a * b * values[i + j]
        return total

    gaps = [n[k] - n[k + 1] for k in range(2 * ITERS - 1)]
    residual = [one]
    heading = [one]
    moved = [zero] * ITERS
    size = n[0]
    for step in range(ITERS):
        alpha = size / paired(heading, gaps)
        for i, h in enumerate(heading):
            moved[i] = moved[i] + alpha * h
        change = [
            (heading[i] if i < len(heading) else zero) - (heading[i - 1] if i > 0 else zero)
            for i in range(len(heading) + 1)
        ]
        residual = [
            (residual[i] if i < len(residual) else zero) - alpha * change[i]
            for i in range(len(change))
        ]
        if step + 1 < ITERS:
            following = paired(residual, n)
            beta = following / size
            heading = [
                residual[i] + (beta * heading[i] if i < len(heading) else zero)
                for i in range(len(residual))
            ]
            size = following
    held = [b0[...], b1[...], b2[...], last]
    total = guess[...]
    for c, b in zip(moved, held):
        total = total + c * b
    field[...] = total
    left = zero
    for c, b in zip(residual, held):
        left = left + c * b
    defect[...] = left * diagonal[...]


def mate_of(place, first, size):
    mate = ((place - first) ^ 1) + first
    return mate if place >= first and mate < size else None


def swaps(sizes, turn):
    along, first = MATCHINGS[turn]
    pairs = []
    for dom in range(sizes[0]):
        for sub in range(sizes[1]):
            to = [dom, sub]
            mate = mate_of(to[along], first, sizes[along])
            other = 1 - along
            if mate is not None:
                to[along] = mate
            elif to[other] ^ 1 < sizes[other]:
                to[other] ^= 1
            pairs.append((dom * sizes[1] + sub, to[0] * sizes[1] + to[1]))
    return pairs


def places_of_turns():
    at = [lax.axis_index("dom"), lax.axis_index("sub")]
    sizes = [lax.axis_size("dom"), lax.axis_size("sub")]

    def side(along, first):
        odd = at[along] % 2
        return 2 * along + (odd if first else 1 - odd)

    def partner(along, first):
        mate = jnp.bitwise_xor(at[along] - first, 1) + first
        to = list(at)
        to[along] = jnp.where((at[along] >= first) & (mate < sizes[along]), mate, at[along])
        return to[0] * sizes[1] + to[1]

    out = [value(*m) for value in (side, partner) for m in MATCHINGS]
    return jnp.stack(out).astype(jnp.int32)


def swap(sent, turn):
    axes = ("dom", "sub")
    return lax.ppermute(sent, axes, swaps([lax.axis_size(axis) for axis in axes], turn))


def exchange(sent, first=0):
    return [swap(s, first + i) for i, s in enumerate(sent)]


def all_to_all(messages):
    return lax.all_to_all(messages, ("dom", "sub"), split_axis=0, concat_axis=0, tiled=True)


def per_device(
    state, tile_values, tile_rows, tile_columns, tile_counts, send_nodes, face_counts, capacity,
    source, w_self, w_neighbour, w_out, gains, bias, w_decode,
):
    nodes, width = state.shape
    slots = send_nodes.shape[2]
    tiles = nodes // LANES
    sizes = (lax.axis_size("dom"), lax.axis_size("sub"))
    devices = sizes[0] * sizes[1]
    field = shape((tiles, LANES))
    features = shape((width, nodes))
    vector_sent = [shape((slots // LANES, LANES))] * 4
    decode = w_decode.reshape(1, width)
    where = places_of_turns()
    capacity = capacity.reshape(tiles, LANES)
    source = source.reshape(tiles, LANES)

    one_sent = [shape((width, slots), BF16)]
    gather_flops = 2 * nodes * slots * width
    lat, first_hits, places, sent = run(
        gather_first,
        [shape((width, nodes), BF16), shape((nodes, slots), BF16), shape((4 * slots // LANES, LANES), jnp.int32)]
        + one_sent,
        (), (where,), (send_nodes, face_counts, state),
        (
            pltpu.VMEM(send_nodes.shape, jnp.int32),
            pltpu.SMEM(face_counts.shape, jnp.int32),
            pltpu.VMEM(state.shape, BF16),
        ),
        waits=3, flops=gather_flops,
    )
    a0 = swap(sent, 0)
    hits, columns, *sent = run(
        gather_rest, [shape((nodes, 3 * slots), BF16), shape((width, 8))] + one_sent * 3,
        (places, lat), (), (gains, bias, decode),
        (pltpu.VMEM(gains.shape, F32), pltpu.VMEM(bias.shape, F32), pltpu.VMEM(decode.shape, F32)),
        waits=3, flops=3 * gather_flops,
    )
    a1, a2, a3 = exchange(sent, 1)
    matrix, half, inverse_rowsum, diagonal, local, own = run(
        build,
        [shape((nodes, nodes)), shape((nodes, nodes), BF16), shape((1, nodes)), field, features, features],
        (places, tile_values, lat, w_self, columns),
        (tile_counts,), (tile_rows, tile_columns, capacity),
        (
            pltpu.SMEM(tile_rows.shape, jnp.int32),
            pltpu.SMEM(tile_columns.shape, jnp.int32),
            pltpu.VMEM(capacity.shape, F32),
        ),
        waits=3, flops=0, moved=0,
    )
    lat, sent = run(
        first_layer, [shape((width, nodes), BF16)] + one_sent,
        (a0, a1, a2, a3, local, own, inverse_rowsum, lat, first_hits, hits, w_neighbour, w_out, columns),
        flops=3 * nodes * nodes * width,
    )
    a0 = swap(sent, 0)
    sent = run(send_rest, one_sent * 3, (lat, hits), flops=3 * gather_flops)
    a1, a2, a3 = exchange(sent, 1)
    local, own, before, decoder = run(
        functools.partial(local_features, LAYERS - 1),
        [features, features, shape((1, nodes)), shape((width, 1))],
        (lat, half, w_self, w_out, columns), flops=0, moved=0,
    )
    guess, *sent = run(
        last_layer, [field] + vector_sent,
        (places, a0, a1, a2, a3, local, own, inverse_rowsum, lat, first_hits, hits, w_neighbour, columns, before, decoder),
        flops=3 * nodes * nodes * width,
    )

    def mapped(vector):
        return run(matvec, [field], (matrix, vector), flops=2 * nodes * nodes, moved=4 * nodes * nodes)[0]

    arrived = exchange(sent)
    local = mapped(guess)
    b0, *sent = run(
        start_basis, [field] + vector_sent, (places, *arrived, local, guess, source, diagonal)
    )
    arrived = exchange(sent)
    local = mapped(b0)
    b1, *sent = run(next_basis, [field] + vector_sent, (places, *arrived, local, diagonal))
    arrived = exchange(sent)
    local = mapped(b1)
    b2, image, packets = run(
        last_basis, [field, field, shape((devices, 1, 4 * slots + LANES))],
        (places, *arrived, local, diagonal, b0, b1, matrix),
    )
    packets = all_to_all(packets)
    heat, defect = run(
        functools.partial(finish, sizes), [field, field],
        (packets, places, image, guess, diagonal, b0, b1, b2), (where,),
    )
    return heat.reshape(nodes), defect.reshape(nodes)


def solution(mesh):
    both = ("dom", "sub")
    return jax.shard_map(
        per_device,
        mesh=mesh,
        in_specs=(
            P(both, None),
            P(both, None, None, None),
            P(both, None),
            P(both, None),
            P(both),
            P(both, None, None),
            P(both, None),
            P(both),
            P(both),
            P(),
            P(),
            P(),
            P(),
            P(),
            P(),
        ),
        out_specs=(P(both), P(both)),
        check_vma=False,
    )
```

```python
import functools

import jax
import jax.numpy as jnp
from jax import lax
from jax.experimental import pallas as pl
from jax.experimental.pallas import tpu as pltpu
from jax.sharding import PartitionSpec as P

LAYERS = 2
ITERS = 3
LANES = 128
MATCHINGS = ((1, 1), (1, 0), (0, 1), (0, 0))
VMEM_LIMIT = 24 * 1024 * 1024

F32 = jnp.float32
BF16 = jnp.bfloat16


def shape(dims, dtype=F32):
    return jax.ShapeDtypeStruct(dims, dtype)


def run(body, outs, operands, scalars=(), raw=(), scratch=(), waits=0, flops=1_000_000, moved=1_000_000):
    smem = pl.BlockSpec(memory_space=pltpu.SMEM)
    vmem = pl.BlockSpec(memory_space=pltpu.VMEM)
    anywhere = pl.BlockSpec(memory_space=pltpu.HBM)
    scratch = list(scratch) + [pltpu.SemaphoreType.DMA((waits,))] * bool(waits)
    return pl.pallas_call(
        body,
        out_shape=outs,
        in_specs=[smem] * len(scalars) + [vmem] * len(operands) + [anywhere] * len(raw),
        out_specs=[vmem] * len(outs),
        scratch_shapes=scratch,
        compiler_params=pltpu.CompilerParams(vmem_limit_bytes=VMEM_LIMIT),
        cost_estimate=pl.CostEstimate(flops=flops, bytes_accessed=moved, transcendentals=0),
    )(*scalars, *operands, *(pltpu.with_memory_space_constraint(r, pltpu.HBM) for r in raw))


def copies(pairs, semaphores):
    started = [pltpu.make_async_copy(*pair, semaphores.at[i]) for i, pair in enumerate(pairs)]
    for copy in started:
        copy.start()
    return started


def slot_rows(places):
    return [places[r : r + 1, :] for r in range(places.shape[0])]


def pick(vector, rows):
    index = jnp.concatenate(rows, axis=0)
    low = jnp.bitwise_and(index, LANES - 1)
    high = jnp.right_shift(index, 7)
    out = jnp.zeros(index.shape, F32)
    for t in range(vector.shape[0]):
        spread = jnp.broadcast_to(vector[t : t + 1, :], index.shape)
        got = jnp.take_along_axis(spread, low, axis=1, mode="promise_in_bounds")
        out = jnp.where(high == t, got, out)
    return out


def pieces(value):
    first = value.astype(BF16)
    rest = value - first.astype(F32)
    second = rest.astype(BF16)
    third = (rest - second.astype(F32)).astype(BF16)
    return first, second, third


def low_hits(rows):
    lane = lax.broadcasted_iota(jnp.int32, (LANES, LANES), 0)
    return jnp.concatenate(
        [(lane == jnp.bitwise_and(row, LANES - 1)).astype(F32).astype(BF16) for row in rows], axis=1
    )


def spread_sum(values, rows, tiles):
    tile = lax.broadcasted_iota(jnp.int32, (tiles, LANES), 0)
    parts = [
        jnp.where(tile == jnp.right_shift(row, 7), value, 0.0) for value, row in zip(values, rows)
    ]
    held = jnp.concatenate(parts, axis=1)
    stacked = jnp.concatenate([p.astype(F32) for p in pieces(held)], axis=0).astype(BF16)
    out = lax.dot_general(
        stacked, low_hits(rows), (((1,), (1,)), ((), ())), preferred_element_type=F32
    )
    return out[:tiles] + out[tiles : 2 * tiles] + out[2 * tiles :]


def arrived_rows(refs):
    return [ref[h : h + 1, :] for ref in refs for h in range(ref.shape[0])]


def store_sent(refs, sent):
    per = refs[0].shape[0]
    for k, ref in enumerate(refs):
        ref[...] = sent[k * per : (k + 1) * per, :]


def lane_rows(vector):
    return jnp.concatenate([vector[t : t + 1, :] for t in range(vector.shape[0])], axis=1)


def tile_rows_of(row):
    return jnp.concatenate(
        [row[:, t * LANES : (t + 1) * LANES] for t in range(row.shape[1] // LANES)], axis=0
    )


def fill_hits(hits, rows, first, last):
    nodes = hits.shape[0]
    node = lax.broadcasted_iota(jnp.int32, (nodes, LANES), 0).astype(jnp.int16).reshape(nodes // 16, 16, LANES)
    one, zero = jnp.ones(node.shape, BF16), jnp.zeros(node.shape, BF16)
    for c in range(first, last):
        wide = jnp.broadcast_to(rows[c], (16, LANES)).astype(jnp.int16)
        at = (c - first) * LANES
        hits[:, at : at + LANES] = jnp.where(node == wide[None], one, zero).reshape(nodes, LANES)


def gather_first(
    where, index_in, counts_in, state_in, lat, hits, places, sent, index, counts, state, sems
):
    first, second, third = copies(((index_in, index), (counts_in, counts), (state_in, state)), sems)
    per = index.shape[2] // LANES
    first.wait()
    second.wait()
    for g in range(index.shape[1]):
        side = where[g]
        for h in range(per):
            span = slice(h * LANES, (h + 1) * LANES)
            row = index[0, 0:1, span]
            for k in range(1, index.shape[1]):
                row = jnp.where(side == k, index[0, k : k + 1, span], row)
            slot = lax.broadcasted_iota(jnp.int32, (1, LANES), 1) + h * LANES
            r = g * per + h
            places[r : r + 1, :] = jnp.where(slot < counts[0, side], row, -1)
    fill_hits(hits, slot_rows(places), 0, per)
    third.wait()
    lat[...] = state[...].T
    send_features(lat[...], hits, (sent,))


def gather_rest(places, lat, gains_in, bias_in, decode_in, hits, columns, s1, s2, s3, gains, bias, decode, sems):
    waits = copies(((gains_in, gains), (bias_in, bias), (decode_in, decode)), sems)
    rows = slot_rows(places)
    fill_hits(hits, rows, len(rows) // 4, len(rows))
    send_features(lat[...], hits, (s1, s2, s3))
    for copy in waits:
        copy.wait()
    lines = [gains[layer] for layer in range(LAYERS)] + [bias[...], decode[...]]
    lines.append(jnp.zeros((8 - 3 * LAYERS - 1, bias.shape[1]), F32))
    columns[...] = jnp.concatenate(lines, axis=0).T


def send_features(lat, hits, outs):
    width = outs[0].shape[1]
    for k, out in enumerate(outs):
        out[...] = jnp.dot(
            lat, hits[:, k * width : (k + 1) * width], preferred_element_type=F32
        ).astype(BF16)


def send_rest(lat, hits, s1, s2, s3):
    send_features(lat[...], hits, (s1, s2, s3))


def build(
    tile_counts, places, tiles, lat, w_self, columns, rows_in, columns_in, capacity_in,
    matrix, half, inverse_rowsum, diagonal, local, own,
    tile_rows, tile_columns, capacity, sems,
):
    waits = copies(((rows_in, tile_rows), (columns_in, tile_columns), (capacity_in, capacity)), sems)
    count = tiles.shape[2]
    node_tiles = matrix.shape[0] // count
    matrix[...] = jnp.zeros(matrix.shape, F32)
    for t in range(node_tiles):
        span = slice(t * count, (t + 1) * count)
        block = tiles[0, t]
        matrix[span, span] = block + block.T
    for copy in waits:
        copy.wait()

    known = tiles.shape[1]
    live = tile_counts[0]
    together = 4

    def add(step, carry):
        for k in range(together):
            t = node_tiles + step * together + k
            at = jnp.minimum(t, known - 1)
            r = pl.multiple_of(tile_rows[0, at] * count, count)
            c = pl.multiple_of(tile_columns[0, at] * count, count)
            block = jnp.where(t < live, tiles[0, at], 0.0)
            matrix[pl.ds(r, count), pl.ds(c, count)] += block
            matrix[pl.ds(c, count), pl.ds(r, count)] += block.T
        return carry

    lax.fori_loop(0, (live - node_tiles + together - 1) // together, add, 0)
    rows = slot_rows(places)
    faces = spread_sum([jnp.ones((1, LANES), F32)] * len(rows), rows, node_tiles)
    total = jnp.zeros((8, matrix.shape[1]), F32)
    for t in range(node_tiles):
        block = matrix[t * count : (t + 1) * count, :]
        half[t * count : (t + 1) * count, :] = block.astype(BF16)
        total = total + jnp.sum(block.reshape(count // 8, 8, matrix.shape[1]), axis=0)
    rowsum = tile_rows_of(jnp.sum(total, axis=0, keepdims=True)) + faces
    inverse_rowsum[...] = lane_rows(1.0 / rowsum)
    diagonal[...] = capacity[...] + rowsum
    local[...] = jnp.dot(lat[...], half[...], preferred_element_type=F32)
    own[...] = own_part(0, lat[...], w_self, columns)


def normed(value, gain):
    scale = lax.rsqrt(jnp.mean(value * value, axis=0, keepdims=True) + 1e-06)
    return (value * scale * gain).astype(BF16)


def project(weight, value):
    return lax.dot_general(weight, value, (((0,), (0,)), ((), ())), preferred_element_type=F32)


def own_part(layer, lat, w_self, columns):
    gain = columns[:, 2 * layer : 2 * layer + 1]
    bias = columns[:, 2 * LAYERS + layer : 2 * LAYERS + layer + 1]
    return project(w_self[layer], normed(lat.astype(F32), gain)) + bias


def local_features(layer, lat, half, w_self, w_out, columns, local, own, before, decoder):
    local[...] = jnp.dot(lat[...], half[...], preferred_element_type=F32)
    own[...] = own_part(layer, lat[...], w_self, columns)
    decode = columns[:, 3 * LAYERS : 3 * LAYERS + 1]
    before[...] = jnp.sum(lat[...].astype(F32) * decode, axis=0, keepdims=True)
    line = jnp.broadcast_to(decode, (decode.shape[0], LANES)).T[0:1, :]
    decoder[...] = jnp.sum(w_out[layer].astype(F32) * line, axis=1, keepdims=True)


def with_slots(local, came, hits):
    return local + lax.dot_general(came, hits, (((1,), (1,)), ((), ())), preferred_element_type=F32)


def activation(layer, arrived, local, own, inverse_rowsum, first_hits, hits, w_neighbour, columns):
    total = with_slots(local[...], arrived[0][...], first_hits[...])
    total = with_slots(total, jnp.concatenate([a[...] for a in arrived[1:]], axis=1), hits[...])
    mean = total * inverse_rowsum[...]
    gain = columns[:, 2 * layer + 1 : 2 * layer + 2]
    linear = own[...] + project(w_neighbour[layer], normed(mean, gain))
    return linear / (1.0 + jnp.exp(-linear))


def first_layer(
    a0, a1, a2, a3, local, own, inverse_rowsum, lat, first_hits, hits, w_neighbour, w_out, columns, new, sent
):
    activated = activation(
        0, (a0, a1, a2, a3), local, own, inverse_rowsum, first_hits, hits, w_neighbour, columns
    ).astype(BF16)
    value = (lat[...].astype(F32) + project(w_out[0], activated)).astype(BF16)
    new[...] = value
    send_features(value, first_hits, (sent,))


def last_layer(
    places, a0, a1, a2, a3, local, own, inverse_rowsum, lat, first_hits, hits, w_neighbour, columns, before, decoder,
    guess, s0, s1, s2, s3,
):
    activated = activation(
        LAYERS - 1, (a0, a1, a2, a3), local, own, inverse_rowsum, first_hits, hits, w_neighbour, columns
    ).astype(BF16)
    row = before[...] + jnp.sum(activated.astype(F32) * decoder[...], axis=0, keepdims=True)
    field = tile_rows_of(row)
    guess[...] = field
    store_sent((s0, s1, s2, s3), pick(field, slot_rows(places)))


def product(matrix, field):
    count = LANES
    width = matrix.shape[1]
    total = jnp.zeros((8, width), F32)
    for t in range(field.shape[0]):
        column = jnp.broadcast_to(field[t : t + 1, :], (count, count)).T
        wide = jnp.concatenate([column] * (width // count), axis=1)
        part = matrix[t * count : (t + 1) * count, :] * wide
        total = total + jnp.sum(part.reshape(count // 8, 8, width), axis=0)
    return tile_rows_of(jnp.sum(total, axis=0, keepdims=True))


def matvec(matrix, vector, out):
    out[...] = product(matrix, vector[...])


def start_basis(places, a0, a1, a2, a3, local, guess, source, diagonal, basis, s0, s1, s2, s3):
    rows = slot_rows(places)
    came = spread_sum(arrived_rows((a0, a1, a2, a3)), rows, guess.shape[0])
    value = (source[...] + local[...] + came) / diagonal[...] - guess[...]
    basis[...] = value
    store_sent((s0, s1, s2, s3), pick(value, rows))


def next_basis(places, a0, a1, a2, a3, local, diagonal, basis, s0, s1, s2, s3):
    rows = slot_rows(places)
    came = spread_sum(arrived_rows((a0, a1, a2, a3)), rows, local.shape[0])
    value = (local[...] + came) / diagonal[...]
    basis[...] = value
    store_sent((s0, s1, s2, s3), pick(value, rows))


def diagonal_mask():
    return lax.broadcasted_iota(jnp.int32, (8, LANES), 0) == lax.broadcasted_iota(jnp.int32, (8, LANES), 1)


def last_basis(places, a0, a1, a2, a3, local, diagonal, b0, b1, matrix, basis, image, packets):
    rows = slot_rows(places)
    came = spread_sum(arrived_rows((a0, a1, a2, a3)), rows, local.shape[0])
    value = (local[...] + came) / diagonal[...]
    basis[...] = value
    mapped = product(matrix, value)
    image[...] = mapped
    held = [b0[...], b1[...], value]
    parts = []
    for k in range(2 * ITERS - 1):
        left, right = held[k // 2], held[(k + 1) // 2]
        parts.append(jnp.sum(left * right * diagonal[...], axis=0, keepdims=True))
    parts.append(jnp.sum(value * mapped, axis=0, keepdims=True))
    parts.append(jnp.zeros((8 - 2 * ITERS, LANES), F32))
    sums = jnp.sum(jnp.concatenate(parts, axis=0), axis=1, keepdims=True)
    row = jnp.sum(jnp.where(diagonal_mask(), sums, 0.0), axis=0, keepdims=True)
    packet = jnp.concatenate([lane_rows(pick(value, rows)), row], axis=1)
    for device in range(packets.shape[0]):
        packets[device] = packet


def added(values):
    values = list(values)
    while len(values) > 1:
        values = [sum(values[i : i + 2][1:], values[i]) for i in range(0, len(values), 2)]
    return values[0]


def finish(sizes, where, packets, places, image, guess, diagonal, b0, b1, b2, field, defect):
    doms, subs = sizes
    width = packets.shape[2] - LANES
    per = width // 4

    def slots(device, g):
        return packets[device, :, g * per : (g + 1) * per]

    edges = []
    for d in range(doms):
        for s in range(subs):
            for m, (i, j) in (((0, d % 2), (d + 1, s)), ((1, s % 2), (d, s + 1))):
                g = MATCHINGS.index(m)
                if i < doms and j < subs:
                    edges.append(slots(d * subs + s, g) * slots(i * subs + j, g))
    edges = added(edges)
    edges = added([edges[:, h : h + LANES] for h in range(0, per, LANES)])
    sums = added([packets[e, :, width : width + LANES] for e in range(doms * subs)])
    last_row = lax.broadcasted_iota(jnp.int32, (8, LANES), 0) == 2 * ITERS - 1
    table = jnp.where(diagonal_mask(), jnp.broadcast_to(sums, (8, LANES)), 0.0)
    table = table + jnp.where(last_row, jnp.broadcast_to(2.0 * edges, (8, LANES)), 0.0)
    columns = jnp.sum(table, axis=1, keepdims=True)
    n = [jnp.broadcast_to(columns[k : k + 1, :], (8, LANES)) for k in range(2 * ITERS)]
    came = []
    for g in range(4):
        mine = slots(where[4 + g], g)
        came += [mine[:, h : h + LANES] for h in range(0, per, LANES)]
    last = (image[...] + spread_sum(came, slot_rows(places), image.shape[0])) / diagonal[...]
    one, zero = jnp.ones((8, LANES), F32), jnp.zeros((8, LANES), F32)

    def paired(left, values):
        total = zero
        for i, a in enumerate(left):
            for j, b in enumerate(left):
                total = total + a * b * values[i + j]
        return total

    gaps = [n[k] - n[k + 1] for k in range(2 * ITERS - 1)]
    residual = [one]
    heading = [one]
    moved = [zero] * ITERS
    size = n[0]
    for step in range(ITERS):
        alpha = size / paired(heading, gaps)
        for i, h in enumerate(heading):
            moved[i] = moved[i] + alpha * h
        change = [
            (heading[i] if i < len(heading) else zero) - (heading[i - 1] if i > 0 else zero)
            for i in range(len(heading) + 1)
        ]
        residual = [
            (residual[i] if i < len(residual) else zero) - alpha * change[i]
            for i in range(len(change))
        ]
        if step + 1 < ITERS:
            following = paired(residual, n)
            beta = following / size
            heading = [
                residual[i] + (beta * heading[i] if i < len(heading) else zero)
                for i in range(len(residual))
            ]
            size = following
    held = [b0[...], b1[...], b2[...], last]
    total = guess[...]
    for c, b in zip(moved, held):
        total = total + c * b
    field[...] = total
    left = zero
    for c, b in zip(residual, held):
        left = left + c * b
    defect[...] = left * diagonal[...]


def mate_of(place, first, size):
    mate = ((place - first) ^ 1) + first
    return mate if place >= first and mate < size else None


def swaps(sizes, turn):
    along, first = MATCHINGS[turn]
    pairs = []
    for dom in range(sizes[0]):
        for sub in range(sizes[1]):
            to = [dom, sub]
            mate = mate_of(to[along], first, sizes[along])
            other = 1 - along
            if mate is not None:
                to[along] = mate
            elif to[other] ^ 1 < sizes[other]:
                to[other] ^= 1
            pairs.append((dom * sizes[1] + sub, to[0] * sizes[1] + to[1]))
    return pairs


def places_of_turns():
    at = [lax.axis_index("dom"), lax.axis_index("sub")]
    sizes = [lax.axis_size("dom"), lax.axis_size("sub")]

    def side(along, first):
        odd = at[along] % 2
        return 2 * along + (odd if first else 1 - odd)

    def partner(along, first):
        mate = jnp.bitwise_xor(at[along] - first, 1) + first
        to = list(at)
        to[along] = jnp.where((at[along] >= first) & (mate < sizes[along]), mate, at[along])
        return to[0] * sizes[1] + to[1]

    out = [value(*m) for value in (side, partner) for m in MATCHINGS]
    return jnp.stack(out).astype(jnp.int32)


def swap(sent, turn):
    axes = ("dom", "sub")
    return lax.ppermute(sent, axes, swaps([lax.axis_size(axis) for axis in axes], turn))


def exchange(sent, first=0):
    return [swap(s, first + i) for i, s in enumerate(sent)]


def all_to_all(messages):
    return lax.all_to_all(messages, ("dom", "sub"), split_axis=0, concat_axis=0, tiled=True)


def per_device(
    state, tile_values, tile_rows, tile_columns, tile_counts, send_nodes, face_counts, capacity,
    source, w_self, w_neighbour, w_out, gains, bias, w_decode,
):
    nodes, width = state.shape
    slots = send_nodes.shape[2]
    tiles = nodes // LANES
    sizes = (lax.axis_size("dom"), lax.axis_size("sub"))
    devices = sizes[0] * sizes[1]
    field = shape((tiles, LANES))
    features = shape((width, nodes))
    vector_sent = [shape((slots // LANES, LANES))] * 4
    decode = w_decode.reshape(1, width)
    where = places_of_turns()
    capacity = capacity.reshape(tiles, LANES)
    source = source.reshape(tiles, LANES)

    one_sent = [shape((width, slots), BF16)]
    gather_flops = 2 * nodes * slots * width
    lat, first_hits, places, sent = run(
        gather_first,
        [shape((width, nodes), BF16), shape((nodes, slots), BF16), shape((4 * slots // LANES, LANES), jnp.int32)]
        + one_sent,
        (), (where,), (send_nodes, face_counts, state),
        (
            pltpu.VMEM(send_nodes.shape, jnp.int32),
            pltpu.SMEM(face_counts.shape, jnp.int32),
            pltpu.VMEM(state.shape, BF16),
        ),
        waits=3, flops=gather_flops,
    )
    a0 = swap(sent, 0)
    hits, columns, *sent = run(
        gather_rest, [shape((nodes, 3 * slots), BF16), shape((width, 8))] + one_sent * 3,
        (places, lat), (), (gains, bias, decode),
        (pltpu.VMEM(gains.shape, F32), pltpu.VMEM(bias.shape, F32), pltpu.VMEM(decode.shape, F32)),
        waits=3, flops=3 * gather_flops,
    )
    a1, a2, a3 = exchange(sent, 1)
    matrix, half, inverse_rowsum, diagonal, local, own = run(
        build,
        [shape((nodes, nodes)), shape((nodes, nodes), BF16), shape((1, nodes)), field, features, features],
        (places, tile_values, lat, w_self, columns),
        (tile_counts,), (tile_rows, tile_columns, capacity),
        (
            pltpu.SMEM(tile_rows.shape, jnp.int32),
            pltpu.SMEM(tile_columns.shape, jnp.int32),
            pltpu.VMEM(capacity.shape, F32),
        ),
        waits=3, flops=0, moved=0,
    )
    lat, sent = run(
        first_layer, [shape((width, nodes), BF16)] + one_sent,
        (a0, a1, a2, a3, local, own, inverse_rowsum, lat, first_hits, hits, w_neighbour, w_out, columns),
        flops=3 * nodes * nodes * width,
    )
    a0 = swap(sent, 0)
    sent = run(send_rest, one_sent * 3, (lat, hits), flops=3 * gather_flops)
    a1, a2, a3 = exchange(sent, 1)
    local, own, before, decoder = run(
        functools.partial(local_features, LAYERS - 1),
        [features, features, shape((1, nodes)), shape((width, 1))],
        (lat, half, w_self, w_out, columns), flops=0, moved=0,
    )
    guess, *sent = run(
        last_layer, [field] + vector_sent,
        (places, a0, a1, a2, a3, local, own, inverse_rowsum, lat, first_hits, hits, w_neighbour, columns, before, decoder),
        flops=3 * nodes * nodes * width,
    )

    def mapped(vector):
        return run(matvec, [field], (matrix, vector), flops=2 * nodes * nodes, moved=4 * nodes * nodes)[0]

    arrived = exchange(sent)
    local = mapped(guess)
    b0, *sent = run(
        start_basis, [field] + vector_sent, (places, *arrived, local, guess, source, diagonal)
    )
    arrived = exchange(sent)
    local = mapped(b0)
    b1, *sent = run(next_basis, [field] + vector_sent, (places, *arrived, local, diagonal))
    arrived = exchange(sent)
    local = mapped(b1)
    b2, image, packets = run(
        last_basis, [field, field, shape((devices, 1, 4 * slots + LANES))],
        (places, *arrived, local, diagonal, b0, b1, matrix),
    )
    packets = all_to_all(packets)
    heat, defect = run(
        functools.partial(finish, sizes), [field, field],
        (packets, places, image, guess, diagonal, b0, b1, b2), (where,),
    )
    return heat.reshape(nodes), defect.reshape(nodes)


def solution(mesh):
    both = ("dom", "sub")
    return jax.shard_map(
        per_device,
        mesh=mesh,
        in_specs=(
            P(both, None),
            P(both, None, None, None),
            P(both, None),
            P(both, None),
            P(both),
            P(both, None, None),
            P(both, None),
            P(both),
            P(both),
            P(),
            P(),
            P(),
            P(),
            P(),
            P(),
        ),
        out_specs=(P(both), P(both)),
        check_vma=False,
    )
```

```python
import functools

import jax
import jax.numpy as jnp
from jax import lax
from jax.experimental import pallas as pl
from jax.experimental.pallas import tpu as pltpu
from jax.sharding import PartitionSpec as P

LAYERS = 2
ITERS = 3
LANES = 128
MATCHINGS = ((1, 1), (1, 0), (0, 0), (0, 1))
VMEM_LIMIT = 24 * 1024 * 1024

F32 = jnp.float32
BF16 = jnp.bfloat16


def shape(dims, dtype=F32):
    return jax.ShapeDtypeStruct(dims, dtype)


def run(body, outs, operands, scalars=(), raw=(), scratch=(), waits=0, flops=1_000_000, moved=1_000_000):
    smem = pl.BlockSpec(memory_space=pltpu.SMEM)
    vmem = pl.BlockSpec(memory_space=pltpu.VMEM)
    anywhere = pl.BlockSpec(memory_space=pltpu.HBM)
    scratch = list(scratch) + [pltpu.SemaphoreType.DMA((waits,))] * bool(waits)
    return pl.pallas_call(
        body,
        out_shape=outs,
        in_specs=[smem] * len(scalars) + [vmem] * len(operands) + [anywhere] * len(raw),
        out_specs=[vmem] * len(outs),
        scratch_shapes=scratch,
        compiler_params=pltpu.CompilerParams(vmem_limit_bytes=VMEM_LIMIT),
        cost_estimate=pl.CostEstimate(flops=flops, bytes_accessed=moved, transcendentals=0),
    )(*scalars, *operands, *(pltpu.with_memory_space_constraint(r, pltpu.HBM) for r in raw))


def copies(pairs, semaphores):
    started = [pltpu.make_async_copy(*pair, semaphores.at[i]) for i, pair in enumerate(pairs)]
    for copy in started:
        copy.start()
    return started


def slot_rows(places):
    return [places[r : r + 1, :] for r in range(places.shape[0])]


def pick(vector, rows):
    index = jnp.concatenate(rows, axis=0)
    low = jnp.bitwise_and(index, LANES - 1)
    high = jnp.right_shift(index, 7)
    out = jnp.zeros(index.shape, F32)
    for t in range(vector.shape[0]):
        spread = jnp.broadcast_to(vector[t : t + 1, :], index.shape)
        got = jnp.take_along_axis(spread, low, axis=1, mode="promise_in_bounds")
        out = jnp.where(high == t, got, out)
    return out


def pieces(value):
    first = value.astype(BF16)
    rest = value - first.astype(F32)
    second = rest.astype(BF16)
    third = (rest - second.astype(F32)).astype(BF16)
    return first, second, third


def low_hits(rows):
    lane = lax.broadcasted_iota(jnp.int32, (LANES, LANES), 0)
    return jnp.concatenate(
        [(lane == jnp.bitwise_and(row, LANES - 1)).astype(F32).astype(BF16) for row in rows], axis=1
    )


def spread_sum(values, rows, tiles):
    tile = lax.broadcasted_iota(jnp.int32, (tiles, LANES), 0)
    parts = [
        jnp.where(tile == jnp.right_shift(row, 7), value, 0.0) for value, row in zip(values, rows)
    ]
    held = jnp.concatenate(parts, axis=1)
    stacked = jnp.concatenate([p.astype(F32) for p in pieces(held)], axis=0).astype(BF16)
    out = lax.dot_general(
        stacked, low_hits(rows), (((1,), (1,)), ((), ())), preferred_element_type=F32
    )
    return out[:tiles] + out[tiles : 2 * tiles] + out[2 * tiles :]


def arrived_rows(refs):
    return [ref[h : h + 1, :] for ref in refs for h in range(ref.shape[0])]


def store_sent(refs, sent):
    per = refs[0].shape[0]
    for k, ref in enumerate(refs):
        ref[...] = sent[k * per : (k + 1) * per, :]


def lane_rows(vector):
    return jnp.concatenate([vector[t : t + 1, :] for t in range(vector.shape[0])], axis=1)


def tile_rows_of(row):
    return jnp.concatenate(
        [row[:, t * LANES : (t + 1) * LANES] for t in range(row.shape[1] // LANES)], axis=0
    )


def fill_hits(hits, rows, first, last):
    nodes = hits.shape[0]
    node = lax.broadcasted_iota(jnp.int32, (nodes, LANES), 0).astype(jnp.int16).reshape(nodes // 16, 16, LANES)
    one, zero = jnp.ones(node.shape, BF16), jnp.zeros(node.shape, BF16)
    for c in range(first, last):
        wide = jnp.broadcast_to(rows[c], (16, LANES)).astype(jnp.int16)
        at = (c - first) * LANES
        hits[:, at : at + LANES] = jnp.where(node == wide[None], one, zero).reshape(nodes, LANES)


def gather_first(
    where, index_in, counts_in, state_in, lat, hits, places, sent, index, counts, state, sems
):
    first, second, third = copies(((index_in, index), (counts_in, counts), (state_in, state)), sems)
    per = index.shape[2] // LANES
    first.wait()
    second.wait()
    for g in range(index.shape[1]):
        side = where[g]
        for h in range(per):
            span = slice(h * LANES, (h + 1) * LANES)
            row = index[0, 0:1, span]
            for k in range(1, index.shape[1]):
                row = jnp.where(side == k, index[0, k : k + 1, span], row)
            slot = lax.broadcasted_iota(jnp.int32, (1, LANES), 1) + h * LANES
            r = g * per + h
            places[r : r + 1, :] = jnp.where(slot < counts[0, side], row, -1)
    fill_hits(hits, slot_rows(places), 0, per)
    third.wait()
    lat[...] = state[...].T
    send_features(lat[...], hits, (sent,))


def gather_rest(places, lat, gains_in, bias_in, decode_in, hits, columns, s1, s2, s3, gains, bias, decode, sems):
    waits = copies(((gains_in, gains), (bias_in, bias), (decode_in, decode)), sems)
    rows = slot_rows(places)
    fill_hits(hits, rows, len(rows) // 4, len(rows))
    send_features(lat[...], hits, (s1, s2, s3))
    for copy in waits:
        copy.wait()
    lines = [gains[layer] for layer in range(LAYERS)] + [bias[...], decode[...]]
    lines.append(jnp.zeros((8 - 3 * LAYERS - 1, bias.shape[1]), F32))
    columns[...] = jnp.concatenate(lines, axis=0).T


def send_features(lat, hits, outs):
    width = outs[0].shape[1]
    for k, out in enumerate(outs):
        out[...] = jnp.dot(
            lat, hits[:, k * width : (k + 1) * width], preferred_element_type=F32
        ).astype(BF16)


def send_rest(lat, hits, s1, s2, s3):
    send_features(lat[...], hits, (s1, s2, s3))


def build(
    tile_counts, places, tiles, lat, w_self, columns, rows_in, columns_in, capacity_in,
    matrix, half, inverse_rowsum, diagonal, local, own,
    tile_rows, tile_columns, capacity, sems,
):
    waits = copies(((rows_in, tile_rows), (columns_in, tile_columns), (capacity_in, capacity)), sems)
    count = tiles.shape[2]
    node_tiles = matrix.shape[0] // count
    matrix[...] = jnp.zeros(matrix.shape, F32)
    for t in range(node_tiles):
        span = slice(t * count, (t + 1) * count)
        block = tiles[0, t]
        matrix[span, span] = block + block.T
    for copy in waits:
        copy.wait()

    known = tiles.shape[1]
    live = tile_counts[0]
    together = 4

    def add(step, carry):
        for k in range(together):
            t = node_tiles + step * together + k
            at = jnp.minimum(t, known - 1)
            r = pl.multiple_of(tile_rows[0, at] * count, count)
            c = pl.multiple_of(tile_columns[0, at] * count, count)
            block = jnp.where(t < live, tiles[0, at], 0.0)
            matrix[pl.ds(r, count), pl.ds(c, count)] += block
            matrix[pl.ds(c, count), pl.ds(r, count)] += block.T
        return carry

    lax.fori_loop(0, (live - node_tiles + together - 1) // together, add, 0)
    rows = slot_rows(places)
    faces = spread_sum([jnp.ones((1, LANES), F32)] * len(rows), rows, node_tiles)
    total = jnp.zeros((8, matrix.shape[1]), F32)
    for t in range(node_tiles):
        block = matrix[t * count : (t + 1) * count, :]
        half[t * count : (t + 1) * count, :] = block.astype(BF16)
        total = total + jnp.sum(block.reshape(count // 8, 8, matrix.shape[1]), axis=0)
    rowsum = tile_rows_of(jnp.sum(total, axis=0, keepdims=True)) + faces
    inverse_rowsum[...] = lane_rows(1.0 / rowsum)
    diagonal[...] = capacity[...] + rowsum
    local[...] = jnp.dot(lat[...], half[...], preferred_element_type=F32)
    own[...] = own_part(0, lat[...], w_self, columns)


def normed(value, gain):
    scale = lax.rsqrt(jnp.mean(value * value, axis=0, keepdims=True) + 1e-06)
    return (value * scale * gain).astype(BF16)


def project(weight, value):
    return lax.dot_general(weight, value, (((0,), (0,)), ((), ())), preferred_element_type=F32)


def own_part(layer, lat, w_self, columns):
    gain = columns[:, 2 * layer : 2 * layer + 1]
    bias = columns[:, 2 * LAYERS + layer : 2 * LAYERS + layer + 1]
    return project(w_self[layer], normed(lat.astype(F32), gain)) + bias


def local_features(layer, lat, half, w_self, w_out, columns, local, own, before, decoder):
    local[...] = jnp.dot(lat[...], half[...], preferred_element_type=F32)
    own[...] = own_part(layer, lat[...], w_self, columns)
    decode = columns[:, 3 * LAYERS : 3 * LAYERS + 1]
    before[...] = jnp.sum(lat[...].astype(F32) * decode, axis=0, keepdims=True)
    line = jnp.broadcast_to(decode, (decode.shape[0], LANES)).T[0:1, :]
    decoder[...] = jnp.sum(w_out[layer].astype(F32) * line, axis=1, keepdims=True)


def with_slots(local, came, hits):
    return local + lax.dot_general(came, hits, (((1,), (1,)), ((), ())), preferred_element_type=F32)


def activation(layer, arrived, local, own, inverse_rowsum, first_hits, hits, w_neighbour, columns):
    total = with_slots(local[...], arrived[0][...], first_hits[...])
    total = with_slots(total, jnp.concatenate([a[...] for a in arrived[1:]], axis=1), hits[...])
    mean = total * inverse_rowsum[...]
    gain = columns[:, 2 * layer + 1 : 2 * layer + 2]
    linear = own[...] + project(w_neighbour[layer], normed(mean, gain))
    return linear / (1.0 + jnp.exp(-linear))


def first_layer(
    a0, a1, a2, a3, local, own, inverse_rowsum, lat, first_hits, hits, w_neighbour, w_out, columns, new, sent
):
    activated = activation(
        0, (a0, a1, a2, a3), local, own, inverse_rowsum, first_hits, hits, w_neighbour, columns
    ).astype(BF16)
    value = (lat[...].astype(F32) + project(w_out[0], activated)).astype(BF16)
    new[...] = value
    send_features(value, first_hits, (sent,))


def last_layer(
    places, a0, a1, a2, a3, local, own, inverse_rowsum, lat, first_hits, hits, w_neighbour, columns, before, decoder,
    guess, s0, s1, s2, s3,
):
    activated = activation(
        LAYERS - 1, (a0, a1, a2, a3), local, own, inverse_rowsum, first_hits, hits, w_neighbour, columns
    ).astype(BF16)
    row = before[...] + jnp.sum(activated.astype(F32) * decoder[...], axis=0, keepdims=True)
    field = tile_rows_of(row)
    guess[...] = field
    store_sent((s0, s1, s2, s3), pick(field, slot_rows(places)))


def product(matrix, field):
    count = LANES
    width = matrix.shape[1]
    total = jnp.zeros((8, width), F32)
    for t in range(field.shape[0]):
        column = jnp.broadcast_to(field[t : t + 1, :], (count, count)).T
        wide = jnp.concatenate([column] * (width // count), axis=1)
        part = matrix[t * count : (t + 1) * count, :] * wide
        total = total + jnp.sum(part.reshape(count // 8, 8, width), axis=0)
    return tile_rows_of(jnp.sum(total, axis=0, keepdims=True))


def matvec(matrix, vector, out):
    out[...] = product(matrix, vector[...])


def start_basis(places, a0, a1, a2, a3, local, guess, source, diagonal, basis, s0, s1, s2, s3):
    rows = slot_rows(places)
    came = spread_sum(arrived_rows((a0, a1, a2, a3)), rows, guess.shape[0])
    value = (source[...] + local[...] + came) / diagonal[...] - guess[...]
    basis[...] = value
    store_sent((s0, s1, s2, s3), pick(value, rows))


def next_basis(places, a0, a1, a2, a3, local, diagonal, basis, s0, s1, s2, s3):
    rows = slot_rows(places)
    came = spread_sum(arrived_rows((a0, a1, a2, a3)), rows, local.shape[0])
    value = (local[...] + came) / diagonal[...]
    basis[...] = value
    store_sent((s0, s1, s2, s3), pick(value, rows))


def diagonal_mask():
    return lax.broadcasted_iota(jnp.int32, (8, LANES), 0) == lax.broadcasted_iota(jnp.int32, (8, LANES), 1)


def last_basis(places, a0, a1, a2, a3, local, diagonal, b0, b1, matrix, basis, image, packets):
    rows = slot_rows(places)
    came = spread_sum(arrived_rows((a0, a1, a2, a3)), rows, local.shape[0])
    value = (local[...] + came) / diagonal[...]
    basis[...] = value
    mapped = product(matrix, value)
    image[...] = mapped
    held = [b0[...], b1[...], value]
    parts = []
    for k in range(2 * ITERS - 1):
        left, right = held[k // 2], held[(k + 1) // 2]
        parts.append(jnp.sum(left * right * diagonal[...], axis=0, keepdims=True))
    parts.append(jnp.sum(value * mapped, axis=0, keepdims=True))
    parts.append(jnp.zeros((8 - 2 * ITERS, LANES), F32))
    sums = jnp.sum(jnp.concatenate(parts, axis=0), axis=1, keepdims=True)
    row = jnp.sum(jnp.where(diagonal_mask(), sums, 0.0), axis=0, keepdims=True)
    packet = jnp.concatenate([lane_rows(pick(value, rows)), row], axis=1)
    for device in range(packets.shape[0]):
        packets[device] = packet


def added(values):
    values = list(values)
    while len(values) > 1:
        values = [sum(values[i : i + 2][1:], values[i]) for i in range(0, len(values), 2)]
    return values[0]


def finish(sizes, where, packets, places, image, guess, diagonal, b0, b1, b2, field, defect):
    doms, subs = sizes
    width = packets.shape[2] - LANES
    per = width // 4

    def slots(device, g):
        return packets[device, :, g * per : (g + 1) * per]

    edges = []
    for d in range(doms):
        for s in range(subs):
            for m, (i, j) in (((0, d % 2), (d + 1, s)), ((1, s % 2), (d, s + 1))):
                g = MATCHINGS.index(m)
                if i < doms and j < subs:
                    edges.append(slots(d * subs + s, g) * slots(i * subs + j, g))
    edges = added(edges)
    edges = added([edges[:, h : h + LANES] for h in range(0, per, LANES)])
    sums = added([packets[e, :, width : width + LANES] for e in range(doms * subs)])
    last_row = lax.broadcasted_iota(jnp.int32, (8, LANES), 0) == 2 * ITERS - 1
    table = jnp.where(diagonal_mask(), jnp.broadcast_to(sums, (8, LANES)), 0.0)
    table = table + jnp.where(last_row, jnp.broadcast_to(2.0 * edges, (8, LANES)), 0.0)
    columns = jnp.sum(table, axis=1, keepdims=True)
    n = [jnp.broadcast_to(columns[k : k + 1, :], (8, LANES)) for k in range(2 * ITERS)]
    came = []
    for g in range(4):
        mine = slots(where[4 + g], g)
        came += [mine[:, h : h + LANES] for h in range(0, per, LANES)]
    last = (image[...] + spread_sum(came, slot_rows(places), image.shape[0])) / diagonal[...]
    one, zero = jnp.ones((8, LANES), F32), jnp.zeros((8, LANES), F32)

    def paired(left, values):
        total = zero
        for i, a in enumerate(left):
            for j, b in enumerate(left):
                total = total + a * b * values[i + j]
        return total

    gaps = [n[k] - n[k + 1] for k in range(2 * ITERS - 1)]
    residual = [one]
    heading = [one]
    moved = [zero] * ITERS
    size = n[0]
    for step in range(ITERS):
        alpha = size / paired(heading, gaps)
        for i, h in enumerate(heading):
            moved[i] = moved[i] + alpha * h
        change = [
            (heading[i] if i < len(heading) else zero) - (heading[i - 1] if i > 0 else zero)
            for i in range(len(heading) + 1)
        ]
        residual = [
            (residual[i] if i < len(residual) else zero) - alpha * change[i]
            for i in range(len(change))
        ]
        if step + 1 < ITERS:
            following = paired(residual, n)
            beta = following / size
            heading = [
                residual[i] + (beta * heading[i] if i < len(heading) else zero)
                for i in range(len(residual))
            ]
            size = following
    held = [b0[...], b1[...], b2[...], last]
    total = guess[...]
    for c, b in zip(moved, held):
        total = total + c * b
    field[...] = total
    left = zero
    for c, b in zip(residual, held):
        left = left + c * b
    defect[...] = left * diagonal[...]


def mate_of(place, first, size):
    mate = ((place - first) ^ 1) + first
    return mate if place >= first and mate < size else None


def swaps(sizes, turn):
    along, first = MATCHINGS[turn]
    pairs = []
    for dom in range(sizes[0]):
        for sub in range(sizes[1]):
            to = [dom, sub]
            mate = mate_of(to[along], first, sizes[along])
            other = 1 - along
            if mate is not None:
                to[along] = mate
            elif to[other] ^ 1 < sizes[other]:
                to[other] ^= 1
            pairs.append((dom * sizes[1] + sub, to[0] * sizes[1] + to[1]))
    return pairs


def places_of_turns():
    at = [lax.axis_index("dom"), lax.axis_index("sub")]
    sizes = [lax.axis_size("dom"), lax.axis_size("sub")]

    def side(along, first):
        odd = at[along] % 2
        return 2 * along + (odd if first else 1 - odd)

    def partner(along, first):
        mate = jnp.bitwise_xor(at[along] - first, 1) + first
        to = list(at)
        to[along] = jnp.where((at[along] >= first) & (mate < sizes[along]), mate, at[along])
        return to[0] * sizes[1] + to[1]

    out = [value(*m) for value in (side, partner) for m in MATCHINGS]
    return jnp.stack(out).astype(jnp.int32)


def swap(sent, turn):
    axes = ("dom", "sub")
    return lax.ppermute(sent, axes, swaps([lax.axis_size(axis) for axis in axes], turn))


def exchange(sent, first=0):
    return [swap(s, first + i) for i, s in enumerate(sent)]


def all_to_all(messages):
    return lax.all_to_all(messages, ("dom", "sub"), split_axis=0, concat_axis=0, tiled=True)


def per_device(
    state, tile_values, tile_rows, tile_columns, tile_counts, send_nodes, face_counts, capacity,
    source, w_self, w_neighbour, w_out, gains, bias, w_decode,
):
    nodes, width = state.shape
    slots = send_nodes.shape[2]
    tiles = nodes // LANES
    sizes = (lax.axis_size("dom"), lax.axis_size("sub"))
    devices = sizes[0] * sizes[1]
    field = shape((tiles, LANES))
    features = shape((width, nodes))
    vector_sent = [shape((slots // LANES, LANES))] * 4
    decode = w_decode.reshape(1, width)
    where = places_of_turns()
    capacity = capacity.reshape(tiles, LANES)
    source = source.reshape(tiles, LANES)

    one_sent = [shape((width, slots), BF16)]
    gather_flops = 2 * nodes * slots * width
    lat, first_hits, places, sent = run(
        gather_first,
        [shape((width, nodes), BF16), shape((nodes, slots), BF16), shape((4 * slots // LANES, LANES), jnp.int32)]
        + one_sent,
        (), (where,), (send_nodes, face_counts, state),
        (
            pltpu.VMEM(send_nodes.shape, jnp.int32),
            pltpu.SMEM(face_counts.shape, jnp.int32),
            pltpu.VMEM(state.shape, BF16),
        ),
        waits=3, flops=gather_flops,
    )
    a0 = swap(sent, 0)
    hits, columns, *sent = run(
        gather_rest, [shape((nodes, 3 * slots), BF16), shape((width, 8))] + one_sent * 3,
        (places, lat), (), (gains, bias, decode),
        (pltpu.VMEM(gains.shape, F32), pltpu.VMEM(bias.shape, F32), pltpu.VMEM(decode.shape, F32)),
        waits=3, flops=3 * gather_flops,
    )
    a1, a2, a3 = exchange(sent, 1)
    matrix, half, inverse_rowsum, diagonal, local, own = run(
        build,
        [shape((nodes, nodes)), shape((nodes, nodes), BF16), shape((1, nodes)), field, features, features],
        (places, tile_values, lat, w_self, columns),
        (tile_counts,), (tile_rows, tile_columns, capacity),
        (
            pltpu.SMEM(tile_rows.shape, jnp.int32),
            pltpu.SMEM(tile_columns.shape, jnp.int32),
            pltpu.VMEM(capacity.shape, F32),
        ),
        waits=3, flops=0, moved=0,
    )
    lat, sent = run(
        first_layer, [shape((width, nodes), BF16)] + one_sent,
        (a0, a1, a2, a3, local, own, inverse_rowsum, lat, first_hits, hits, w_neighbour, w_out, columns),
        flops=3 * nodes * nodes * width,
    )
    a0 = swap(sent, 0)
    sent = run(send_rest, one_sent * 3, (lat, hits), flops=3 * gather_flops)
    a1, a2, a3 = exchange(sent, 1)
    local, own, before, decoder = run(
        functools.partial(local_features, LAYERS - 1),
        [features, features, shape((1, nodes)), shape((width, 1))],
        (lat, half, w_self, w_out, columns), flops=0, moved=0,
    )
    guess, *sent = run(
        last_layer, [field] + vector_sent,
        (places, a0, a1, a2, a3, local, own, inverse_rowsum, lat, first_hits, hits, w_neighbour, columns, before, decoder),
        flops=3 * nodes * nodes * width,
    )

    def mapped(vector):
        return run(matvec, [field], (matrix, vector), flops=2 * nodes * nodes, moved=4 * nodes * nodes)[0]

    arrived = exchange(sent)
    local = mapped(guess)
    b0, *sent = run(
        start_basis, [field] + vector_sent, (places, *arrived, local, guess, source, diagonal)
    )
    arrived = exchange(sent)
    local = mapped(b0)
    b1, *sent = run(next_basis, [field] + vector_sent, (places, *arrived, local, diagonal))
    arrived = exchange(sent)
    local = mapped(b1)
    b2, image, packets = run(
        last_basis, [field, field, shape((devices, 1, 4 * slots + LANES))],
        (places, *arrived, local, diagonal, b0, b1, matrix),
    )
    packets = all_to_all(packets)
    heat, defect = run(
        functools.partial(finish, sizes), [field, field],
        (packets, places, image, guess, diagonal, b0, b1, b2), (where,),
    )
    return heat.reshape(nodes), defect.reshape(nodes)


def solution(mesh):
    both = ("dom", "sub")
    return jax.shard_map(
        per_device,
        mesh=mesh,
        in_specs=(
            P(both, None),
            P(both, None, None, None),
            P(both, None),
            P(both, None),
            P(both),
            P(both, None, None),
            P(both, None),
            P(both),
            P(both),
            P(),
            P(),
            P(),
            P(),
            P(),
            P(),
        ),
        out_specs=(P(both), P(both)),
        check_vma=False,
    )
```

```python
import functools

import jax
import jax.numpy as jnp
from jax import lax
from jax.experimental import pallas as pl
from jax.experimental.pallas import tpu as pltpu
from jax.sharding import PartitionSpec as P

LAYERS = 2
ITERS = 3
LANES = 128
MATCHINGS = ((1, 1), (1, 0), (0, 0), (0, 1))
VMEM_LIMIT = 24 * 1024 * 1024

F32 = jnp.float32
BF16 = jnp.bfloat16


def shape(dims, dtype=F32):
    return jax.ShapeDtypeStruct(dims, dtype)


def run(body, outs, operands, scalars=(), raw=(), scratch=(), waits=0, flops=1_000_000, moved=1_000_000):
    smem = pl.BlockSpec(memory_space=pltpu.SMEM)
    vmem = pl.BlockSpec(memory_space=pltpu.VMEM)
    anywhere = pl.BlockSpec(memory_space=pltpu.HBM)
    scratch = list(scratch) + [pltpu.SemaphoreType.DMA((waits,))] * bool(waits)
    return pl.pallas_call(
        body,
        out_shape=outs,
        in_specs=[smem] * len(scalars) + [vmem] * len(operands) + [anywhere] * len(raw),
        out_specs=[vmem] * len(outs),
        scratch_shapes=scratch,
        compiler_params=pltpu.CompilerParams(vmem_limit_bytes=VMEM_LIMIT),
        cost_estimate=pl.CostEstimate(flops=flops, bytes_accessed=moved, transcendentals=0),
    )(*scalars, *operands, *(pltpu.with_memory_space_constraint(r, pltpu.HBM) for r in raw))


def copies(pairs, semaphores):
    started = [pltpu.make_async_copy(*pair, semaphores.at[i]) for i, pair in enumerate(pairs)]
    for copy in started:
        copy.start()
    return started


def slot_rows(places):
    return [places[r : r + 1, :] for r in range(places.shape[0])]


def pick(vector, rows):
    index = jnp.concatenate(rows, axis=0)
    low = jnp.bitwise_and(index, LANES - 1)
    high = jnp.right_shift(index, 7)
    out = jnp.zeros(index.shape, F32)
    for t in range(vector.shape[0]):
        spread = jnp.broadcast_to(vector[t : t + 1, :], index.shape)
        got = jnp.take_along_axis(spread, low, axis=1, mode="promise_in_bounds")
        out = jnp.where(high == t, got, out)
    return out


def pieces(value):
    first = value.astype(BF16)
    rest = value - first.astype(F32)
    second = rest.astype(BF16)
    third = (rest - second.astype(F32)).astype(BF16)
    return first, second, third


def low_hits(rows):
    lane = lax.broadcasted_iota(jnp.int32, (LANES, LANES), 0)
    return jnp.concatenate(
        [(lane == jnp.bitwise_and(row, LANES - 1)).astype(F32).astype(BF16) for row in rows], axis=1
    )


def spread_sum(values, rows, tiles):
    tile = lax.broadcasted_iota(jnp.int32, (tiles, LANES), 0)
    parts = [
        jnp.where(tile == jnp.right_shift(row, 7), value, 0.0) for value, row in zip(values, rows)
    ]
    held = jnp.concatenate(parts, axis=1)
    stacked = jnp.concatenate([p.astype(F32) for p in pieces(held)], axis=0).astype(BF16)
    out = lax.dot_general(
        stacked, low_hits(rows), (((1,), (1,)), ((), ())), preferred_element_type=F32
    )
    return out[:tiles] + out[tiles : 2 * tiles] + out[2 * tiles :]


def arrived_rows(refs):
    return [ref[h : h + 1, :] for ref in refs for h in range(ref.shape[0])]


def store_sent(refs, sent):
    per = refs[0].shape[0]
    for k, ref in enumerate(refs):
        ref[...] = sent[k * per : (k + 1) * per, :]


def lane_rows(vector):
    return jnp.concatenate([vector[t : t + 1, :] for t in range(vector.shape[0])], axis=1)


def tile_rows_of(row):
    return jnp.concatenate(
        [row[:, t * LANES : (t + 1) * LANES] for t in range(row.shape[1] // LANES)], axis=0
    )


def fill_hits(hits, rows, first, last):
    nodes = hits.shape[0]
    node = lax.broadcasted_iota(jnp.int32, (nodes, LANES), 0).astype(jnp.int16).reshape(nodes // 16, 16, LANES)
    one, zero = jnp.ones(node.shape, BF16), jnp.zeros(node.shape, BF16)
    for c in range(first, last):
        wide = jnp.broadcast_to(rows[c], (16, LANES)).astype(jnp.int16)
        at = (c - first) * LANES
        hits[:, at : at + LANES] = jnp.where(node == wide[None], one, zero).reshape(nodes, LANES)


def gather_first(
    where, index_in, counts_in, state_in, lat, hits, places, sent, index, counts, state, sems
):
    first, second, third = copies(((index_in, index), (counts_in, counts), (state_in, state)), sems)
    per = index.shape[2] // LANES
    first.wait()
    second.wait()
    for g in range(index.shape[1]):
        side = where[g]
        for h in range(per):
            span = slice(h * LANES, (h + 1) * LANES)
            row = index[0, 0:1, span]
            for k in range(1, index.shape[1]):
                row = jnp.where(side == k, index[0, k : k + 1, span], row)
            slot = lax.broadcasted_iota(jnp.int32, (1, LANES), 1) + h * LANES
            r = g * per + h
            places[r : r + 1, :] = jnp.where(slot < counts[0, side], row, -1)
    fill_hits(hits, slot_rows(places), 0, per)
    third.wait()
    lat[...] = state[...].T
    send_features(lat[...], hits, (sent,))


def gather_rest(places, lat, gains_in, bias_in, decode_in, hits, columns, s1, s2, s3, gains, bias, decode, sems):
    waits = copies(((gains_in, gains), (bias_in, bias), (decode_in, decode)), sems)
    rows = slot_rows(places)
    fill_hits(hits, rows, len(rows) // 4, len(rows))
    send_features(lat[...], hits, (s1, s2, s3))
    for copy in waits:
        copy.wait()
    lines = [gains[layer] for layer in range(LAYERS)] + [bias[...], decode[...]]
    lines.append(jnp.zeros((8 - 3 * LAYERS - 1, bias.shape[1]), F32))
    columns[...] = jnp.concatenate(lines, axis=0).T


def send_features(lat, hits, outs):
    width = outs[0].shape[1]
    for k, out in enumerate(outs):
        out[...] = jnp.dot(
            lat, hits[:, k * width : (k + 1) * width], preferred_element_type=F32
        ).astype(BF16)


def send_rest(lat, hits, s1, s2, s3):
    send_features(lat[...], hits, (s1, s2, s3))


def build(
    tile_counts, places, tiles, lat, w_self, columns, rows_in, columns_in, capacity_in,
    matrix, half, inverse_rowsum, diagonal, local, own,
    tile_rows, tile_columns, capacity, sems,
):
    waits = copies(((rows_in, tile_rows), (columns_in, tile_columns), (capacity_in, capacity)), sems)
    count = tiles.shape[2]
    node_tiles = matrix.shape[0] // count
    matrix[...] = jnp.zeros(matrix.shape, F32)
    for t in range(node_tiles):
        span = slice(t * count, (t + 1) * count)
        block = tiles[0, t]
        matrix[span, span] = block + block.T
    for copy in waits:
        copy.wait()

    known = tiles.shape[1]
    live = tile_counts[0]
    together = 4

    def add(step, carry):
        for k in range(together):
            t = node_tiles + step * together + k
            at = jnp.minimum(t, known - 1)
            r = pl.multiple_of(tile_rows[0, at] * count, count)
            c = pl.multiple_of(tile_columns[0, at] * count, count)
            block = jnp.where(t < live, tiles[0, at], 0.0)
            matrix[pl.ds(r, count), pl.ds(c, count)] += block
            matrix[pl.ds(c, count), pl.ds(r, count)] += block.T
        return carry

    lax.fori_loop(0, (live - node_tiles + together - 1) // together, add, 0)
    rows = slot_rows(places)
    faces = spread_sum([jnp.ones((1, LANES), F32)] * len(rows), rows, node_tiles)
    total = jnp.zeros((8, matrix.shape[1]), F32)
    for t in range(node_tiles):
        block = matrix[t * count : (t + 1) * count, :]
        half[t * count : (t + 1) * count, :] = block.astype(BF16)
        total = total + jnp.sum(block.reshape(count // 8, 8, matrix.shape[1]), axis=0)
    rowsum = tile_rows_of(jnp.sum(total, axis=0, keepdims=True)) + faces
    inverse_rowsum[...] = lane_rows(1.0 / rowsum)
    diagonal[...] = capacity[...] + rowsum
    local[...] = jnp.dot(lat[...], half[...], preferred_element_type=F32)
    own[...] = own_part(0, lat[...], w_self, columns)


def normed(value, gain):
    scale = lax.rsqrt(jnp.mean(value * value, axis=0, keepdims=True) + 1e-06)
    return (value * scale * gain).astype(BF16)


def project(weight, value):
    return lax.dot_general(weight, value, (((0,), (0,)), ((), ())), preferred_element_type=F32)


def own_part(layer, lat, w_self, columns):
    gain = columns[:, 2 * layer : 2 * layer + 1]
    bias = columns[:, 2 * LAYERS + layer : 2 * LAYERS + layer + 1]
    return project(w_self[layer], normed(lat.astype(F32), gain)) + bias


def local_features(layer, lat, half, w_self, w_out, columns, local, own, before, decoder):
    local[...] = jnp.dot(lat[...], half[...], preferred_element_type=F32)
    own[...] = own_part(layer, lat[...], w_self, columns)
    decode = columns[:, 3 * LAYERS : 3 * LAYERS + 1]
    before[...] = jnp.sum(lat[...].astype(F32) * decode, axis=0, keepdims=True)
    line = jnp.broadcast_to(decode, (decode.shape[0], LANES)).T[0:1, :]
    decoder[...] = jnp.sum(w_out[layer].astype(F32) * line, axis=1, keepdims=True)


def with_slots(local, came, hits):
    return local + lax.dot_general(came, hits, (((1,), (1,)), ((), ())), preferred_element_type=F32)


def activation(layer, arrived, local, own, inverse_rowsum, first_hits, hits, w_neighbour, columns):
    total = with_slots(local[...], arrived[0][...], first_hits[...])
    total = with_slots(total, jnp.concatenate([a[...] for a in arrived[1:]], axis=1), hits[...])
    mean = total * inverse_rowsum[...]
    gain = columns[:, 2 * layer + 1 : 2 * layer + 2]
    linear = own[...] + project(w_neighbour[layer], normed(mean, gain))
    return linear / (1.0 + jnp.exp(-linear))


def first_layer(
    a0, a1, a2, a3, local, own, inverse_rowsum, lat, first_hits, hits, w_neighbour, w_out, columns, new, sent
):
    activated = activation(
        0, (a0, a1, a2, a3), local, own, inverse_rowsum, first_hits, hits, w_neighbour, columns
    ).astype(BF16)
    value = (lat[...].astype(F32) + project(w_out[0], activated)).astype(BF16)
    new[...] = value
    send_features(value, first_hits, (sent,))


def last_layer(
    places, a0, a1, a2, a3, local, own, inverse_rowsum, lat, first_hits, hits, w_neighbour, columns, before, decoder,
    guess, s0, s1, s2, s3,
):
    activated = activation(
        LAYERS - 1, (a0, a1, a2, a3), local, own, inverse_rowsum, first_hits, hits, w_neighbour, columns
    ).astype(BF16)
    row = before[...] + jnp.sum(activated.astype(F32) * decoder[...], axis=0, keepdims=True)
    field = tile_rows_of(row)
    guess[...] = field
    store_sent((s0, s1, s2, s3), pick(field, slot_rows(places)))


def product(matrix, field):
    count = LANES
    width = matrix.shape[1]
    total = jnp.zeros((8, width), F32)
    for t in range(field.shape[0]):
        column = jnp.broadcast_to(field[t : t + 1, :], (count, count)).T
        wide = jnp.concatenate([column] * (width // count), axis=1)
        part = matrix[t * count : (t + 1) * count, :] * wide
        total = total + jnp.sum(part.reshape(count // 8, 8, width), axis=0)
    return tile_rows_of(jnp.sum(total, axis=0, keepdims=True))


def matvec(matrix, vector, out):
    out[...] = product(matrix, vector[...])


def start_basis(places, a0, a1, a2, a3, local, guess, source, diagonal, basis, s0, s1, s2, s3):
    rows = slot_rows(places)
    came = spread_sum(arrived_rows((a0, a1, a2, a3)), rows, guess.shape[0])
    value = (source[...] + local[...] + came) / diagonal[...] - guess[...]
    basis[...] = value
    store_sent((s0, s1, s2, s3), pick(value, rows))


def next_basis(places, a0, a1, a2, a3, local, diagonal, basis, s0, s1, s2, s3):
    rows = slot_rows(places)
    came = spread_sum(arrived_rows((a0, a1, a2, a3)), rows, local.shape[0])
    value = (local[...] + came) / diagonal[...]
    basis[...] = value
    store_sent((s0, s1, s2, s3), pick(value, rows))


def diagonal_mask():
    return lax.broadcasted_iota(jnp.int32, (8, LANES), 0) == lax.broadcasted_iota(jnp.int32, (8, LANES), 1)


def last_basis(places, a0, a1, a2, a3, local, diagonal, b0, b1, matrix, basis, image, packets):
    rows = slot_rows(places)
    came = spread_sum(arrived_rows((a0, a1, a2, a3)), rows, local.shape[0])
    value = (local[...] + came) / diagonal[...]
    basis[...] = value
    mapped = product(matrix, value)
    image[...] = mapped
    held = [b0[...], b1[...], value]
    parts = []
    for k in range(2 * ITERS - 1):
        left, right = held[k // 2], held[(k + 1) // 2]
        parts.append(jnp.sum(left * right * diagonal[...], axis=0, keepdims=True))
    parts.append(jnp.sum(value * mapped, axis=0, keepdims=True))
    parts.append(jnp.zeros((8 - 2 * ITERS, LANES), F32))
    sums = jnp.sum(jnp.concatenate(parts, axis=0), axis=1, keepdims=True)
    row = jnp.sum(jnp.where(diagonal_mask(), sums, 0.0), axis=0, keepdims=True)
    packet = jnp.concatenate([lane_rows(pick(value, rows)), row], axis=1)
    for device in range(packets.shape[0]):
        packets[device] = packet


def added(values):
    values = list(values)
    while len(values) > 1:
        values = [sum(values[i : i + 2][1:], values[i]) for i in range(0, len(values), 2)]
    return values[0]


def finish(sizes, where, packets, places, image, guess, diagonal, b0, b1, b2, field, defect):
    doms, subs = sizes
    width = packets.shape[2] - LANES
    per = width // 4

    def slots(device, g):
        return packets[device, :, g * per : (g + 1) * per]

    edges = []
    for d in range(doms):
        for s in range(subs):
            for m, (i, j) in (((0, d % 2), (d + 1, s)), ((1, s % 2), (d, s + 1))):
                g = MATCHINGS.index(m)
                if i < doms and j < subs:
                    edges.append(slots(d * subs + s, g) * slots(i * subs + j, g))
    edges = added(edges)
    edges = added([edges[:, h : h + LANES] for h in range(0, per, LANES)])
    sums = added([packets[e, :, width : width + LANES] for e in range(doms * subs)])
    last_row = lax.broadcasted_iota(jnp.int32, (8, LANES), 0) == 2 * ITERS - 1
    table = jnp.where(diagonal_mask(), jnp.broadcast_to(sums, (8, LANES)), 0.0)
    table = table + jnp.where(last_row, jnp.broadcast_to(2.0 * edges, (8, LANES)), 0.0)
    columns = jnp.sum(table, axis=1, keepdims=True)
    n = [jnp.broadcast_to(columns[k : k + 1, :], (8, LANES)) for k in range(2 * ITERS)]
    came = []
    for g in range(4):
        mine = slots(where[4 + g], g)
        came += [mine[:, h : h + LANES] for h in range(0, per, LANES)]
    last = (image[...] + spread_sum(came, slot_rows(places), image.shape[0])) / diagonal[...]
    one, zero = jnp.ones((8, LANES), F32), jnp.zeros((8, LANES), F32)

    def paired(left, values):
        total = zero
        for i, a in enumerate(left):
            for j, b in enumerate(left):
                total = total + a * b * values[i + j]
        return total

    gaps = [n[k] - n[k + 1] for k in range(2 * ITERS - 1)]
    residual = [one]
    heading = [one]
    moved = [zero] * ITERS
    size = n[0]
    for step in range(ITERS):
        alpha = size / paired(heading, gaps)
        for i, h in enumerate(heading):
            moved[i] = moved[i] + alpha * h
        change = [
            (heading[i] if i < len(heading) else zero) - (heading[i - 1] if i > 0 else zero)
            for i in range(len(heading) + 1)
        ]
        residual = [
            (residual[i] if i < len(residual) else zero) - alpha * change[i]
            for i in range(len(change))
        ]
        if step + 1 < ITERS:
            following = paired(residual, n)
            beta = following / size
            heading = [
                residual[i] + (beta * heading[i] if i < len(heading) else zero)
                for i in range(len(residual))
            ]
            size = following
    held = [b0[...], b1[...], b2[...], last]
    total = guess[...]
    for c, b in zip(moved, held):
        total = total + c * b
    field[...] = total
    left = zero
    for c, b in zip(residual, held):
        left = left + c * b
    defect[...] = left * diagonal[...]


def mate_of(place, first, size):
    mate = ((place - first) ^ 1) + first
    return mate if place >= first and mate < size else None


def swaps(sizes, turn):
    along, first = MATCHINGS[turn]
    pairs = []
    for dom in range(sizes[0]):
        for sub in range(sizes[1]):
            to = [dom, sub]
            mate = mate_of(to[along], first, sizes[along])
            if mate is not None:
                to[along] = mate
            elif along == 0 and sizes[0] % 2 == 0:
                to[0] = sizes[0] - 1 - dom
            elif along == 1 and sizes[0] % 2 == 0:
                to[0] = dom ^ 1
            pairs.append((dom * sizes[1] + sub, to[0] * sizes[1] + to[1]))
    return pairs


def places_of_turns():
    at = [lax.axis_index("dom"), lax.axis_index("sub")]
    sizes = [lax.axis_size("dom"), lax.axis_size("sub")]

    def side(along, first):
        odd = at[along] % 2
        return 2 * along + (odd if first else 1 - odd)

    def partner(along, first):
        mate = jnp.bitwise_xor(at[along] - first, 1) + first
        to = list(at)
        to[along] = jnp.where((at[along] >= first) & (mate < sizes[along]), mate, at[along])
        return to[0] * sizes[1] + to[1]

    out = [value(*m) for value in (side, partner) for m in MATCHINGS]
    return jnp.stack(out).astype(jnp.int32)


def swap(sent, turn):
    axes = ("dom", "sub")
    return lax.ppermute(sent, axes, swaps([lax.axis_size(axis) for axis in axes], turn))


def exchange(sent, first=0):
    return [swap(s, first + i) for i, s in enumerate(sent)]


def all_to_all(messages):
    return lax.all_to_all(messages, ("dom", "sub"), split_axis=0, concat_axis=0, tiled=True)


def per_device(
    state, tile_values, tile_rows, tile_columns, tile_counts, send_nodes, face_counts, capacity,
    source, w_self, w_neighbour, w_out, gains, bias, w_decode,
):
    nodes, width = state.shape
    slots = send_nodes.shape[2]
    tiles = nodes // LANES
    sizes = (lax.axis_size("dom"), lax.axis_size("sub"))
    devices = sizes[0] * sizes[1]
    field = shape((tiles, LANES))
    features = shape((width, nodes))
    vector_sent = [shape((slots // LANES, LANES))] * 4
    decode = w_decode.reshape(1, width)
    where = places_of_turns()
    capacity = capacity.reshape(tiles, LANES)
    source = source.reshape(tiles, LANES)

    one_sent = [shape((width, slots), BF16)]
    gather_flops = 2 * nodes * slots * width
    lat, first_hits, places, sent = run(
        gather_first,
        [shape((width, nodes), BF16), shape((nodes, slots), BF16), shape((4 * slots // LANES, LANES), jnp.int32)]
        + one_sent,
        (), (where,), (send_nodes, face_counts, state),
        (
            pltpu.VMEM(send_nodes.shape, jnp.int32),
            pltpu.SMEM(face_counts.shape, jnp.int32),
            pltpu.VMEM(state.shape, BF16),
        ),
        waits=3, flops=gather_flops,
    )
    a0 = swap(sent, 0)
    hits, columns, *sent = run(
        gather_rest, [shape((nodes, 3 * slots), BF16), shape((width, 8))] + one_sent * 3,
        (places, lat), (), (gains, bias, decode),
        (pltpu.VMEM(gains.shape, F32), pltpu.VMEM(bias.shape, F32), pltpu.VMEM(decode.shape, F32)),
        waits=3, flops=3 * gather_flops,
    )
    a1, a2, a3 = exchange(sent, 1)
    matrix, half, inverse_rowsum, diagonal, local, own = run(
        build,
        [shape((nodes, nodes)), shape((nodes, nodes), BF16), shape((1, nodes)), field, features, features],
        (places, tile_values, lat, w_self, columns),
        (tile_counts,), (tile_rows, tile_columns, capacity),
        (
            pltpu.SMEM(tile_rows.shape, jnp.int32),
            pltpu.SMEM(tile_columns.shape, jnp.int32),
            pltpu.VMEM(capacity.shape, F32),
        ),
        waits=3, flops=0, moved=0,
    )
    lat, sent = run(
        first_layer, [shape((width, nodes), BF16)] + one_sent,
        (a0, a1, a2, a3, local, own, inverse_rowsum, lat, first_hits, hits, w_neighbour, w_out, columns),
        flops=3 * nodes * nodes * width,
    )
    a0 = swap(sent, 0)
    sent = run(send_rest, one_sent * 3, (lat, hits), flops=3 * gather_flops)
    a1, a2, a3 = exchange(sent, 1)
    local, own, before, decoder = run(
        functools.partial(local_features, LAYERS - 1),
        [features, features, shape((1, nodes)), shape((width, 1))],
        (lat, half, w_self, w_out, columns), flops=0, moved=0,
    )
    guess, *sent = run(
        last_layer, [field] + vector_sent,
        (places, a0, a1, a2, a3, local, own, inverse_rowsum, lat, first_hits, hits, w_neighbour, columns, before, decoder),
        flops=3 * nodes * nodes * width,
    )

    def mapped(vector):
        return run(matvec, [field], (matrix, vector), flops=2 * nodes * nodes, moved=4 * nodes * nodes)[0]

    arrived = exchange(sent)
    local = mapped(guess)
    b0, *sent = run(
        start_basis, [field] + vector_sent, (places, *arrived, local, guess, source, diagonal)
    )
    arrived = exchange(sent)
    local = mapped(b0)
    b1, *sent = run(next_basis, [field] + vector_sent, (places, *arrived, local, diagonal))
    arrived = exchange(sent)
    local = mapped(b1)
    b2, image, packets = run(
        last_basis, [field, field, shape((devices, 1, 4 * slots + LANES))],
        (places, *arrived, local, diagonal, b0, b1, matrix),
    )
    packets = all_to_all(packets)
    heat, defect = run(
        functools.partial(finish, sizes), [field, field],
        (packets, places, image, guess, diagonal, b0, b1, b2), (where,),
    )
    return heat.reshape(nodes), defect.reshape(nodes)


def solution(mesh):
    both = ("dom", "sub")
    return jax.shard_map(
        per_device,
        mesh=mesh,
        in_specs=(
            P(both, None),
            P(both, None, None, None),
            P(both, None),
            P(both, None),
            P(both),
            P(both, None, None),
            P(both, None),
            P(both),
            P(both),
            P(),
            P(),
            P(),
            P(),
            P(),
            P(),
        ),
        out_specs=(P(both), P(both)),
        check_vma=False,
    )
```

```python
import functools

import jax
import jax.numpy as jnp
from jax import lax
from jax.experimental import pallas as pl
from jax.experimental.pallas import tpu as pltpu
from jax.sharding import PartitionSpec as P

LAYERS = 2
ITERS = 3
LANES = 128
MATCHINGS = ((1, 1), (1, 0), (0, 0), (0, 1))
VMEM_LIMIT = 24 * 1024 * 1024

F32 = jnp.float32
BF16 = jnp.bfloat16


def shape(dims, dtype=F32):
    return jax.ShapeDtypeStruct(dims, dtype)


def run(body, outs, operands, scalars=(), raw=(), scratch=(), waits=0, flops=1_000_000, moved=1_000_000):
    smem = pl.BlockSpec(memory_space=pltpu.SMEM)
    vmem = pl.BlockSpec(memory_space=pltpu.VMEM)
    anywhere = pl.BlockSpec(memory_space=pltpu.HBM)
    scratch = list(scratch) + [pltpu.SemaphoreType.DMA((waits,))] * bool(waits)
    return pl.pallas_call(
        body,
        out_shape=outs,
        in_specs=[smem] * len(scalars) + [vmem] * len(operands) + [anywhere] * len(raw),
        out_specs=[vmem] * len(outs),
        scratch_shapes=scratch,
        compiler_params=pltpu.CompilerParams(vmem_limit_bytes=VMEM_LIMIT),
        cost_estimate=pl.CostEstimate(flops=flops, bytes_accessed=moved, transcendentals=0),
    )(*scalars, *operands, *(pltpu.with_memory_space_constraint(r, pltpu.HBM) for r in raw))


def copies(pairs, semaphores):
    started = [pltpu.make_async_copy(*pair, semaphores.at[i]) for i, pair in enumerate(pairs)]
    for copy in started:
        copy.start()
    return started


def slot_rows(places):
    return [places[r : r + 1, :] for r in range(places.shape[0])]


def pick(vector, rows):
    index = jnp.concatenate(rows, axis=0)
    low = jnp.bitwise_and(index, LANES - 1)
    high = jnp.right_shift(index, 7)
    out = jnp.zeros(index.shape, F32)
    for t in range(vector.shape[0]):
        spread = jnp.broadcast_to(vector[t : t + 1, :], index.shape)
        got = jnp.take_along_axis(spread, low, axis=1, mode="promise_in_bounds")
        out = jnp.where(high == t, got, out)
    return out


def pieces(value):
    first = value.astype(BF16)
    rest = value - first.astype(F32)
    second = rest.astype(BF16)
    third = (rest - second.astype(F32)).astype(BF16)
    return first, second, third


def low_hits(rows):
    lane = lax.broadcasted_iota(jnp.int32, (LANES, LANES), 0)
    return jnp.concatenate(
        [(lane == jnp.bitwise_and(row, LANES - 1)).astype(F32).astype(BF16) for row in rows], axis=1
    )


def spread_sum(values, rows, tiles):
    tile = lax.broadcasted_iota(jnp.int32, (tiles, LANES), 0)
    parts = [
        jnp.where(tile == jnp.right_shift(row, 7), value, 0.0) for value, row in zip(values, rows)
    ]
    held = jnp.concatenate(parts, axis=1)
    stacked = jnp.concatenate([p.astype(F32) for p in pieces(held)], axis=0).astype(BF16)
    out = lax.dot_general(
        stacked, low_hits(rows), (((1,), (1,)), ((), ())), preferred_element_type=F32
    )
    return out[:tiles] + out[tiles : 2 * tiles] + out[2 * tiles :]


def arrived_rows(refs):
    return [ref[h : h + 1, :] for ref in refs for h in range(ref.shape[0])]


def store_sent(refs, sent):
    per = refs[0].shape[0]
    for k, ref in enumerate(refs):
        ref[...] = sent[k * per : (k + 1) * per, :]


def lane_rows(vector):
    return jnp.concatenate([vector[t : t + 1, :] for t in range(vector.shape[0])], axis=1)


def tile_rows_of(row):
    return jnp.concatenate(
        [row[:, t * LANES : (t + 1) * LANES] for t in range(row.shape[1] // LANES)], axis=0
    )


def fill_hits(hits, rows, first, last):
    nodes = hits.shape[0]
    node = lax.broadcasted_iota(jnp.int32, (nodes, LANES), 0).astype(jnp.int16).reshape(nodes // 16, 16, LANES)
    one, zero = jnp.ones(node.shape, BF16), jnp.zeros(node.shape, BF16)
    for c in range(first, last):
        wide = jnp.broadcast_to(rows[c], (16, LANES)).astype(jnp.int16)
        at = (c - first) * LANES
        hits[:, at : at + LANES] = jnp.where(node == wide[None], one, zero).reshape(nodes, LANES)


def gather_first(
    where, index_in, counts_in, state_in, lat, hits, places, sent, index, counts, state, sems
):
    first, second, third = copies(((index_in, index), (counts_in, counts), (state_in, state)), sems)
    per = index.shape[2] // LANES
    first.wait()
    second.wait()
    for g in range(index.shape[1]):
        side = where[g]
        for h in range(per):
            span = slice(h * LANES, (h + 1) * LANES)
            row = index[0, 0:1, span]
            for k in range(1, index.shape[1]):
                row = jnp.where(side == k, index[0, k : k + 1, span], row)
            slot = lax.broadcasted_iota(jnp.int32, (1, LANES), 1) + h * LANES
            r = g * per + h
            places[r : r + 1, :] = jnp.where(slot < counts[0, side], row, -1)
    fill_hits(hits, slot_rows(places), 0, per)
    third.wait()
    lat[...] = state[...].T
    send_features(lat[...], hits, (sent,))


def gather_rest(places, lat, gains_in, bias_in, decode_in, hits, columns, s1, s2, s3, gains, bias, decode, sems):
    waits = copies(((gains_in, gains), (bias_in, bias), (decode_in, decode)), sems)
    rows = slot_rows(places)
    fill_hits(hits, rows, len(rows) // 4, len(rows))
    send_features(lat[...], hits, (s1, s2, s3))
    for copy in waits:
        copy.wait()
    lines = [gains[layer] for layer in range(LAYERS)] + [bias[...], decode[...]]
    lines.append(jnp.zeros((8 - 3 * LAYERS - 1, bias.shape[1]), F32))
    columns[...] = jnp.concatenate(lines, axis=0).T


def send_features(lat, hits, outs):
    width = outs[0].shape[1]
    for k, out in enumerate(outs):
        out[...] = jnp.dot(
            lat, hits[:, k * width : (k + 1) * width], preferred_element_type=F32
        ).astype(BF16)


def send_rest(lat, hits, s1, s2, s3):
    send_features(lat[...], hits, (s1, s2, s3))


def build(
    tile_counts, places, tiles, lat, w_self, columns, rows_in, columns_in, capacity_in,
    matrix, half, inverse_rowsum, diagonal, local, own,
    tile_rows, tile_columns, capacity, sems,
):
    waits = copies(((rows_in, tile_rows), (columns_in, tile_columns), (capacity_in, capacity)), sems)
    count = tiles.shape[2]
    node_tiles = matrix.shape[0] // count
    matrix[...] = jnp.zeros(matrix.shape, F32)
    for t in range(node_tiles):
        span = slice(t * count, (t + 1) * count)
        block = tiles[0, t]
        matrix[span, span] = block + block.T
    for copy in waits:
        copy.wait()

    known = tiles.shape[1]
    live = tile_counts[0]
    together = 4

    def add(step, carry):
        for k in range(together):
            t = node_tiles + step * together + k
            at = jnp.minimum(t, known - 1)
            r = pl.multiple_of(tile_rows[0, at] * count, count)
            c = pl.multiple_of(tile_columns[0, at] * count, count)
            block = jnp.where(t < live, tiles[0, at], 0.0)
            matrix[pl.ds(r, count), pl.ds(c, count)] += block
            matrix[pl.ds(c, count), pl.ds(r, count)] += block.T
        return carry

    lax.fori_loop(0, (live - node_tiles + together - 1) // together, add, 0)
    rows = slot_rows(places)
    faces = spread_sum([jnp.ones((1, LANES), F32)] * len(rows), rows, node_tiles)
    total = jnp.zeros((8, matrix.shape[1]), F32)
    for t in range(node_tiles):
        block = matrix[t * count : (t + 1) * count, :]
        half[t * count : (t + 1) * count, :] = block.astype(BF16)
        total = total + jnp.sum(block.reshape(count // 8, 8, matrix.shape[1]), axis=0)
    rowsum = tile_rows_of(jnp.sum(total, axis=0, keepdims=True)) + faces
    inverse_rowsum[...] = lane_rows(1.0 / rowsum)
    diagonal[...] = capacity[...] + rowsum
    local[...] = jnp.dot(lat[...], half[...], preferred_element_type=F32)
    own[...] = own_part(0, lat[...], w_self, columns)


def normed(value, gain):
    scale = lax.rsqrt(jnp.mean(value * value, axis=0, keepdims=True) + 1e-06)
    return (value * scale * gain).astype(BF16)


def project(weight, value):
    return lax.dot_general(weight, value, (((0,), (0,)), ((), ())), preferred_element_type=F32)


def own_part(layer, lat, w_self, columns):
    gain = columns[:, 2 * layer : 2 * layer + 1]
    bias = columns[:, 2 * LAYERS + layer : 2 * LAYERS + layer + 1]
    return project(w_self[layer], normed(lat.astype(F32), gain)) + bias


def local_features(layer, lat, half, w_self, w_out, columns, local, own, before, decoder):
    local[...] = jnp.dot(lat[...], half[...], preferred_element_type=F32)
    own[...] = own_part(layer, lat[...], w_self, columns)
    decode = columns[:, 3 * LAYERS : 3 * LAYERS + 1]
    before[...] = jnp.sum(lat[...].astype(F32) * decode, axis=0, keepdims=True)
    line = jnp.broadcast_to(decode, (decode.shape[0], LANES)).T[0:1, :]
    decoder[...] = jnp.sum(w_out[layer].astype(F32) * line, axis=1, keepdims=True)


def with_slots(local, came, hits):
    return local + lax.dot_general(came, hits, (((1,), (1,)), ((), ())), preferred_element_type=F32)


def add_early(a0, a2, a3, local, first_hits, hits, out):
    width = a0.shape[1]
    total = with_slots(local[...], a0[...], first_hits[...])
    out[...] = with_slots(total, jnp.concatenate([a2[...], a3[...]], axis=1), hits[:, width:])


def activation(layer, late, local, own, inverse_rowsum, hits, w_neighbour, columns):
    total = with_slots(local[...], late[...], hits[:, : late.shape[1]])
    mean = total * inverse_rowsum[...]
    gain = columns[:, 2 * layer + 1 : 2 * layer + 2]
    linear = own[...] + project(w_neighbour[layer], normed(mean, gain))
    return linear / (1.0 + jnp.exp(-linear))


def first_layer(
    late, local, own, inverse_rowsum, lat, first_hits, hits, w_neighbour, w_out, columns, new, sent
):
    activated = activation(0, late, local, own, inverse_rowsum, hits, w_neighbour, columns).astype(BF16)
    value = (lat[...].astype(F32) + project(w_out[0], activated)).astype(BF16)
    new[...] = value
    send_features(value, first_hits, (sent,))


def last_layer(
    places, late, local, own, inverse_rowsum, lat, hits, w_neighbour, columns, before, decoder,
    guess, s0, s1, s2, s3,
):
    activated = activation(LAYERS - 1, late, local, own, inverse_rowsum, hits, w_neighbour, columns).astype(BF16)
    row = before[...] + jnp.sum(activated.astype(F32) * decoder[...], axis=0, keepdims=True)
    field = tile_rows_of(row)
    guess[...] = field
    store_sent((s0, s1, s2, s3), pick(field, slot_rows(places)))


def product(matrix, field):
    count = LANES
    width = matrix.shape[1]
    total = jnp.zeros((8, width), F32)
    for t in range(field.shape[0]):
        column = jnp.broadcast_to(field[t : t + 1, :], (count, count)).T
        wide = jnp.concatenate([column] * (width // count), axis=1)
        part = matrix[t * count : (t + 1) * count, :] * wide
        total = total + jnp.sum(part.reshape(count // 8, 8, width), axis=0)
    return tile_rows_of(jnp.sum(total, axis=0, keepdims=True))


def matvec(matrix, vector, out):
    out[...] = product(matrix, vector[...])


def start_basis(places, a0, a1, a2, a3, local, guess, source, diagonal, basis, s0, s1, s2, s3):
    rows = slot_rows(places)
    came = spread_sum(arrived_rows((a0, a1, a2, a3)), rows, guess.shape[0])
    value = (source[...] + local[...] + came) / diagonal[...] - guess[...]
    basis[...] = value
    store_sent((s0, s1, s2, s3), pick(value, rows))


def next_basis(places, a0, a1, a2, a3, local, diagonal, basis, s0, s1, s2, s3):
    rows = slot_rows(places)
    came = spread_sum(arrived_rows((a0, a1, a2, a3)), rows, local.shape[0])
    value = (local[...] + came) / diagonal[...]
    basis[...] = value
    store_sent((s0, s1, s2, s3), pick(value, rows))


def diagonal_mask():
    return lax.broadcasted_iota(jnp.int32, (8, LANES), 0) == lax.broadcasted_iota(jnp.int32, (8, LANES), 1)


def last_basis(places, a0, a1, a2, a3, local, diagonal, b0, b1, matrix, basis, image, packets):
    rows = slot_rows(places)
    came = spread_sum(arrived_rows((a0, a1, a2, a3)), rows, local.shape[0])
    value = (local[...] + came) / diagonal[...]
    basis[...] = value
    mapped = product(matrix, value)
    image[...] = mapped
    held = [b0[...], b1[...], value]
    parts = []
    for k in range(2 * ITERS - 1):
        left, right = held[k // 2], held[(k + 1) // 2]
        parts.append(jnp.sum(left * right * diagonal[...], axis=0, keepdims=True))
    parts.append(jnp.sum(value * mapped, axis=0, keepdims=True))
    parts.append(jnp.zeros((8 - 2 * ITERS, LANES), F32))
    sums = jnp.sum(jnp.concatenate(parts, axis=0), axis=1, keepdims=True)
    row = jnp.sum(jnp.where(diagonal_mask(), sums, 0.0), axis=0, keepdims=True)
    packet = jnp.concatenate([lane_rows(pick(value, rows)), row], axis=1)
    for device in range(packets.shape[0]):
        packets[device] = packet


def added(values):
    values = list(values)
    while len(values) > 1:
        values = [sum(values[i : i + 2][1:], values[i]) for i in range(0, len(values), 2)]
    return values[0]


def finish(sizes, where, packets, places, image, guess, diagonal, b0, b1, b2, field, defect):
    doms, subs = sizes
    width = packets.shape[2] - LANES
    per = width // 4

    def slots(device, g):
        return packets[device, :, g * per : (g + 1) * per]

    edges = []
    for d in range(doms):
        for s in range(subs):
            for m, (i, j) in (((0, d % 2), (d + 1, s)), ((1, s % 2), (d, s + 1))):
                g = MATCHINGS.index(m)
                if i < doms and j < subs:
                    edges.append(slots(d * subs + s, g) * slots(i * subs + j, g))
    edges = added(edges)
    edges = added([edges[:, h : h + LANES] for h in range(0, per, LANES)])
    sums = added([packets[e, :, width : width + LANES] for e in range(doms * subs)])
    last_row = lax.broadcasted_iota(jnp.int32, (8, LANES), 0) == 2 * ITERS - 1
    table = jnp.where(diagonal_mask(), jnp.broadcast_to(sums, (8, LANES)), 0.0)
    table = table + jnp.where(last_row, jnp.broadcast_to(2.0 * edges, (8, LANES)), 0.0)
    columns = jnp.sum(table, axis=1, keepdims=True)
    n = [jnp.broadcast_to(columns[k : k + 1, :], (8, LANES)) for k in range(2 * ITERS)]
    came = []
    for g in range(4):
        mine = slots(where[4 + g], g)
        came += [mine[:, h : h + LANES] for h in range(0, per, LANES)]
    last = (image[...] + spread_sum(came, slot_rows(places), image.shape[0])) / diagonal[...]
    one, zero = jnp.ones((8, LANES), F32), jnp.zeros((8, LANES), F32)

    def paired(left, values):
        total = zero
        for i, a in enumerate(left):
            for j, b in enumerate(left):
                total = total + a * b * values[i + j]
        return total

    gaps = [n[k] - n[k + 1] for k in range(2 * ITERS - 1)]
    residual = [one]
    heading = [one]
    moved = [zero] * ITERS
    size = n[0]
    for step in range(ITERS):
        alpha = size / paired(heading, gaps)
        for i, h in enumerate(heading):
            moved[i] = moved[i] + alpha * h
        change = [
            (heading[i] if i < len(heading) else zero) - (heading[i - 1] if i > 0 else zero)
            for i in range(len(heading) + 1)
        ]
        residual = [
            (residual[i] if i < len(residual) else zero) - alpha * change[i]
            for i in range(len(change))
        ]
        if step + 1 < ITERS:
            following = paired(residual, n)
            beta = following / size
            heading = [
                residual[i] + (beta * heading[i] if i < len(heading) else zero)
                for i in range(len(residual))
            ]
            size = following
    held = [b0[...], b1[...], b2[...], last]
    total = guess[...]
    for c, b in zip(moved, held):
        total = total + c * b
    field[...] = total
    left = zero
    for c, b in zip(residual, held):
        left = left + c * b
    defect[...] = left * diagonal[...]


def mate_of(place, first, size):
    mate = ((place - first) ^ 1) + first
    return mate if place >= first and mate < size else None


def swaps(sizes, turn):
    along, first = MATCHINGS[turn]
    pairs = []
    for dom in range(sizes[0]):
        for sub in range(sizes[1]):
            to = [dom, sub]
            mate = mate_of(to[along], first, sizes[along])
            other = 1 - along
            if mate is not None:
                to[along] = mate
            elif to[other] ^ 1 < sizes[other]:
                to[other] ^= 1
            pairs.append((dom * sizes[1] + sub, to[0] * sizes[1] + to[1]))
    return pairs


def places_of_turns():
    at = [lax.axis_index("dom"), lax.axis_index("sub")]
    sizes = [lax.axis_size("dom"), lax.axis_size("sub")]

    def side(along, first):
        odd = at[along] % 2
        return 2 * along + (odd if first else 1 - odd)

    def partner(along, first):
        mate = jnp.bitwise_xor(at[along] - first, 1) + first
        to = list(at)
        to[along] = jnp.where((at[along] >= first) & (mate < sizes[along]), mate, at[along])
        return to[0] * sizes[1] + to[1]

    out = [value(*m) for value in (side, partner) for m in MATCHINGS]
    return jnp.stack(out).astype(jnp.int32)


def swap(sent, turn):
    axes = ("dom", "sub")
    return lax.ppermute(sent, axes, swaps([lax.axis_size(axis) for axis in axes], turn))


def exchange(sent, first=0):
    return [swap(s, first + i) for i, s in enumerate(sent)]


def all_to_all(messages):
    return lax.all_to_all(messages, ("dom", "sub"), split_axis=0, concat_axis=0, tiled=True)


def per_device(
    state, tile_values, tile_rows, tile_columns, tile_counts, send_nodes, face_counts, capacity,
    source, w_self, w_neighbour, w_out, gains, bias, w_decode,
):
    nodes, width = state.shape
    slots = send_nodes.shape[2]
    tiles = nodes // LANES
    sizes = (lax.axis_size("dom"), lax.axis_size("sub"))
    devices = sizes[0] * sizes[1]
    field = shape((tiles, LANES))
    features = shape((width, nodes))
    vector_sent = [shape((slots // LANES, LANES))] * 4
    decode = w_decode.reshape(1, width)
    where = places_of_turns()
    capacity = capacity.reshape(tiles, LANES)
    source = source.reshape(tiles, LANES)

    one_sent = [shape((width, slots), BF16)]
    gather_flops = 2 * nodes * slots * width
    lat, first_hits, places, sent = run(
        gather_first,
        [shape((width, nodes), BF16), shape((nodes, slots), BF16), shape((4 * slots // LANES, LANES), jnp.int32)]
        + one_sent,
        (), (where,), (send_nodes, face_counts, state),
        (
            pltpu.VMEM(send_nodes.shape, jnp.int32),
            pltpu.SMEM(face_counts.shape, jnp.int32),
            pltpu.VMEM(state.shape, BF16),
        ),
        waits=3, flops=gather_flops,
    )
    a0 = swap(sent, 0)
    hits, columns, *sent = run(
        gather_rest, [shape((nodes, 3 * slots), BF16), shape((width, 8))] + one_sent * 3,
        (places, lat), (), (gains, bias, decode),
        (pltpu.VMEM(gains.shape, F32), pltpu.VMEM(bias.shape, F32), pltpu.VMEM(decode.shape, F32)),
        waits=3, flops=3 * gather_flops,
    )
    a1, a2, a3 = exchange(sent, 1)
    matrix, half, inverse_rowsum, diagonal, local, own = run(
        build,
        [shape((nodes, nodes)), shape((nodes, nodes), BF16), shape((1, nodes)), field, features, features],
        (places, tile_values, lat, w_self, columns),
        (tile_counts,), (tile_rows, tile_columns, capacity),
        (
            pltpu.SMEM(tile_rows.shape, jnp.int32),
            pltpu.SMEM(tile_columns.shape, jnp.int32),
            pltpu.VMEM(capacity.shape, F32),
        ),
        waits=3, flops=0, moved=0,
    )
    (local,) = run(add_early, [features], (a0, a2, a3, local, first_hits, hits), flops=3 * gather_flops)
    lat, sent = run(
        first_layer, [shape((width, nodes), BF16)] + one_sent,
        (a1, local, own, inverse_rowsum, lat, first_hits, hits, w_neighbour, w_out, columns),
        flops=3 * nodes * nodes * width,
    )
    a0 = swap(sent, 0)
    sent = run(send_rest, one_sent * 3, (lat, hits), flops=3 * gather_flops)
    a1, a2, a3 = exchange(sent, 1)
    local, own, before, decoder = run(
        functools.partial(local_features, LAYERS - 1),
        [features, features, shape((1, nodes)), shape((width, 1))],
        (lat, half, w_self, w_out, columns), flops=0, moved=0,
    )
    (local,) = run(add_early, [features], (a0, a2, a3, local, first_hits, hits), flops=3 * gather_flops)
    guess, *sent = run(
        last_layer, [field] + vector_sent,
        (places, a1, local, own, inverse_rowsum, lat, hits, w_neighbour, columns, before, decoder),
        flops=3 * nodes * nodes * width,
    )

    def mapped(vector):
        return run(matvec, [field], (matrix, vector), flops=2 * nodes * nodes, moved=4 * nodes * nodes)[0]

    arrived = exchange(sent)
    local = mapped(guess)
    b0, *sent = run(
        start_basis, [field] + vector_sent, (places, *arrived, local, guess, source, diagonal)
    )
    arrived = exchange(sent)
    local = mapped(b0)
    b1, *sent = run(next_basis, [field] + vector_sent, (places, *arrived, local, diagonal))
    arrived = exchange(sent)
    local = mapped(b1)
    b2, image, packets = run(
        last_basis, [field, field, shape((devices, 1, 4 * slots + LANES))],
        (places, *arrived, local, diagonal, b0, b1, matrix),
    )
    packets = all_to_all(packets)
    heat, defect = run(
        functools.partial(finish, sizes), [field, field],
        (packets, places, image, guess, diagonal, b0, b1, b2), (where,),
    )
    return heat.reshape(nodes), defect.reshape(nodes)


def solution(mesh):
    both = ("dom", "sub")
    return jax.shard_map(
        per_device,
        mesh=mesh,
        in_specs=(
            P(both, None),
            P(both, None, None, None),
            P(both, None),
            P(both, None),
            P(both),
            P(both, None, None),
            P(both, None),
            P(both),
            P(both),
            P(),
            P(),
            P(),
            P(),
            P(),
            P(),
        ),
        out_specs=(P(both), P(both)),
        check_vma=False,
    )
```

```python
import functools

import jax
import jax.numpy as jnp
from jax import lax
from jax.experimental import pallas as pl
from jax.experimental.pallas import tpu as pltpu
from jax.sharding import PartitionSpec as P

LAYERS = 2
ITERS = 3
LANES = 128
MATCHINGS = ((1, 1), (1, 0), (0, 0), (0, 1))
VMEM_LIMIT = 24 * 1024 * 1024

F32 = jnp.float32
BF16 = jnp.bfloat16


def shape(dims, dtype=F32):
    return jax.ShapeDtypeStruct(dims, dtype)


def run(body, outs, operands, scalars=(), raw=(), scratch=(), waits=0, flops=1_000_000, moved=1_000_000):
    smem = pl.BlockSpec(memory_space=pltpu.SMEM)
    vmem = pl.BlockSpec(memory_space=pltpu.VMEM)
    anywhere = pl.BlockSpec(memory_space=pltpu.HBM)
    scratch = list(scratch) + [pltpu.SemaphoreType.DMA((waits,))] * bool(waits)
    return pl.pallas_call(
        body,
        out_shape=outs,
        in_specs=[smem] * len(scalars) + [vmem] * len(operands) + [anywhere] * len(raw),
        out_specs=[vmem] * len(outs),
        scratch_shapes=scratch,
        compiler_params=pltpu.CompilerParams(vmem_limit_bytes=VMEM_LIMIT),
        cost_estimate=pl.CostEstimate(flops=flops, bytes_accessed=moved, transcendentals=0),
    )(*scalars, *operands, *(pltpu.with_memory_space_constraint(r, pltpu.HBM) for r in raw))


def copies(pairs, semaphores):
    started = [pltpu.make_async_copy(*pair, semaphores.at[i]) for i, pair in enumerate(pairs)]
    for copy in started:
        copy.start()
    return started


def slot_rows(places):
    return [places[r : r + 1, :] for r in range(places.shape[0])]


def pick(vector, rows):
    index = jnp.concatenate(rows, axis=0)
    low = jnp.bitwise_and(index, LANES - 1)
    high = jnp.right_shift(index, 7)
    out = jnp.zeros(index.shape, F32)
    for t in range(vector.shape[0]):
        spread = jnp.broadcast_to(vector[t : t + 1, :], index.shape)
        got = jnp.take_along_axis(spread, low, axis=1, mode="promise_in_bounds")
        out = jnp.where(high == t, got, out)
    return out


def pieces(value):
    first = value.astype(BF16)
    rest = value - first.astype(F32)
    second = rest.astype(BF16)
    third = (rest - second.astype(F32)).astype(BF16)
    return first, second, third


def low_hits(rows):
    lane = lax.broadcasted_iota(jnp.int32, (LANES, LANES), 0)
    return jnp.concatenate(
        [(lane == jnp.bitwise_and(row, LANES - 1)).astype(F32).astype(BF16) for row in rows], axis=1
    )


def spread_sum(values, rows, tiles):
    tile = lax.broadcasted_iota(jnp.int32, (tiles, LANES), 0)
    parts = [
        jnp.where(tile == jnp.right_shift(row, 7), value, 0.0) for value, row in zip(values, rows)
    ]
    held = jnp.concatenate(parts, axis=1)
    stacked = jnp.concatenate([p.astype(F32) for p in pieces(held)], axis=0).astype(BF16)
    out = lax.dot_general(
        stacked, low_hits(rows), (((1,), (1,)), ((), ())), preferred_element_type=F32
    )
    return out[:tiles] + out[tiles : 2 * tiles] + out[2 * tiles :]


def arrived_rows(refs):
    return [ref[h : h + 1, :] for ref in refs for h in range(ref.shape[0])]


def store_sent(refs, sent):
    per = refs[0].shape[0]
    for k, ref in enumerate(refs):
        ref[...] = sent[k * per : (k + 1) * per, :]


def lane_rows(vector):
    return jnp.concatenate([vector[t : t + 1, :] for t in range(vector.shape[0])], axis=1)


def tile_rows_of(row):
    return jnp.concatenate(
        [row[:, t * LANES : (t + 1) * LANES] for t in range(row.shape[1] // LANES)], axis=0
    )


def fill_hits(hits, rows, first, last):
    nodes = hits.shape[0]
    node = lax.broadcasted_iota(jnp.int32, (nodes, LANES), 0).astype(jnp.int16).reshape(nodes // 16, 16, LANES)
    one, zero = jnp.ones(node.shape, BF16), jnp.zeros(node.shape, BF16)
    for c in range(first, last):
        wide = jnp.broadcast_to(rows[c], (16, LANES)).astype(jnp.int16)
        at = (c - first) * LANES
        hits[:, at : at + LANES] = jnp.where(node == wide[None], one, zero).reshape(nodes, LANES)


def gather_first(
    where, index_in, counts_in, state_in, lat, hits, places, sent, index, counts, state, sems
):
    first, second, third = copies(((index_in, index), (counts_in, counts), (state_in, state)), sems)
    per = index.shape[2] // LANES
    first.wait()
    second.wait()
    for g in range(index.shape[1]):
        side = where[g]
        for h in range(per):
            span = slice(h * LANES, (h + 1) * LANES)
            row = index[0, 0:1, span]
            for k in range(1, index.shape[1]):
                row = jnp.where(side == k, index[0, k : k + 1, span], row)
            slot = lax.broadcasted_iota(jnp.int32, (1, LANES), 1) + h * LANES
            r = g * per + h
            places[r : r + 1, :] = jnp.where(slot < counts[0, side], row, -1)
    fill_hits(hits, slot_rows(places), 0, per)
    third.wait()
    lat[...] = state[...].T
    send_features(lat[...], hits, (sent,))


def gather_rest(places, lat, gains_in, bias_in, decode_in, hits, columns, s1, s2, s3, gains, bias, decode, sems):
    waits = copies(((gains_in, gains), (bias_in, bias), (decode_in, decode)), sems)
    rows = slot_rows(places)
    fill_hits(hits, rows, len(rows) // 4, len(rows))
    send_features(lat[...], hits, (s1, s2, s3))
    for copy in waits:
        copy.wait()
    lines = [gains[layer] for layer in range(LAYERS)] + [bias[...], decode[...]]
    lines.append(jnp.zeros((8 - 3 * LAYERS - 1, bias.shape[1]), F32))
    columns[...] = jnp.concatenate(lines, axis=0).T


def send_features(lat, hits, outs):
    width = outs[0].shape[1]
    for k, out in enumerate(outs):
        out[...] = jnp.dot(
            lat, hits[:, k * width : (k + 1) * width], preferred_element_type=F32
        ).astype(BF16)


def send_rest(lat, hits, s1, s2, s3):
    send_features(lat[...], hits, (s1, s2, s3))


def build(
    tile_counts, places, tiles, lat, w_self, columns, rows_in, columns_in, capacity_in,
    matrix, half, inverse_rowsum, diagonal, local, own,
    tile_rows, tile_columns, capacity, sems,
):
    waits = copies(((rows_in, tile_rows), (columns_in, tile_columns), (capacity_in, capacity)), sems)
    count = tiles.shape[2]
    node_tiles = matrix.shape[0] // count
    matrix[...] = jnp.zeros(matrix.shape, F32)
    for t in range(node_tiles):
        span = slice(t * count, (t + 1) * count)
        block = tiles[0, t]
        matrix[span, span] = block + block.T
    for copy in waits:
        copy.wait()

    known = tiles.shape[1]
    live = tile_counts[0]
    together = 4

    def add(step, carry):
        for k in range(together):
            t = node_tiles + step * together + k
            at = jnp.minimum(t, known - 1)
            r = pl.multiple_of(tile_rows[0, at] * count, count)
            c = pl.multiple_of(tile_columns[0, at] * count, count)
            block = jnp.where(t < live, tiles[0, at], 0.0)
            matrix[pl.ds(r, count), pl.ds(c, count)] += block
            matrix[pl.ds(c, count), pl.ds(r, count)] += block.T
        return carry

    lax.fori_loop(0, (live - node_tiles + together - 1) // together, add, 0)
    rows = slot_rows(places)
    faces = spread_sum([jnp.ones((1, LANES), F32)] * len(rows), rows, node_tiles)
    total = jnp.zeros((8, matrix.shape[1]), F32)
    for t in range(node_tiles):
        block = matrix[t * count : (t + 1) * count, :]
        half[t * count : (t + 1) * count, :] = block.astype(BF16)
        total = total + jnp.sum(block.reshape(count // 8, 8, matrix.shape[1]), axis=0)
    rowsum = tile_rows_of(jnp.sum(total, axis=0, keepdims=True)) + faces
    inverse_rowsum[...] = lane_rows(1.0 / rowsum)
    diagonal[...] = capacity[...] + rowsum
    local[...] = jnp.dot(lat[...], half[...], preferred_element_type=F32)
    own[...] = own_part(0, lat[...], w_self, columns)


def normed(value, gain):
    scale = lax.rsqrt(jnp.mean(value * value, axis=0, keepdims=True) + 1e-06)
    return (value * scale * gain).astype(BF16)


def project(weight, value):
    return lax.dot_general(weight, value, (((0,), (0,)), ((), ())), preferred_element_type=F32)


def own_part(layer, lat, w_self, columns):
    gain = columns[:, 2 * layer : 2 * layer + 1]
    bias = columns[:, 2 * LAYERS + layer : 2 * LAYERS + layer + 1]
    return project(w_self[layer], normed(lat.astype(F32), gain)) + bias


def local_features(layer, lat, half, w_self, w_out, columns, local, own, before, decoder):
    local[...] = jnp.dot(lat[...], half[...], preferred_element_type=F32)
    own[...] = own_part(layer, lat[...], w_self, columns)
    decode = columns[:, 3 * LAYERS : 3 * LAYERS + 1]
    before[...] = jnp.sum(lat[...].astype(F32) * decode, axis=0, keepdims=True)
    line = jnp.broadcast_to(decode, (decode.shape[0], LANES)).T[0:1, :]
    decoder[...] = jnp.sum(w_out[layer].astype(F32) * line, axis=1, keepdims=True)


def with_slots(local, came, hits):
    return local + lax.dot_general(came, hits, (((1,), (1,)), ((), ())), preferred_element_type=F32)


def activation(layer, arrived, local, own, inverse_rowsum, first_hits, hits, w_neighbour, columns):
    total = with_slots(local[...], arrived[0][...], first_hits[...])
    total = with_slots(total, jnp.concatenate([a[...] for a in arrived[1:]], axis=1), hits[...])
    mean = total * inverse_rowsum[...]
    gain = columns[:, 2 * layer + 1 : 2 * layer + 2]
    linear = own[...] + project(w_neighbour[layer], normed(mean, gain))
    return linear / (1.0 + jnp.exp(-linear))


def first_layer(
    a0, a1, a2, a3, local, own, inverse_rowsum, lat, first_hits, hits, w_neighbour, w_out, columns, new, sent
):
    activated = activation(
        0, (a0, a1, a2, a3), local, own, inverse_rowsum, first_hits, hits, w_neighbour, columns
    ).astype(BF16)
    value = (lat[...].astype(F32) + project(w_out[0], activated)).astype(BF16)
    new[...] = value
    send_features(value, first_hits, (sent,))


def last_layer(
    places, a0, a1, a2, a3, local, own, inverse_rowsum, lat, first_hits, hits, w_neighbour, columns, before, decoder,
    guess, s0, s1, s2, s3,
):
    activated = activation(
        LAYERS - 1, (a0, a1, a2, a3), local, own, inverse_rowsum, first_hits, hits, w_neighbour, columns
    ).astype(BF16)
    row = before[...] + jnp.sum(activated.astype(F32) * decoder[...], axis=0, keepdims=True)
    field = tile_rows_of(row)
    guess[...] = field
    store_sent((s0, s1, s2, s3), pick(field, slot_rows(places)))


def product(matrix, field):
    count = LANES
    width = matrix.shape[1]
    total = jnp.zeros((8, width), F32)
    for t in range(field.shape[0]):
        column = jnp.broadcast_to(field[t : t + 1, :], (count, count)).T
        wide = jnp.concatenate([column] * (width // count), axis=1)
        part = matrix[t * count : (t + 1) * count, :] * wide
        total = total + jnp.sum(part.reshape(count // 8, 8, width), axis=0)
    return tile_rows_of(jnp.sum(total, axis=0, keepdims=True))


def matvec(matrix, vector, out):
    out[...] = product(matrix, vector[...])


def start_basis(places, a0, a1, a2, a3, local, guess, source, diagonal, basis, s0, s1, s2, s3):
    rows = slot_rows(places)
    came = spread_sum(arrived_rows((a0, a1, a2, a3)), rows, guess.shape[0])
    value = (source[...] + local[...] + came) / diagonal[...] - guess[...]
    basis[...] = value
    store_sent((s0, s1, s2, s3), pick(value, rows))


def next_basis(places, a0, a1, a2, a3, local, diagonal, basis, s0, s1, s2, s3):
    rows = slot_rows(places)
    came = spread_sum(arrived_rows((a0, a1, a2, a3)), rows, local.shape[0])
    value = (local[...] + came) / diagonal[...]
    basis[...] = value
    store_sent((s0, s1, s2, s3), pick(value, rows))


def diagonal_mask():
    return lax.broadcasted_iota(jnp.int32, (8, LANES), 0) == lax.broadcasted_iota(jnp.int32, (8, LANES), 1)


def last_basis(places, a0, a1, a2, a3, local, diagonal, b0, b1, matrix, basis, image, packets):
    rows = slot_rows(places)
    came = spread_sum(arrived_rows((a0, a1, a2, a3)), rows, local.shape[0])
    value = (local[...] + came) / diagonal[...]
    basis[...] = value
    mapped = product(matrix, value)
    image[...] = mapped
    held = [b0[...], b1[...], value]
    parts = []
    for k in range(2 * ITERS - 1):
        left, right = held[k // 2], held[(k + 1) // 2]
        parts.append(jnp.sum(left * right * diagonal[...], axis=0, keepdims=True))
    parts.append(jnp.sum(value * mapped, axis=0, keepdims=True))
    parts.append(jnp.zeros((8 - 2 * ITERS, LANES), F32))
    sums = jnp.sum(jnp.concatenate(parts, axis=0), axis=1, keepdims=True)
    row = jnp.sum(jnp.where(diagonal_mask(), sums, 0.0), axis=0, keepdims=True)
    packet = jnp.concatenate([lane_rows(pick(value, rows)), row], axis=1)
    for device in range(packets.shape[0]):
        packets[device] = packet


def added(values):
    values = list(values)
    while len(values) > 1:
        values = [sum(values[i : i + 2][1:], values[i]) for i in range(0, len(values), 2)]
    return values[0]


def finish(sizes, where, packets, places, image, guess, diagonal, b0, b1, b2, field, defect):
    doms, subs = sizes
    width = packets.shape[2] - LANES
    per = width // 4

    def slots(device, g):
        return packets[device, :, g * per : (g + 1) * per]

    edges = []
    for d in range(doms):
        for s in range(subs):
            for m, (i, j) in (((0, d % 2), (d + 1, s)), ((1, s % 2), (d, s + 1))):
                g = MATCHINGS.index(m)
                if i < doms and j < subs:
                    edges.append(slots(d * subs + s, g) * slots(i * subs + j, g))
    edges = added(edges)
    edges = added([edges[:, h : h + LANES] for h in range(0, per, LANES)])
    sums = added([packets[e, :, width : width + LANES] for e in range(doms * subs)])
    last_row = lax.broadcasted_iota(jnp.int32, (8, LANES), 0) == 2 * ITERS - 1
    table = jnp.where(diagonal_mask(), jnp.broadcast_to(sums, (8, LANES)), 0.0)
    table = table + jnp.where(last_row, jnp.broadcast_to(2.0 * edges, (8, LANES)), 0.0)
    columns = jnp.sum(table, axis=1, keepdims=True)
    n = [jnp.broadcast_to(columns[k : k + 1, :], (8, LANES)) for k in range(2 * ITERS)]
    came = []
    for g in range(4):
        mine = slots(where[4 + g], g)
        came += [mine[:, h : h + LANES] for h in range(0, per, LANES)]
    last = (image[...] + spread_sum(came, slot_rows(places), image.shape[0])) / diagonal[...]
    one, zero = jnp.ones((8, LANES), F32), jnp.zeros((8, LANES), F32)

    def paired(left, values):
        total = zero
        for i, a in enumerate(left):
            for j, b in enumerate(left):
                total = total + a * b * values[i + j]
        return total

    gaps = [n[k] - n[k + 1] for k in range(2 * ITERS - 1)]
    residual = [one]
    heading = [one]
    moved = [zero] * ITERS
    size = n[0]
    for step in range(ITERS):
        alpha = size / paired(heading, gaps)
        for i, h in enumerate(heading):
            moved[i] = moved[i] + alpha * h
        change = [
            (heading[i] if i < len(heading) else zero) - (heading[i - 1] if i > 0 else zero)
            for i in range(len(heading) + 1)
        ]
        residual = [
            (residual[i] if i < len(residual) else zero) - alpha * change[i]
            for i in range(len(change))
        ]
        if step + 1 < ITERS:
            following = paired(residual, n)
            beta = following / size
            heading = [
                residual[i] + (beta * heading[i] if i < len(heading) else zero)
                for i in range(len(residual))
            ]
            size = following
    held = [b0[...], b1[...], b2[...], last]
    total = guess[...]
    for c, b in zip(moved, held):
        total = total + c * b
    field[...] = total
    left = zero
    for c, b in zip(residual, held):
        left = left + c * b
    defect[...] = left * diagonal[...]


def mate_of(place, first, size):
    mate = ((place - first) ^ 1) + first
    return mate if place >= first and mate < size else None


def swaps(sizes, turn):
    along, first = MATCHINGS[turn]
    pairs = []
    for dom in range(sizes[0]):
        for sub in range(sizes[1]):
            to = [dom, sub]
            mate = mate_of(to[along], first, sizes[along])
            if mate is not None:
                to[along] = mate
            elif along == 1 and sizes[0] % 2 == 0:
                to[0] ^= 1
            elif along == 0 and sizes[1] % 2 == 0:
                to[1] = (sub + sizes[1] // 2) % sizes[1]
            pairs.append((dom * sizes[1] + sub, to[0] * sizes[1] + to[1]))
    return pairs


def places_of_turns():
    at = [lax.axis_index("dom"), lax.axis_index("sub")]
    sizes = [lax.axis_size("dom"), lax.axis_size("sub")]

    def side(along, first):
        odd = at[along] % 2
        return 2 * along + (odd if first else 1 - odd)

    def partner(along, first):
        mate = jnp.bitwise_xor(at[along] - first, 1) + first
        to = list(at)
        to[along] = jnp.where((at[along] >= first) & (mate < sizes[along]), mate, at[along])
        return to[0] * sizes[1] + to[1]

    out = [value(*m) for value in (side, partner) for m in MATCHINGS]
    return jnp.stack(out).astype(jnp.int32)


def swap(sent, turn):
    axes = ("dom", "sub")
    return lax.ppermute(sent, axes, swaps([lax.axis_size(axis) for axis in axes], turn))


def exchange(sent, first=0):
    return [swap(s, first + i) for i, s in enumerate(sent)]


def all_to_all(messages):
    return lax.all_to_all(messages, ("dom", "sub"), split_axis=0, concat_axis=0, tiled=True)


def per_device(
    state, tile_values, tile_rows, tile_columns, tile_counts, send_nodes, face_counts, capacity,
    source, w_self, w_neighbour, w_out, gains, bias, w_decode,
):
    nodes, width = state.shape
    slots = send_nodes.shape[2]
    tiles = nodes // LANES
    sizes = (lax.axis_size("dom"), lax.axis_size("sub"))
    devices = sizes[0] * sizes[1]
    field = shape((tiles, LANES))
    features = shape((width, nodes))
    vector_sent = [shape((slots // LANES, LANES))] * 4
    decode = w_decode.reshape(1, width)
    where = places_of_turns()
    capacity = capacity.reshape(tiles, LANES)
    source = source.reshape(tiles, LANES)

    one_sent = [shape((width, slots), BF16)]
    gather_flops = 2 * nodes * slots * width
    lat, first_hits, places, sent = run(
        gather_first,
        [shape((width, nodes), BF16), shape((nodes, slots), BF16), shape((4 * slots // LANES, LANES), jnp.int32)]
        + one_sent,
        (), (where,), (send_nodes, face_counts, state),
        (
            pltpu.VMEM(send_nodes.shape, jnp.int32),
            pltpu.SMEM(face_counts.shape, jnp.int32),
            pltpu.VMEM(state.shape, BF16),
        ),
        waits=3, flops=gather_flops,
    )
    a0 = swap(sent, 0)
    hits, columns, *sent = run(
        gather_rest, [shape((nodes, 3 * slots), BF16), shape((width, 8))] + one_sent * 3,
        (places, lat), (), (gains, bias, decode),
        (pltpu.VMEM(gains.shape, F32), pltpu.VMEM(bias.shape, F32), pltpu.VMEM(decode.shape, F32)),
        waits=3, flops=3 * gather_flops,
    )
    a1, a2, a3 = exchange(sent, 1)
    matrix, half, inverse_rowsum, diagonal, local, own = run(
        build,
        [shape((nodes, nodes)), shape((nodes, nodes), BF16), shape((1, nodes)), field, features, features],
        (places, tile_values, lat, w_self, columns),
        (tile_counts,), (tile_rows, tile_columns, capacity),
        (
            pltpu.SMEM(tile_rows.shape, jnp.int32),
            pltpu.SMEM(tile_columns.shape, jnp.int32),
            pltpu.VMEM(capacity.shape, F32),
        ),
        waits=3, flops=0, moved=0,
    )
    lat, sent = run(
        first_layer, [shape((width, nodes), BF16)] + one_sent,
        (a0, a1, a2, a3, local, own, inverse_rowsum, lat, first_hits, hits, w_neighbour, w_out, columns),
        flops=3 * nodes * nodes * width,
    )
    a0 = swap(sent, 0)
    sent = run(send_rest, one_sent * 3, (lat, hits), flops=3 * gather_flops)
    a1, a2, a3 = exchange(sent, 1)
    local, own, before, decoder = run(
        functools.partial(local_features, LAYERS - 1),
        [features, features, shape((1, nodes)), shape((width, 1))],
        (lat, half, w_self, w_out, columns), flops=0, moved=0,
    )
    guess, *sent = run(
        last_layer, [field] + vector_sent,
        (places, a0, a1, a2, a3, local, own, inverse_rowsum, lat, first_hits, hits, w_neighbour, columns, before, decoder),
        flops=3 * nodes * nodes * width,
    )

    def mapped(vector):
        return run(matvec, [field], (matrix, vector), flops=2 * nodes * nodes, moved=4 * nodes * nodes)[0]

    arrived = exchange(sent)
    local = mapped(guess)
    b0, *sent = run(
        start_basis, [field] + vector_sent, (places, *arrived, local, guess, source, diagonal)
    )
    arrived = exchange(sent)
    local = mapped(b0)
    b1, *sent = run(next_basis, [field] + vector_sent, (places, *arrived, local, diagonal))
    arrived = exchange(sent)
    local = mapped(b1)
    b2, image, packets = run(
        last_basis, [field, field, shape((devices, 1, 4 * slots + LANES))],
        (places, *arrived, local, diagonal, b0, b1, matrix),
    )
    packets = all_to_all(packets)
    heat, defect = run(
        functools.partial(finish, sizes), [field, field],
        (packets, places, image, guess, diagonal, b0, b1, b2), (where,),
    )
    return heat.reshape(nodes), defect.reshape(nodes)


def solution(mesh):
    both = ("dom", "sub")
    return jax.shard_map(
        per_device,
        mesh=mesh,
        in_specs=(
            P(both, None),
            P(both, None, None, None),
            P(both, None),
            P(both, None),
            P(both),
            P(both, None, None),
            P(both, None),
            P(both),
            P(both),
            P(),
            P(),
            P(),
            P(),
            P(),
            P(),
        ),
        out_specs=(P(both), P(both)),
        check_vma=False,
    )
```

```python
import functools

import jax
import jax.numpy as jnp
from jax import lax
from jax.experimental import pallas as pl
from jax.experimental.pallas import tpu as pltpu
from jax.sharding import PartitionSpec as P

LAYERS = 2
ITERS = 3
LANES = 128
MATCHINGS = ((1, 1), (1, 0), (0, 0), (0, 1))
VMEM_LIMIT = 24 * 1024 * 1024

F32 = jnp.float32
BF16 = jnp.bfloat16


def shape(dims, dtype=F32):
    return jax.ShapeDtypeStruct(dims, dtype)


def run(body, outs, operands, scalars=(), raw=(), scratch=(), waits=0, flops=1_000_000, moved=1_000_000):
    smem = pl.BlockSpec(memory_space=pltpu.SMEM)
    vmem = pl.BlockSpec(memory_space=pltpu.VMEM)
    anywhere = pl.BlockSpec(memory_space=pltpu.HBM)
    scratch = list(scratch) + [pltpu.SemaphoreType.DMA((waits,))] * bool(waits)
    return pl.pallas_call(
        body,
        out_shape=outs,
        in_specs=[smem] * len(scalars) + [vmem] * len(operands) + [anywhere] * len(raw),
        out_specs=[vmem] * len(outs),
        scratch_shapes=scratch,
        compiler_params=pltpu.CompilerParams(vmem_limit_bytes=VMEM_LIMIT),
        cost_estimate=pl.CostEstimate(flops=flops, bytes_accessed=moved, transcendentals=0),
    )(*scalars, *operands, *(pltpu.with_memory_space_constraint(r, pltpu.HBM) for r in raw))


def copies(pairs, semaphores):
    started = [pltpu.make_async_copy(*pair, semaphores.at[i]) for i, pair in enumerate(pairs)]
    for copy in started:
        copy.start()
    return started


def slot_rows(places):
    return [places[r : r + 1, :] for r in range(places.shape[0])]


def pick(vector, rows):
    index = jnp.concatenate(rows, axis=0)
    low = jnp.bitwise_and(index, LANES - 1)
    high = jnp.right_shift(index, 7)
    out = jnp.zeros(index.shape, F32)
    for t in range(vector.shape[0]):
        spread = jnp.broadcast_to(vector[t : t + 1, :], index.shape)
        got = jnp.take_along_axis(spread, low, axis=1, mode="promise_in_bounds")
        out = jnp.where(high == t, got, out)
    return out


def pieces(value):
    first = value.astype(BF16)
    rest = value - first.astype(F32)
    second = rest.astype(BF16)
    third = (rest - second.astype(F32)).astype(BF16)
    return first, second, third


def low_hits(rows):
    lane = lax.broadcasted_iota(jnp.int32, (LANES, LANES), 0)
    return jnp.concatenate(
        [(lane == jnp.bitwise_and(row, LANES - 1)).astype(F32).astype(BF16) for row in rows], axis=1
    )


def spread_sum(values, rows, tiles):
    tile = lax.broadcasted_iota(jnp.int32, (tiles, LANES), 0)
    parts = [
        jnp.where(tile == jnp.right_shift(row, 7), value, 0.0) for value, row in zip(values, rows)
    ]
    held = jnp.concatenate(parts, axis=1)
    stacked = jnp.concatenate([p.astype(F32) for p in pieces(held)], axis=0).astype(BF16)
    out = lax.dot_general(
        stacked, low_hits(rows), (((1,), (1,)), ((), ())), preferred_element_type=F32
    )
    return out[:tiles] + out[tiles : 2 * tiles] + out[2 * tiles :]


def arrived_rows(refs):
    return [ref[h : h + 1, :] for ref in refs for h in range(ref.shape[0])]


def store_sent(refs, sent):
    per = refs[0].shape[0]
    for k, ref in enumerate(refs):
        ref[...] = sent[k * per : (k + 1) * per, :]


def lane_rows(vector):
    return jnp.concatenate([vector[t : t + 1, :] for t in range(vector.shape[0])], axis=1)


def tile_rows_of(row):
    return jnp.concatenate(
        [row[:, t * LANES : (t + 1) * LANES] for t in range(row.shape[1] // LANES)], axis=0
    )


def fill_hits(hits, rows, first, last):
    nodes = hits.shape[0]
    node = lax.broadcasted_iota(jnp.int32, (nodes, LANES), 0).astype(jnp.int16).reshape(nodes // 16, 16, LANES)
    one, zero = jnp.ones(node.shape, BF16), jnp.zeros(node.shape, BF16)
    for c in range(first, last):
        wide = jnp.broadcast_to(rows[c], (16, LANES)).astype(jnp.int16)
        at = (c - first) * LANES
        hits[:, at : at + LANES] = jnp.where(node == wide[None], one, zero).reshape(nodes, LANES)


def gather_first(
    where, index_in, counts_in, state_in, lat, hits, places, sent, index, counts, state, sems
):
    first, second, third = copies(((index_in, index), (counts_in, counts), (state_in, state)), sems)
    per = index.shape[2] // LANES
    first.wait()
    second.wait()
    for g in range(index.shape[1]):
        side = where[g]
        for h in range(per):
            span = slice(h * LANES, (h + 1) * LANES)
            row = index[0, 0:1, span]
            for k in range(1, index.shape[1]):
                row = jnp.where(side == k, index[0, k : k + 1, span], row)
            slot = lax.broadcasted_iota(jnp.int32, (1, LANES), 1) + h * LANES
            r = g * per + h
            places[r : r + 1, :] = jnp.where(slot < counts[0, side], row, -1)
    fill_hits(hits, slot_rows(places), 0, per)
    third.wait()
    lat[...] = state[...].T
    send_features(lat[...], hits, (sent,))


def gather_rest(places, lat, gains_in, bias_in, decode_in, hits, columns, s1, s2, s3, gains, bias, decode, sems):
    waits = copies(((gains_in, gains), (bias_in, bias), (decode_in, decode)), sems)
    rows = slot_rows(places)
    fill_hits(hits, rows, len(rows) // 4, len(rows))
    send_features(lat[...], hits, (s1, s2, s3))
    for copy in waits:
        copy.wait()
    lines = [gains[layer] for layer in range(LAYERS)] + [bias[...], decode[...]]
    lines.append(jnp.zeros((8 - 3 * LAYERS - 1, bias.shape[1]), F32))
    columns[...] = jnp.concatenate(lines, axis=0).T


def send_features(lat, hits, outs):
    width = outs[0].shape[1]
    for k, out in enumerate(outs):
        out[...] = jnp.dot(
            lat, hits[:, k * width : (k + 1) * width], preferred_element_type=F32
        ).astype(BF16)


def send_rest(lat, hits, s1, s2, s3):
    send_features(lat[...], hits, (s1, s2, s3))


def build(
    tile_counts, places, tiles, lat, w_self, columns, rows_in, columns_in, capacity_in,
    matrix, half, inverse_rowsum, diagonal, local, own,
    tile_rows, tile_columns, capacity, sems,
):
    waits = copies(((rows_in, tile_rows), (columns_in, tile_columns), (capacity_in, capacity)), sems)
    count = tiles.shape[2]
    node_tiles = matrix.shape[0] // count
    matrix[...] = jnp.zeros(matrix.shape, F32)
    for t in range(node_tiles):
        span = slice(t * count, (t + 1) * count)
        block = tiles[0, t]
        matrix[span, span] = block + block.T
    for copy in waits:
        copy.wait()

    known = tiles.shape[1]
    live = tile_counts[0]
    together = 4

    def add(step, carry):
        for k in range(together):
            t = node_tiles + step * together + k
            at = jnp.minimum(t, known - 1)
            r = pl.multiple_of(tile_rows[0, at] * count, count)
            c = pl.multiple_of(tile_columns[0, at] * count, count)
            block = jnp.where(t < live, tiles[0, at], 0.0)
            matrix[pl.ds(r, count), pl.ds(c, count)] += block
            matrix[pl.ds(c, count), pl.ds(r, count)] += block.T
        return carry

    lax.fori_loop(0, (live - node_tiles + together - 1) // together, add, 0)
    rows = slot_rows(places)
    faces = spread_sum([jnp.ones((1, LANES), F32)] * len(rows), rows, node_tiles)
    total = jnp.zeros((8, matrix.shape[1]), F32)
    for t in range(node_tiles):
        block = matrix[t * count : (t + 1) * count, :]
        half[t * count : (t + 1) * count, :] = block.astype(BF16)
        total = total + jnp.sum(block.reshape(count // 8, 8, matrix.shape[1]), axis=0)
    rowsum = tile_rows_of(jnp.sum(total, axis=0, keepdims=True)) + faces
    inverse_rowsum[...] = lane_rows(1.0 / rowsum)
    diagonal[...] = capacity[...] + rowsum
    local[...] = jnp.dot(lat[...], half[...], preferred_element_type=F32)
    own[...] = own_part(0, lat[...], w_self, columns)


def normed(value, gain):
    scale = lax.rsqrt(jnp.mean(value * value, axis=0, keepdims=True) + 1e-06)
    return (value * scale * gain).astype(BF16)


def project(weight, value):
    return lax.dot_general(weight, value, (((0,), (0,)), ((), ())), preferred_element_type=F32)


def own_part(layer, lat, w_self, columns):
    gain = columns[:, 2 * layer : 2 * layer + 1]
    bias = columns[:, 2 * LAYERS + layer : 2 * LAYERS + layer + 1]
    return project(w_self[layer], normed(lat.astype(F32), gain)) + bias


def local_features(layer, lat, half, w_self, w_out, columns, local, own, before, decoder):
    local[...] = jnp.dot(lat[...], half[...], preferred_element_type=F32)
    own[...] = own_part(layer, lat[...], w_self, columns)
    decode = columns[:, 3 * LAYERS : 3 * LAYERS + 1]
    before[...] = jnp.sum(lat[...].astype(F32) * decode, axis=0, keepdims=True)
    line = jnp.broadcast_to(decode, (decode.shape[0], LANES)).T[0:1, :]
    decoder[...] = jnp.sum(w_out[layer].astype(F32) * line, axis=1, keepdims=True)


def with_slots(local, came, hits):
    return local + lax.dot_general(came, hits, (((1,), (1,)), ((), ())), preferred_element_type=F32)


def add_early(a0, a2, a3, local, first_hits, hits, out):
    width = a0.shape[1]
    total = with_slots(local[...], a0[...], first_hits[...])
    out[...] = with_slots(total, jnp.concatenate([a2[...], a3[...]], axis=1), hits[:, width:])


def activation(layer, late, local, own, inverse_rowsum, hits, w_neighbour, columns):
    total = with_slots(local[...], late[...], hits[:, : late.shape[1]])
    mean = total * inverse_rowsum[...]
    gain = columns[:, 2 * layer + 1 : 2 * layer + 2]
    linear = own[...] + project(w_neighbour[layer], normed(mean, gain))
    return linear / (1.0 + jnp.exp(-linear))


def first_layer(
    late, local, own, inverse_rowsum, lat, first_hits, hits, w_neighbour, w_out, columns, new, sent
):
    activated = activation(0, late, local, own, inverse_rowsum, hits, w_neighbour, columns).astype(BF16)
    value = (lat[...].astype(F32) + project(w_out[0], activated)).astype(BF16)
    new[...] = value
    send_features(value, first_hits, (sent,))


def last_layer(
    places, late, local, own, inverse_rowsum, lat, hits, w_neighbour, columns, before, decoder,
    guess, s0, s1, s2, s3,
):
    activated = activation(LAYERS - 1, late, local, own, inverse_rowsum, hits, w_neighbour, columns).astype(BF16)
    row = before[...] + jnp.sum(activated.astype(F32) * decoder[...], axis=0, keepdims=True)
    field = tile_rows_of(row)
    guess[...] = field
    store_sent((s0, s1, s2, s3), pick(field, slot_rows(places)))


def product(matrix, field):
    count = LANES
    width = matrix.shape[1]
    total = jnp.zeros((8, width), F32)
    for t in range(field.shape[0]):
        column = jnp.broadcast_to(field[t : t + 1, :], (count, count)).T
        wide = jnp.concatenate([column] * (width // count), axis=1)
        part = matrix[t * count : (t + 1) * count, :] * wide
        total = total + jnp.sum(part.reshape(count // 8, 8, width), axis=0)
    return tile_rows_of(jnp.sum(total, axis=0, keepdims=True))


def matvec(matrix, vector, out):
    out[...] = product(matrix, vector[...])


def start_basis(places, a0, a1, a2, a3, local, guess, source, diagonal, basis, s0, s1, s2, s3):
    rows = slot_rows(places)
    came = spread_sum(arrived_rows((a0, a1, a2, a3)), rows, guess.shape[0])
    value = (source[...] + local[...] + came) / diagonal[...] - guess[...]
    basis[...] = value
    store_sent((s0, s1, s2, s3), pick(value, rows))


def next_basis(places, a0, a1, a2, a3, local, diagonal, basis, s0, s1, s2, s3):
    rows = slot_rows(places)
    came = spread_sum(arrived_rows((a0, a1, a2, a3)), rows, local.shape[0])
    value = (local[...] + came) / diagonal[...]
    basis[...] = value
    store_sent((s0, s1, s2, s3), pick(value, rows))


def diagonal_mask():
    return lax.broadcasted_iota(jnp.int32, (8, LANES), 0) == lax.broadcasted_iota(jnp.int32, (8, LANES), 1)


def last_basis(places, a0, a1, a2, a3, local, diagonal, b0, b1, matrix, basis, image, packets):
    rows = slot_rows(places)
    came = spread_sum(arrived_rows((a0, a1, a2, a3)), rows, local.shape[0])
    value = (local[...] + came) / diagonal[...]
    basis[...] = value
    mapped = product(matrix, value)
    image[...] = mapped
    held = [b0[...], b1[...], value]
    parts = []
    for k in range(2 * ITERS - 1):
        left, right = held[k // 2], held[(k + 1) // 2]
        parts.append(jnp.sum(left * right * diagonal[...], axis=0, keepdims=True))
    parts.append(jnp.sum(value * mapped, axis=0, keepdims=True))
    parts.append(jnp.zeros((8 - 2 * ITERS, LANES), F32))
    sums = jnp.sum(jnp.concatenate(parts, axis=0), axis=1, keepdims=True)
    row = jnp.sum(jnp.where(diagonal_mask(), sums, 0.0), axis=0, keepdims=True)
    packet = jnp.concatenate([lane_rows(pick(value, rows)), row], axis=1)
    for device in range(packets.shape[0]):
        packets[device] = packet


def added(values):
    values = list(values)
    while len(values) > 1:
        values = [sum(values[i : i + 2][1:], values[i]) for i in range(0, len(values), 2)]
    return values[0]


def finish(sizes, where, packets, places, image, guess, diagonal, b0, b1, b2, field, defect):
    doms, subs = sizes
    width = packets.shape[2] - LANES
    per = width // 4

    def slots(device, g):
        return packets[device, :, g * per : (g + 1) * per]

    edges = []
    for d in range(doms):
        for s in range(subs):
            for m, (i, j) in (((0, d % 2), (d + 1, s)), ((1, s % 2), (d, s + 1))):
                g = MATCHINGS.index(m)
                if i < doms and j < subs:
                    edges.append(slots(d * subs + s, g) * slots(i * subs + j, g))
    edges = added(edges)
    edges = added([edges[:, h : h + LANES] for h in range(0, per, LANES)])
    sums = added([packets[e, :, width : width + LANES] for e in range(doms * subs)])
    last_row = lax.broadcasted_iota(jnp.int32, (8, LANES), 0) == 2 * ITERS - 1
    table = jnp.where(diagonal_mask(), jnp.broadcast_to(sums, (8, LANES)), 0.0)
    table = table + jnp.where(last_row, jnp.broadcast_to(2.0 * edges, (8, LANES)), 0.0)
    columns = jnp.sum(table, axis=1, keepdims=True)
    n = [jnp.broadcast_to(columns[k : k + 1, :], (8, LANES)) for k in range(2 * ITERS)]
    came = []
    for g in range(4):
        mine = slots(where[4 + g], g)
        came += [mine[:, h : h + LANES] for h in range(0, per, LANES)]
    last = (image[...] + spread_sum(came, slot_rows(places), image.shape[0])) / diagonal[...]
    one, zero = jnp.ones((8, LANES), F32), jnp.zeros((8, LANES), F32)

    def paired(left, values):
        total = zero
        for i, a in enumerate(left):
            for j, b in enumerate(left):
                total = total + a * b * values[i + j]
        return total

    gaps = [n[k] - n[k + 1] for k in range(2 * ITERS - 1)]
    residual = [one]
    heading = [one]
    moved = [zero] * ITERS
    size = n[0]
    for step in range(ITERS):
        alpha = size / paired(heading, gaps)
        for i, h in enumerate(heading):
            moved[i] = moved[i] + alpha * h
        change = [
            (heading[i] if i < len(heading) else zero) - (heading[i - 1] if i > 0 else zero)
            for i in range(len(heading) + 1)
        ]
        residual = [
            (residual[i] if i < len(residual) else zero) - alpha * change[i]
            for i in range(len(change))
        ]
        if step + 1 < ITERS:
            following = paired(residual, n)
            beta = following / size
            heading = [
                residual[i] + (beta * heading[i] if i < len(heading) else zero)
                for i in range(len(residual))
            ]
            size = following
    held = [b0[...], b1[...], b2[...], last]
    total = guess[...]
    for c, b in zip(moved, held):
        total = total + c * b
    field[...] = total
    left = zero
    for c, b in zip(residual, held):
        left = left + c * b
    defect[...] = left * diagonal[...]


def mate_of(place, first, size):
    mate = ((place - first) ^ 1) + first
    return mate if place >= first and mate < size else None


def swaps(sizes, turn):
    along, first = MATCHINGS[turn]
    pairs = []
    for dom in range(sizes[0]):
        for sub in range(sizes[1]):
            to = [dom, sub]
            mate = mate_of(to[along], first, sizes[along])
            if mate is not None:
                to[along] = mate
            elif along == 1 and sizes[0] % 2 == 0:
                to[0] ^= 1
            elif along == 0 and sizes[1] % 2 == 0:
                to[1] = (sub + sizes[1] // 2) % sizes[1]
            pairs.append((dom * sizes[1] + sub, to[0] * sizes[1] + to[1]))
    return pairs


def places_of_turns():
    at = [lax.axis_index("dom"), lax.axis_index("sub")]
    sizes = [lax.axis_size("dom"), lax.axis_size("sub")]

    def side(along, first):
        odd = at[along] % 2
        return 2 * along + (odd if first else 1 - odd)

    def partner(along, first):
        mate = jnp.bitwise_xor(at[along] - first, 1) + first
        to = list(at)
        to[along] = jnp.where((at[along] >= first) & (mate < sizes[along]), mate, at[along])
        return to[0] * sizes[1] + to[1]

    out = [value(*m) for value in (side, partner) for m in MATCHINGS]
    return jnp.stack(out).astype(jnp.int32)


def swap(sent, turn):
    axes = ("dom", "sub")
    return lax.ppermute(sent, axes, swaps([lax.axis_size(axis) for axis in axes], turn))


def exchange(sent, first=0):
    return [swap(s, first + i) for i, s in enumerate(sent)]


def all_to_all(messages):
    return lax.all_to_all(messages, ("dom", "sub"), split_axis=0, concat_axis=0, tiled=True)


def per_device(
    state, tile_values, tile_rows, tile_columns, tile_counts, send_nodes, face_counts, capacity,
    source, w_self, w_neighbour, w_out, gains, bias, w_decode,
):
    nodes, width = state.shape
    slots = send_nodes.shape[2]
    tiles = nodes // LANES
    sizes = (lax.axis_size("dom"), lax.axis_size("sub"))
    devices = sizes[0] * sizes[1]
    field = shape((tiles, LANES))
    features = shape((width, nodes))
    vector_sent = [shape((slots // LANES, LANES))] * 4
    decode = w_decode.reshape(1, width)
    where = places_of_turns()
    capacity = capacity.reshape(tiles, LANES)
    source = source.reshape(tiles, LANES)

    one_sent = [shape((width, slots), BF16)]
    gather_flops = 2 * nodes * slots * width
    lat, first_hits, places, sent = run(
        gather_first,
        [shape((width, nodes), BF16), shape((nodes, slots), BF16), shape((4 * slots // LANES, LANES), jnp.int32)]
        + one_sent,
        (), (where,), (send_nodes, face_counts, state),
        (
            pltpu.VMEM(send_nodes.shape, jnp.int32),
            pltpu.SMEM(face_counts.shape, jnp.int32),
            pltpu.VMEM(state.shape, BF16),
        ),
        waits=3, flops=gather_flops,
    )
    a0 = swap(sent, 0)
    hits, columns, *sent = run(
        gather_rest, [shape((nodes, 3 * slots), BF16), shape((width, 8))] + one_sent * 3,
        (places, lat), (), (gains, bias, decode),
        (pltpu.VMEM(gains.shape, F32), pltpu.VMEM(bias.shape, F32), pltpu.VMEM(decode.shape, F32)),
        waits=3, flops=3 * gather_flops,
    )
    a1, a2, a3 = exchange(sent, 1)
    matrix, half, inverse_rowsum, diagonal, local, own = run(
        build,
        [shape((nodes, nodes)), shape((nodes, nodes), BF16), shape((1, nodes)), field, features, features],
        (places, tile_values, lat, w_self, columns),
        (tile_counts,), (tile_rows, tile_columns, capacity),
        (
            pltpu.SMEM(tile_rows.shape, jnp.int32),
            pltpu.SMEM(tile_columns.shape, jnp.int32),
            pltpu.VMEM(capacity.shape, F32),
        ),
        waits=3, flops=0, moved=0,
    )
    (local,) = run(add_early, [features], (a0, a2, a3, local, first_hits, hits), flops=3 * gather_flops)
    lat, sent = run(
        first_layer, [shape((width, nodes), BF16)] + one_sent,
        (a1, local, own, inverse_rowsum, lat, first_hits, hits, w_neighbour, w_out, columns),
        flops=3 * nodes * nodes * width,
    )
    a0 = swap(sent, 0)
    sent = run(send_rest, one_sent * 3, (lat, hits), flops=3 * gather_flops)
    a1, a2, a3 = exchange(sent, 1)
    local, own, before, decoder = run(
        functools.partial(local_features, LAYERS - 1),
        [features, features, shape((1, nodes)), shape((width, 1))],
        (lat, half, w_self, w_out, columns), flops=0, moved=0,
    )
    (local,) = run(add_early, [features], (a0, a2, a3, local, first_hits, hits), flops=3 * gather_flops)
    guess, *sent = run(
        last_layer, [field] + vector_sent,
        (places, a1, local, own, inverse_rowsum, lat, hits, w_neighbour, columns, before, decoder),
        flops=3 * nodes * nodes * width,
    )

    def mapped(vector):
        return run(matvec, [field], (matrix, vector), flops=2 * nodes * nodes, moved=4 * nodes * nodes)[0]

    arrived = exchange(sent)
    local = mapped(guess)
    b0, *sent = run(
        start_basis, [field] + vector_sent, (places, *arrived, local, guess, source, diagonal)
    )
    arrived = exchange(sent)
    local = mapped(b0)
    b1, *sent = run(next_basis, [field] + vector_sent, (places, *arrived, local, diagonal))
    arrived = exchange(sent)
    local = mapped(b1)
    b2, image, packets = run(
        last_basis, [field, field, shape((devices, 1, 4 * slots + LANES))],
        (places, *arrived, local, diagonal, b0, b1, matrix),
    )
    packets = all_to_all(packets)
    heat, defect = run(
        functools.partial(finish, sizes), [field, field],
        (packets, places, image, guess, diagonal, b0, b1, b2), (where,),
    )
    return heat.reshape(nodes), defect.reshape(nodes)


def solution(mesh):
    both = ("dom", "sub")
    return jax.shard_map(
        per_device,
        mesh=mesh,
        in_specs=(
            P(both, None),
            P(both, None, None, None),
            P(both, None),
            P(both, None),
            P(both),
            P(both, None, None),
            P(both, None),
            P(both),
            P(both),
            P(),
            P(),
            P(),
            P(),
            P(),
            P(),
        ),
        out_specs=(P(both), P(both)),
        check_vma=False,
    )
```

```python
import functools

import jax
import jax.numpy as jnp
from jax import lax
from jax.experimental import pallas as pl
from jax.experimental.pallas import tpu as pltpu
from jax.sharding import PartitionSpec as P

LAYERS = 2
ITERS = 3
LANES = 128
MATCHINGS = ((1, 1), (1, 0), (0, 0), (0, 1))
VMEM_LIMIT = 24 * 1024 * 1024

F32 = jnp.float32
BF16 = jnp.bfloat16


def shape(dims, dtype=F32):
    return jax.ShapeDtypeStruct(dims, dtype)


def run(body, outs, operands, scalars=(), raw=(), scratch=(), waits=0, flops=1_000_000, moved=1_000_000, aliases={}):
    operands = [
        pltpu.with_memory_space_constraint(x, pltpu.VMEM) if i in aliases else x for i, x in enumerate(operands)
    ]
    smem = pl.BlockSpec(memory_space=pltpu.SMEM)
    vmem = pl.BlockSpec(memory_space=pltpu.VMEM)
    anywhere = pl.BlockSpec(memory_space=pltpu.HBM)
    scratch = list(scratch) + [pltpu.SemaphoreType.DMA((waits,))] * bool(waits)
    return pl.pallas_call(
        body,
        out_shape=outs,
        in_specs=[smem] * len(scalars) + [vmem] * len(operands) + [anywhere] * len(raw),
        out_specs=[vmem] * len(outs),
        scratch_shapes=scratch,
        input_output_aliases={len(scalars) + i: o for i, o in aliases.items()},
        compiler_params=pltpu.CompilerParams(vmem_limit_bytes=VMEM_LIMIT),
        cost_estimate=pl.CostEstimate(flops=flops, bytes_accessed=moved, transcendentals=0),
    )(*scalars, *operands, *(pltpu.with_memory_space_constraint(r, pltpu.HBM) for r in raw))


def copies(pairs, semaphores):
    started = [pltpu.make_async_copy(*pair, semaphores.at[i]) for i, pair in enumerate(pairs)]
    for copy in started:
        copy.start()
    return started


def slot_rows(places):
    return [places[r : r + 1, :] for r in range(places.shape[0])]


def pick(vector, rows):
    index = jnp.concatenate(rows, axis=0)
    low = jnp.bitwise_and(index, LANES - 1)
    high = jnp.right_shift(index, 7)
    out = jnp.zeros(index.shape, F32)
    for t in range(vector.shape[0]):
        spread = jnp.broadcast_to(vector[t : t + 1, :], index.shape)
        got = jnp.take_along_axis(spread, low, axis=1, mode="promise_in_bounds")
        out = jnp.where(high == t, got, out)
    return out


def pieces(value):
    first = value.astype(BF16)
    rest = value - first.astype(F32)
    second = rest.astype(BF16)
    third = (rest - second.astype(F32)).astype(BF16)
    return first, second, third


def low_hits(rows):
    lane = lax.broadcasted_iota(jnp.int32, (LANES, LANES), 0)
    return jnp.concatenate(
        [(lane == jnp.bitwise_and(row, LANES - 1)).astype(F32).astype(BF16) for row in rows], axis=1
    )


def spread_sum(values, rows, tiles):
    tile = lax.broadcasted_iota(jnp.int32, (tiles, LANES), 0)
    parts = [
        jnp.where(tile == jnp.right_shift(row, 7), value, 0.0) for value, row in zip(values, rows)
    ]
    held = jnp.concatenate(parts, axis=1)
    stacked = jnp.concatenate([p.astype(F32) for p in pieces(held)], axis=0).astype(BF16)
    out = lax.dot_general(
        stacked, low_hits(rows), (((1,), (1,)), ((), ())), preferred_element_type=F32
    )
    return out[:tiles] + out[tiles : 2 * tiles] + out[2 * tiles :]


def arrived_rows(refs):
    return [ref[h : h + 1, :] for ref in refs for h in range(ref.shape[0])]


def store_sent(refs, sent):
    per = refs[0].shape[0]
    for k, ref in enumerate(refs):
        ref[...] = sent[k * per : (k + 1) * per, :]


def lane_rows(vector):
    return jnp.concatenate([vector[t : t + 1, :] for t in range(vector.shape[0])], axis=1)


def tile_rows_of(row):
    return jnp.concatenate(
        [row[:, t * LANES : (t + 1) * LANES] for t in range(row.shape[1] // LANES)], axis=0
    )


def fill_hits(hits, rows, first, last):
    nodes = hits.shape[0]
    node = lax.broadcasted_iota(jnp.int32, (nodes, LANES), 0).astype(jnp.int16).reshape(nodes // 16, 16, LANES)
    one, zero = jnp.ones(node.shape, BF16), jnp.zeros(node.shape, BF16)
    for c in range(first, last):
        wide = jnp.broadcast_to(rows[c], (16, LANES)).astype(jnp.int16)
        at = (c - first) * LANES
        hits[:, at : at + LANES] = jnp.where(node == wide[None], one, zero).reshape(nodes, LANES)


def gather_first(
    where, index_in, counts_in, state_in, lat, hits, places, sent, blank, index, counts, state, sems
):
    first, second, third = copies(((index_in, index), (counts_in, counts), (state_in, state)), sems)
    blank[...] = jnp.zeros(blank.shape, F32)
    per = index.shape[2] // LANES
    first.wait()
    second.wait()
    for g in range(index.shape[1]):
        side = where[g]
        for h in range(per):
            span = slice(h * LANES, (h + 1) * LANES)
            row = index[0, 0:1, span]
            for k in range(1, index.shape[1]):
                row = jnp.where(side == k, index[0, k : k + 1, span], row)
            slot = lax.broadcasted_iota(jnp.int32, (1, LANES), 1) + h * LANES
            r = g * per + h
            places[r : r + 1, :] = jnp.where(slot < counts[0, side], row, -1)
    fill_hits(hits, slot_rows(places), 0, per)
    third.wait()
    lat[...] = state[...].T
    send_features(lat[...], hits, (sent,))


def gather_rest(places, lat, gains_in, bias_in, decode_in, hits, columns, s1, s2, s3, gains, bias, decode, sems):
    waits = copies(((gains_in, gains), (bias_in, bias), (decode_in, decode)), sems)
    rows = slot_rows(places)
    fill_hits(hits, rows, len(rows) // 4, len(rows))
    send_features(lat[...], hits, (s1, s2, s3))
    for copy in waits:
        copy.wait()
    lines = [gains[layer] for layer in range(LAYERS)] + [bias[...], decode[...]]
    lines.append(jnp.zeros((8 - 3 * LAYERS - 1, bias.shape[1]), F32))
    columns[...] = jnp.concatenate(lines, axis=0).T


def send_features(lat, hits, outs):
    width = outs[0].shape[1]
    for k, out in enumerate(outs):
        out[...] = jnp.dot(
            lat, hits[:, k * width : (k + 1) * width], preferred_element_type=F32
        ).astype(BF16)


def send_rest(lat, hits, s1, s2, s3):
    send_features(lat[...], hits, (s1, s2, s3))


def build(
    tile_counts, blank, places, tiles, lat, w_self, columns, rows_in, columns_in, capacity_in,
    matrix, half, inverse_rowsum, diagonal, local, own,
    tile_rows, tile_columns, capacity, sems,
):
    waits = copies(((rows_in, tile_rows), (columns_in, tile_columns), (capacity_in, capacity)), sems)
    count = tiles.shape[2]
    node_tiles = matrix.shape[0] // count
    for t in range(node_tiles):
        span = slice(t * count, (t + 1) * count)
        block = tiles[0, t]
        matrix[span, span] = block + block.T
    for copy in waits:
        copy.wait()

    known = tiles.shape[1]
    live = tile_counts[0]
    together = 4

    def add(step, carry):
        for k in range(together):
            t = node_tiles + step * together + k
            at = jnp.minimum(t, known - 1)
            r = pl.multiple_of(tile_rows[0, at] * count, count)
            c = pl.multiple_of(tile_columns[0, at] * count, count)
            block = jnp.where(t < live, tiles[0, at], 0.0)
            matrix[pl.ds(r, count), pl.ds(c, count)] += block
            matrix[pl.ds(c, count), pl.ds(r, count)] += block.T
        return carry

    lax.fori_loop(0, (live - node_tiles + together - 1) // together, add, 0)
    rows = slot_rows(places)
    faces = spread_sum([jnp.ones((1, LANES), F32)] * len(rows), rows, node_tiles)
    total = jnp.zeros((8, matrix.shape[1]), F32)
    for t in range(node_tiles):
        block = matrix[t * count : (t + 1) * count, :]
        half[t * count : (t + 1) * count, :] = block.astype(BF16)
        total = total + jnp.sum(block.reshape(count // 8, 8, matrix.shape[1]), axis=0)
    rowsum = tile_rows_of(jnp.sum(total, axis=0, keepdims=True)) + faces
    inverse_rowsum[...] = lane_rows(1.0 / rowsum)
    diagonal[...] = capacity[...] + rowsum
    local[...] = jnp.dot(lat[...], half[...], preferred_element_type=F32)
    own[...] = own_part(0, lat[...], w_self, columns)


def normed(value, gain):
    scale = lax.rsqrt(jnp.mean(value * value, axis=0, keepdims=True) + 1e-06)
    return (value * scale * gain).astype(BF16)


def project(weight, value):
    return lax.dot_general(weight, value, (((0,), (0,)), ((), ())), preferred_element_type=F32)


def own_part(layer, lat, w_self, columns):
    gain = columns[:, 2 * layer : 2 * layer + 1]
    bias = columns[:, 2 * LAYERS + layer : 2 * LAYERS + layer + 1]
    return project(w_self[layer], normed(lat.astype(F32), gain)) + bias


def local_features(layer, lat, half, w_self, w_out, columns, local, own, before, decoder):
    local[...] = jnp.dot(lat[...], half[...], preferred_element_type=F32)
    own[...] = own_part(layer, lat[...], w_self, columns)
    decode = columns[:, 3 * LAYERS : 3 * LAYERS + 1]
    before[...] = jnp.sum(lat[...].astype(F32) * decode, axis=0, keepdims=True)
    line = jnp.broadcast_to(decode, (decode.shape[0], LANES)).T[0:1, :]
    decoder[...] = jnp.sum(w_out[layer].astype(F32) * line, axis=1, keepdims=True)


def with_slots(local, came, hits):
    return local + lax.dot_general(came, hits, (((1,), (1,)), ((), ())), preferred_element_type=F32)


def activation(layer, arrived, local, own, inverse_rowsum, first_hits, hits, w_neighbour, columns):
    total = with_slots(local[...], arrived[0][...], first_hits[...])
    total = with_slots(total, jnp.concatenate([a[...] for a in arrived[1:]], axis=1), hits[...])
    mean = total * inverse_rowsum[...]
    gain = columns[:, 2 * layer + 1 : 2 * layer + 2]
    linear = own[...] + project(w_neighbour[layer], normed(mean, gain))
    return linear / (1.0 + jnp.exp(-linear))


def first_layer(
    a0, a1, a2, a3, local, own, inverse_rowsum, lat, first_hits, hits, w_neighbour, w_out, columns, new, sent
):
    activated = activation(
        0, (a0, a1, a2, a3), local, own, inverse_rowsum, first_hits, hits, w_neighbour, columns
    ).astype(BF16)
    value = (lat[...].astype(F32) + project(w_out[0], activated)).astype(BF16)
    new[...] = value
    send_features(value, first_hits, (sent,))


def last_layer(
    places, a0, a1, a2, a3, local, own, inverse_rowsum, lat, first_hits, hits, w_neighbour, columns, before, decoder,
    guess, s0, s1, s2, s3,
):
    activated = activation(
        LAYERS - 1, (a0, a1, a2, a3), local, own, inverse_rowsum, first_hits, hits, w_neighbour, columns
    ).astype(BF16)
    row = before[...] + jnp.sum(activated.astype(F32) * decoder[...], axis=0, keepdims=True)
    field = tile_rows_of(row)
    guess[...] = field
    store_sent((s0, s1, s2, s3), pick(field, slot_rows(places)))


def product(matrix, field):
    count = LANES
    width = matrix.shape[1]
    total = jnp.zeros((8, width), F32)
    for t in range(field.shape[0]):
        column = jnp.broadcast_to(field[t : t + 1, :], (count, count)).T
        wide = jnp.concatenate([column] * (width // count), axis=1)
        part = matrix[t * count : (t + 1) * count, :] * wide
        total = total + jnp.sum(part.reshape(count // 8, 8, width), axis=0)
    return tile_rows_of(jnp.sum(total, axis=0, keepdims=True))


def matvec(matrix, vector, out):
    out[...] = product(matrix, vector[...])


def start_basis(places, a0, a1, a2, a3, local, guess, source, diagonal, basis, s0, s1, s2, s3):
    rows = slot_rows(places)
    came = spread_sum(arrived_rows((a0, a1, a2, a3)), rows, guess.shape[0])
    value = (source[...] + local[...] + came) / diagonal[...] - guess[...]
    basis[...] = value
    store_sent((s0, s1, s2, s3), pick(value, rows))


def next_basis(places, a0, a1, a2, a3, local, diagonal, basis, s0, s1, s2, s3):
    rows = slot_rows(places)
    came = spread_sum(arrived_rows((a0, a1, a2, a3)), rows, local.shape[0])
    value = (local[...] + came) / diagonal[...]
    basis[...] = value
    store_sent((s0, s1, s2, s3), pick(value, rows))


def diagonal_mask():
    return lax.broadcasted_iota(jnp.int32, (8, LANES), 0) == lax.broadcasted_iota(jnp.int32, (8, LANES), 1)


def last_basis(places, a0, a1, a2, a3, local, diagonal, b0, b1, matrix, basis, image, packets):
    rows = slot_rows(places)
    came = spread_sum(arrived_rows((a0, a1, a2, a3)), rows, local.shape[0])
    value = (local[...] + came) / diagonal[...]
    basis[...] = value
    mapped = product(matrix, value)
    image[...] = mapped
    held = [b0[...], b1[...], value]
    parts = []
    for k in range(2 * ITERS - 1):
        left, right = held[k // 2], held[(k + 1) // 2]
        parts.append(jnp.sum(left * right * diagonal[...], axis=0, keepdims=True))
    parts.append(jnp.sum(value * mapped, axis=0, keepdims=True))
    parts.append(jnp.zeros((8 - 2 * ITERS, LANES), F32))
    sums = jnp.sum(jnp.concatenate(parts, axis=0), axis=1, keepdims=True)
    row = jnp.sum(jnp.where(diagonal_mask(), sums, 0.0), axis=0, keepdims=True)
    packet = jnp.concatenate([lane_rows(pick(value, rows)), row], axis=1)
    for device in range(packets.shape[0]):
        packets[device] = packet


def added(values):
    values = list(values)
    while len(values) > 1:
        values = [sum(values[i : i + 2][1:], values[i]) for i in range(0, len(values), 2)]
    return values[0]


def finish(sizes, where, packets, places, image, guess, diagonal, b0, b1, b2, field, defect):
    doms, subs = sizes
    width = packets.shape[2] - LANES
    per = width // 4

    def slots(device, g):
        return packets[device, :, g * per : (g + 1) * per]

    edges = []
    for d in range(doms):
        for s in range(subs):
            for m, (i, j) in (((0, d % 2), (d + 1, s)), ((1, s % 2), (d, s + 1))):
                g = MATCHINGS.index(m)
                if i < doms and j < subs:
                    edges.append(slots(d * subs + s, g) * slots(i * subs + j, g))
    edges = added(edges)
    edges = added([edges[:, h : h + LANES] for h in range(0, per, LANES)])
    sums = added([packets[e, :, width : width + LANES] for e in range(doms * subs)])
    last_row = lax.broadcasted_iota(jnp.int32, (8, LANES), 0) == 2 * ITERS - 1
    table = jnp.where(diagonal_mask(), jnp.broadcast_to(sums, (8, LANES)), 0.0)
    table = table + jnp.where(last_row, jnp.broadcast_to(2.0 * edges, (8, LANES)), 0.0)
    columns = jnp.sum(table, axis=1, keepdims=True)
    n = [jnp.broadcast_to(columns[k : k + 1, :], (8, LANES)) for k in range(2 * ITERS)]
    came = []
    for g in range(4):
        mine = slots(where[4 + g], g)
        came += [mine[:, h : h + LANES] for h in range(0, per, LANES)]
    last = (image[...] + spread_sum(came, slot_rows(places), image.shape[0])) / diagonal[...]
    one, zero = jnp.ones((8, LANES), F32), jnp.zeros((8, LANES), F32)

    def paired(left, values):
        total = zero
        for i, a in enumerate(left):
            for j, b in enumerate(left):
                total = total + a * b * values[i + j]
        return total

    gaps = [n[k] - n[k + 1] for k in range(2 * ITERS - 1)]
    residual = [one]
    heading = [one]
    moved = [zero] * ITERS
    size = n[0]
    for step in range(ITERS):
        alpha = size / paired(heading, gaps)
        for i, h in enumerate(heading):
            moved[i] = moved[i] + alpha * h
        change = [
            (heading[i] if i < len(heading) else zero) - (heading[i - 1] if i > 0 else zero)
            for i in range(len(heading) + 1)
        ]
        residual = [
            (residual[i] if i < len(residual) else zero) - alpha * change[i]
            for i in range(len(change))
        ]
        if step + 1 < ITERS:
            following = paired(residual, n)
            beta = following / size
            heading = [
                residual[i] + (beta * heading[i] if i < len(heading) else zero)
                for i in range(len(residual))
            ]
            size = following
    held = [b0[...], b1[...], b2[...], last]
    total = guess[...]
    for c, b in zip(moved, held):
        total = total + c * b
    field[...] = total
    left = zero
    for c, b in zip(residual, held):
        left = left + c * b
    defect[...] = left * diagonal[...]


def mate_of(place, first, size):
    mate = ((place - first) ^ 1) + first
    return mate if place >= first and mate < size else None


def swaps(sizes, turn):
    along, first = MATCHINGS[turn]
    pairs = []
    for dom in range(sizes[0]):
        for sub in range(sizes[1]):
            to = [dom, sub]
            mate = mate_of(to[along], first, sizes[along])
            if mate is not None:
                to[along] = mate
            elif along == 1 and sizes[0] % 2 == 0:
                to[0] ^= 1
            elif along == 0 and sizes[1] % 2 == 0:
                to[1] = (sub + sizes[1] // 2) % sizes[1]
            pairs.append((dom * sizes[1] + sub, to[0] * sizes[1] + to[1]))
    return pairs


def places_of_turns():
    at = [lax.axis_index("dom"), lax.axis_index("sub")]
    sizes = [lax.axis_size("dom"), lax.axis_size("sub")]

    def side(along, first):
        odd = at[along] % 2
        return 2 * along + (odd if first else 1 - odd)

    def partner(along, first):
        mate = jnp.bitwise_xor(at[along] - first, 1) + first
        to = list(at)
        to[along] = jnp.where((at[along] >= first) & (mate < sizes[along]), mate, at[along])
        return to[0] * sizes[1] + to[1]

    out = [value(*m) for value in (side, partner) for m in MATCHINGS]
    return jnp.stack(out).astype(jnp.int32)


def swap(sent, turn):
    axes = ("dom", "sub")
    return lax.ppermute(sent, axes, swaps([lax.axis_size(axis) for axis in axes], turn))


def exchange(sent, first=0):
    return [swap(s, first + i) for i, s in enumerate(sent)]


def all_to_all(messages):
    return lax.all_to_all(messages, ("dom", "sub"), split_axis=0, concat_axis=0, tiled=True)


def per_device(
    state, tile_values, tile_rows, tile_columns, tile_counts, send_nodes, face_counts, capacity,
    source, w_self, w_neighbour, w_out, gains, bias, w_decode,
):
    nodes, width = state.shape
    slots = send_nodes.shape[2]
    tiles = nodes // LANES
    sizes = (lax.axis_size("dom"), lax.axis_size("sub"))
    devices = sizes[0] * sizes[1]
    field = shape((tiles, LANES))
    features = shape((width, nodes))
    vector_sent = [shape((slots // LANES, LANES))] * 4
    decode = w_decode.reshape(1, width)
    where = places_of_turns()
    capacity = capacity.reshape(tiles, LANES)
    source = source.reshape(tiles, LANES)

    one_sent = [shape((width, slots), BF16)]
    square = pltpu.VMEM((nodes, nodes), F32)
    gather_flops = 2 * nodes * slots * width
    lat, first_hits, places, sent, blank = run(
        gather_first,
        [shape((width, nodes), BF16), shape((nodes, slots), BF16), shape((4 * slots // LANES, LANES), jnp.int32)]
        + one_sent + [square],
        (), (where,), (send_nodes, face_counts, state),
        (
            pltpu.VMEM(send_nodes.shape, jnp.int32),
            pltpu.SMEM(face_counts.shape, jnp.int32),
            pltpu.VMEM(state.shape, BF16),
        ),
        waits=3, flops=gather_flops,
    )
    a0 = swap(sent, 0)
    hits, columns, *sent = run(
        gather_rest, [shape((nodes, 3 * slots), BF16), shape((width, 8))] + one_sent * 3,
        (places, lat), (), (gains, bias, decode),
        (pltpu.VMEM(gains.shape, F32), pltpu.VMEM(bias.shape, F32), pltpu.VMEM(decode.shape, F32)),
        waits=3, flops=3 * gather_flops,
    )
    a1, a2, a3 = exchange(sent, 1)
    matrix, half, inverse_rowsum, diagonal, local, own = run(
        build,
        [square, shape((nodes, nodes), BF16), shape((1, nodes)), field, features, features],
        (blank, places, tile_values, lat, w_self, columns),
        (tile_counts,), (tile_rows, tile_columns, capacity),
        (
            pltpu.SMEM(tile_rows.shape, jnp.int32),
            pltpu.SMEM(tile_columns.shape, jnp.int32),
            pltpu.VMEM(capacity.shape, F32),
        ),
        waits=3, flops=0, moved=0, aliases={0: 0},
    )
    lat, sent = run(
        first_layer, [shape((width, nodes), BF16)] + one_sent,
        (a0, a1, a2, a3, local, own, inverse_rowsum, lat, first_hits, hits, w_neighbour, w_out, columns),
        flops=3 * nodes * nodes * width,
    )
    a0 = swap(sent, 0)
    sent = run(send_rest, one_sent * 3, (lat, hits), flops=3 * gather_flops)
    a1, a2, a3 = exchange(sent, 1)
    local, own, before, decoder = run(
        functools.partial(local_features, LAYERS - 1),
        [features, features, shape((1, nodes)), shape((width, 1))],
        (lat, half, w_self, w_out, columns), flops=0, moved=0,
    )
    guess, *sent = run(
        last_layer, [field] + vector_sent,
        (places, a0, a1, a2, a3, local, own, inverse_rowsum, lat, first_hits, hits, w_neighbour, columns, before, decoder),
        flops=3 * nodes * nodes * width,
    )

    def mapped(vector):
        return run(matvec, [field], (matrix, vector), flops=2 * nodes * nodes, moved=4 * nodes * nodes)[0]

    arrived = exchange(sent)
    local = mapped(guess)
    b0, *sent = run(
        start_basis, [field] + vector_sent, (places, *arrived, local, guess, source, diagonal)
    )
    arrived = exchange(sent)
    local = mapped(b0)
    b1, *sent = run(next_basis, [field] + vector_sent, (places, *arrived, local, diagonal))
    arrived = exchange(sent)
    local = mapped(b1)
    b2, image, packets = run(
        last_basis, [field, field, shape((devices, 1, 4 * slots + LANES))],
        (places, *arrived, local, diagonal, b0, b1, matrix),
    )
    packets = all_to_all(packets)
    heat, defect = run(
        functools.partial(finish, sizes), [field, field],
        (packets, places, image, guess, diagonal, b0, b1, b2), (where,),
    )
    return heat.reshape(nodes), defect.reshape(nodes)


def solution(mesh):
    both = ("dom", "sub")
    return jax.shard_map(
        per_device,
        mesh=mesh,
        in_specs=(
            P(both, None),
            P(both, None, None, None),
            P(both, None),
            P(both, None),
            P(both),
            P(both, None, None),
            P(both, None),
            P(both),
            P(both),
            P(),
            P(),
            P(),
            P(),
            P(),
            P(),
        ),
        out_specs=(P(both), P(both)),
        check_vma=False,
    )
```

```python
import functools

import jax
import jax.numpy as jnp
from jax import lax
from jax.experimental import pallas as pl
from jax.experimental.pallas import tpu as pltpu
from jax.sharding import PartitionSpec as P

LAYERS = 2
ITERS = 3
LANES = 128
MATCHINGS = ((1, 1), (1, 0), (0, 0), (0, 1))
VMEM_LIMIT = 24 * 1024 * 1024

F32 = jnp.float32
BF16 = jnp.bfloat16


def shape(dims, dtype=F32):
    return jax.ShapeDtypeStruct(dims, dtype)


def run(body, outs, operands, scalars=(), raw=(), scratch=(), waits=0, flops=1_000_000, moved=1_000_000, aliases={}):
    operands = [
        pltpu.with_memory_space_constraint(x, pltpu.VMEM) if i in aliases else x for i, x in enumerate(operands)
    ]
    smem = pl.BlockSpec(memory_space=pltpu.SMEM)
    vmem = pl.BlockSpec(memory_space=pltpu.VMEM)
    anywhere = pl.BlockSpec(memory_space=pltpu.HBM)
    scratch = list(scratch) + [pltpu.SemaphoreType.DMA((waits,))] * bool(waits)
    return pl.pallas_call(
        body,
        out_shape=outs,
        in_specs=[smem] * len(scalars) + [vmem] * len(operands) + [anywhere] * len(raw),
        out_specs=[vmem] * len(outs),
        scratch_shapes=scratch,
        input_output_aliases={len(scalars) + i: o for i, o in aliases.items()},
        compiler_params=pltpu.CompilerParams(vmem_limit_bytes=VMEM_LIMIT),
        cost_estimate=pl.CostEstimate(flops=flops, bytes_accessed=moved, transcendentals=0),
    )(*scalars, *operands, *(pltpu.with_memory_space_constraint(r, pltpu.HBM) for r in raw))


def copies(pairs, semaphores):
    started = [pltpu.make_async_copy(*pair, semaphores.at[i]) for i, pair in enumerate(pairs)]
    for copy in started:
        copy.start()
    return started


def slot_rows(places):
    return [places[r : r + 1, :] for r in range(places.shape[0])]


def pick(vector, rows):
    index = jnp.concatenate(rows, axis=0)
    low = jnp.bitwise_and(index, LANES - 1)
    high = jnp.right_shift(index, 7)
    out = jnp.zeros(index.shape, F32)
    for t in range(vector.shape[0]):
        spread = jnp.broadcast_to(vector[t : t + 1, :], index.shape)
        got = jnp.take_along_axis(spread, low, axis=1, mode="promise_in_bounds")
        out = jnp.where(high == t, got, out)
    return out


def pieces(value):
    first = value.astype(BF16)
    rest = value - first.astype(F32)
    second = rest.astype(BF16)
    third = (rest - second.astype(F32)).astype(BF16)
    return first, second, third


def low_hits(rows):
    lane = lax.broadcasted_iota(jnp.int32, (LANES, LANES), 0)
    return jnp.concatenate(
        [(lane == jnp.bitwise_and(row, LANES - 1)).astype(F32).astype(BF16) for row in rows], axis=1
    )


def spread_sum(values, rows, tiles):
    tile = lax.broadcasted_iota(jnp.int32, (tiles, LANES), 0)
    parts = [
        jnp.where(tile == jnp.right_shift(row, 7), value, 0.0) for value, row in zip(values, rows)
    ]
    held = jnp.concatenate(parts, axis=1)
    stacked = jnp.concatenate([p.astype(F32) for p in pieces(held)], axis=0).astype(BF16)
    out = lax.dot_general(
        stacked, low_hits(rows), (((1,), (1,)), ((), ())), preferred_element_type=F32
    )
    return out[:tiles] + out[tiles : 2 * tiles] + out[2 * tiles :]


def arrived_rows(refs):
    return [ref[h : h + 1, :] for ref in refs for h in range(ref.shape[0])]


def store_sent(refs, sent):
    per = refs[0].shape[0]
    for k, ref in enumerate(refs):
        ref[...] = sent[k * per : (k + 1) * per, :]


def lane_rows(vector):
    return jnp.concatenate([vector[t : t + 1, :] for t in range(vector.shape[0])], axis=1)


def tile_rows_of(row):
    return jnp.concatenate(
        [row[:, t * LANES : (t + 1) * LANES] for t in range(row.shape[1] // LANES)], axis=0
    )


def fill_hits(hits, rows, first, last):
    nodes = hits.shape[0]
    node = lax.broadcasted_iota(jnp.int32, (nodes, LANES), 0).astype(jnp.int16).reshape(nodes // 16, 16, LANES)
    one, zero = jnp.ones(node.shape, BF16), jnp.zeros(node.shape, BF16)
    for c in range(first, last):
        wide = jnp.broadcast_to(rows[c], (16, LANES)).astype(jnp.int16)
        at = (c - first) * LANES
        hits[:, at : at + LANES] = jnp.where(node == wide[None], one, zero).reshape(nodes, LANES)


def gather_first(
    where, index_in, counts_in, state_in, lat, hits, places, sent, blank, index, counts, state, sems
):
    first, second, third = copies(((index_in, index), (counts_in, counts), (state_in, state)), sems)
    blank[...] = jnp.zeros(blank.shape, F32)
    per = index.shape[2] // LANES
    first.wait()
    second.wait()
    for g in range(index.shape[1]):
        side = where[g]
        for h in range(per):
            span = slice(h * LANES, (h + 1) * LANES)
            row = index[0, 0:1, span]
            for k in range(1, index.shape[1]):
                row = jnp.where(side == k, index[0, k : k + 1, span], row)
            slot = lax.broadcasted_iota(jnp.int32, (1, LANES), 1) + h * LANES
            r = g * per + h
            places[r : r + 1, :] = jnp.where(slot < counts[0, side], row, -1)
    fill_hits(hits, slot_rows(places), 0, per)
    third.wait()
    lat[...] = state[...].T
    send_features(lat[...], hits, (sent,))


def gather_rest(
    places, lat, gains_in, bias_in, decode_in, rows_in, columns_in, capacity_in,
    hits, columns, tile_rows, tile_columns, capacity, s1, s2, s3, gains, bias, decode, sems,
):
    waits = copies(
        (
            (gains_in, gains), (bias_in, bias), (decode_in, decode), (rows_in, tile_rows),
            (columns_in, tile_columns), (capacity_in, capacity),
        ),
        sems,
    )
    rows = slot_rows(places)
    fill_hits(hits, rows, len(rows) // 4, len(rows))
    send_features(lat[...], hits, (s1, s2, s3))
    for copy in waits:
        copy.wait()
    lines = [gains[layer] for layer in range(LAYERS)] + [bias[...], decode[...]]
    lines.append(jnp.zeros((8 - 3 * LAYERS - 1, bias.shape[1]), F32))
    columns[...] = jnp.concatenate(lines, axis=0).T


def send_features(lat, hits, outs):
    width = outs[0].shape[1]
    for k, out in enumerate(outs):
        out[...] = jnp.dot(
            lat, hits[:, k * width : (k + 1) * width], preferred_element_type=F32
        ).astype(BF16)


def send_rest(lat, hits, s1, s2, s3):
    send_features(lat[...], hits, (s1, s2, s3))


def build(
    tile_counts, blank, places, tiles, lat, w_self, columns, rows_in, columns_in, capacity,
    matrix, half, inverse_rowsum, diagonal, local, own,
    tile_rows, tile_columns, sems,
):
    waits = copies(((rows_in, tile_rows), (columns_in, tile_columns)), sems)
    count = tiles.shape[2]
    node_tiles = matrix.shape[0] // count
    for t in range(node_tiles):
        span = slice(t * count, (t + 1) * count)
        block = tiles[0, t]
        matrix[span, span] = block + block.T
    for copy in waits:
        copy.wait()

    known = tiles.shape[1]
    live = tile_counts[0]
    together = 4

    def add(step, carry):
        for k in range(together):
            t = node_tiles + step * together + k
            at = jnp.minimum(t, known - 1)
            r = pl.multiple_of(tile_rows[0, at] * count, count)
            c = pl.multiple_of(tile_columns[0, at] * count, count)
            block = jnp.where(t < live, tiles[0, at], 0.0)
            matrix[pl.ds(r, count), pl.ds(c, count)] += block
            matrix[pl.ds(c, count), pl.ds(r, count)] += block.T
        return carry

    lax.fori_loop(0, (live - node_tiles + together - 1) // together, add, 0)
    rows = slot_rows(places)
    faces = spread_sum([jnp.ones((1, LANES), F32)] * len(rows), rows, node_tiles)
    total = jnp.zeros((8, matrix.shape[1]), F32)
    for t in range(node_tiles):
        block = matrix[t * count : (t + 1) * count, :]
        half[t * count : (t + 1) * count, :] = block.astype(BF16)
        total = total + jnp.sum(block.reshape(count // 8, 8, matrix.shape[1]), axis=0)
    rowsum = tile_rows_of(jnp.sum(total, axis=0, keepdims=True)) + faces
    inverse_rowsum[...] = lane_rows(1.0 / rowsum)
    diagonal[...] = capacity[...] + rowsum
    local[...] = jnp.dot(lat[...], half[...], preferred_element_type=F32)
    own[...] = own_part(0, lat[...], w_self, columns)


def normed(value, gain):
    scale = lax.rsqrt(jnp.mean(value * value, axis=0, keepdims=True) + 1e-06)
    return (value * scale * gain).astype(BF16)


def project(weight, value):
    return lax.dot_general(weight, value, (((0,), (0,)), ((), ())), preferred_element_type=F32)


def own_part(layer, lat, w_self, columns):
    gain = columns[:, 2 * layer : 2 * layer + 1]
    bias = columns[:, 2 * LAYERS + layer : 2 * LAYERS + layer + 1]
    return project(w_self[layer], normed(lat.astype(F32), gain)) + bias


def local_features(layer, lat, half, w_self, w_out, columns, local, own, before, decoder):
    local[...] = jnp.dot(lat[...], half[...], preferred_element_type=F32)
    own[...] = own_part(layer, lat[...], w_self, columns)
    decode = columns[:, 3 * LAYERS : 3 * LAYERS + 1]
    before[...] = jnp.sum(lat[...].astype(F32) * decode, axis=0, keepdims=True)
    line = jnp.broadcast_to(decode, (decode.shape[0], LANES)).T[0:1, :]
    decoder[...] = jnp.sum(w_out[layer].astype(F32) * line, axis=1, keepdims=True)


def with_slots(local, came, hits):
    return local + lax.dot_general(came, hits, (((1,), (1,)), ((), ())), preferred_element_type=F32)


def activation(layer, arrived, local, own, inverse_rowsum, first_hits, hits, w_neighbour, columns):
    total = with_slots(local[...], arrived[0][...], first_hits[...])
    total = with_slots(total, jnp.concatenate([a[...] for a in arrived[1:]], axis=1), hits[...])
    mean = total * inverse_rowsum[...]
    gain = columns[:, 2 * layer + 1 : 2 * layer + 2]
    linear = own[...] + project(w_neighbour[layer], normed(mean, gain))
    return linear / (1.0 + jnp.exp(-linear))


def first_layer(
    a0, a1, a2, a3, local, own, inverse_rowsum, lat, first_hits, hits, w_neighbour, w_out, columns, new, sent
):
    activated = activation(
        0, (a0, a1, a2, a3), local, own, inverse_rowsum, first_hits, hits, w_neighbour, columns
    ).astype(BF16)
    value = (lat[...].astype(F32) + project(w_out[0], activated)).astype(BF16)
    new[...] = value
    send_features(value, first_hits, (sent,))


def last_layer(
    places, a0, a1, a2, a3, local, own, inverse_rowsum, lat, first_hits, hits, w_neighbour, columns, before, decoder,
    guess, s0, s1, s2, s3,
):
    activated = activation(
        LAYERS - 1, (a0, a1, a2, a3), local, own, inverse_rowsum, first_hits, hits, w_neighbour, columns
    ).astype(BF16)
    row = before[...] + jnp.sum(activated.astype(F32) * decoder[...], axis=0, keepdims=True)
    field = tile_rows_of(row)
    guess[...] = field
    store_sent((s0, s1, s2, s3), pick(field, slot_rows(places)))


def product(matrix, field):
    count = LANES
    width = matrix.shape[1]
    total = jnp.zeros((8, width), F32)
    for t in range(field.shape[0]):
        column = jnp.broadcast_to(field[t : t + 1, :], (count, count)).T
        wide = jnp.concatenate([column] * (width // count), axis=1)
        part = matrix[t * count : (t + 1) * count, :] * wide
        total = total + jnp.sum(part.reshape(count // 8, 8, width), axis=0)
    return tile_rows_of(jnp.sum(total, axis=0, keepdims=True))


def matvec(matrix, vector, out):
    out[...] = product(matrix, vector[...])


def start_basis(places, a0, a1, a2, a3, local, guess, source, diagonal, basis, s0, s1, s2, s3):
    rows = slot_rows(places)
    came = spread_sum(arrived_rows((a0, a1, a2, a3)), rows, guess.shape[0])
    value = (source[...] + local[...] + came) / diagonal[...] - guess[...]
    basis[...] = value
    store_sent((s0, s1, s2, s3), pick(value, rows))


def next_basis(places, a0, a1, a2, a3, local, diagonal, basis, s0, s1, s2, s3):
    rows = slot_rows(places)
    came = spread_sum(arrived_rows((a0, a1, a2, a3)), rows, local.shape[0])
    value = (local[...] + came) / diagonal[...]
    basis[...] = value
    store_sent((s0, s1, s2, s3), pick(value, rows))


def diagonal_mask():
    return lax.broadcasted_iota(jnp.int32, (8, LANES), 0) == lax.broadcasted_iota(jnp.int32, (8, LANES), 1)


def last_basis(places, a0, a1, a2, a3, local, diagonal, b0, b1, matrix, basis, image, packets):
    rows = slot_rows(places)
    came = spread_sum(arrived_rows((a0, a1, a2, a3)), rows, local.shape[0])
    value = (local[...] + came) / diagonal[...]
    basis[...] = value
    mapped = product(matrix, value)
    image[...] = mapped
    held = [b0[...], b1[...], value]
    parts = []
    for k in range(2 * ITERS - 1):
        left, right = held[k // 2], held[(k + 1) // 2]
        parts.append(jnp.sum(left * right * diagonal[...], axis=0, keepdims=True))
    parts.append(jnp.sum(value * mapped, axis=0, keepdims=True))
    parts.append(jnp.zeros((8 - 2 * ITERS, LANES), F32))
    sums = jnp.sum(jnp.concatenate(parts, axis=0), axis=1, keepdims=True)
    row = jnp.sum(jnp.where(diagonal_mask(), sums, 0.0), axis=0, keepdims=True)
    packet = jnp.concatenate([lane_rows(pick(value, rows)), row], axis=1)
    for device in range(packets.shape[0]):
        packets[device] = packet


def added(values):
    values = list(values)
    while len(values) > 1:
        values = [sum(values[i : i + 2][1:], values[i]) for i in range(0, len(values), 2)]
    return values[0]


def finish(sizes, where, packets, places, image, guess, diagonal, b0, b1, b2, field, defect):
    doms, subs = sizes
    width = packets.shape[2] - LANES
    per = width // 4

    def slots(device, g):
        return packets[device, :, g * per : (g + 1) * per]

    edges = []
    for d in range(doms):
        for s in range(subs):
            for m, (i, j) in (((0, d % 2), (d + 1, s)), ((1, s % 2), (d, s + 1))):
                g = MATCHINGS.index(m)
                if i < doms and j < subs:
                    edges.append(slots(d * subs + s, g) * slots(i * subs + j, g))
    edges = added(edges)
    edges = added([edges[:, h : h + LANES] for h in range(0, per, LANES)])
    sums = added([packets[e, :, width : width + LANES] for e in range(doms * subs)])
    last_row = lax.broadcasted_iota(jnp.int32, (8, LANES), 0) == 2 * ITERS - 1
    table = jnp.where(diagonal_mask(), jnp.broadcast_to(sums, (8, LANES)), 0.0)
    table = table + jnp.where(last_row, jnp.broadcast_to(2.0 * edges, (8, LANES)), 0.0)
    columns = jnp.sum(table, axis=1, keepdims=True)
    n = [jnp.broadcast_to(columns[k : k + 1, :], (8, LANES)) for k in range(2 * ITERS)]
    came = []
    for g in range(4):
        mine = slots(where[4 + g], g)
        came += [mine[:, h : h + LANES] for h in range(0, per, LANES)]
    last = (image[...] + spread_sum(came, slot_rows(places), image.shape[0])) / diagonal[...]
    one, zero = jnp.ones((8, LANES), F32), jnp.zeros((8, LANES), F32)

    def paired(left, values):
        total = zero
        for i, a in enumerate(left):
            for j, b in enumerate(left):
                total = total + a * b * values[i + j]
        return total

    gaps = [n[k] - n[k + 1] for k in range(2 * ITERS - 1)]
    residual = [one]
    heading = [one]
    moved = [zero] * ITERS
    size = n[0]
    for step in range(ITERS):
        alpha = size / paired(heading, gaps)
        for i, h in enumerate(heading):
            moved[i] = moved[i] + alpha * h
        change = [
            (heading[i] if i < len(heading) else zero) - (heading[i - 1] if i > 0 else zero)
            for i in range(len(heading) + 1)
        ]
        residual = [
            (residual[i] if i < len(residual) else zero) - alpha * change[i]
            for i in range(len(change))
        ]
        if step + 1 < ITERS:
            following = paired(residual, n)
            beta = following / size
            heading = [
                residual[i] + (beta * heading[i] if i < len(heading) else zero)
                for i in range(len(residual))
            ]
            size = following
    held = [b0[...], b1[...], b2[...], last]
    total = guess[...]
    for c, b in zip(moved, held):
        total = total + c * b
    field[...] = total
    left = zero
    for c, b in zip(residual, held):
        left = left + c * b
    defect[...] = left * diagonal[...]


def mate_of(place, first, size):
    mate = ((place - first) ^ 1) + first
    return mate if place >= first and mate < size else None


def swaps(sizes, turn):
    along, first = MATCHINGS[turn]
    pairs = []
    for dom in range(sizes[0]):
        for sub in range(sizes[1]):
            to = [dom, sub]
            mate = mate_of(to[along], first, sizes[along])
            if mate is not None:
                to[along] = mate
            elif along == 1 and sizes[0] % 2 == 0:
                to[0] ^= 1
            elif along == 0 and sizes[1] % 2 == 0:
                to[1] = (sub + sizes[1] // 2) % sizes[1]
            pairs.append((dom * sizes[1] + sub, to[0] * sizes[1] + to[1]))
    return pairs


def places_of_turns():
    at = [lax.axis_index("dom"), lax.axis_index("sub")]
    sizes = [lax.axis_size("dom"), lax.axis_size("sub")]

    def side(along, first):
        odd = at[along] % 2
        return 2 * along + (odd if first else 1 - odd)

    def partner(along, first):
        mate = jnp.bitwise_xor(at[along] - first, 1) + first
        to = list(at)
        to[along] = jnp.where((at[along] >= first) & (mate < sizes[along]), mate, at[along])
        return to[0] * sizes[1] + to[1]

    out = [value(*m) for value in (side, partner) for m in MATCHINGS]
    return jnp.stack(out).astype(jnp.int32)


def swap(sent, turn):
    axes = ("dom", "sub")
    return lax.ppermute(sent, axes, swaps([lax.axis_size(axis) for axis in axes], turn))


def exchange(sent, first=0):
    return [swap(s, first + i) for i, s in enumerate(sent)]


def all_to_all(messages):
    return lax.all_to_all(messages, ("dom", "sub"), split_axis=0, concat_axis=0, tiled=True)


def per_device(
    state, tile_values, tile_rows, tile_columns, tile_counts, send_nodes, face_counts, capacity,
    source, w_self, w_neighbour, w_out, gains, bias, w_decode,
):
    nodes, width = state.shape
    slots = send_nodes.shape[2]
    tiles = nodes // LANES
    sizes = (lax.axis_size("dom"), lax.axis_size("sub"))
    devices = sizes[0] * sizes[1]
    field = shape((tiles, LANES))
    features = shape((width, nodes))
    vector_sent = [shape((slots // LANES, LANES))] * 4
    decode = w_decode.reshape(1, width)
    where = places_of_turns()
    capacity = capacity.reshape(tiles, LANES)
    source = source.reshape(tiles, LANES)

    one_sent = [shape((width, slots), BF16)]
    square = pltpu.VMEM((nodes, nodes), F32)
    gather_flops = 2 * nodes * slots * width
    lat, first_hits, places, sent, blank = run(
        gather_first,
        [shape((width, nodes), BF16), shape((nodes, slots), BF16), shape((4 * slots // LANES, LANES), jnp.int32)]
        + one_sent + [square],
        (), (where,), (send_nodes, face_counts, state),
        (
            pltpu.VMEM(send_nodes.shape, jnp.int32),
            pltpu.SMEM(face_counts.shape, jnp.int32),
            pltpu.VMEM(state.shape, BF16),
        ),
        waits=3, flops=gather_flops,
    )
    a0 = swap(sent, 0)
    hits, columns, tile_rows, tile_columns, capacity, *sent = run(
        gather_rest,
        [shape((nodes, 3 * slots), BF16), shape((width, 8)), shape(tile_rows.shape, jnp.int32),
         shape(tile_columns.shape, jnp.int32), field] + one_sent * 3,
        (places, lat), (), (gains, bias, decode, tile_rows, tile_columns, capacity),
        (pltpu.VMEM(gains.shape, F32), pltpu.VMEM(bias.shape, F32), pltpu.VMEM(decode.shape, F32)),
        waits=6, flops=3 * gather_flops,
    )
    a1, a2, a3 = exchange(sent, 1)
    matrix, half, inverse_rowsum, diagonal, local, own = run(
        build,
        [square, shape((nodes, nodes), BF16), shape((1, nodes)), field, features, features],
        (blank, places, tile_values, lat, w_self, columns, tile_rows, tile_columns, capacity),
        (tile_counts,), (),
        (
            pltpu.SMEM(tile_rows.shape, jnp.int32),
            pltpu.SMEM(tile_columns.shape, jnp.int32),
        ),
        waits=2, flops=0, moved=0, aliases={0: 0},
    )
    lat, sent = run(
        first_layer, [shape((width, nodes), BF16)] + one_sent,
        (a0, a1, a2, a3, local, own, inverse_rowsum, lat, first_hits, hits, w_neighbour, w_out, columns),
        flops=3 * nodes * nodes * width,
    )
    a0 = swap(sent, 0)
    sent = run(send_rest, one_sent * 3, (lat, hits), flops=3 * gather_flops)
    a1, a2, a3 = exchange(sent, 1)
    local, own, before, decoder = run(
        functools.partial(local_features, LAYERS - 1),
        [features, features, shape((1, nodes)), shape((width, 1))],
        (lat, half, w_self, w_out, columns), flops=0, moved=0,
    )
    guess, *sent = run(
        last_layer, [field] + vector_sent,
        (places, a0, a1, a2, a3, local, own, inverse_rowsum, lat, first_hits, hits, w_neighbour, columns, before, decoder),
        flops=3 * nodes * nodes * width,
    )

    def mapped(vector):
        return run(matvec, [field], (matrix, vector), flops=2 * nodes * nodes, moved=4 * nodes * nodes)[0]

    arrived = exchange(sent)
    local = mapped(guess)
    b0, *sent = run(
        start_basis, [field] + vector_sent, (places, *arrived, local, guess, source, diagonal)
    )
    arrived = exchange(sent)
    local = mapped(b0)
    b1, *sent = run(next_basis, [field] + vector_sent, (places, *arrived, local, diagonal))
    arrived = exchange(sent)
    local = mapped(b1)
    b2, image, packets = run(
        last_basis, [field, field, shape((devices, 1, 4 * slots + LANES))],
        (places, *arrived, local, diagonal, b0, b1, matrix),
    )
    packets = all_to_all(packets)
    heat, defect = run(
        functools.partial(finish, sizes), [field, field],
        (packets, places, image, guess, diagonal, b0, b1, b2), (where,),
    )
    return heat.reshape(nodes), defect.reshape(nodes)


def solution(mesh):
    both = ("dom", "sub")
    return jax.shard_map(
        per_device,
        mesh=mesh,
        in_specs=(
            P(both, None),
            P(both, None, None, None),
            P(both, None),
            P(both, None),
            P(both),
            P(both, None, None),
            P(both, None),
            P(both),
            P(both),
            P(),
            P(),
            P(),
            P(),
            P(),
            P(),
        ),
        out_specs=(P(both), P(both)),
        check_vma=False,
    )
```

```python
import functools

import jax
import jax.numpy as jnp
from jax import lax
from jax.experimental import pallas as pl
from jax.experimental.pallas import tpu as pltpu
from jax.sharding import PartitionSpec as P

LAYERS = 2
ITERS = 3
LANES = 128
MATCHINGS = ((1, 1), (1, 0), (0, 0), (0, 1))
VMEM_LIMIT = 24 * 1024 * 1024

F32 = jnp.float32
BF16 = jnp.bfloat16


def shape(dims, dtype=F32):
    return jax.ShapeDtypeStruct(dims, dtype)


def run(body, outs, operands, scalars=(), raw=(), scratch=(), waits=0, flops=1_000_000, moved=1_000_000):
    smem = pl.BlockSpec(memory_space=pltpu.SMEM)
    vmem = pl.BlockSpec(memory_space=pltpu.VMEM)
    anywhere = pl.BlockSpec(memory_space=pltpu.HBM)
    scratch = list(scratch) + [pltpu.SemaphoreType.DMA((waits,))] * bool(waits)
    return pl.pallas_call(
        body,
        out_shape=outs,
        in_specs=[smem] * len(scalars) + [vmem] * len(operands) + [anywhere] * len(raw),
        out_specs=[vmem] * len(outs),
        scratch_shapes=scratch,
        compiler_params=pltpu.CompilerParams(vmem_limit_bytes=VMEM_LIMIT),
        cost_estimate=pl.CostEstimate(flops=flops, bytes_accessed=moved, transcendentals=0),
    )(*scalars, *operands, *(pltpu.with_memory_space_constraint(r, pltpu.HBM) for r in raw))


def copies(pairs, semaphores):
    started = [pltpu.make_async_copy(*pair, semaphores.at[i]) for i, pair in enumerate(pairs)]
    for copy in started:
        copy.start()
    return started


def slot_rows(places):
    return [places[r : r + 1, :] for r in range(places.shape[0])]


def pick(vector, rows):
    index = jnp.concatenate(rows, axis=0)
    low = jnp.bitwise_and(index, LANES - 1)
    high = jnp.right_shift(index, 7)
    out = jnp.zeros(index.shape, F32)
    for t in range(vector.shape[0]):
        spread = jnp.broadcast_to(vector[t : t + 1, :], index.shape)
        got = jnp.take_along_axis(spread, low, axis=1, mode="promise_in_bounds")
        out = jnp.where(high == t, got, out)
    return out


def pieces(value):
    first = value.astype(BF16)
    rest = value - first.astype(F32)
    second = rest.astype(BF16)
    third = (rest - second.astype(F32)).astype(BF16)
    return first, second, third


def low_hits(rows):
    lane = lax.broadcasted_iota(jnp.int32, (LANES, LANES), 0)
    return jnp.concatenate(
        [(lane == jnp.bitwise_and(row, LANES - 1)).astype(F32).astype(BF16) for row in rows], axis=1
    )


def spread_sum(values, rows, tiles):
    tile = lax.broadcasted_iota(jnp.int32, (tiles, LANES), 0)
    parts = [
        jnp.where(tile == jnp.right_shift(row, 7), value, 0.0) for value, row in zip(values, rows)
    ]
    held = jnp.concatenate(parts, axis=1)
    stacked = jnp.concatenate([p.astype(F32) for p in pieces(held)], axis=0).astype(BF16)
    out = lax.dot_general(
        stacked, low_hits(rows), (((1,), (1,)), ((), ())), preferred_element_type=F32
    )
    return out[:tiles] + out[tiles : 2 * tiles] + out[2 * tiles :]


def arrived_rows(refs):
    return [ref[h : h + 1, :] for ref in refs for h in range(ref.shape[0])]


def store_sent(refs, sent):
    per = refs[0].shape[0]
    for k, ref in enumerate(refs):
        ref[...] = sent[k * per : (k + 1) * per, :]


def lane_rows(vector):
    return jnp.concatenate([vector[t : t + 1, :] for t in range(vector.shape[0])], axis=1)


def tile_rows_of(row):
    return jnp.concatenate(
        [row[:, t * LANES : (t + 1) * LANES] for t in range(row.shape[1] // LANES)], axis=0
    )


def fill_hits(hits, rows, first, last):
    nodes = hits.shape[0]
    node = lax.broadcasted_iota(jnp.int32, (nodes, LANES), 0).astype(jnp.int16).reshape(nodes // 16, 16, LANES)
    one, zero = jnp.ones(node.shape, BF16), jnp.zeros(node.shape, BF16)
    for c in range(first, last):
        wide = jnp.broadcast_to(rows[c], (16, LANES)).astype(jnp.int16)
        at = (c - first) * LANES
        hits[:, at : at + LANES] = jnp.where(node == wide[None], one, zero).reshape(nodes, LANES)


def gather_first(
    where, index_in, counts_in, state_in, lat, hits, places, sent, index, counts, state, sems
):
    first, second, third = copies(((index_in, index), (counts_in, counts), (state_in, state)), sems)
    per = index.shape[2] // LANES
    first.wait()
    second.wait()
    for g in range(index.shape[1]):
        side = where[g]
        for h in range(per):
            span = slice(h * LANES, (h + 1) * LANES)
            row = index[0, 0:1, span]
            for k in range(1, index.shape[1]):
                row = jnp.where(side == k, index[0, k : k + 1, span], row)
            slot = lax.broadcasted_iota(jnp.int32, (1, LANES), 1) + h * LANES
            r = g * per + h
            places[r : r + 1, :] = jnp.where(slot < counts[0, side], row, -1)
    fill_hits(hits, slot_rows(places), 0, per)
    third.wait()
    lat[...] = state[...].T
    send_features(lat[...], hits, (sent,))


def gather_rest(places, lat, gains_in, bias_in, decode_in, hits, columns, s1, s2, s3, gains, bias, decode, sems):
    waits = copies(((gains_in, gains), (bias_in, bias), (decode_in, decode)), sems)
    rows = slot_rows(places)
    fill_hits(hits, rows, len(rows) // 4, len(rows))
    send_features(lat[...], hits, (s1, s2, s3))
    for copy in waits:
        copy.wait()
    lines = [gains[layer] for layer in range(LAYERS)] + [bias[...], decode[...]]
    lines.append(jnp.zeros((8 - 3 * LAYERS - 1, bias.shape[1]), F32))
    columns[...] = jnp.concatenate(lines, axis=0).T


def send_features(lat, hits, outs):
    width = outs[0].shape[1]
    for k, out in enumerate(outs):
        out[...] = jnp.dot(
            lat, hits[:, k * width : (k + 1) * width], preferred_element_type=F32
        ).astype(BF16)


def send_rest(lat, hits, s1, s2, s3):
    send_features(lat[...], hits, (s1, s2, s3))


def build(
    tile_counts, places, tiles, lat, w_self, columns, rows_in, columns_in, capacity_in,
    matrix, half, inverse_rowsum, diagonal, local, own,
    tile_rows, tile_columns, capacity, sems,
):
    waits = copies(((rows_in, tile_rows), (columns_in, tile_columns), (capacity_in, capacity)), sems)
    count = tiles.shape[2]
    node_tiles = matrix.shape[0] // count
    matrix[...] = jnp.zeros(matrix.shape, F32)
    for t in range(node_tiles):
        span = slice(t * count, (t + 1) * count)
        block = tiles[0, t]
        matrix[span, span] = block + block.T
    for copy in waits:
        copy.wait()

    known = tiles.shape[1]
    live = tile_counts[0]
    together = 4

    def add(step, carry):
        for k in range(together):
            t = node_tiles + step * together + k
            at = jnp.minimum(t, known - 1)
            r = pl.multiple_of(tile_rows[0, at] * count, count)
            c = pl.multiple_of(tile_columns[0, at] * count, count)
            block = jnp.where(t < live, tiles[0, at], 0.0)
            matrix[pl.ds(r, count), pl.ds(c, count)] += block
            matrix[pl.ds(c, count), pl.ds(r, count)] += block.T
        return carry

    lax.fori_loop(0, (live - node_tiles + together - 1) // together, add, 0)
    rows = slot_rows(places)
    faces = spread_sum([jnp.ones((1, LANES), F32)] * len(rows), rows, node_tiles)
    total = jnp.zeros((8, matrix.shape[1]), F32)
    for t in range(node_tiles):
        block = matrix[t * count : (t + 1) * count, :]
        half[t * count : (t + 1) * count, :] = block.astype(BF16)
        total = total + jnp.sum(block.reshape(count // 8, 8, matrix.shape[1]), axis=0)
    rowsum = tile_rows_of(jnp.sum(total, axis=0, keepdims=True)) + faces
    inverse_rowsum[...] = lane_rows(1.0 / rowsum)
    diagonal[...] = capacity[...] + rowsum
    local[...] = jnp.dot(lat[...], half[...], preferred_element_type=F32)
    own[...] = own_part(0, lat[...], w_self, columns)


def normed(value, gain):
    scale = lax.rsqrt(jnp.mean(value * value, axis=0, keepdims=True) + 1e-06)
    return (value * scale * gain).astype(BF16)


def project(weight, value):
    return lax.dot_general(weight, value, (((0,), (0,)), ((), ())), preferred_element_type=F32)


def own_part(layer, lat, w_self, columns):
    gain = columns[:, 2 * layer : 2 * layer + 1]
    bias = columns[:, 2 * LAYERS + layer : 2 * LAYERS + layer + 1]
    return project(w_self[layer], normed(lat.astype(F32), gain)) + bias


def local_features(layer, lat, half, w_self, w_out, columns, local, own, before, decoder):
    local[...] = jnp.dot(lat[...], half[...], preferred_element_type=F32)
    own[...] = own_part(layer, lat[...], w_self, columns)
    decode = columns[:, 3 * LAYERS : 3 * LAYERS + 1]
    before[...] = jnp.sum(lat[...].astype(F32) * decode, axis=0, keepdims=True)
    line = jnp.broadcast_to(decode, (decode.shape[0], LANES)).T[0:1, :]
    decoder[...] = jnp.sum(w_out[layer].astype(F32) * line, axis=1, keepdims=True)


def with_slots(local, came, hits):
    return local + lax.dot_general(came, hits, (((1,), (1,)), ((), ())), preferred_element_type=F32)


def activation(layer, arrived, local, own, inverse_rowsum, first_hits, hits, w_neighbour, columns):
    total = with_slots(local[...], arrived[0][...], first_hits[...])
    total = with_slots(total, jnp.concatenate([a[...] for a in arrived[1:]], axis=1), hits[...])
    mean = total * inverse_rowsum[...]
    gain = columns[:, 2 * layer + 1 : 2 * layer + 2]
    linear = own[...] + project(w_neighbour[layer], normed(mean, gain))
    return linear / (1.0 + jnp.exp(-linear))


def first_layer(
    a0, a1, a2, a3, local, own, inverse_rowsum, lat, first_hits, hits, w_neighbour, w_out, columns, new, sent
):
    activated = activation(
        0, (a0, a1, a2, a3), local, own, inverse_rowsum, first_hits, hits, w_neighbour, columns
    ).astype(BF16)
    value = (lat[...].astype(F32) + project(w_out[0], activated)).astype(BF16)
    new[...] = value
    send_features(value, first_hits, (sent,))


def last_layer(
    places, a0, a1, a2, a3, local, own, inverse_rowsum, lat, first_hits, hits, w_neighbour, columns, before, decoder,
    guess, s0, s1, s2, s3,
):
    activated = activation(
        LAYERS - 1, (a0, a1, a2, a3), local, own, inverse_rowsum, first_hits, hits, w_neighbour, columns
    ).astype(BF16)
    row = before[...] + jnp.sum(activated.astype(F32) * decoder[...], axis=0, keepdims=True)
    field = tile_rows_of(row)
    guess[...] = field
    store_sent((s0, s1, s2, s3), pick(field, slot_rows(places)))


def product(matrix, field):
    count = LANES
    width = matrix.shape[1]
    total = jnp.zeros((8, width), F32)
    for t in range(field.shape[0]):
        column = jnp.broadcast_to(field[t : t + 1, :], (count, count)).T
        wide = jnp.concatenate([column] * (width // count), axis=1)
        part = matrix[t * count : (t + 1) * count, :] * wide
        total = total + jnp.sum(part.reshape(count // 8, 8, width), axis=0)
    return tile_rows_of(jnp.sum(total, axis=0, keepdims=True))


def matvec(matrix, vector, out):
    out[...] = product(matrix, vector[...])


def start_basis(places, a0, a1, a2, a3, local, guess, source, diagonal, basis, s0, s1, s2, s3):
    rows = slot_rows(places)
    came = spread_sum(arrived_rows((a0, a1, a2, a3)), rows, guess.shape[0])
    value = (source[...] + local[...] + came) / diagonal[...] - guess[...]
    basis[...] = value
    store_sent((s0, s1, s2, s3), pick(value, rows))


def next_basis(places, a0, a1, a2, a3, local, diagonal, basis, s0, s1, s2, s3):
    rows = slot_rows(places)
    came = spread_sum(arrived_rows((a0, a1, a2, a3)), rows, local.shape[0])
    value = (local[...] + came) / diagonal[...]
    basis[...] = value
    store_sent((s0, s1, s2, s3), pick(value, rows))


def diagonal_mask():
    return lax.broadcasted_iota(jnp.int32, (8, LANES), 0) == lax.broadcasted_iota(jnp.int32, (8, LANES), 1)


def last_basis(places, a0, a1, a2, a3, local, diagonal, b0, b1, matrix, basis, image, packets):
    rows = slot_rows(places)
    came = spread_sum(arrived_rows((a0, a1, a2, a3)), rows, local.shape[0])
    value = (local[...] + came) / diagonal[...]
    basis[...] = value
    mapped = product(matrix, value)
    image[...] = mapped
    held = [b0[...], b1[...], value]
    parts = []
    for k in range(2 * ITERS - 1):
        left, right = held[k // 2], held[(k + 1) // 2]
        parts.append(jnp.sum(left * right * diagonal[...], axis=0, keepdims=True))
    parts.append(jnp.sum(value * mapped, axis=0, keepdims=True))
    parts.append(jnp.zeros((8 - 2 * ITERS, LANES), F32))
    sums = jnp.sum(jnp.concatenate(parts, axis=0), axis=1, keepdims=True)
    row = jnp.sum(jnp.where(diagonal_mask(), sums, 0.0), axis=0, keepdims=True)
    packet = jnp.concatenate([lane_rows(pick(value, rows)), row], axis=1)
    for device in range(packets.shape[0]):
        packets[device] = packet


def added(values):
    values = list(values)
    while len(values) > 1:
        values = [sum(values[i : i + 2][1:], values[i]) for i in range(0, len(values), 2)]
    return values[0]


def finish(sizes, where, packets, places, image, guess, diagonal, b0, b1, b2, field, defect):
    doms, subs = sizes
    width = packets.shape[2] - LANES
    per = width // 4

    def slots(device, g):
        return packets[device, :, g * per : (g + 1) * per]

    edges = []
    for d in range(doms):
        for s in range(subs):
            for m, (i, j) in (((0, d % 2), (d + 1, s)), ((1, s % 2), (d, s + 1))):
                g = MATCHINGS.index(m)
                if i < doms and j < subs:
                    edges.append(slots(d * subs + s, g) * slots(i * subs + j, g))
    edges = added(edges)
    edges = added([edges[:, h : h + LANES] for h in range(0, per, LANES)])
    sums = added([packets[e, :, width : width + LANES] for e in range(doms * subs)])
    last_row = lax.broadcasted_iota(jnp.int32, (8, LANES), 0) == 2 * ITERS - 1
    table = jnp.where(diagonal_mask(), jnp.broadcast_to(sums, (8, LANES)), 0.0)
    table = table + jnp.where(last_row, jnp.broadcast_to(2.0 * edges, (8, LANES)), 0.0)
    columns = jnp.sum(table, axis=1, keepdims=True)
    n = [jnp.broadcast_to(columns[k : k + 1, :], (8, LANES)) for k in range(2 * ITERS)]
    came = []
    for g in range(4):
        mine = slots(where[4 + g], g)
        came += [mine[:, h : h + LANES] for h in range(0, per, LANES)]
    last = (image[...] + spread_sum(came, slot_rows(places), image.shape[0])) / diagonal[...]
    one, zero = jnp.ones((8, LANES), F32), jnp.zeros((8, LANES), F32)

    def paired(left, values):
        total = zero
        for i, a in enumerate(left):
            for j, b in enumerate(left):
                total = total + a * b * values[i + j]
        return total

    gaps = [n[k] - n[k + 1] for k in range(2 * ITERS - 1)]
    residual = [one]
    heading = [one]
    moved = [zero] * ITERS
    size = n[0]
    for step in range(ITERS):
        alpha = size / paired(heading, gaps)
        for i, h in enumerate(heading):
            moved[i] = moved[i] + alpha * h
        change = [
            (heading[i] if i < len(heading) else zero) - (heading[i - 1] if i > 0 else zero)
            for i in range(len(heading) + 1)
        ]
        residual = [
            (residual[i] if i < len(residual) else zero) - alpha * change[i]
            for i in range(len(change))
        ]
        if step + 1 < ITERS:
            following = paired(residual, n)
            beta = following / size
            heading = [
                residual[i] + (beta * heading[i] if i < len(heading) else zero)
                for i in range(len(residual))
            ]
            size = following
    held = [b0[...], b1[...], b2[...], last]
    total = guess[...]
    for c, b in zip(moved, held):
        total = total + c * b
    field[...] = total
    left = zero
    for c, b in zip(residual, held):
        left = left + c * b
    defect[...] = left * diagonal[...]


def mate_of(place, first, size):
    mate = ((place - first) ^ 1) + first
    return mate if place >= first and mate < size else None


def swaps(sizes, turn, mirrored):
    along, first = MATCHINGS[turn]
    pairs = []
    for dom in range(sizes[0]):
        for sub in range(sizes[1]):
            to = [dom, sub]
            mate = mate_of(to[along], first, sizes[along])
            if mate is not None:
                to[along] = mate
            elif along == 1 and sizes[0] % 2 == 0:
                to[0] ^= 1
            elif along == 0 and sizes[1] % 2 == 0:
                to[1] = sizes[1] - 1 - sub if mirrored else (sub + sizes[1] // 2) % sizes[1]
            pairs.append((dom * sizes[1] + sub, to[0] * sizes[1] + to[1]))
    return pairs


def places_of_turns():
    at = [lax.axis_index("dom"), lax.axis_index("sub")]
    sizes = [lax.axis_size("dom"), lax.axis_size("sub")]

    def side(along, first):
        odd = at[along] % 2
        return 2 * along + (odd if first else 1 - odd)

    def partner(along, first):
        mate = jnp.bitwise_xor(at[along] - first, 1) + first
        to = list(at)
        to[along] = jnp.where((at[along] >= first) & (mate < sizes[along]), mate, at[along])
        return to[0] * sizes[1] + to[1]

    out = [value(*m) for value in (side, partner) for m in MATCHINGS]
    return jnp.stack(out).astype(jnp.int32)


def swap(sent, turn):
    axes = ("dom", "sub")
    small = sent.dtype == F32
    return lax.ppermute(sent, axes, swaps([lax.axis_size(axis) for axis in axes], turn, small))


def exchange(sent, first=0):
    return [swap(s, first + i) for i, s in enumerate(sent)]


def all_to_all(messages):
    return lax.all_to_all(messages, ("dom", "sub"), split_axis=0, concat_axis=0, tiled=True)


def per_device(
    state, tile_values, tile_rows, tile_columns, tile_counts, send_nodes, face_counts, capacity,
    source, w_self, w_neighbour, w_out, gains, bias, w_decode,
):
    nodes, width = state.shape
    slots = send_nodes.shape[2]
    tiles = nodes // LANES
    sizes = (lax.axis_size("dom"), lax.axis_size("sub"))
    devices = sizes[0] * sizes[1]
    field = shape((tiles, LANES))
    features = shape((width, nodes))
    vector_sent = [shape((slots // LANES, LANES))] * 4
    decode = w_decode.reshape(1, width)
    where = places_of_turns()
    capacity = capacity.reshape(tiles, LANES)
    source = source.reshape(tiles, LANES)

    one_sent = [shape((width, slots), BF16)]
    gather_flops = 2 * nodes * slots * width
    lat, first_hits, places, sent = run(
        gather_first,
        [shape((width, nodes), BF16), shape((nodes, slots), BF16), shape((4 * slots // LANES, LANES), jnp.int32)]
        + one_sent,
        (), (where,), (send_nodes, face_counts, state),
        (
            pltpu.VMEM(send_nodes.shape, jnp.int32),
            pltpu.SMEM(face_counts.shape, jnp.int32),
            pltpu.VMEM(state.shape, BF16),
        ),
        waits=3, flops=gather_flops,
    )
    a0 = swap(sent, 0)
    hits, columns, *sent = run(
        gather_rest, [shape((nodes, 3 * slots), BF16), shape((width, 8))] + one_sent * 3,
        (places, lat), (), (gains, bias, decode),
        (pltpu.VMEM(gains.shape, F32), pltpu.VMEM(bias.shape, F32), pltpu.VMEM(decode.shape, F32)),
        waits=3, flops=3 * gather_flops,
    )
    a1, a2, a3 = exchange(sent, 1)
    matrix, half, inverse_rowsum, diagonal, local, own = run(
        build,
        [shape((nodes, nodes)), shape((nodes, nodes), BF16), shape((1, nodes)), field, features, features],
        (places, tile_values, lat, w_self, columns),
        (tile_counts,), (tile_rows, tile_columns, capacity),
        (
            pltpu.SMEM(tile_rows.shape, jnp.int32),
            pltpu.SMEM(tile_columns.shape, jnp.int32),
            pltpu.VMEM(capacity.shape, F32),
        ),
        waits=3, flops=0, moved=0,
    )
    lat, sent = run(
        first_layer, [shape((width, nodes), BF16)] + one_sent,
        (a0, a1, a2, a3, local, own, inverse_rowsum, lat, first_hits, hits, w_neighbour, w_out, columns),
        flops=3 * nodes * nodes * width,
    )
    a0 = swap(sent, 0)
    sent = run(send_rest, one_sent * 3, (lat, hits), flops=3 * gather_flops)
    a1, a2, a3 = exchange(sent, 1)
    local, own, before, decoder = run(
        functools.partial(local_features, LAYERS - 1),
        [features, features, shape((1, nodes)), shape((width, 1))],
        (lat, half, w_self, w_out, columns), flops=0, moved=0,
    )
    guess, *sent = run(
        last_layer, [field] + vector_sent,
        (places, a0, a1, a2, a3, local, own, inverse_rowsum, lat, first_hits, hits, w_neighbour, columns, before, decoder),
        flops=3 * nodes * nodes * width,
    )

    def mapped(vector):
        return run(matvec, [field], (matrix, vector), flops=2 * nodes * nodes, moved=4 * nodes * nodes)[0]

    arrived = exchange(sent)
    local = mapped(guess)
    b0, *sent = run(
        start_basis, [field] + vector_sent, (places, *arrived, local, guess, source, diagonal)
    )
    arrived = exchange(sent)
    local = mapped(b0)
    b1, *sent = run(next_basis, [field] + vector_sent, (places, *arrived, local, diagonal))
    arrived = exchange(sent)
    local = mapped(b1)
    b2, image, packets = run(
        last_basis, [field, field, shape((devices, 1, 4 * slots + LANES))],
        (places, *arrived, local, diagonal, b0, b1, matrix),
    )
    packets = all_to_all(packets)
    heat, defect = run(
        functools.partial(finish, sizes), [field, field],
        (packets, places, image, guess, diagonal, b0, b1, b2), (where,),
    )
    return heat.reshape(nodes), defect.reshape(nodes)


def solution(mesh):
    both = ("dom", "sub")
    return jax.shard_map(
        per_device,
        mesh=mesh,
        in_specs=(
            P(both, None),
            P(both, None, None, None),
            P(both, None),
            P(both, None),
            P(both),
            P(both, None, None),
            P(both, None),
            P(both),
            P(both),
            P(),
            P(),
            P(),
            P(),
            P(),
            P(),
        ),
        out_specs=(P(both), P(both)),
        check_vma=False,
    )
```

```python
import functools

import jax
import jax.numpy as jnp
from jax import lax
from jax.experimental import pallas as pl
from jax.experimental.pallas import tpu as pltpu
from jax.sharding import PartitionSpec as P

LAYERS = 2
ITERS = 3
LANES = 128
MATCHINGS = ((1, 1), (1, 0), (0, 1), (0, 0))
VMEM_LIMIT = 24 * 1024 * 1024

F32 = jnp.float32
BF16 = jnp.bfloat16


def shape(dims, dtype=F32):
    return jax.ShapeDtypeStruct(dims, dtype)


def run(body, outs, operands, scalars=(), raw=(), scratch=(), waits=0, flops=1_000_000, moved=1_000_000):
    smem = pl.BlockSpec(memory_space=pltpu.SMEM)
    vmem = pl.BlockSpec(memory_space=pltpu.VMEM)
    anywhere = pl.BlockSpec(memory_space=pltpu.HBM)
    scratch = list(scratch) + [pltpu.SemaphoreType.DMA((waits,))] * bool(waits)
    return pl.pallas_call(
        body,
        out_shape=outs,
        in_specs=[smem] * len(scalars) + [vmem] * len(operands) + [anywhere] * len(raw),
        out_specs=[vmem] * len(outs),
        scratch_shapes=scratch,
        compiler_params=pltpu.CompilerParams(vmem_limit_bytes=VMEM_LIMIT),
        cost_estimate=pl.CostEstimate(flops=flops, bytes_accessed=moved, transcendentals=0),
    )(*scalars, *operands, *(pltpu.with_memory_space_constraint(r, pltpu.HBM) for r in raw))


def copies(pairs, semaphores):
    started = [pltpu.make_async_copy(*pair, semaphores.at[i]) for i, pair in enumerate(pairs)]
    for copy in started:
        copy.start()
    return started


def slot_rows(places):
    return [places[r : r + 1, :] for r in range(places.shape[0])]


def pick(vector, rows):
    index = jnp.concatenate(rows, axis=0)
    low = jnp.bitwise_and(index, LANES - 1)
    high = jnp.right_shift(index, 7)
    out = jnp.zeros(index.shape, F32)
    for t in range(vector.shape[0]):
        spread = jnp.broadcast_to(vector[t : t + 1, :], index.shape)
        got = jnp.take_along_axis(spread, low, axis=1, mode="promise_in_bounds")
        out = jnp.where(high == t, got, out)
    return out


def pieces(value):
    first = value.astype(BF16)
    rest = value - first.astype(F32)
    second = rest.astype(BF16)
    third = (rest - second.astype(F32)).astype(BF16)
    return first, second, third


def low_hits(rows):
    lane = lax.broadcasted_iota(jnp.int32, (LANES, LANES), 0)
    return jnp.concatenate(
        [(lane == jnp.bitwise_and(row, LANES - 1)).astype(F32).astype(BF16) for row in rows], axis=1
    )


def spread_sum(values, rows, tiles):
    tile = lax.broadcasted_iota(jnp.int32, (tiles, LANES), 0)
    parts = [
        jnp.where(tile == jnp.right_shift(row, 7), value, 0.0) for value, row in zip(values, rows)
    ]
    held = jnp.concatenate(parts, axis=1)
    stacked = jnp.concatenate([p.astype(F32) for p in pieces(held)], axis=0).astype(BF16)
    out = lax.dot_general(
        stacked, low_hits(rows), (((1,), (1,)), ((), ())), preferred_element_type=F32
    )
    return out[:tiles] + out[tiles : 2 * tiles] + out[2 * tiles :]


def arrived_rows(refs):
    return [ref[h : h + 1, :] for ref in refs for h in range(ref.shape[0])]


def store_sent(refs, sent):
    per = refs[0].shape[0]
    for k, ref in enumerate(refs):
        ref[...] = sent[k * per : (k + 1) * per, :]


def lane_rows(vector):
    return jnp.concatenate([vector[t : t + 1, :] for t in range(vector.shape[0])], axis=1)


def tile_rows_of(row):
    return jnp.concatenate(
        [row[:, t * LANES : (t + 1) * LANES] for t in range(row.shape[1] // LANES)], axis=0
    )


def fill_hits(hits, rows, first, last):
    nodes = hits.shape[0]
    node = lax.broadcasted_iota(jnp.int32, (nodes, LANES), 0).astype(jnp.int16).reshape(nodes // 16, 16, LANES)
    one, zero = jnp.ones(node.shape, BF16), jnp.zeros(node.shape, BF16)
    for c in range(first, last):
        wide = jnp.broadcast_to(rows[c], (16, LANES)).astype(jnp.int16)
        at = (c - first) * LANES
        hits[:, at : at + LANES] = jnp.where(node == wide[None], one, zero).reshape(nodes, LANES)


def gather_first(
    where, index_in, counts_in, state_in, lat, hits, places, sent, index, counts, state, sems
):
    first, second, third = copies(((index_in, index), (counts_in, counts), (state_in, state)), sems)
    per = index.shape[2] // LANES
    first.wait()
    second.wait()
    for g in range(index.shape[1]):
        side = where[g]
        for h in range(per):
            span = slice(h * LANES, (h + 1) * LANES)
            row = index[0, 0:1, span]
            for k in range(1, index.shape[1]):
                row = jnp.where(side == k, index[0, k : k + 1, span], row)
            slot = lax.broadcasted_iota(jnp.int32, (1, LANES), 1) + h * LANES
            r = g * per + h
            places[r : r + 1, :] = jnp.where(slot < counts[0, side], row, -1)
    fill_hits(hits, slot_rows(places), 0, per)
    third.wait()
    lat[...] = state[...].T
    send_features(lat[...], hits, (sent,))


def gather_rest(places, lat, gains_in, bias_in, decode_in, hits, columns, s1, s2, s3, gains, bias, decode, sems):
    waits = copies(((gains_in, gains), (bias_in, bias), (decode_in, decode)), sems)
    rows = slot_rows(places)
    fill_hits(hits, rows, len(rows) // 4, len(rows))
    send_features(lat[...], hits, (s1, s2, s3))
    for copy in waits:
        copy.wait()
    lines = [gains[layer] for layer in range(LAYERS)] + [bias[...], decode[...]]
    lines.append(jnp.zeros((8 - 3 * LAYERS - 1, bias.shape[1]), F32))
    columns[...] = jnp.concatenate(lines, axis=0).T


def send_features(lat, hits, outs):
    width = outs[0].shape[1]
    for k, out in enumerate(outs):
        out[...] = jnp.dot(
            lat, hits[:, k * width : (k + 1) * width], preferred_element_type=F32
        ).astype(BF16)


def send_rest(lat, hits, s1, s2, s3):
    send_features(lat[...], hits, (s1, s2, s3))


def build(
    tile_counts, places, tiles, lat, w_self, columns, rows_in, columns_in, capacity_in,
    matrix, half, inverse_rowsum, diagonal, local, own,
    tile_rows, tile_columns, capacity, sems,
):
    waits = copies(((rows_in, tile_rows), (columns_in, tile_columns), (capacity_in, capacity)), sems)
    count = tiles.shape[2]
    node_tiles = matrix.shape[0] // count
    matrix[...] = jnp.zeros(matrix.shape, F32)
    for t in range(node_tiles):
        span = slice(t * count, (t + 1) * count)
        block = tiles[0, t]
        matrix[span, span] = block + block.T
    for copy in waits:
        copy.wait()

    known = tiles.shape[1]
    live = tile_counts[0]
    together = 4

    def add(step, carry):
        for k in range(together):
            t = node_tiles + step * together + k
            at = jnp.minimum(t, known - 1)
            r = pl.multiple_of(tile_rows[0, at] * count, count)
            c = pl.multiple_of(tile_columns[0, at] * count, count)
            block = jnp.where(t < live, tiles[0, at], 0.0)
            matrix[pl.ds(r, count), pl.ds(c, count)] += block
            matrix[pl.ds(c, count), pl.ds(r, count)] += block.T
        return carry

    lax.fori_loop(0, (live - node_tiles + together - 1) // together, add, 0)
    rows = slot_rows(places)
    faces = spread_sum([jnp.ones((1, LANES), F32)] * len(rows), rows, node_tiles)
    total = jnp.zeros((8, matrix.shape[1]), F32)
    for t in range(node_tiles):
        block = matrix[t * count : (t + 1) * count, :]
        half[t * count : (t + 1) * count, :] = block.astype(BF16)
        total = total + jnp.sum(block.reshape(count // 8, 8, matrix.shape[1]), axis=0)
    rowsum = tile_rows_of(jnp.sum(total, axis=0, keepdims=True)) + faces
    inverse_rowsum[...] = lane_rows(1.0 / rowsum)
    diagonal[...] = capacity[...] + rowsum
    local[...] = jnp.dot(lat[...], half[...], preferred_element_type=F32)
    own[...] = own_part(0, lat[...], w_self, columns)


def normed(value, gain):
    scale = lax.rsqrt(jnp.mean(value * value, axis=0, keepdims=True) + 1e-06)
    return (value * scale * gain).astype(BF16)


def project(weight, value):
    return lax.dot_general(weight, value, (((0,), (0,)), ((), ())), preferred_element_type=F32)


def own_part(layer, lat, w_self, columns):
    gain = columns[:, 2 * layer : 2 * layer + 1]
    bias = columns[:, 2 * LAYERS + layer : 2 * LAYERS + layer + 1]
    return project(w_self[layer], normed(lat.astype(F32), gain)) + bias


def local_features(layer, lat, half, w_self, w_out, columns, local, own, before, decoder):
    local[...] = jnp.dot(lat[...], half[...], preferred_element_type=F32)
    own[...] = own_part(layer, lat[...], w_self, columns)
    decode = columns[:, 3 * LAYERS : 3 * LAYERS + 1]
    before[...] = jnp.sum(lat[...].astype(F32) * decode, axis=0, keepdims=True)
    line = jnp.broadcast_to(decode, (decode.shape[0], LANES)).T[0:1, :]
    decoder[...] = jnp.sum(w_out[layer].astype(F32) * line, axis=1, keepdims=True)


def with_slots(local, came, hits):
    return local + lax.dot_general(came, hits, (((1,), (1,)), ((), ())), preferred_element_type=F32)


def activation(layer, arrived, local, own, inverse_rowsum, first_hits, hits, w_neighbour, columns):
    total = with_slots(local[...], arrived[0][...], first_hits[...])
    total = with_slots(total, jnp.concatenate([a[...] for a in arrived[1:]], axis=1), hits[...])
    mean = total * inverse_rowsum[...]
    gain = columns[:, 2 * layer + 1 : 2 * layer + 2]
    linear = own[...] + project(w_neighbour[layer], normed(mean, gain))
    return linear / (1.0 + jnp.exp(-linear))


def first_layer(
    a0, a1, a2, a3, local, own, inverse_rowsum, lat, first_hits, hits, w_neighbour, w_out, columns, new, sent
):
    activated = activation(
        0, (a0, a1, a2, a3), local, own, inverse_rowsum, first_hits, hits, w_neighbour, columns
    ).astype(BF16)
    value = (lat[...].astype(F32) + project(w_out[0], activated)).astype(BF16)
    new[...] = value
    send_features(value, first_hits, (sent,))


def last_layer(
    places, a0, a1, a2, a3, local, own, inverse_rowsum, lat, first_hits, hits, w_neighbour, columns, before, decoder,
    guess, s0, s1, s2, s3,
):
    activated = activation(
        LAYERS - 1, (a0, a1, a2, a3), local, own, inverse_rowsum, first_hits, hits, w_neighbour, columns
    ).astype(BF16)
    row = before[...] + jnp.sum(activated.astype(F32) * decoder[...], axis=0, keepdims=True)
    field = tile_rows_of(row)
    guess[...] = field
    store_sent((s0, s1, s2, s3), pick(field, slot_rows(places)))


def product(matrix, field):
    count = LANES
    width = matrix.shape[1]
    total = jnp.zeros((8, width), F32)
    for t in range(field.shape[0]):
        column = jnp.broadcast_to(field[t : t + 1, :], (count, count)).T
        wide = jnp.concatenate([column] * (width // count), axis=1)
        part = matrix[t * count : (t + 1) * count, :] * wide
        total = total + jnp.sum(part.reshape(count // 8, 8, width), axis=0)
    return tile_rows_of(jnp.sum(total, axis=0, keepdims=True))


def matvec(matrix, vector, out):
    out[...] = product(matrix, vector[...])


def start_basis(places, a0, a1, a2, a3, local, guess, source, diagonal, basis, s0, s1, s2, s3):
    rows = slot_rows(places)
    came = spread_sum(arrived_rows((a0, a1, a2, a3)), rows, guess.shape[0])
    value = (source[...] + local[...] + came) / diagonal[...] - guess[...]
    basis[...] = value
    store_sent((s0, s1, s2, s3), pick(value, rows))


def next_basis(places, a0, a1, a2, a3, local, diagonal, basis, s0, s1, s2, s3):
    rows = slot_rows(places)
    came = spread_sum(arrived_rows((a0, a1, a2, a3)), rows, local.shape[0])
    value = (local[...] + came) / diagonal[...]
    basis[...] = value
    store_sent((s0, s1, s2, s3), pick(value, rows))


def diagonal_mask():
    return lax.broadcasted_iota(jnp.int32, (8, LANES), 0) == lax.broadcasted_iota(jnp.int32, (8, LANES), 1)


def last_basis(places, a0, a1, a2, a3, local, diagonal, b0, b1, matrix, basis, image, packets):
    rows = slot_rows(places)
    came = spread_sum(arrived_rows((a0, a1, a2, a3)), rows, local.shape[0])
    value = (local[...] + came) / diagonal[...]
    basis[...] = value
    mapped = product(matrix, value)
    image[...] = mapped
    held = [b0[...], b1[...], value]
    parts = []
    for k in range(2 * ITERS - 1):
        left, right = held[k // 2], held[(k + 1) // 2]
        parts.append(jnp.sum(left * right * diagonal[...], axis=0, keepdims=True))
    parts.append(jnp.sum(value * mapped, axis=0, keepdims=True))
    parts.append(jnp.zeros((8 - 2 * ITERS, LANES), F32))
    sums = jnp.sum(jnp.concatenate(parts, axis=0), axis=1, keepdims=True)
    row = jnp.sum(jnp.where(diagonal_mask(), sums, 0.0), axis=0, keepdims=True)
    packet = jnp.concatenate([lane_rows(pick(value, rows)), row], axis=1)
    for device in range(packets.shape[0]):
        packets[device] = packet


def added(values):
    values = list(values)
    while len(values) > 1:
        values = [sum(values[i : i + 2][1:], values[i]) for i in range(0, len(values), 2)]
    return values[0]


def finish(sizes, where, packets, places, image, guess, diagonal, b0, b1, b2, field, defect):
    doms, subs = sizes
    width = packets.shape[2] - LANES
    per = width // 4

    def slots(device, g):
        return packets[device, :, g * per : (g + 1) * per]

    edges = []
    for d in range(doms):
        for s in range(subs):
            for m, (i, j) in (((0, d % 2), (d + 1, s)), ((1, s % 2), (d, s + 1))):
                g = MATCHINGS.index(m)
                if i < doms and j < subs:
                    edges.append(slots(d * subs + s, g) * slots(i * subs + j, g))
    edges = added(edges)
    edges = added([edges[:, h : h + LANES] for h in range(0, per, LANES)])
    sums = added([packets[e, :, width : width + LANES] for e in range(doms * subs)])
    last_row = lax.broadcasted_iota(jnp.int32, (8, LANES), 0) == 2 * ITERS - 1
    table = jnp.where(diagonal_mask(), jnp.broadcast_to(sums, (8, LANES)), 0.0)
    table = table + jnp.where(last_row, jnp.broadcast_to(2.0 * edges, (8, LANES)), 0.0)
    columns = jnp.sum(table, axis=1, keepdims=True)
    n = [jnp.broadcast_to(columns[k : k + 1, :], (8, LANES)) for k in range(2 * ITERS)]
    came = []
    for g in range(4):
        mine = slots(where[4 + g], g)
        came += [mine[:, h : h + LANES] for h in range(0, per, LANES)]
    last = (image[...] + spread_sum(came, slot_rows(places), image.shape[0])) / diagonal[...]
    one, zero = jnp.ones((8, LANES), F32), jnp.zeros((8, LANES), F32)

    def paired(left, values):
        total = zero
        for i, a in enumerate(left):
            for j, b in enumerate(left):
                total = total + a * b * values[i + j]
        return total

    gaps = [n[k] - n[k + 1] for k in range(2 * ITERS - 1)]
    residual = [one]
    heading = [one]
    moved = [zero] * ITERS
    size = n[0]
    for step in range(ITERS):
        alpha = size / paired(heading, gaps)
        for i, h in enumerate(heading):
            moved[i] = moved[i] + alpha * h
        change = [
            (heading[i] if i < len(heading) else zero) - (heading[i - 1] if i > 0 else zero)
            for i in range(len(heading) + 1)
        ]
        residual = [
            (residual[i] if i < len(residual) else zero) - alpha * change[i]
            for i in range(len(change))
        ]
        if step + 1 < ITERS:
            following = paired(residual, n)
            beta = following / size
            heading = [
                residual[i] + (beta * heading[i] if i < len(heading) else zero)
                for i in range(len(residual))
            ]
            size = following
    held = [b0[...], b1[...], b2[...], last]
    total = guess[...]
    for c, b in zip(moved, held):
        total = total + c * b
    field[...] = total
    left = zero
    for c, b in zip(residual, held):
        left = left + c * b
    defect[...] = left * diagonal[...]


def mate_of(place, first, size):
    mate = ((place - first) ^ 1) + first
    return mate if place >= first and mate < size else None


def swaps(sizes, turn):
    along, first = MATCHINGS[turn]
    pairs = []
    for dom in range(sizes[0]):
        for sub in range(sizes[1]):
            to = [dom, sub]
            mate = mate_of(to[along], first, sizes[along])
            if mate is not None:
                to[along] = mate
            elif along == 1 and sizes[0] % 2 == 0:
                to[0] ^= 1
            elif along == 0 and sizes[1] % 2 == 0:
                to[1] = (sub + sizes[1] // 2) % sizes[1]
            pairs.append((dom * sizes[1] + sub, to[0] * sizes[1] + to[1]))
    return pairs


def places_of_turns():
    at = [lax.axis_index("dom"), lax.axis_index("sub")]
    sizes = [lax.axis_size("dom"), lax.axis_size("sub")]

    def side(along, first):
        odd = at[along] % 2
        return 2 * along + (odd if first else 1 - odd)

    def partner(along, first):
        mate = jnp.bitwise_xor(at[along] - first, 1) + first
        to = list(at)
        to[along] = jnp.where((at[along] >= first) & (mate < sizes[along]), mate, at[along])
        return to[0] * sizes[1] + to[1]

    out = [value(*m) for value in (side, partner) for m in MATCHINGS]
    return jnp.stack(out).astype(jnp.int32)


def swap(sent, turn):
    axes = ("dom", "sub")
    return lax.ppermute(sent, axes, swaps([lax.axis_size(axis) for axis in axes], turn))


def exchange(sent, first=0):
    return [swap(s, first + i) for i, s in enumerate(sent)]


def all_to_all(messages):
    return lax.all_to_all(messages, ("dom", "sub"), split_axis=0, concat_axis=0, tiled=True)


def per_device(
    state, tile_values, tile_rows, tile_columns, tile_counts, send_nodes, face_counts, capacity,
    source, w_self, w_neighbour, w_out, gains, bias, w_decode,
):
    nodes, width = state.shape
    slots = send_nodes.shape[2]
    tiles = nodes // LANES
    sizes = (lax.axis_size("dom"), lax.axis_size("sub"))
    devices = sizes[0] * sizes[1]
    field = shape((tiles, LANES))
    features = shape((width, nodes))
    vector_sent = [shape((slots // LANES, LANES))] * 4
    decode = w_decode.reshape(1, width)
    where = places_of_turns()
    capacity = capacity.reshape(tiles, LANES)
    source = source.reshape(tiles, LANES)

    one_sent = [shape((width, slots), BF16)]
    gather_flops = 2 * nodes * slots * width
    lat, first_hits, places, sent = run(
        gather_first,
        [shape((width, nodes), BF16), shape((nodes, slots), BF16), shape((4 * slots // LANES, LANES), jnp.int32)]
        + one_sent,
        (), (where,), (send_nodes, face_counts, state),
        (
            pltpu.VMEM(send_nodes.shape, jnp.int32),
            pltpu.SMEM(face_counts.shape, jnp.int32),
            pltpu.VMEM(state.shape, BF16),
        ),
        waits=3, flops=gather_flops,
    )
    a0 = swap(sent, 0)
    hits, columns, *sent = run(
        gather_rest, [shape((nodes, 3 * slots), BF16), shape((width, 8))] + one_sent * 3,
        (places, lat), (), (gains, bias, decode),
        (pltpu.VMEM(gains.shape, F32), pltpu.VMEM(bias.shape, F32), pltpu.VMEM(decode.shape, F32)),
        waits=3, flops=3 * gather_flops,
    )
    a1, a2, a3 = exchange(sent, 1)
    matrix, half, inverse_rowsum, diagonal, local, own = run(
        build,
        [shape((nodes, nodes)), shape((nodes, nodes), BF16), shape((1, nodes)), field, features, features],
        (places, tile_values, lat, w_self, columns),
        (tile_counts,), (tile_rows, tile_columns, capacity),
        (
            pltpu.SMEM(tile_rows.shape, jnp.int32),
            pltpu.SMEM(tile_columns.shape, jnp.int32),
            pltpu.VMEM(capacity.shape, F32),
        ),
        waits=3, flops=0, moved=0,
    )
    lat, sent = run(
        first_layer, [shape((width, nodes), BF16)] + one_sent,
        (a0, a1, a2, a3, local, own, inverse_rowsum, lat, first_hits, hits, w_neighbour, w_out, columns),
        flops=3 * nodes * nodes * width,
    )
    a0 = swap(sent, 0)
    sent = run(send_rest, one_sent * 3, (lat, hits), flops=3 * gather_flops)
    a1, a2, a3 = exchange(sent, 1)
    local, own, before, decoder = run(
        functools.partial(local_features, LAYERS - 1),
        [features, features, shape((1, nodes)), shape((width, 1))],
        (lat, half, w_self, w_out, columns), flops=0, moved=0,
    )
    guess, *sent = run(
        last_layer, [field] + vector_sent,
        (places, a0, a1, a2, a3, local, own, inverse_rowsum, lat, first_hits, hits, w_neighbour, columns, before, decoder),
        flops=3 * nodes * nodes * width,
    )

    def mapped(vector):
        return run(matvec, [field], (matrix, vector), flops=2 * nodes * nodes, moved=4 * nodes * nodes)[0]

    arrived = exchange(sent)
    local = mapped(guess)
    b0, *sent = run(
        start_basis, [field] + vector_sent, (places, *arrived, local, guess, source, diagonal)
    )
    arrived = exchange(sent)
    local = mapped(b0)
    b1, *sent = run(next_basis, [field] + vector_sent, (places, *arrived, local, diagonal))
    arrived = exchange(sent)
    local = mapped(b1)
    b2, image, packets = run(
        last_basis, [field, field, shape((devices, 1, 4 * slots + LANES))],
        (places, *arrived, local, diagonal, b0, b1, matrix),
    )
    packets = all_to_all(packets)
    heat, defect = run(
        functools.partial(finish, sizes), [field, field],
        (packets, places, image, guess, diagonal, b0, b1, b2), (where,),
    )
    return heat.reshape(nodes), defect.reshape(nodes)


def solution(mesh):
    both = ("dom", "sub")
    return jax.shard_map(
        per_device,
        mesh=mesh,
        in_specs=(
            P(both, None),
            P(both, None, None, None),
            P(both, None),
            P(both, None),
            P(both),
            P(both, None, None),
            P(both, None),
            P(both),
            P(both),
            P(),
            P(),
            P(),
            P(),
            P(),
            P(),
        ),
        out_specs=(P(both), P(both)),
        check_vma=False,
    )
```

```python
import functools

import jax
import jax.numpy as jnp
from jax import lax
from jax.experimental import pallas as pl
from jax.experimental.pallas import tpu as pltpu
from jax.sharding import PartitionSpec as P

LAYERS = 2
ITERS = 3
LANES = 128
MATCHINGS = ((1, 1), (1, 0), (0, 1), (0, 0))
VMEM_LIMIT = 24 * 1024 * 1024

F32 = jnp.float32
BF16 = jnp.bfloat16


def shape(dims, dtype=F32):
    return jax.ShapeDtypeStruct(dims, dtype)


def run(body, outs, operands, scalars=(), raw=(), scratch=(), waits=0, flops=1_000_000, moved=1_000_000, aliases={}):
    operands = [
        pltpu.with_memory_space_constraint(x, pltpu.VMEM) if i in aliases else x for i, x in enumerate(operands)
    ]
    smem = pl.BlockSpec(memory_space=pltpu.SMEM)
    vmem = pl.BlockSpec(memory_space=pltpu.VMEM)
    anywhere = pl.BlockSpec(memory_space=pltpu.HBM)
    scratch = list(scratch) + [pltpu.SemaphoreType.DMA((waits,))] * bool(waits)
    return pl.pallas_call(
        body,
        out_shape=outs,
        in_specs=[smem] * len(scalars) + [vmem] * len(operands) + [anywhere] * len(raw),
        out_specs=[vmem] * len(outs),
        scratch_shapes=scratch,
        input_output_aliases={len(scalars) + i: o for i, o in aliases.items()},
        compiler_params=pltpu.CompilerParams(vmem_limit_bytes=VMEM_LIMIT),
        cost_estimate=pl.CostEstimate(flops=flops, bytes_accessed=moved, transcendentals=0),
    )(*scalars, *operands, *(pltpu.with_memory_space_constraint(r, pltpu.HBM) for r in raw))


def copies(pairs, semaphores):
    started = [pltpu.make_async_copy(*pair, semaphores.at[i]) for i, pair in enumerate(pairs)]
    for copy in started:
        copy.start()
    return started


def slot_rows(places):
    return [places[r : r + 1, :] for r in range(places.shape[0])]


def pick(vector, rows):
    index = jnp.concatenate(rows, axis=0)
    low = jnp.bitwise_and(index, LANES - 1)
    high = jnp.right_shift(index, 7)
    out = jnp.zeros(index.shape, F32)
    for t in range(vector.shape[0]):
        spread = jnp.broadcast_to(vector[t : t + 1, :], index.shape)
        got = jnp.take_along_axis(spread, low, axis=1, mode="promise_in_bounds")
        out = jnp.where(high == t, got, out)
    return out


def pieces(value):
    first = value.astype(BF16)
    rest = value - first.astype(F32)
    second = rest.astype(BF16)
    third = (rest - second.astype(F32)).astype(BF16)
    return first, second, third


def low_hits(rows):
    lane = lax.broadcasted_iota(jnp.int32, (LANES, LANES), 0)
    return jnp.concatenate(
        [(lane == jnp.bitwise_and(row, LANES - 1)).astype(F32).astype(BF16) for row in rows], axis=1
    )


def spread_sum(values, rows, tiles):
    tile = lax.broadcasted_iota(jnp.int32, (tiles, LANES), 0)
    parts = [
        jnp.where(tile == jnp.right_shift(row, 7), value, 0.0) for value, row in zip(values, rows)
    ]
    held = jnp.concatenate(parts, axis=1)
    stacked = jnp.concatenate([p.astype(F32) for p in pieces(held)], axis=0).astype(BF16)
    out = lax.dot_general(
        stacked, low_hits(rows), (((1,), (1,)), ((), ())), preferred_element_type=F32
    )
    return out[:tiles] + out[tiles : 2 * tiles] + out[2 * tiles :]


def arrived_rows(refs):
    return [ref[h : h + 1, :] for ref in refs for h in range(ref.shape[0])]


def store_sent(refs, sent):
    per = refs[0].shape[0]
    for k, ref in enumerate(refs):
        ref[...] = sent[k * per : (k + 1) * per, :]


def lane_rows(vector):
    return jnp.concatenate([vector[t : t + 1, :] for t in range(vector.shape[0])], axis=1)


def tile_rows_of(row):
    return jnp.concatenate(
        [row[:, t * LANES : (t + 1) * LANES] for t in range(row.shape[1] // LANES)], axis=0
    )


def fill_hits(hits, rows, first, last):
    nodes = hits.shape[0]
    node = lax.broadcasted_iota(jnp.int32, (nodes, LANES), 0).astype(jnp.int16).reshape(nodes // 16, 16, LANES)
    one, zero = jnp.ones(node.shape, BF16), jnp.zeros(node.shape, BF16)
    for c in range(first, last):
        wide = jnp.broadcast_to(rows[c], (16, LANES)).astype(jnp.int16)
        at = (c - first) * LANES
        hits[:, at : at + LANES] = jnp.where(node == wide[None], one, zero).reshape(nodes, LANES)


def gather_first(
    where, index_in, counts_in, state_in, lat, hits, places, sent, blank, index, counts, state, sems
):
    first, second, third = copies(((index_in, index), (counts_in, counts), (state_in, state)), sems)
    blank[...] = jnp.zeros(blank.shape, F32)
    per = index.shape[2] // LANES
    first.wait()
    second.wait()
    for g in range(index.shape[1]):
        side = where[g]
        for h in range(per):
            span = slice(h * LANES, (h + 1) * LANES)
            row = index[0, 0:1, span]
            for k in range(1, index.shape[1]):
                row = jnp.where(side == k, index[0, k : k + 1, span], row)
            slot = lax.broadcasted_iota(jnp.int32, (1, LANES), 1) + h * LANES
            r = g * per + h
            places[r : r + 1, :] = jnp.where(slot < counts[0, side], row, -1)
    fill_hits(hits, slot_rows(places), 0, per)
    third.wait()
    lat[...] = state[...].T
    send_features(lat[...], hits, (sent,))


def gather_rest(
    places, lat, gains_in, bias_in, decode_in, rows_in, columns_in, capacity_in,
    hits, columns, tile_rows, tile_columns, capacity, s1, s2, s3, gains, bias, decode, sems,
):
    waits = copies(
        (
            (gains_in, gains), (bias_in, bias), (decode_in, decode), (rows_in, tile_rows),
            (columns_in, tile_columns), (capacity_in, capacity),
        ),
        sems,
    )
    rows = slot_rows(places)
    fill_hits(hits, rows, len(rows) // 4, len(rows))
    send_features(lat[...], hits, (s1, s2, s3))
    for copy in waits:
        copy.wait()
    lines = [gains[layer] for layer in range(LAYERS)] + [bias[...], decode[...]]
    lines.append(jnp.zeros((8 - 3 * LAYERS - 1, bias.shape[1]), F32))
    columns[...] = jnp.concatenate(lines, axis=0).T


def send_features(lat, hits, outs):
    width = outs[0].shape[1]
    for k, out in enumerate(outs):
        out[...] = jnp.dot(
            lat, hits[:, k * width : (k + 1) * width], preferred_element_type=F32
        ).astype(BF16)


def send_rest(lat, hits, s1, s2, s3):
    send_features(lat[...], hits, (s1, s2, s3))


def build(
    tile_counts, blank, places, tiles, lat, w_self, columns, rows_in, columns_in, capacity,
    matrix, half, inverse_rowsum, diagonal, local, own,
    tile_rows, tile_columns, sems,
):
    waits = copies(((rows_in, tile_rows), (columns_in, tile_columns)), sems)
    count = tiles.shape[2]
    node_tiles = matrix.shape[0] // count
    for t in range(node_tiles):
        span = slice(t * count, (t + 1) * count)
        block = tiles[0, t]
        matrix[span, span] = block + block.T
    for copy in waits:
        copy.wait()

    known = tiles.shape[1]
    live = tile_counts[0]
    together = 4

    def add(step, carry):
        for k in range(together):
            t = node_tiles + step * together + k
            at = jnp.minimum(t, known - 1)
            r = pl.multiple_of(tile_rows[0, at] * count, count)
            c = pl.multiple_of(tile_columns[0, at] * count, count)
            block = jnp.where(t < live, tiles[0, at], 0.0)
            matrix[pl.ds(r, count), pl.ds(c, count)] += block
            matrix[pl.ds(c, count), pl.ds(r, count)] += block.T
        return carry

    lax.fori_loop(0, (live - node_tiles + together - 1) // together, add, 0)
    rows = slot_rows(places)
    faces = spread_sum([jnp.ones((1, LANES), F32)] * len(rows), rows, node_tiles)
    total = jnp.zeros((8, matrix.shape[1]), F32)
    for t in range(node_tiles):
        block = matrix[t * count : (t + 1) * count, :]
        half[t * count : (t + 1) * count, :] = block.astype(BF16)
        total = total + jnp.sum(block.reshape(count // 8, 8, matrix.shape[1]), axis=0)
    rowsum = tile_rows_of(jnp.sum(total, axis=0, keepdims=True)) + faces
    inverse_rowsum[...] = lane_rows(1.0 / rowsum)
    diagonal[...] = capacity[...] + rowsum
    local[...] = jnp.dot(lat[...], half[...], preferred_element_type=F32)
    own[...] = own_part(0, lat[...], w_self, columns)


def normed(value, gain):
    scale = lax.rsqrt(jnp.mean(value * value, axis=0, keepdims=True) + 1e-06)
    return (value * scale * gain).astype(BF16)


def project(weight, value):
    return lax.dot_general(weight, value, (((0,), (0,)), ((), ())), preferred_element_type=F32)


def own_part(layer, lat, w_self, columns):
    gain = columns[:, 2 * layer : 2 * layer + 1]
    bias = columns[:, 2 * LAYERS + layer : 2 * LAYERS + layer + 1]
    return project(w_self[layer], normed(lat.astype(F32), gain)) + bias


def local_features(layer, lat, half, w_self, w_out, columns, local, own, before, decoder):
    local[...] = jnp.dot(lat[...], half[...], preferred_element_type=F32)
    own[...] = own_part(layer, lat[...], w_self, columns)
    decode = columns[:, 3 * LAYERS : 3 * LAYERS + 1]
    before[...] = jnp.sum(lat[...].astype(F32) * decode, axis=0, keepdims=True)
    line = jnp.broadcast_to(decode, (decode.shape[0], LANES)).T[0:1, :]
    decoder[...] = jnp.sum(w_out[layer].astype(F32) * line, axis=1, keepdims=True)


def with_slots(local, came, hits):
    return local + lax.dot_general(came, hits, (((1,), (1,)), ((), ())), preferred_element_type=F32)


def activation(layer, arrived, local, own, inverse_rowsum, first_hits, hits, w_neighbour, columns):
    total = with_slots(local[...], arrived[0][...], first_hits[...])
    total = with_slots(total, jnp.concatenate([a[...] for a in arrived[1:]], axis=1), hits[...])
    mean = total * inverse_rowsum[...]
    gain = columns[:, 2 * layer + 1 : 2 * layer + 2]
    linear = own[...] + project(w_neighbour[layer], normed(mean, gain))
    return linear / (1.0 + jnp.exp(-linear))


def first_layer(
    a0, a1, a2, a3, local, own, inverse_rowsum, lat, first_hits, hits, w_neighbour, w_out, columns, new, sent
):
    activated = activation(
        0, (a0, a1, a2, a3), local, own, inverse_rowsum, first_hits, hits, w_neighbour, columns
    ).astype(BF16)
    value = (lat[...].astype(F32) + project(w_out[0], activated)).astype(BF16)
    new[...] = value
    send_features(value, first_hits, (sent,))


def last_layer(
    places, a0, a1, a2, a3, local, own, inverse_rowsum, lat, first_hits, hits, w_neighbour, columns, before, decoder,
    guess, s0, s1, s2, s3,
):
    activated = activation(
        LAYERS - 1, (a0, a1, a2, a3), local, own, inverse_rowsum, first_hits, hits, w_neighbour, columns
    ).astype(BF16)
    row = before[...] + jnp.sum(activated.astype(F32) * decoder[...], axis=0, keepdims=True)
    field = tile_rows_of(row)
    guess[...] = field
    store_sent((s0, s1, s2, s3), pick(field, slot_rows(places)))


def product(matrix, field):
    count = LANES
    width = matrix.shape[1]
    total = jnp.zeros((8, width), F32)
    for t in range(field.shape[0]):
        column = jnp.broadcast_to(field[t : t + 1, :], (count, count)).T
        wide = jnp.concatenate([column] * (width // count), axis=1)
        part = matrix[t * count : (t + 1) * count, :] * wide
        total = total + jnp.sum(part.reshape(count // 8, 8, width), axis=0)
    return tile_rows_of(jnp.sum(total, axis=0, keepdims=True))


def matvec(matrix, vector, out):
    out[...] = product(matrix, vector[...])


def start_basis(places, a0, a1, a2, a3, local, guess, source, diagonal, basis, s0, s1, s2, s3):
    rows = slot_rows(places)
    came = spread_sum(arrived_rows((a0, a1, a2, a3)), rows, guess.shape[0])
    value = (source[...] + local[...] + came) / diagonal[...] - guess[...]
    basis[...] = value
    store_sent((s0, s1, s2, s3), pick(value, rows))


def next_basis(places, a0, a1, a2, a3, local, diagonal, basis, s0, s1, s2, s3):
    rows = slot_rows(places)
    came = spread_sum(arrived_rows((a0, a1, a2, a3)), rows, local.shape[0])
    value = (local[...] + came) / diagonal[...]
    basis[...] = value
    store_sent((s0, s1, s2, s3), pick(value, rows))


def diagonal_mask():
    return lax.broadcasted_iota(jnp.int32, (8, LANES), 0) == lax.broadcasted_iota(jnp.int32, (8, LANES), 1)


def last_basis(places, a0, a1, a2, a3, local, diagonal, b0, b1, matrix, basis, image, packets):
    rows = slot_rows(places)
    came = spread_sum(arrived_rows((a0, a1, a2, a3)), rows, local.shape[0])
    value = (local[...] + came) / diagonal[...]
    basis[...] = value
    mapped = product(matrix, value)
    image[...] = mapped
    held = [b0[...], b1[...], value]
    parts = []
    for k in range(2 * ITERS - 1):
        left, right = held[k // 2], held[(k + 1) // 2]
        parts.append(jnp.sum(left * right * diagonal[...], axis=0, keepdims=True))
    parts.append(jnp.sum(value * mapped, axis=0, keepdims=True))
    parts.append(jnp.zeros((8 - 2 * ITERS, LANES), F32))
    sums = jnp.sum(jnp.concatenate(parts, axis=0), axis=1, keepdims=True)
    row = jnp.sum(jnp.where(diagonal_mask(), sums, 0.0), axis=0, keepdims=True)
    packet = jnp.concatenate([lane_rows(pick(value, rows)), row], axis=1)
    for device in range(packets.shape[0]):
        packets[device] = packet


def added(values):
    values = list(values)
    while len(values) > 1:
        values = [sum(values[i : i + 2][1:], values[i]) for i in range(0, len(values), 2)]
    return values[0]


def finish(sizes, where, packets, places, image, guess, diagonal, b0, b1, b2, field, defect):
    doms, subs = sizes
    width = packets.shape[2] - LANES
    per = width // 4

    def slots(device, g):
        return packets[device, :, g * per : (g + 1) * per]

    edges = []
    for d in range(doms):
        for s in range(subs):
            for m, (i, j) in (((0, d % 2), (d + 1, s)), ((1, s % 2), (d, s + 1))):
                g = MATCHINGS.index(m)
                if i < doms and j < subs:
                    edges.append(slots(d * subs + s, g) * slots(i * subs + j, g))
    edges = added(edges)
    edges = added([edges[:, h : h + LANES] for h in range(0, per, LANES)])
    sums = added([packets[e, :, width : width + LANES] for e in range(doms * subs)])
    last_row = lax.broadcasted_iota(jnp.int32, (8, LANES), 0) == 2 * ITERS - 1
    table = jnp.where(diagonal_mask(), jnp.broadcast_to(sums, (8, LANES)), 0.0)
    table = table + jnp.where(last_row, jnp.broadcast_to(2.0 * edges, (8, LANES)), 0.0)
    columns = jnp.sum(table, axis=1, keepdims=True)
    n = [jnp.broadcast_to(columns[k : k + 1, :], (8, LANES)) for k in range(2 * ITERS)]
    came = []
    for g in range(4):
        mine = slots(where[4 + g], g)
        came += [mine[:, h : h + LANES] for h in range(0, per, LANES)]
    last = (image[...] + spread_sum(came, slot_rows(places), image.shape[0])) / diagonal[...]
    one, zero = jnp.ones((8, LANES), F32), jnp.zeros((8, LANES), F32)

    def paired(left, values):
        total = zero
        for i, a in enumerate(left):
            for j, b in enumerate(left):
                total = total + a * b * values[i + j]
        return total

    gaps = [n[k] - n[k + 1] for k in range(2 * ITERS - 1)]
    residual = [one]
    heading = [one]
    moved = [zero] * ITERS
    size = n[0]
    for step in range(ITERS):
        alpha = size / paired(heading, gaps)
        for i, h in enumerate(heading):
            moved[i] = moved[i] + alpha * h
        change = [
            (heading[i] if i < len(heading) else zero) - (heading[i - 1] if i > 0 else zero)
            for i in range(len(heading) + 1)
        ]
        residual = [
            (residual[i] if i < len(residual) else zero) - alpha * change[i]
            for i in range(len(change))
        ]
        if step + 1 < ITERS:
            following = paired(residual, n)
            beta = following / size
            heading = [
                residual[i] + (beta * heading[i] if i < len(heading) else zero)
                for i in range(len(residual))
            ]
            size = following
    held = [b0[...], b1[...], b2[...], last]
    total = guess[...]
    for c, b in zip(moved, held):
        total = total + c * b
    field[...] = total
    left = zero
    for c, b in zip(residual, held):
        left = left + c * b
    defect[...] = left * diagonal[...]


def mate_of(place, first, size):
    mate = ((place - first) ^ 1) + first
    return mate if place >= first and mate < size else None


def swaps(sizes, turn):
    along, first = MATCHINGS[turn]
    pairs = []
    for dom in range(sizes[0]):
        for sub in range(sizes[1]):
            to = [dom, sub]
            mate = mate_of(to[along], first, sizes[along])
            if mate is not None:
                to[along] = mate
            elif along == 1 and sizes[0] % 2 == 0:
                to[0] ^= 1
            elif along == 0 and sizes[1] % 2 == 0:
                to[1] = (sub + sizes[1] // 2) % sizes[1]
            pairs.append((dom * sizes[1] + sub, to[0] * sizes[1] + to[1]))
    return pairs


def places_of_turns():
    at = [lax.axis_index("dom"), lax.axis_index("sub")]
    sizes = [lax.axis_size("dom"), lax.axis_size("sub")]

    def side(along, first):
        odd = at[along] % 2
        return 2 * along + (odd if first else 1 - odd)

    def partner(along, first):
        mate = jnp.bitwise_xor(at[along] - first, 1) + first
        to = list(at)
        to[along] = jnp.where((at[along] >= first) & (mate < sizes[along]), mate, at[along])
        return to[0] * sizes[1] + to[1]

    out = [value(*m) for value in (side, partner) for m in MATCHINGS]
    return jnp.stack(out).astype(jnp.int32)


def swap(sent, turn):
    axes = ("dom", "sub")
    return lax.ppermute(sent, axes, swaps([lax.axis_size(axis) for axis in axes], turn))


def exchange(sent, first=0):
    return [swap(s, first + i) for i, s in enumerate(sent)]


def all_to_all(messages):
    return lax.all_to_all(messages, ("dom", "sub"), split_axis=0, concat_axis=0, tiled=True)


def per_device(
    state, tile_values, tile_rows, tile_columns, tile_counts, send_nodes, face_counts, capacity,
    source, w_self, w_neighbour, w_out, gains, bias, w_decode,
):
    nodes, width = state.shape
    slots = send_nodes.shape[2]
    tiles = nodes // LANES
    sizes = (lax.axis_size("dom"), lax.axis_size("sub"))
    devices = sizes[0] * sizes[1]
    field = shape((tiles, LANES))
    features = shape((width, nodes))
    vector_sent = [shape((slots // LANES, LANES))] * 4
    decode = w_decode.reshape(1, width)
    where = places_of_turns()
    capacity = capacity.reshape(tiles, LANES)
    source = source.reshape(tiles, LANES)

    one_sent = [shape((width, slots), BF16)]
    square = pltpu.VMEM((nodes, nodes), F32)
    gather_flops = 2 * nodes * slots * width
    lat, first_hits, places, sent, blank = run(
        gather_first,
        [shape((width, nodes), BF16), shape((nodes, slots), BF16), shape((4 * slots // LANES, LANES), jnp.int32)]
        + one_sent + [square],
        (), (where,), (send_nodes, face_counts, state),
        (
            pltpu.VMEM(send_nodes.shape, jnp.int32),
            pltpu.SMEM(face_counts.shape, jnp.int32),
            pltpu.VMEM(state.shape, BF16),
        ),
        waits=3, flops=gather_flops,
    )
    a0 = swap(sent, 0)
    hits, columns, tile_rows, tile_columns, capacity, *sent = run(
        gather_rest,
        [shape((nodes, 3 * slots), BF16), shape((width, 8)), shape(tile_rows.shape, jnp.int32),
         shape(tile_columns.shape, jnp.int32), field] + one_sent * 3,
        (places, lat), (), (gains, bias, decode, tile_rows, tile_columns, capacity),
        (pltpu.VMEM(gains.shape, F32), pltpu.VMEM(bias.shape, F32), pltpu.VMEM(decode.shape, F32)),
        waits=6, flops=3 * gather_flops,
    )
    a1, a2, a3 = exchange(sent, 1)
    matrix, half, inverse_rowsum, diagonal, local, own = run(
        build,
        [square, shape((nodes, nodes), BF16), shape((1, nodes)), field, features, features],
        (blank, places, tile_values, lat, w_self, columns, tile_rows, tile_columns, capacity),
        (tile_counts,), (),
        (
            pltpu.SMEM(tile_rows.shape, jnp.int32),
            pltpu.SMEM(tile_columns.shape, jnp.int32),
        ),
        waits=2, flops=0, moved=0, aliases={0: 0},
    )
    lat, sent = run(
        first_layer, [shape((width, nodes), BF16)] + one_sent,
        (a0, a1, a2, a3, local, own, inverse_rowsum, lat, first_hits, hits, w_neighbour, w_out, columns),
        flops=3 * nodes * nodes * width,
    )
    a0 = swap(sent, 0)
    sent = run(send_rest, one_sent * 3, (lat, hits), flops=3 * gather_flops)
    a1, a2, a3 = exchange(sent, 1)
    local, own, before, decoder = run(
        functools.partial(local_features, LAYERS - 1),
        [features, features, shape((1, nodes)), shape((width, 1))],
        (lat, half, w_self, w_out, columns), flops=0, moved=0,
    )
    guess, *sent = run(
        last_layer, [field] + vector_sent,
        (places, a0, a1, a2, a3, local, own, inverse_rowsum, lat, first_hits, hits, w_neighbour, columns, before, decoder),
        flops=3 * nodes * nodes * width,
    )

    def mapped(vector):
        return run(matvec, [field], (matrix, vector), flops=2 * nodes * nodes, moved=4 * nodes * nodes)[0]

    arrived = exchange(sent)
    local = mapped(guess)
    b0, *sent = run(
        start_basis, [field] + vector_sent, (places, *arrived, local, guess, source, diagonal)
    )
    arrived = exchange(sent)
    local = mapped(b0)
    b1, *sent = run(next_basis, [field] + vector_sent, (places, *arrived, local, diagonal))
    arrived = exchange(sent)
    local = mapped(b1)
    b2, image, packets = run(
        last_basis, [field, field, shape((devices, 1, 4 * slots + LANES))],
        (places, *arrived, local, diagonal, b0, b1, matrix),
    )
    packets = all_to_all(packets)
    heat, defect = run(
        functools.partial(finish, sizes), [field, field],
        (packets, places, image, guess, diagonal, b0, b1, b2), (where,),
    )
    return heat.reshape(nodes), defect.reshape(nodes)


def solution(mesh):
    both = ("dom", "sub")
    return jax.shard_map(
        per_device,
        mesh=mesh,
        in_specs=(
            P(both, None),
            P(both, None, None, None),
            P(both, None),
            P(both, None),
            P(both),
            P(both, None, None),
            P(both, None),
            P(both),
            P(both),
            P(),
            P(),
            P(),
            P(),
            P(),
            P(),
        ),
        out_specs=(P(both), P(both)),
        check_vma=False,
    )
```

```python
import functools

import jax
import jax.numpy as jnp
from jax import lax
from jax.experimental import pallas as pl
from jax.experimental.pallas import tpu as pltpu
from jax.sharding import PartitionSpec as P

LAYERS = 2
ITERS = 3
LANES = 128
MATCHINGS = ((1, 1), (0, 1), (1, 0), (0, 0))
VMEM_LIMIT = 24 * 1024 * 1024

F32 = jnp.float32
BF16 = jnp.bfloat16


def shape(dims, dtype=F32):
    return jax.ShapeDtypeStruct(dims, dtype)


def run(body, outs, operands, scalars=(), raw=(), scratch=(), waits=0, flops=1_000_000, moved=1_000_000):
    smem = pl.BlockSpec(memory_space=pltpu.SMEM)
    vmem = pl.BlockSpec(memory_space=pltpu.VMEM)
    anywhere = pl.BlockSpec(memory_space=pltpu.HBM)
    scratch = list(scratch) + [pltpu.SemaphoreType.DMA((waits,))] * bool(waits)
    return pl.pallas_call(
        body,
        out_shape=outs,
        in_specs=[smem] * len(scalars) + [vmem] * len(operands) + [anywhere] * len(raw),
        out_specs=[vmem] * len(outs),
        scratch_shapes=scratch,
        compiler_params=pltpu.CompilerParams(vmem_limit_bytes=VMEM_LIMIT),
        cost_estimate=pl.CostEstimate(flops=flops, bytes_accessed=moved, transcendentals=0),
    )(*scalars, *operands, *(pltpu.with_memory_space_constraint(r, pltpu.HBM) for r in raw))


def copies(pairs, semaphores):
    started = [pltpu.make_async_copy(*pair, semaphores.at[i]) for i, pair in enumerate(pairs)]
    for copy in started:
        copy.start()
    return started


def slot_rows(places):
    return [places[r : r + 1, :] for r in range(places.shape[0])]


def pick(vector, rows):
    index = jnp.concatenate(rows, axis=0)
    low = jnp.bitwise_and(index, LANES - 1)
    high = jnp.right_shift(index, 7)
    out = jnp.zeros(index.shape, F32)
    for t in range(vector.shape[0]):
        spread = jnp.broadcast_to(vector[t : t + 1, :], index.shape)
        got = jnp.take_along_axis(spread, low, axis=1, mode="promise_in_bounds")
        out = jnp.where(high == t, got, out)
    return out


def pieces(value):
    first = value.astype(BF16)
    rest = value - first.astype(F32)
    second = rest.astype(BF16)
    third = (rest - second.astype(F32)).astype(BF16)
    return first, second, third


def low_hits(rows):
    lane = lax.broadcasted_iota(jnp.int32, (LANES, LANES), 0)
    return jnp.concatenate(
        [(lane == jnp.bitwise_and(row, LANES - 1)).astype(F32).astype(BF16) for row in rows], axis=1
    )


def spread_sum(values, rows, tiles):
    tile = lax.broadcasted_iota(jnp.int32, (tiles, LANES), 0)
    parts = [
        jnp.where(tile == jnp.right_shift(row, 7), value, 0.0) for value, row in zip(values, rows)
    ]
    held = jnp.concatenate(parts, axis=1)
    stacked = jnp.concatenate([p.astype(F32) for p in pieces(held)], axis=0).astype(BF16)
    out = lax.dot_general(
        stacked, low_hits(rows), (((1,), (1,)), ((), ())), preferred_element_type=F32
    )
    return out[:tiles] + out[tiles : 2 * tiles] + out[2 * tiles :]


def arrived_rows(refs):
    return [ref[h : h + 1, :] for ref in refs for h in range(ref.shape[0])]


def store_sent(refs, sent):
    per = refs[0].shape[0]
    for k, ref in enumerate(refs):
        ref[...] = sent[k * per : (k + 1) * per, :]


def lane_rows(vector):
    return jnp.concatenate([vector[t : t + 1, :] for t in range(vector.shape[0])], axis=1)


def tile_rows_of(row):
    return jnp.concatenate(
        [row[:, t * LANES : (t + 1) * LANES] for t in range(row.shape[1] // LANES)], axis=0
    )


def fill_hits(hits, rows, first, last):
    nodes = hits.shape[0]
    node = lax.broadcasted_iota(jnp.int32, (nodes, LANES), 0).astype(jnp.int16).reshape(nodes // 16, 16, LANES)
    one, zero = jnp.ones(node.shape, BF16), jnp.zeros(node.shape, BF16)
    for c in range(first, last):
        wide = jnp.broadcast_to(rows[c], (16, LANES)).astype(jnp.int16)
        at = (c - first) * LANES
        hits[:, at : at + LANES] = jnp.where(node == wide[None], one, zero).reshape(nodes, LANES)


def gather_first(
    where, index_in, counts_in, state_in, lat, hits, places, sent, index, counts, state, sems
):
    first, second, third = copies(((index_in, index), (counts_in, counts), (state_in, state)), sems)
    per = index.shape[2] // LANES
    first.wait()
    second.wait()
    for g in range(index.shape[1]):
        side = where[g]
        for h in range(per):
            span = slice(h * LANES, (h + 1) * LANES)
            row = index[0, 0:1, span]
            for k in range(1, index.shape[1]):
                row = jnp.where(side == k, index[0, k : k + 1, span], row)
            slot = lax.broadcasted_iota(jnp.int32, (1, LANES), 1) + h * LANES
            r = g * per + h
            places[r : r + 1, :] = jnp.where(slot < counts[0, side], row, -1)
    fill_hits(hits, slot_rows(places), 0, per)
    third.wait()
    lat[...] = state[...].T
    send_features(lat[...], hits, (sent,))


def gather_rest(places, lat, gains_in, bias_in, decode_in, hits, columns, s1, s2, s3, gains, bias, decode, sems):
    waits = copies(((gains_in, gains), (bias_in, bias), (decode_in, decode)), sems)
    rows = slot_rows(places)
    fill_hits(hits, rows, len(rows) // 4, len(rows))
    send_features(lat[...], hits, (s1, s2, s3))
    for copy in waits:
        copy.wait()
    lines = [gains[layer] for layer in range(LAYERS)] + [bias[...], decode[...]]
    lines.append(jnp.zeros((8 - 3 * LAYERS - 1, bias.shape[1]), F32))
    columns[...] = jnp.concatenate(lines, axis=0).T


def send_features(lat, hits, outs):
    width = outs[0].shape[1]
    for k, out in enumerate(outs):
        out[...] = jnp.dot(
            lat, hits[:, k * width : (k + 1) * width], preferred_element_type=F32
        ).astype(BF16)


def send_rest(lat, hits, s1, s2, s3):
    send_features(lat[...], hits, (s1, s2, s3))


def build(
    tile_counts, places, tiles, lat, w_self, columns, rows_in, columns_in, capacity_in,
    matrix, half, inverse_rowsum, diagonal, local, own,
    tile_rows, tile_columns, capacity, sems,
):
    waits = copies(((rows_in, tile_rows), (columns_in, tile_columns), (capacity_in, capacity)), sems)
    count = tiles.shape[2]
    node_tiles = matrix.shape[0] // count
    matrix[...] = jnp.zeros(matrix.shape, F32)
    for t in range(node_tiles):
        span = slice(t * count, (t + 1) * count)
        block = tiles[0, t]
        matrix[span, span] = block + block.T
    for copy in waits:
        copy.wait()

    known = tiles.shape[1]
    live = tile_counts[0]
    together = 4

    def add(step, carry):
        for k in range(together):
            t = node_tiles + step * together + k
            at = jnp.minimum(t, known - 1)
            r = pl.multiple_of(tile_rows[0, at] * count, count)
            c = pl.multiple_of(tile_columns[0, at] * count, count)
            block = jnp.where(t < live, tiles[0, at], 0.0)
            matrix[pl.ds(r, count), pl.ds(c, count)] += block
            matrix[pl.ds(c, count), pl.ds(r, count)] += block.T
        return carry

    lax.fori_loop(0, (live - node_tiles + together - 1) // together, add, 0)
    rows = slot_rows(places)
    faces = spread_sum([jnp.ones((1, LANES), F32)] * len(rows), rows, node_tiles)
    total = jnp.zeros((8, matrix.shape[1]), F32)
    for t in range(node_tiles):
        block = matrix[t * count : (t + 1) * count, :]
        half[t * count : (t + 1) * count, :] = block.astype(BF16)
        total = total + jnp.sum(block.reshape(count // 8, 8, matrix.shape[1]), axis=0)
    rowsum = tile_rows_of(jnp.sum(total, axis=0, keepdims=True)) + faces
    inverse_rowsum[...] = lane_rows(1.0 / rowsum)
    diagonal[...] = capacity[...] + rowsum
    local[...] = jnp.dot(lat[...], half[...], preferred_element_type=F32)
    own[...] = own_part(0, lat[...], w_self, columns)


def normed(value, gain):
    scale = lax.rsqrt(jnp.mean(value * value, axis=0, keepdims=True) + 1e-06)
    return (value * scale * gain).astype(BF16)


def project(weight, value):
    return lax.dot_general(weight, value, (((0,), (0,)), ((), ())), preferred_element_type=F32)


def own_part(layer, lat, w_self, columns):
    gain = columns[:, 2 * layer : 2 * layer + 1]
    bias = columns[:, 2 * LAYERS + layer : 2 * LAYERS + layer + 1]
    return project(w_self[layer], normed(lat.astype(F32), gain)) + bias


def local_features(layer, lat, half, w_self, w_out, columns, local, own, before, decoder):
    local[...] = jnp.dot(lat[...], half[...], preferred_element_type=F32)
    own[...] = own_part(layer, lat[...], w_self, columns)
    decode = columns[:, 3 * LAYERS : 3 * LAYERS + 1]
    before[...] = jnp.sum(lat[...].astype(F32) * decode, axis=0, keepdims=True)
    line = jnp.broadcast_to(decode, (decode.shape[0], LANES)).T[0:1, :]
    decoder[...] = jnp.sum(w_out[layer].astype(F32) * line, axis=1, keepdims=True)


def with_slots(local, came, hits):
    return local + lax.dot_general(came, hits, (((1,), (1,)), ((), ())), preferred_element_type=F32)


def activation(layer, arrived, local, own, inverse_rowsum, first_hits, hits, w_neighbour, columns):
    total = with_slots(local[...], arrived[0][...], first_hits[...])
    total = with_slots(total, jnp.concatenate([a[...] for a in arrived[1:]], axis=1), hits[...])
    mean = total * inverse_rowsum[...]
    gain = columns[:, 2 * layer + 1 : 2 * layer + 2]
    linear = own[...] + project(w_neighbour[layer], normed(mean, gain))
    return linear / (1.0 + jnp.exp(-linear))


def first_layer(
    a0, a1, a2, a3, local, own, inverse_rowsum, lat, first_hits, hits, w_neighbour, w_out, columns, new, sent
):
    activated = activation(
        0, (a0, a1, a2, a3), local, own, inverse_rowsum, first_hits, hits, w_neighbour, columns
    ).astype(BF16)
    value = (lat[...].astype(F32) + project(w_out[0], activated)).astype(BF16)
    new[...] = value
    send_features(value, first_hits, (sent,))


def last_layer(
    places, a0, a1, a2, a3, local, own, inverse_rowsum, lat, first_hits, hits, w_neighbour, columns, before, decoder,
    guess, s0, s1, s2, s3,
):
    activated = activation(
        LAYERS - 1, (a0, a1, a2, a3), local, own, inverse_rowsum, first_hits, hits, w_neighbour, columns
    ).astype(BF16)
    row = before[...] + jnp.sum(activated.astype(F32) * decoder[...], axis=0, keepdims=True)
    field = tile_rows_of(row)
    guess[...] = field
    store_sent((s0, s1, s2, s3), pick(field, slot_rows(places)))


def product(matrix, field):
    count = LANES
    width = matrix.shape[1]
    total = jnp.zeros((8, width), F32)
    for t in range(field.shape[0]):
        column = jnp.broadcast_to(field[t : t + 1, :], (count, count)).T
        wide = jnp.concatenate([column] * (width // count), axis=1)
        part = matrix[t * count : (t + 1) * count, :] * wide
        total = total + jnp.sum(part.reshape(count // 8, 8, width), axis=0)
    return tile_rows_of(jnp.sum(total, axis=0, keepdims=True))


def matvec(matrix, vector, out):
    out[...] = product(matrix, vector[...])


def start_basis(places, a0, a1, a2, a3, local, guess, source, diagonal, basis, s0, s1, s2, s3):
    rows = slot_rows(places)
    came = spread_sum(arrived_rows((a0, a1, a2, a3)), rows, guess.shape[0])
    value = (source[...] + local[...] + came) / diagonal[...] - guess[...]
    basis[...] = value
    store_sent((s0, s1, s2, s3), pick(value, rows))


def next_basis(places, a0, a1, a2, a3, local, diagonal, basis, s0, s1, s2, s3):
    rows = slot_rows(places)
    came = spread_sum(arrived_rows((a0, a1, a2, a3)), rows, local.shape[0])
    value = (local[...] + came) / diagonal[...]
    basis[...] = value
    store_sent((s0, s1, s2, s3), pick(value, rows))


def diagonal_mask():
    return lax.broadcasted_iota(jnp.int32, (8, LANES), 0) == lax.broadcasted_iota(jnp.int32, (8, LANES), 1)


def last_basis(places, a0, a1, a2, a3, local, diagonal, b0, b1, matrix, basis, image, packets):
    rows = slot_rows(places)
    came = spread_sum(arrived_rows((a0, a1, a2, a3)), rows, local.shape[0])
    value = (local[...] + came) / diagonal[...]
    basis[...] = value
    mapped = product(matrix, value)
    image[...] = mapped
    held = [b0[...], b1[...], value]
    parts = []
    for k in range(2 * ITERS - 1):
        left, right = held[k // 2], held[(k + 1) // 2]
        parts.append(jnp.sum(left * right * diagonal[...], axis=0, keepdims=True))
    parts.append(jnp.sum(value * mapped, axis=0, keepdims=True))
    parts.append(jnp.zeros((8 - 2 * ITERS, LANES), F32))
    sums = jnp.sum(jnp.concatenate(parts, axis=0), axis=1, keepdims=True)
    row = jnp.sum(jnp.where(diagonal_mask(), sums, 0.0), axis=0, keepdims=True)
    packet = jnp.concatenate([lane_rows(pick(value, rows)), row], axis=1)
    for device in range(packets.shape[0]):
        packets[device] = packet


def added(values):
    values = list(values)
    while len(values) > 1:
        values = [sum(values[i : i + 2][1:], values[i]) for i in range(0, len(values), 2)]
    return values[0]


def finish(sizes, where, packets, places, image, guess, diagonal, b0, b1, b2, field, defect):
    doms, subs = sizes
    width = packets.shape[2] - LANES
    per = width // 4

    def slots(device, g):
        return packets[device, :, g * per : (g + 1) * per]

    edges = []
    for d in range(doms):
        for s in range(subs):
            for m, (i, j) in (((0, d % 2), (d + 1, s)), ((1, s % 2), (d, s + 1))):
                g = MATCHINGS.index(m)
                if i < doms and j < subs:
                    edges.append(slots(d * subs + s, g) * slots(i * subs + j, g))
    edges = added(edges)
    edges = added([edges[:, h : h + LANES] for h in range(0, per, LANES)])
    sums = added([packets[e, :, width : width + LANES] for e in range(doms * subs)])
    last_row = lax.broadcasted_iota(jnp.int32, (8, LANES), 0) == 2 * ITERS - 1
    table = jnp.where(diagonal_mask(), jnp.broadcast_to(sums, (8, LANES)), 0.0)
    table = table + jnp.where(last_row, jnp.broadcast_to(2.0 * edges, (8, LANES)), 0.0)
    columns = jnp.sum(table, axis=1, keepdims=True)
    n = [jnp.broadcast_to(columns[k : k + 1, :], (8, LANES)) for k in range(2 * ITERS)]
    came = []
    for g in range(4):
        mine = slots(where[4 + g], g)
        came += [mine[:, h : h + LANES] for h in range(0, per, LANES)]
    last = (image[...] + spread_sum(came, slot_rows(places), image.shape[0])) / diagonal[...]
    one, zero = jnp.ones((8, LANES), F32), jnp.zeros((8, LANES), F32)

    def paired(left, values):
        total = zero
        for i, a in enumerate(left):
            for j, b in enumerate(left):
                total = total + a * b * values[i + j]
        return total

    gaps = [n[k] - n[k + 1] for k in range(2 * ITERS - 1)]
    residual = [one]
    heading = [one]
    moved = [zero] * ITERS
    size = n[0]
    for step in range(ITERS):
        alpha = size / paired(heading, gaps)
        for i, h in enumerate(heading):
            moved[i] = moved[i] + alpha * h
        change = [
            (heading[i] if i < len(heading) else zero) - (heading[i - 1] if i > 0 else zero)
            for i in range(len(heading) + 1)
        ]
        residual = [
            (residual[i] if i < len(residual) else zero) - alpha * change[i]
            for i in range(len(change))
        ]
        if step + 1 < ITERS:
            following = paired(residual, n)
            beta = following / size
            heading = [
                residual[i] + (beta * heading[i] if i < len(heading) else zero)
                for i in range(len(residual))
            ]
            size = following
    held = [b0[...], b1[...], b2[...], last]
    total = guess[...]
    for c, b in zip(moved, held):
        total = total + c * b
    field[...] = total
    left = zero
    for c, b in zip(residual, held):
        left = left + c * b
    defect[...] = left * diagonal[...]


def mate_of(place, first, size):
    mate = ((place - first) ^ 1) + first
    return mate if place >= first and mate < size else None


def swaps(sizes, turn):
    along, first = MATCHINGS[turn]
    pairs = []
    for dom in range(sizes[0]):
        for sub in range(sizes[1]):
            to = [dom, sub]
            mate = mate_of(to[along], first, sizes[along])
            if mate is not None:
                to[along] = mate
            elif along == 1 and sizes[0] % 2 == 0:
                to[0] ^= 1
            elif along == 0 and sizes[1] % 2 == 0:
                to[1] = (sub + sizes[1] // 2) % sizes[1]
            pairs.append((dom * sizes[1] + sub, to[0] * sizes[1] + to[1]))
    return pairs


def places_of_turns():
    at = [lax.axis_index("dom"), lax.axis_index("sub")]
    sizes = [lax.axis_size("dom"), lax.axis_size("sub")]

    def side(along, first):
        odd = at[along] % 2
        return 2 * along + (odd if first else 1 - odd)

    def partner(along, first):
        mate = jnp.bitwise_xor(at[along] - first, 1) + first
        to = list(at)
        to[along] = jnp.where((at[along] >= first) & (mate < sizes[along]), mate, at[along])
        return to[0] * sizes[1] + to[1]

    out = [value(*m) for value in (side, partner) for m in MATCHINGS]
    return jnp.stack(out).astype(jnp.int32)


def swap(sent, turn):
    axes = ("dom", "sub")
    return lax.ppermute(sent, axes, swaps([lax.axis_size(axis) for axis in axes], turn))


def exchange(sent, first=0):
    return [swap(s, first + i) for i, s in enumerate(sent)]


def all_to_all(messages):
    return lax.all_to_all(messages, ("dom", "sub"), split_axis=0, concat_axis=0, tiled=True)


def per_device(
    state, tile_values, tile_rows, tile_columns, tile_counts, send_nodes, face_counts, capacity,
    source, w_self, w_neighbour, w_out, gains, bias, w_decode,
):
    nodes, width = state.shape
    slots = send_nodes.shape[2]
    tiles = nodes // LANES
    sizes = (lax.axis_size("dom"), lax.axis_size("sub"))
    devices = sizes[0] * sizes[1]
    field = shape((tiles, LANES))
    features = shape((width, nodes))
    vector_sent = [shape((slots // LANES, LANES))] * 4
    decode = w_decode.reshape(1, width)
    where = places_of_turns()
    capacity = capacity.reshape(tiles, LANES)
    source = source.reshape(tiles, LANES)

    one_sent = [shape((width, slots), BF16)]
    gather_flops = 2 * nodes * slots * width
    lat, first_hits, places, sent = run(
        gather_first,
        [shape((width, nodes), BF16), shape((nodes, slots), BF16), shape((4 * slots // LANES, LANES), jnp.int32)]
        + one_sent,
        (), (where,), (send_nodes, face_counts, state),
        (
            pltpu.VMEM(send_nodes.shape, jnp.int32),
            pltpu.SMEM(face_counts.shape, jnp.int32),
            pltpu.VMEM(state.shape, BF16),
        ),
        waits=3, flops=gather_flops,
    )
    a0 = swap(sent, 0)
    hits, columns, *sent = run(
        gather_rest, [shape((nodes, 3 * slots), BF16), shape((width, 8))] + one_sent * 3,
        (places, lat), (), (gains, bias, decode),
        (pltpu.VMEM(gains.shape, F32), pltpu.VMEM(bias.shape, F32), pltpu.VMEM(decode.shape, F32)),
        waits=3, flops=3 * gather_flops,
    )
    a1, a2, a3 = exchange(sent, 1)
    matrix, half, inverse_rowsum, diagonal, local, own = run(
        build,
        [shape((nodes, nodes)), shape((nodes, nodes), BF16), shape((1, nodes)), field, features, features],
        (places, tile_values, lat, w_self, columns),
        (tile_counts,), (tile_rows, tile_columns, capacity),
        (
            pltpu.SMEM(tile_rows.shape, jnp.int32),
            pltpu.SMEM(tile_columns.shape, jnp.int32),
            pltpu.VMEM(capacity.shape, F32),
        ),
        waits=3, flops=0, moved=0,
    )
    lat, sent = run(
        first_layer, [shape((width, nodes), BF16)] + one_sent,
        (a0, a1, a2, a3, local, own, inverse_rowsum, lat, first_hits, hits, w_neighbour, w_out, columns),
        flops=3 * nodes * nodes * width,
    )
    a0 = swap(sent, 0)
    sent = run(send_rest, one_sent * 3, (lat, hits), flops=3 * gather_flops)
    a1, a2, a3 = exchange(sent, 1)
    local, own, before, decoder = run(
        functools.partial(local_features, LAYERS - 1),
        [features, features, shape((1, nodes)), shape((width, 1))],
        (lat, half, w_self, w_out, columns), flops=0, moved=0,
    )
    guess, *sent = run(
        last_layer, [field] + vector_sent,
        (places, a0, a1, a2, a3, local, own, inverse_rowsum, lat, first_hits, hits, w_neighbour, columns, before, decoder),
        flops=3 * nodes * nodes * width,
    )

    def mapped(vector):
        return run(matvec, [field], (matrix, vector), flops=2 * nodes * nodes, moved=4 * nodes * nodes)[0]

    arrived = exchange(sent)
    local = mapped(guess)
    b0, *sent = run(
        start_basis, [field] + vector_sent, (places, *arrived, local, guess, source, diagonal)
    )
    arrived = exchange(sent)
    local = mapped(b0)
    b1, *sent = run(next_basis, [field] + vector_sent, (places, *arrived, local, diagonal))
    arrived = exchange(sent)
    local = mapped(b1)
    b2, image, packets = run(
        last_basis, [field, field, shape((devices, 1, 4 * slots + LANES))],
        (places, *arrived, local, diagonal, b0, b1, matrix),
    )
    packets = all_to_all(packets)
    heat, defect = run(
        functools.partial(finish, sizes), [field, field],
        (packets, places, image, guess, diagonal, b0, b1, b2), (where,),
    )
    return heat.reshape(nodes), defect.reshape(nodes)


def solution(mesh):
    both = ("dom", "sub")
    return jax.shard_map(
        per_device,
        mesh=mesh,
        in_specs=(
            P(both, None),
            P(both, None, None, None),
            P(both, None),
            P(both, None),
            P(both),
            P(both, None, None),
            P(both, None),
            P(both),
            P(both),
            P(),
            P(),
            P(),
            P(),
            P(),
            P(),
        ),
        out_specs=(P(both), P(both)),
        check_vma=False,
    )
```
